32 devices in a mesh: dp: 4 (over y, x), fsdp: 8 (over z, core).
Axes of the slice: x: 2, y: 2, z: 4, core: 2. Of those that a mesh axis runs over, the one named last changes fastest.
Arguments:
- tokens: bfloat16 [16384, 1152], P(('dp', 'fsdp')), may hold values from -6 to 6
- condition: bfloat16 [128, 1152], P(('dp', 'fsdp')), may hold values from -6 to 6
- kept_index: int32 [16384], P(('dp', 'fsdp')), may hold values from 0 to 1023, as said below
- segment: int32 [16384], P(('dp', 'fsdp')), may hold values from 0 to 3, as said below
- grid_side: int32 [128], P(('dp', 'fsdp')), may hold values from 16 to 32, as said below
- ada_weight: bfloat16 [1152, 6912], P('fsdp', 'dp'), may hold values from -0.1875 to 0.1875
- ada_bias: bfloat16 [6912], P(('dp', 'fsdp')), may hold values from -3 to 3
- attn_weight: bfloat16 [1152, 3456], P('fsdp', 'dp'), may hold values from -0.1875 to 0.1875
- attn_bias: bfloat16 [2304], P(('dp', 'fsdp')), may hold values from -1 to 1
- proj_weight: bfloat16 [1152, 1152], P('fsdp', 'dp'), may hold values from -2 to 2
- out_bias: bfloat16 [2304], P(('dp', 'fsdp')), may hold values from -3 to 3
- up_weight: bfloat16 [1152, 4608], P('fsdp', 'dp'), may hold values from -0.1875 to 0.1875
- up_bias: bfloat16 [4608], P(('dp', 'fsdp')), may hold values from -3 to 3
- down_weight: bfloat16 [4608, 1152], P('fsdp', 'dp'), may hold values from -0.09375 to 0.09375
- grad_out: bfloat16 [16384, 1152], P(('dp', 'fsdp')), may hold values from -6 to 6
Outputs:
- mixed: bfloat16 [16384, 1152], P(('dp', 'fsdp'))
- tokens_grad: float32 [16384, 1152], P(('dp', 'fsdp'))
- condition_grad: float32 [128, 1152], P(('dp', 'fsdp'))
- ada_weight_grad: float32 [1152, 6912], P('fsdp', 'dp')
- ada_bias_grad: float32 [6912], P(('dp', 'fsdp'))
- attn_weight_grad: float32 [1152, 3456], P('fsdp', 'dp')
- attn_bias_grad: float32 [2304], P(('dp', 'fsdp'))
- proj_weight_grad: float32 [1152, 1152], P('fsdp', 'dp')
- out_bias_grad: float32 [2304], P(('dp', 'fsdp'))
- up_weight_grad: float32 [1152, 4608], P('fsdp', 'dp')
- up_bias_grad: float32 [4608], P(('dp', 'fsdp'))
- down_weight_grad: float32 [4608, 1152], P('fsdp', 'dp')
The draws below stay inside these ranges and needn't reach their ends.
Inputs may be any that keep to these rules, and one draw needn't show every extreme that they name: `segment`: each device's 512 rows hold whole images in rising slot order: a 512px image is 512 rows of one slot, a 256px image 128 rows of one slot; 512px images come first on a device. Slots without rows may exist on a device. `grid_side`: A slot that holds a 512px image has 32, one that holds a 256px image has 16; a slot without rows has either. `kept_index`: within one image the kept patch numbers are distinct, rise, and lie below the square of its slot's grid_side; every 512px image keeps its last patch.
All inputs are finite; a program needn't handle non-finite values.
Results may differ from the reference program's by a relative error of at most 0.015.
The reference program's roundings to bfloat16 on the way count: a program that leaves them out, or rounds other values in their place, can miss the bound.
Values may be sent and summed in bfloat16 or wider, within the bound.
A program may use at most 384 MiB of HBM per device.

```python
import math
import jax
import jax.numpy as jnp
from jax import lax

D = 1152
HEADS = 16
HEAD_DIM = 72
FF = 4608
TOK_DEV = 512
SIDE_SMALL = 16
SIDE_LARGE = 32
KEEP_SMALL = 128
KEEP_LARGE = 512
SLOTS_DEV = 4
IMAGES = 128
TOKENS = 16384


def image_layout(key):
    device_count = TOKENS // TOK_DEV
    slot_count = TOK_DEV // KEEP_SMALL
    most_large = TOK_DEV // KEEP_LARGE
    large_count = jax.random.randint(jax.random.fold_in(key, 11), (device_count,), 0, most_large + 1)
    shuffled = jax.random.permutation(jax.random.fold_in(key, 12), device_count)
    large_count = large_count.at[shuffled[0]].set(0).at[shuffled[1]].set(most_large)
    row_ids = jnp.arange(TOK_DEV, dtype=jnp.int32)[None, :]
    large_rows = (large_count * KEEP_LARGE)[:, None]
    in_large = row_ids < large_rows
    slot_rows = jnp.where(in_large, row_ids // KEEP_LARGE, large_count[:, None] + (row_ids - large_rows) // KEEP_SMALL)
    within = jnp.where(in_large, row_ids % KEEP_LARGE, (row_ids - large_rows) % KEEP_SMALL)
    used_small = (TOK_DEV - large_count * KEEP_LARGE) // KEEP_SMALL
    slot_ids = jnp.arange(slot_count, dtype=jnp.int32)[None, :]
    coin_flip = jax.random.randint(jax.random.fold_in(key, 13), (device_count, slot_count), 0, 2)
    free_side = jnp.where(coin_flip == 1, SIDE_LARGE, SIDE_SMALL)
    side_table = jnp.where(slot_ids < large_count[:, None], SIDE_LARGE, jnp.where(slot_ids < (large_count + used_small)[:, None], SIDE_SMALL, free_side))
    image_keys = jax.random.split(jax.random.fold_in(key, 14), device_count * slot_count)

    def large_subset(image_key):
        last_patch = SIDE_LARGE * SIDE_LARGE - 1
        others = jax.random.permutation(image_key, last_patch)[:KEEP_LARGE - 1]
        return jnp.sort(jnp.concatenate([others, jnp.full((1,), last_patch, others.dtype)]))

    def small_subset(image_key):
        return jnp.sort(jax.random.permutation(jax.random.fold_in(image_key, 1), SIDE_SMALL * SIDE_SMALL)[:KEEP_SMALL])
    large_kept = jax.vmap(large_subset)(image_keys).reshape(device_count, slot_count * KEEP_LARGE)
    small_kept = jax.vmap(small_subset)(image_keys).reshape(device_count, slot_count * KEEP_SMALL)
    large_pick = jnp.minimum(slot_rows * KEEP_LARGE + within, slot_count * KEEP_LARGE - 1)
    small_pick = jnp.minimum(slot_rows * KEEP_SMALL + within, slot_count * KEEP_SMALL - 1)
    kept_rows = jnp.where(in_large, jnp.take_along_axis(large_kept, large_pick, axis=1), jnp.take_along_axis(small_kept, small_pick, axis=1))
    return (kept_rows.reshape(TOKENS).astype(jnp.int32), slot_rows.reshape(TOKENS).astype(jnp.int32), side_table.reshape(IMAGES).astype(jnp.int32))


def draw_kept_index(key, part):
    layout = image_layout(key)
    return layout[0]


def draw_segment(key, part):
    layout = image_layout(key)
    return layout[1]


def draw_grid_side(key, part):
    layout = image_layout(key)
    return layout[2]


def raised(values, own_key, source, target, parts, factor):
    def block_of(dim):
        return (jnp.arange(values.shape[dim]) // (values.shape[dim] // parts)).reshape((-1,) + (1,) * (values.ndim - 1 - dim))

    first = jax.random.permutation(own_key, parts)[block_of(target)]
    far = (block_of(target) + parts // 2) % parts
    return jnp.where((block_of(source) == first) | (block_of(source) == far), factor * values, values)


def steps_of(stream_key, extent, cuts, smallest, largest):
    level = 1.0
    for position, blocks in cuts:
        draws = jax.random.uniform(jax.random.fold_in(jax.random.fold_in(stream_key, 6), position), (blocks,), jnp.float32, smallest / len(cuts), largest / len(cuts))
        level = level * jnp.repeat(jnp.exp(draws), extent[position] // blocks).reshape((-1,) + (1,) * (len(extent) - 1 - position))
    return level


def gaussian(key, dims, spread, bound, shards=(), kind=jnp.bfloat16):
    factor_of = steps_of(key, dims, shards, -0.22, 0.18) if shards else 1.0
    drawn = jax.random.normal(key, dims, jnp.float32) * spread * factor_of
    return jnp.minimum(jnp.maximum(drawn, -bound), bound).astype(kind)


def gaussian_with(own_key, dims, scale, limit, shards, heavy, kind=jnp.bfloat16):
    values = scale * jax.random.normal(own_key, dims, jnp.float32)
    if shards:
        values = values * steps_of(own_key, dims, shards, -0.22, 0.18)
    return jnp.clip(raised(values, jax.random.fold_in(own_key, 3), *heavy), -limit, limit).astype(kind)


def setup_inputs(seed: int = 0) -> dict:
    seeds = jax.random.split(jax.random.key(seed), 16)
    return {
        "tokens": gaussian(seeds[0], (TOKENS, D), 1.0, 6.0, ((0, 32),)),
        "condition": gaussian(seeds[1], (IMAGES, D), 1.0, 6.0, ((0, 32),)),
        "kept_index": draw_kept_index(jax.random.fold_in(seeds[15], 71), 0),
        "segment": draw_segment(jax.random.fold_in(seeds[15], 71), 0),
        "grid_side": draw_grid_side(jax.random.fold_in(seeds[15], 71), 0),
        "ada_weight": gaussian(seeds[5], (D, 6 * D), D ** -0.5, 0.1875, ((0, 8), (1, 4))),
        "ada_bias": gaussian(seeds[6], (6 * D,), 0.5, 3.0, ((0, 32),)),
        "attn_weight": gaussian(seeds[7], (D, 3 * D), D ** -0.5, 0.1875, ((0, 8), (1, 4))),
        "attn_bias": gaussian(seeds[8], (2 * D,), 0.15, 1.0, ((0, 32),)),
        "proj_weight": gaussian(seeds[9], (D, D), (max(D // 128, 1)) ** -0.5, 2.0, ((0, 8), (1, 4))),
        "out_bias": gaussian(seeds[10], (2 * D,), 0.5, 3.0, ((0, 32),)),
        "up_weight": gaussian(seeds[11], (D, FF), D ** -0.5, 0.1875, ((0, 8), (1, 4))),
        "up_bias": gaussian(seeds[12], (FF,), 0.5, 3.0, ((0, 32),)),
        "down_weight": gaussian(seeds[13], (FF, D), FF ** -0.5, 0.09375, ((0, 8), (1, 4))),
        "grad_out": gaussian_with(seeds[14], (TOKENS, D), 1.0, 6.0, ((0, 32),), (0, 1, 32, 2.75)),
    }


@jax.custom_vjp
def low(v):
    return lax.optimization_barrier(v.astype(jnp.bfloat16)).astype(jnp.float32)

@jax.custom_vjp
def low_back(v):
    return v

def low_keep(v):
    return (low(v), None)

def low_pass(kept, grad):
    return (grad,)

def back_keep(v):
    return (v, None)

def back_low(kept, grad):
    return (low(grad),)
low.defvjp(low_keep, low_pass)
low_back.defvjp(back_keep, back_low)

def matmul(first_matrix, second_matrix):
    return jnp.dot(first_matrix, second_matrix, precision=lax.Precision.HIGHEST, preferred_element_type=jnp.float32)

def position_code(kept_index, side_rows, model_width):
    quarter = model_width // 4
    exponent = jnp.arange(quarter, dtype=jnp.float32) / quarter
    frequency = 1.0 / 10000.0 ** exponent
    column = (kept_index % side_rows).astype(jnp.float32)[:, None] * frequency[None, :]
    line_pos = (kept_index // side_rows).astype(jnp.float32)[:, None] * frequency[None, :]
    return jnp.concatenate([jnp.sin(column), jnp.cos(column), jnp.sin(line_pos), jnp.cos(line_pos)], axis=1)

def layer_norm(values):
    center = values - lax.optimization_barrier(jnp.mean(values, axis=-1, keepdims=True))
    return center * lax.rsqrt(lax.optimization_barrier(jnp.mean(center * center, axis=-1, keepdims=True)) + 1e-06)

def image_attention(query_rows, key_rows, value_rows, segment_rows):
    row_count = query_rows.shape[0]
    query_heads = query_rows.reshape(row_count, HEADS, HEAD_DIM)
    key_heads = key_rows.reshape(row_count, HEADS, HEAD_DIM)
    value_heads = value_rows.reshape(row_count, HEADS, HEAD_DIM)
    scores = jnp.einsum('qhd,khd->hqk', query_heads, key_heads, precision=lax.Precision.HIGHEST, preferred_element_type=jnp.float32) * (1.0 / math.sqrt(HEAD_DIM))
    scores = low_back(scores)
    same_image = segment_rows[:, None] == segment_rows[None, :]
    scores = jnp.where(same_image[None], scores, -1e+30)
    highest = lax.optimization_barrier(jnp.max(scores, axis=2, keepdims=True))
    powers = jnp.exp(scores - highest)
    probs = low(powers / lax.optimization_barrier(jnp.sum(powers, axis=2, keepdims=True)))
    attended = jnp.einsum('hqk,khd->qhd', probs, value_heads, precision=lax.Precision.HIGHEST, preferred_element_type=jnp.float32)
    return attended.reshape(row_count, HEADS * HEAD_DIM)

def block_rows(start_rows, modulation, global_rows, local_rows, attn_w, attn_b, proj_w, out_b, up_w, up_b, down_w):
    model_width = start_rows.shape[1]
    mod_rows = modulation[global_rows]
    shift_one, scale_one, gate_one, shift_two, scale_two, gate_two = jnp.split(mod_rows, 6, axis=1)
    normed1 = low(layer_norm(start_rows) * (1.0 + scale_one) + shift_one)
    projected = matmul(normed1, attn_w)
    query_rows = low(low_back(projected[:, :model_width] + attn_b[:model_width]))
    key_rows = low(low_back(projected[:, model_width:2 * model_width]))
    value_rows = low(low_back(projected[:, 2 * model_width:] + attn_b[model_width:]))
    group_count = start_rows.shape[0] // TOK_DEV
    attended = jax.vmap(image_attention)(query_rows.reshape(group_count, TOK_DEV, model_width), key_rows.reshape(group_count, TOK_DEV, model_width), value_rows.reshape(group_count, TOK_DEV, model_width), local_rows.reshape(group_count, TOK_DEV)).reshape(start_rows.shape[0], model_width)
    attended = low(low_back(attended))
    branch1 = low_back(matmul(attended, proj_w) + out_b[:model_width])
    middle = start_rows + gate_one * branch1
    normed2 = low(layer_norm(middle) * (1.0 + scale_two) + shift_two)
    hidden_pre = low_back(matmul(normed2, up_w) + up_b)
    hidden = low(jax.nn.gelu(hidden_pre, approximate=True))
    branch2 = low_back(matmul(hidden, down_w) + out_b[model_width:])
    return middle + gate_two * branch2

def reference(tokens, condition, kept_index, segment, grid_side, ada_weight, ada_bias, attn_weight, attn_bias, proj_weight, out_bias, up_weight, up_bias, down_weight, grad_out):
    device_count = TOKENS // TOK_DEV
    device_of_row = jnp.arange(TOKENS, dtype=jnp.int32) // TOK_DEV
    global_slot = (device_of_row * SLOTS_DEV + segment).astype(jnp.int32)
    side_rows = grid_side[global_slot]
    code = position_code(kept_index, side_rows, D)
    group_count = min(device_count, max(1, 4096 // TOK_DEV))
    block_count = device_count // group_count
    block_size = group_count * TOK_DEV
    global_blocks = global_slot.reshape(block_count, block_size)
    local_blocks = segment.reshape(block_count, block_size)

    def forward(tokens_f, condition_f, ada_w, ada_b, attn_w, attn_b, proj_w, out_b, up_w, up_b, down_w):
        silu_cond = low(jax.nn.silu(condition_f))
        modulation = low_back(matmul(silu_cond, ada_w) + ada_b)
        start = tokens_f + code
        start_blocks = start.reshape(block_count, block_size, D)
        checked = jax.checkpoint(block_rows)

        def scan_block(running, pieces):
            start_rows, global_rows, local_rows = pieces
            result = checked(start_rows, modulation, global_rows, local_rows, attn_w, attn_b, proj_w, out_b, up_w, up_b, down_w)
            return (running, result)
        unused, outputs = lax.scan(scan_block, jnp.zeros((), jnp.float32), (start_blocks, global_blocks, local_blocks))
        return outputs.reshape(TOKENS, D)
    floats = (tokens.astype(jnp.float32), condition.astype(jnp.float32), ada_weight.astype(jnp.float32), ada_bias.astype(jnp.float32), attn_weight.astype(jnp.float32), attn_bias.astype(jnp.float32), proj_weight.astype(jnp.float32), out_bias.astype(jnp.float32), up_weight.astype(jnp.float32), up_bias.astype(jnp.float32), down_weight.astype(jnp.float32))
    outputs, pullback = jax.vjp(forward, *floats)
    grads = pullback(grad_out.astype(jnp.float32))
    return (outputs.astype(jnp.bfloat16), grads[0], grads[1], grads[2], grads[3], grads[4], grads[5], grads[6], grads[7], grads[8], grads[9], grads[10])
```

```python
from functools import partial
import math

import jax
import jax.numpy as jnp
from jax import lax
from jax.experimental import pallas as pl
from jax.experimental.pallas import tpu as pltpu
from jax.sharding import PartitionSpec as P

HEADS = 16
AXES = ("dp", "fsdp")


def position_code(kept_index, side_rows, model_width):
    quarter = model_width // 4
    exponent = jnp.arange(quarter, dtype=jnp.float32) / quarter
    frequency = 1.0 / 10000.0**exponent
    column = (kept_index % side_rows).astype(jnp.float32)[:, None] * frequency[None, :]
    line_pos = (kept_index // side_rows).astype(jnp.float32)[:, None] * frequency[None, :]
    return jnp.concatenate(
        [jnp.sin(column), jnp.cos(column), jnp.sin(line_pos), jnp.cos(line_pos)], axis=1
    )


def layer_norm(values):
    center = values - jnp.mean(values, axis=-1, keepdims=True)
    return center * lax.rsqrt(jnp.mean(center * center, axis=-1, keepdims=True) + 1e-06)


def norm_modulate(values, shift_rows, scale_rows):
    return layer_norm(values) * (1.0 + scale_rows) + shift_rows


def matmul_nt(first_matrix, second_matrix):
    return lax.dot_general(
        first_matrix, second_matrix, (((1,), (1,)), ((), ())), preferred_element_type=jnp.float32
    )


def matmul_tn(first_matrix, second_matrix):
    return lax.dot_general(
        first_matrix, second_matrix, (((0,), (0,)), ((), ())), preferred_element_type=jnp.float32
    )


def attend_forward(query_bf, key_bf, value_bf, segment, head_count):
    row_count, model_width = query_bf.shape
    head_size = model_width // head_count
    block_rows = min(row_count, 512)
    block_count = row_count // block_rows
    score_scale = 1.0 / math.sqrt(head_size)
    key_heads = key_bf.reshape(row_count, head_count, head_size)
    value_heads = value_bf.reshape(row_count, head_count, head_size)

    def forward_block(block_index):
        query_rows = query_bf.reshape(block_rows, head_count, head_size)
        same_image = segment[:, None] == segment[None, :]
        scores = (
            jnp.einsum("qhd,khd->hqk", query_rows, key_heads, preferred_element_type=jnp.float32)
            * score_scale
        )
        scores = jnp.where(same_image[None], scores, -1e30)
        highest = jnp.max(scores, axis=2, keepdims=True)
        powers = jnp.exp(scores - highest)
        totals = jnp.sum(powers, axis=2, keepdims=True)
        probs_bf = (powers / totals).astype(jnp.bfloat16)
        attended = jnp.einsum(
            "hqk,khd->qhd", probs_bf, value_heads, preferred_element_type=jnp.float32
        )
        return (attended.reshape(block_rows, model_width), (highest + jnp.log(totals))[:, :, 0])

    attended, log_totals = lax.map(forward_block, jnp.arange(block_count, dtype=jnp.int32))
    return (attended.reshape(row_count, model_width), log_totals)


def attend_backward(query_bf, key_bf, value_bf, attended_grad, segment, log_totals, head_count):
    row_count, model_width = query_bf.shape
    head_size = model_width // head_count
    block_rows = min(row_count, 512)
    block_count = row_count // block_rows
    score_scale = 1.0 / math.sqrt(head_size)
    key_heads = key_bf.reshape(row_count, head_count, head_size)
    value_heads = value_bf.reshape(row_count, head_count, head_size)

    def backward_block(running, pieces):
        key_sum, value_sum = running
        block_index, log_rows = pieces
        query_rows = query_bf.reshape(block_rows, head_count, head_size)
        grad_rows = attended_grad.reshape(block_rows, head_count, head_size)
        same_image = segment[:, None] == segment[None, :]
        scores = (
            jnp.einsum("qhd,khd->hqk", query_rows, key_heads, preferred_element_type=jnp.float32)
            * score_scale
        )
        scores = jnp.where(same_image[None], scores, -1e30)
        probs = jnp.exp(scores - log_rows[:, :, None])
        probs_bf = probs.astype(jnp.bfloat16)
        prob_grad = jnp.einsum(
            "qhd,khd->hqk", grad_rows, value_heads, preferred_element_type=jnp.float32
        )
        row_inner = jnp.sum(probs * prob_grad, axis=2, keepdims=True)
        score_grad = (probs * (prob_grad - row_inner)).astype(jnp.bfloat16)
        query_grad = (
            jnp.einsum("hqk,khd->qhd", score_grad, key_heads, preferred_element_type=jnp.float32)
            * score_scale
        )
        key_sum = (
            key_sum
            + jnp.einsum("hqk,qhd->khd", score_grad, query_rows, preferred_element_type=jnp.float32)
            * score_scale
        )
        value_sum = value_sum + jnp.einsum(
            "hqk,qhd->khd", probs_bf, grad_rows, preferred_element_type=jnp.float32
        )
        return ((key_sum, value_sum), query_grad.reshape(block_rows, model_width))

    empty_sum = jnp.zeros((row_count, head_count, head_size), jnp.float32)
    sums, query_grad = lax.scan(
        backward_block,
        (empty_sum, empty_sum),
        (jnp.arange(block_count, dtype=jnp.int32), log_totals),
    )
    return (
        query_grad.reshape(row_count, model_width),
        sums[0].reshape(row_count, model_width),
        sums[1].reshape(row_count, model_width),
    )


def on_box():
    return lax.axis_size("dp") == 4 and lax.axis_size("fsdp") == 8


def neighbour(index, axis):
    plane, line = index // 8, index % 8
    if axis == "x":
        plane ^= 1
    elif axis == "y":
        plane ^= 2
    elif axis == "core":
        line ^= 1
    else:
        line = (line - 2 * axis) % 8
    return plane * 8 + line


def swap(values, axis):
    return lax.ppermute(values, AXES, [(index, neighbour(index, axis)) for index in range(32)])


HALF_ORDERS = (("x", 1, "y", 2), ("y", 2, "x", 1))


def place():
    plane, line = lax.axis_index("dp"), lax.axis_index("fsdp")
    return plane, line // 2, line % 2


def flipped(plane, flip):
    if flip % 2:
        plane = plane + 1 - 2 * (plane % 2)
    if flip // 2:
        plane = plane + 2 - 4 * (plane // 2)
    return plane


def gather_line(shard):
    return [shard] + [swap(shard, turn) for turn in (1, 2, 3)]


def gather_plane(line):
    depth = place()[1]
    ring = jnp.stack(line + line)
    begin = (4 - depth) % 4
    own = []
    for half, (first, first_flip, second, second_flip) in enumerate(HALF_ORDERS):
        piece = lax.dynamic_slice_in_dim(ring, begin + 2 * half, 2, axis=0)
        beside = swap(piece, first)
        across = [swap(piece, second), swap(beside, second)]
        found = [piece, None, None, across[1]]
        found[first_flip] = beside
        found[second_flip] = across[0]
        own.append(found)
    other = [[swap(piece, "core") for piece in found] for found in own]
    return (own, other)


def lay_out(plane_major, *refs):
    pieces, out, sems = refs[:16], refs[16], refs[17]
    plane, _, core = place()
    copies = []
    for flip_core in range(2):
        for half in range(2):
            for flip in range(4):
                at = flipped(plane, flip)
                side = core if flip_core == 0 else 1 - core
                rows = pl.ds(2 * half, 2)
                target = out.at[at, rows, side] if plane_major else out.at[rows, at, side]
                count = len(copies)
                copies.append(pltpu.make_async_copy(pieces[count], target, sems.at[count]))
    for copy in copies:
        copy.start()
    for copy in copies:
        copy.wait()


def assemble(pieces, plane_major):
    flat = [piece for side in pieces for found in side for piece in found]
    rows, columns = flat[0].shape[1:]
    whole = pl.pallas_call(
        partial(lay_out, plane_major),
        out_shape=jax.ShapeDtypeStruct((4, 4, 2, rows, columns), flat[0].dtype),
        in_specs=[pl.BlockSpec(memory_space=pl.ANY)] * 16,
        out_specs=pl.BlockSpec(memory_space=pl.ANY),
        scratch_shapes=[pltpu.SemaphoreType.DMA((16,))],
        cost_estimate=pl.CostEstimate(
            flops=0, bytes_accessed=2 * 32 * rows * columns * 2, transcendentals=0
        ),
    )(*flat)
    return whole.reshape(4, 8 * rows, columns)


def scatter_terms(sibling, own):
    depth = place()[1]
    totals = []
    for half, (first, first_flip, second, second_flip) in enumerate(HALF_ORDERS):
        summed = [
            own[half][flip].astype(jnp.float32)
            + swap(sibling[half][flip].astype(jnp.bfloat16), "core").astype(jnp.float32)
            for flip in range(4)
        ]
        across = summed[second_flip] + swap(summed[3].astype(jnp.bfloat16), first).astype(jnp.float32)
        home = summed[0] + swap(summed[first_flip].astype(jnp.bfloat16), first).astype(jnp.float32)
        totals.append(home + swap(across.astype(jnp.bfloat16), second).astype(jnp.float32))
    total = jnp.concatenate(totals)
    result = lax.dynamic_index_in_dim(total, depth, axis=0, keepdims=False)
    for turn in (1, 2, 3):
        term = lax.dynamic_index_in_dim(total, (depth - turn) % 4, axis=0, keepdims=False)
        result = result + swap(term.astype(jnp.bfloat16), turn).astype(jnp.float32)
    return result


def halves(terms):
    return [[term[:2] for term in terms], [term[2:] for term in terms]]


def core_columns(values):
    rows, columns = values.shape
    core = place()[2]
    cut = values.reshape(rows, 4, 2, columns // 8)
    return [
        lax.dynamic_index_in_dim(cut, side, axis=2, keepdims=False).reshape(rows, columns // 2)
        for side in (core, 1 - core)
    ]


def pick(values, index):
    return lax.dynamic_index_in_dim(values, index, axis=0, keepdims=False)


def gather_blocks(attn_weight, proj_weight, up_weight, down_weight):
    if not on_box():
        parts = lax.axis_size("dp")
        attn, proj, up, down = [
            lax.all_gather(lax.all_gather(weight, "dp", axis=1, tiled=True), "fsdp", axis=0, tiled=True)
            for weight in (attn_weight, proj_weight, up_weight, down_weight)
        ]
        width = attn.shape[0]

        def by_block(weight):
            return weight.reshape(weight.shape[0], parts, -1).transpose(1, 0, 2)

        joined = jnp.concatenate([by_block(attn), by_block(proj)], axis=2)
        return joined, by_block(up), by_block(down.T.reshape(width, -1))
    core = place()[2]
    rows, _ = up_weight.shape
    joined_line = gather_line(jnp.concatenate([attn_weight, proj_weight], axis=1))
    turned = down_weight.T.reshape(2, rows, down_weight.shape[0])
    mine, theirs = pick(turned, core), pick(turned, 1 - core)
    arrived = swap(theirs, "core")
    down_shard = jnp.where(
        core == 0,
        jnp.concatenate([mine, arrived], axis=1),
        jnp.concatenate([arrived, mine], axis=1),
    )
    up_shard, _ = lax.optimization_barrier((up_weight, joined_line[1:]))
    up_line = gather_line(up_shard)
    down_shard, _ = lax.optimization_barrier((down_shard, up_line[1:]))
    down_line = gather_line(down_shard)
    return (
        assemble(gather_plane(joined_line), True),
        assemble(gather_plane(up_line), True),
        assemble(gather_plane(down_line), False),
    )


def scatter_down(hidden, grad_branch2):
    if not on_box():
        rows = hidden.shape[1]
        flat = hidden.transpose(1, 0, 2).reshape(rows, -1)
        return scatter_whole(matmul_tn(flat, grad_branch2))
    plane, _, core = place()
    width = grad_branch2.shape[1]
    block = width // 8
    columns = grad_branch2.reshape(-1, 4, 2, block)
    order = jnp.stack([flipped(plane, flip) for flip in range(4)])
    columns = jnp.take(columns, order, axis=1)
    terms = []
    for side in (1 - core, core):
        lhs = lax.dynamic_index_in_dim(columns, side, axis=2, keepdims=False).reshape(-1, width // 2)
        found = [matmul_tn(lhs, hidden[part]).reshape(4, block, -1) for part in range(4)]
        if len(terms) == 0:
            found = [value.astype(jnp.bfloat16) for value in found]
        terms.append(
            [
                [jnp.stack([found[2 * half][flip], found[2 * half + 1][flip]]) for flip in range(4)]
                for half in range(2)
            ]
        )
    total = scatter_terms(terms[0], terms[1])
    depth = total.shape[1] // 2
    cut = total.reshape(block, 2, depth).transpose(1, 0, 2)
    mine, theirs = pick(cut, core), pick(cut, 1 - core)
    arrived = swap(theirs, "core")
    whole = jnp.where(
        core == 0, jnp.concatenate([mine, arrived]), jnp.concatenate([arrived, mine])
    )
    return whole.T


def scatter_whole(gradient):
    part = lax.psum_scatter(
        gradient.astype(jnp.bfloat16), "dp", scatter_dimension=1, tiled=True
    ).astype(jnp.float32)
    return lax.psum_scatter(part, "fsdp", scatter_dimension=0, tiled=True)


def scatter_rows(pairs):
    if not on_box():
        return [
            scatter_whole(matmul_tn(left, right.transpose(1, 0, 2).reshape(left.shape[0], -1)))
            for left, right in pairs
        ]
    plane = place()[0]
    cut = [core_columns(left) for left, _ in pairs]
    terms = []
    for side in (1, 0):
        found = []
        for flip in range(4):
            products = [
                matmul_tn(left[side], pick(right, flipped(plane, flip)))
                for left, (_, right) in zip(cut, pairs)
            ]
            joined = jnp.concatenate(products, axis=1)
            if side:
                joined = joined.astype(jnp.bfloat16)
            found.append(joined.reshape(4, -1, joined.shape[1]))
        terms.append(halves(found))
    total = scatter_terms(terms[0], terms[1])
    results, begin = [], 0
    for _, right in pairs:
        results.append(total[:, begin : begin + right.shape[2]])
        begin += right.shape[2]
    return results


def modulate_slots(silu_bf, ada_weight, ada_bias):
    planes, lines = lax.axis_size("dp"), lax.axis_size("fsdp")
    slots = silu_bf.shape[0]
    rows, columns = ada_weight.shape
    everyone = lax.all_gather(silu_bf, AXES, axis=0, tiled=True)
    silu_part = lax.dynamic_slice_in_dim(everyone, lax.axis_index("fsdp") * rows, rows, axis=1)
    term = jnp.dot(silu_part, ada_weight, preferred_element_type=jnp.float32)
    term = lax.psum_scatter(
        term.reshape(planes, lines, slots, columns), "fsdp", scatter_dimension=1, tiled=True
    )
    term = lax.all_to_all(term.reshape(planes, slots, columns), "dp", 0, 0, tiled=True)
    modulation = term.transpose(1, 0, 2).reshape(slots, planes * columns)
    return modulation + ada_bias.astype(jnp.float32), silu_part


def modulation_back(modulation_grad, silu_part, ada_weight):
    planes, lines = lax.axis_size("dp"), lax.axis_size("fsdp")
    slots = modulation_grad.shape[0]
    rows, columns = ada_weight.shape
    cut = modulation_grad.reshape(slots, planes, columns).transpose(1, 0, 2)
    cut = lax.all_to_all(cut, "dp", 0, 0, tiled=True)
    cut = lax.all_gather(cut, "fsdp", axis=1)
    cut = cut.reshape(planes * lines * slots, columns)
    ada_grad = matmul_tn(silu_part, cut)
    sums = jnp.sum(cut, axis=0, dtype=jnp.float32)
    bias_width = columns // lines
    ada_bias_grad = lax.dynamic_slice_in_dim(sums, lax.axis_index("fsdp") * bias_width, bias_width)
    silu_grad = matmul_nt(cut, ada_weight).reshape(planes, lines, slots, rows)
    silu_grad = lax.psum_scatter(silu_grad, "dp", scatter_dimension=0, tiled=True)
    silu_grad = lax.all_to_all(silu_grad.reshape(lines, slots, rows), "fsdp", 0, 0, tiled=True)
    silu_grad = silu_grad.transpose(1, 0, 2).reshape(slots, lines * rows)
    return ada_grad, ada_bias_grad, silu_grad


def by_columns(values, parts):
    rows, columns = values.shape
    return values.reshape(rows, parts, columns // parts).transpose(1, 0, 2)


def per_device(
    tokens,
    condition,
    kept_index,
    segment,
    grid_side,
    ada_weight,
    ada_bias,
    attn_weight,
    attn_bias,
    proj_weight,
    out_bias,
    up_weight,
    up_bias,
    down_weight,
    grad_out,
):
    model_width = tokens.shape[1]
    slot_count = condition.shape[0]
    planes = lax.axis_size("dp")
    joined_w, up_w, down_w = gather_blocks(attn_weight, proj_weight, up_weight, down_weight)
    attn_columns = attn_weight.shape[1]
    small = (ada_bias, attn_bias, out_bias, up_bias)
    everyone = lax.all_gather(jnp.concatenate(small), AXES, axis=0)
    biases, begin = [], 0
    for vector in small:
        biases.append(everyone[:, begin : begin + vector.shape[0]].reshape(-1))
        begin += vector.shape[0]
    ada_bfull, attn_bfull, out_bfull, up_bfull = biases
    slot_ids = jnp.arange(slot_count, dtype=jnp.int32)
    same_slot = segment[:, None] == slot_ids[None, :]
    slot_table = same_slot.astype(jnp.float32)
    side_rows = jnp.sum(jnp.where(same_slot, grid_side[None, :], 0), axis=1)
    start = tokens.astype(jnp.float32) + position_code(kept_index, side_rows, model_width)
    condition_f = condition.astype(jnp.float32)
    silu_cond, silu_back = jax.vjp(jax.nn.silu, condition_f)
    silu_bf = silu_cond.astype(jnp.bfloat16)
    modulation, silu_part = modulate_slots(silu_bf, ada_weight, ada_bfull)
    mod_rows = jnp.dot(
        slot_table, modulation, precision=lax.Precision.HIGHEST, preferred_element_type=jnp.float32
    )
    shift_one, scale_one, gate_one, shift_two, scale_two, gate_two = jnp.split(mod_rows, 6, axis=1)
    normed1, norm1_back = jax.vjp(norm_modulate, start, shift_one, scale_one)
    normed1_bf = normed1.astype(jnp.bfloat16)
    projected = jnp.concatenate(
        [
            jnp.dot(normed1_bf, joined_w[part, :, :attn_columns], preferred_element_type=jnp.float32)
            for part in range(planes)
        ],
        axis=1,
    )
    proj_full = joined_w[:, :, attn_columns:].transpose(1, 0, 2).reshape(model_width, model_width)
    attn_bias_f = attn_bfull.astype(jnp.float32)
    query_bf = (projected[:, :model_width] + attn_bias_f[:model_width]).astype(jnp.bfloat16)
    key_bf = projected[:, model_width : 2 * model_width].astype(jnp.bfloat16)
    value_bf = (projected[:, 2 * model_width :] + attn_bias_f[model_width:]).astype(jnp.bfloat16)
    attended, log_totals = attend_forward(query_bf, key_bf, value_bf, segment, HEADS)
    attended_bf = attended.astype(jnp.bfloat16)
    out_bias_f = out_bfull.astype(jnp.float32)
    branch1 = (
        jnp.dot(attended_bf, proj_full, preferred_element_type=jnp.float32)
        + out_bias_f[:model_width]
    )
    middle = start + gate_one * branch1
    normed2, norm2_back = jax.vjp(norm_modulate, middle, shift_two, scale_two)
    normed2_bf = normed2.astype(jnp.bfloat16)
    hidden_parts, gelu_parts = [], []
    up_bias_f = up_bfull.astype(jnp.float32).reshape(planes, -1)
    branch2 = out_bias_f[model_width:]
    for part in range(planes):
        hidden_pre = (
            jnp.dot(normed2_bf, up_w[part], preferred_element_type=jnp.float32) + up_bias_f[part]
        )
        hidden_act, gelu_back = jax.vjp(partial(jax.nn.gelu, approximate=True), hidden_pre)
        hidden_parts.append(hidden_act.astype(jnp.bfloat16))
        gelu_parts.append(gelu_back)
        branch2 = branch2 + matmul_nt(hidden_parts[part], down_w[part])
    mixed = (middle + gate_two * branch2).astype(jnp.bfloat16)
    out_grad = grad_out.astype(jnp.float32)
    grad_gate_two = out_grad * branch2
    grad_branch2 = (out_grad * gate_two).astype(jnp.bfloat16)
    down_weight_grad = scatter_down(jnp.stack(hidden_parts), grad_branch2)
    pre_parts = []
    for part in range(planes):
        hidden_grad = jnp.dot(grad_branch2, down_w[part], preferred_element_type=jnp.float32)
        pre_parts.append(gelu_parts[part](hidden_grad)[0].astype(jnp.bfloat16))
    pre_grad = jnp.stack(pre_parts)
    (up_weight_grad,) = scatter_rows([(normed2_bf, pre_grad)])
    up_bias_term = jnp.sum(pre_grad, axis=1, dtype=jnp.float32).reshape(-1)
    normed2_grad = sum(matmul_nt(pre_parts[part], up_w[part]) for part in range(planes))
    middle_part, grad_shift_two, grad_scale_two = norm2_back(normed2_grad)
    middle_grad = out_grad + middle_part
    grad_gate_one = middle_grad * branch1
    grad_branch1 = (middle_grad * gate_one).astype(jnp.bfloat16)
    attended_grad = matmul_nt(grad_branch1, proj_full).astype(jnp.bfloat16)
    query_grad, key_grad, value_grad = attend_backward(
        query_bf, key_bf, value_bf, attended_grad, segment, log_totals, HEADS
    )
    query_grad_bf = query_grad.astype(jnp.bfloat16)
    value_grad_bf = value_grad.astype(jnp.bfloat16)
    joined_grad = jnp.concatenate(
        [query_grad_bf, key_grad.astype(jnp.bfloat16), value_grad_bf], axis=1
    )
    joined_parts = by_columns(joined_grad, planes)
    attn_weight_grad, proj_weight_grad = scatter_rows(
        [(normed1_bf, joined_parts), (attended_bf, by_columns(grad_branch1, planes))]
    )
    attn_bias_term = jnp.concatenate(
        [
            jnp.sum(query_grad_bf, axis=0, dtype=jnp.float32),
            jnp.sum(value_grad_bf, axis=0, dtype=jnp.float32),
        ]
    )
    normed1_grad = sum(
        matmul_nt(joined_parts[part], joined_w[part, :, :attn_columns]) for part in range(planes)
    )
    start_part, grad_shift_one, grad_scale_one = norm1_back(normed1_grad)
    tokens_grad = middle_grad + start_part
    mod_rows_grad = jnp.concatenate(
        [
            grad_shift_one,
            grad_scale_one,
            grad_gate_one,
            grad_shift_two,
            grad_scale_two,
            grad_gate_two,
        ],
        axis=1,
    )
    modulation_grad = lax.dot_general(
        slot_table,
        mod_rows_grad,
        (((0,), (0,)), ((), ())),
        precision=lax.Precision.HIGHEST,
        preferred_element_type=jnp.float32,
    ).astype(jnp.bfloat16)
    ada_weight_grad, ada_bias_grad, silu_grad = modulation_back(modulation_grad, silu_part, ada_weight)
    condition_grad = silu_back(silu_grad)[0]
    out_bias_term = jnp.concatenate(
        [
            jnp.sum(grad_branch1, axis=0, dtype=jnp.float32),
            jnp.sum(grad_branch2, axis=0, dtype=jnp.float32),
        ]
    )
    devices = planes * lax.axis_size("fsdp")
    terms = (attn_bias_term, out_bias_term, up_bias_term)
    shared = jnp.concatenate([term.reshape(devices, -1) for term in terms], axis=1)
    shared = lax.psum_scatter(shared, AXES, scatter_dimension=0, tiled=True)[0]
    attn_bias_grad, out_bias_grad, up_bias_grad = jnp.split(
        shared, [attn_bias.shape[0], attn_bias.shape[0] + out_bias.shape[0]]
    )
    return (
        mixed,
        tokens_grad,
        condition_grad,
        ada_weight_grad,
        ada_bias_grad,
        attn_weight_grad,
        attn_bias_grad,
        proj_weight_grad,
        out_bias_grad,
        up_weight_grad,
        up_bias_grad,
        down_weight_grad,
    )


def solution(mesh):
    return jax.shard_map(
        per_device,
        mesh=mesh,
        in_specs=(
            P(("dp", "fsdp"), None),
            P(("dp", "fsdp"), None),
            P(("dp", "fsdp")),
            P(("dp", "fsdp")),
            P(("dp", "fsdp")),
            P("fsdp", "dp"),
            P(("dp", "fsdp")),
            P("fsdp", "dp"),
            P(("dp", "fsdp")),
            P("fsdp", "dp"),
            P(("dp", "fsdp")),
            P("fsdp", "dp"),
            P(("dp", "fsdp")),
            P("fsdp", "dp"),
            P(("dp", "fsdp"), None),
        ),
        out_specs=(
            P(("dp", "fsdp"), None),
            P(("dp", "fsdp"), None),
            P(("dp", "fsdp"), None),
            P("fsdp", "dp"),
            P(("dp", "fsdp")),
            P("fsdp", "dp"),
            P(("dp", "fsdp")),
            P("fsdp", "dp"),
            P(("dp", "fsdp")),
            P("fsdp", "dp"),
            P(("dp", "fsdp")),
            P("fsdp", "dp"),
        ),
        check_vma=False,
    )
```

```python
from functools import partial
import math

import jax
import jax.numpy as jnp
from jax import lax
from jax.experimental import pallas as pl
from jax.experimental.pallas import tpu as pltpu
from jax.sharding import PartitionSpec as P

HEADS = 16
AXES = ("dp", "fsdp")


def position_code(kept_index, side_rows, model_width):
    quarter = model_width // 4
    exponent = jnp.arange(quarter, dtype=jnp.float32) / quarter
    frequency = 1.0 / 10000.0**exponent
    column = (kept_index % side_rows).astype(jnp.float32)[:, None] * frequency[None, :]
    line_pos = (kept_index // side_rows).astype(jnp.float32)[:, None] * frequency[None, :]
    return jnp.concatenate(
        [jnp.sin(column), jnp.cos(column), jnp.sin(line_pos), jnp.cos(line_pos)], axis=1
    )


def layer_norm(values):
    center = values - jnp.mean(values, axis=-1, keepdims=True)
    return center * lax.rsqrt(jnp.mean(center * center, axis=-1, keepdims=True) + 1e-06)


def norm_modulate(values, shift_rows, scale_rows):
    return layer_norm(values) * (1.0 + scale_rows) + shift_rows


def matmul_nt(first_matrix, second_matrix):
    return lax.dot_general(
        first_matrix, second_matrix, (((1,), (1,)), ((), ())), preferred_element_type=jnp.float32
    )


def matmul_tn(first_matrix, second_matrix):
    return lax.dot_general(
        first_matrix, second_matrix, (((0,), (0,)), ((), ())), preferred_element_type=jnp.float32
    )


def attend_forward(query_bf, key_bf, value_bf, segment, head_count):
    row_count, model_width = query_bf.shape
    head_size = model_width // head_count
    block_rows = min(row_count, 512)
    block_count = row_count // block_rows
    score_scale = 1.0 / math.sqrt(head_size)
    key_heads = key_bf.reshape(row_count, head_count, head_size)
    value_heads = value_bf.reshape(row_count, head_count, head_size)

    def forward_block(block_index):
        query_rows = query_bf.reshape(block_rows, head_count, head_size)
        same_image = segment[:, None] == segment[None, :]
        scores = (
            jnp.einsum("qhd,khd->hqk", query_rows, key_heads, preferred_element_type=jnp.float32)
            * score_scale
        )
        scores = jnp.where(same_image[None], scores, -1e30)
        highest = jnp.max(scores, axis=2, keepdims=True)
        powers = jnp.exp(scores - highest)
        totals = jnp.sum(powers, axis=2, keepdims=True)
        probs_bf = (powers / totals).astype(jnp.bfloat16)
        attended = jnp.einsum(
            "hqk,khd->qhd", probs_bf, value_heads, preferred_element_type=jnp.float32
        )
        return (attended.reshape(block_rows, model_width), (highest + jnp.log(totals))[:, :, 0])

    attended, log_totals = lax.map(forward_block, jnp.arange(block_count, dtype=jnp.int32))
    return (attended.reshape(row_count, model_width), log_totals)


def attend_backward(query_bf, key_bf, value_bf, attended_grad, segment, log_totals, head_count):
    row_count, model_width = query_bf.shape
    head_size = model_width // head_count
    block_rows = min(row_count, 512)
    block_count = row_count // block_rows
    score_scale = 1.0 / math.sqrt(head_size)
    key_heads = key_bf.reshape(row_count, head_count, head_size)
    value_heads = value_bf.reshape(row_count, head_count, head_size)

    def backward_block(running, pieces):
        key_sum, value_sum = running
        block_index, log_rows = pieces
        query_rows = query_bf.reshape(block_rows, head_count, head_size)
        grad_rows = attended_grad.reshape(block_rows, head_count, head_size)
        same_image = segment[:, None] == segment[None, :]
        scores = (
            jnp.einsum("qhd,khd->hqk", query_rows, key_heads, preferred_element_type=jnp.float32)
            * score_scale
        )
        scores = jnp.where(same_image[None], scores, -1e30)
        probs = jnp.exp(scores - log_rows[:, :, None])
        probs_bf = probs.astype(jnp.bfloat16)
        prob_grad = jnp.einsum(
            "qhd,khd->hqk", grad_rows, value_heads, preferred_element_type=jnp.float32
        )
        row_inner = jnp.sum(probs * prob_grad, axis=2, keepdims=True)
        score_grad = (probs * (prob_grad - row_inner)).astype(jnp.bfloat16)
        query_grad = (
            jnp.einsum("hqk,khd->qhd", score_grad, key_heads, preferred_element_type=jnp.float32)
            * score_scale
        )
        key_sum = (
            key_sum
            + jnp.einsum("hqk,qhd->khd", score_grad, query_rows, preferred_element_type=jnp.float32)
            * score_scale
        )
        value_sum = value_sum + jnp.einsum(
            "hqk,qhd->khd", probs_bf, grad_rows, preferred_element_type=jnp.float32
        )
        return ((key_sum, value_sum), query_grad.reshape(block_rows, model_width))

    empty_sum = jnp.zeros((row_count, head_count, head_size), jnp.float32)
    sums, query_grad = lax.scan(
        backward_block,
        (empty_sum, empty_sum),
        (jnp.arange(block_count, dtype=jnp.int32), log_totals),
    )
    return (
        query_grad.reshape(row_count, model_width),
        sums[0].reshape(row_count, model_width),
        sums[1].reshape(row_count, model_width),
    )


def on_box():
    return lax.axis_size("dp") == 4 and lax.axis_size("fsdp") == 8


def neighbour(index, axis):
    plane, line = index // 8, index % 8
    if axis == "x":
        plane ^= 1
    elif axis == "y":
        plane ^= 2
    elif axis == "core":
        line ^= 1
    else:
        line = (line - 2 * axis) % 8
    return plane * 8 + line


def swap(values, axis):
    return lax.ppermute(values, AXES, [(index, neighbour(index, axis)) for index in range(32)])


HALF_ORDERS = (("x", 1, "y", 2), ("y", 2, "x", 1))


def place():
    plane, line = lax.axis_index("dp"), lax.axis_index("fsdp")
    return plane, line // 2, line % 2


def flipped(plane, flip):
    if flip % 2:
        plane = plane + 1 - 2 * (plane % 2)
    if flip // 2:
        plane = plane + 2 - 4 * (plane // 2)
    return plane


def gather_line(shard):
    return [shard] + [swap(shard, turn) for turn in (1, 2, 3)]


def gather_plane(line):
    depth = place()[1]
    ring = jnp.stack(line + line)
    begin = (4 - depth) % 4
    own = []
    for half, (first, first_flip, second, second_flip) in enumerate(HALF_ORDERS):
        piece = lax.dynamic_slice_in_dim(ring, begin + 2 * half, 2, axis=0)
        beside = swap(piece, first)
        across = [swap(piece, second), swap(beside, second)]
        found = [piece, None, None, across[1]]
        found[first_flip] = beside
        found[second_flip] = across[0]
        own.append(found)
    other = [[swap(piece, "core") for piece in found] for found in own]
    return (own, other)


def lay_out(plane_major, *refs):
    pieces, out, room, arrive, leave = refs[:16], refs[16], refs[17], refs[18], refs[19]
    plane, _, core = place()
    sides = (core, 1 - core)

    def fill(block):
        slot = block % 2
        copies = []
        for flip_core in range(2):
            for step in range(2 if plane_major else 4):
                if plane_major:
                    source = pieces[flip_core * 8 + step * 4 + block]
                    target = room.at[slot, pl.ds(2 * step, 2), sides[flip_core]]
                else:
                    source = pieces[flip_core * 8 + block // 2 * 4 + step].at[block % 2]
                    target = room.at[slot, flipped(plane, step), sides[flip_core]]
                copies.append(
                    pltpu.make_async_copy(source, target, arrive.at[slot, len(copies)])
                )
        for copy in copies:
            copy.start()
        return copies

    filling, draining = [fill(0), None], [None, None]
    for block in range(4):
        slot = block % 2
        if block < 3:
            if draining[1 - slot] is not None:
                draining[1 - slot].wait()
            filling[1 - slot] = fill(block + 1)
        for copy in filling[slot]:
            copy.wait()
        at = flipped(plane, block) if plane_major else block
        draining[slot] = pltpu.make_async_copy(room.at[slot], out.at[at], leave.at[slot])
        draining[slot].start()
    for copy in draining:
        copy.wait()


def assemble(pieces, plane_major):
    flat = [piece for side in pieces for found in side for piece in found]
    rows, columns = flat[0].shape[1:]
    whole = pl.pallas_call(
        partial(lay_out, plane_major),
        out_shape=jax.ShapeDtypeStruct((4, 4, 2, rows, columns), flat[0].dtype),
        in_specs=[pl.BlockSpec(memory_space=pl.ANY)] * 16,
        out_specs=pl.BlockSpec(memory_space=pl.ANY),
        scratch_shapes=[
            pltpu.VMEM((2, 4, 2, rows, columns), flat[0].dtype),
            pltpu.SemaphoreType.DMA((2, 8)),
            pltpu.SemaphoreType.DMA((2,)),
        ],
        compiler_params=pltpu.CompilerParams(vmem_limit_bytes=16 * 2**20),
        cost_estimate=pl.CostEstimate(
            flops=0, bytes_accessed=2 * 32 * rows * columns * 2, transcendentals=0
        ),
    )(*flat)
    return whole.reshape(4, 8 * rows, columns)


def scatter_terms(sibling, own):
    depth = place()[1]
    totals = []
    for half, (first, first_flip, second, second_flip) in enumerate(HALF_ORDERS):
        summed = [
            own[half][flip].astype(jnp.float32)
            + swap(sibling[half][flip].astype(jnp.bfloat16), "core").astype(jnp.float32)
            for flip in range(4)
        ]
        across = summed[second_flip] + swap(summed[3].astype(jnp.bfloat16), first).astype(jnp.float32)
        home = summed[0] + swap(summed[first_flip].astype(jnp.bfloat16), first).astype(jnp.float32)
        totals.append(home + swap(across.astype(jnp.bfloat16), second).astype(jnp.float32))
    total = jnp.concatenate(totals)
    result = lax.dynamic_index_in_dim(total, depth, axis=0, keepdims=False)
    for turn in (1, 2, 3):
        term = lax.dynamic_index_in_dim(total, (depth - turn) % 4, axis=0, keepdims=False)
        result = result + swap(term.astype(jnp.bfloat16), turn).astype(jnp.float32)
    return result


def halves(terms):
    return [[term[:2] for term in terms], [term[2:] for term in terms]]


def core_columns(values):
    rows, columns = values.shape
    core = place()[2]
    cut = values.reshape(rows, 4, 2, columns // 8)
    return [
        lax.dynamic_index_in_dim(cut, side, axis=2, keepdims=False).reshape(rows, columns // 2)
        for side in (core, 1 - core)
    ]


def pick(values, index):
    return lax.dynamic_index_in_dim(values, index, axis=0, keepdims=False)


def gather_blocks(attn_weight, proj_weight, up_weight, down_weight):
    if not on_box():
        parts = lax.axis_size("dp")
        attn, proj, up, down = [
            lax.all_gather(lax.all_gather(weight, "dp", axis=1, tiled=True), "fsdp", axis=0, tiled=True)
            for weight in (attn_weight, proj_weight, up_weight, down_weight)
        ]
        width = attn.shape[0]

        def by_block(weight):
            return weight.reshape(weight.shape[0], parts, -1).transpose(1, 0, 2)

        joined = jnp.concatenate([by_block(attn), by_block(proj)], axis=2)
        return joined, by_block(up), by_block(down.T.reshape(width, -1))
    core = place()[2]
    rows, _ = up_weight.shape
    joined_line = gather_line(jnp.concatenate([attn_weight, proj_weight], axis=1))
    turned = down_weight.T.reshape(2, rows, down_weight.shape[0])
    mine, theirs = pick(turned, core), pick(turned, 1 - core)
    arrived = swap(theirs, "core")
    down_shard = jnp.where(
        core == 0,
        jnp.concatenate([mine, arrived], axis=1),
        jnp.concatenate([arrived, mine], axis=1),
    )
    up_shard, _ = lax.optimization_barrier((up_weight, joined_line[1:]))
    up_line = gather_line(up_shard)
    down_shard, _ = lax.optimization_barrier((down_shard, up_line[1:]))
    down_line = gather_line(down_shard)
    return (
        assemble(gather_plane(joined_line), True),
        assemble(gather_plane(up_line), True),
        assemble(gather_plane(down_line), False),
    )


def scatter_down(hidden, grad_branch2):
    if not on_box():
        rows = hidden.shape[1]
        flat = hidden.transpose(1, 0, 2).reshape(rows, -1)
        return scatter_whole(matmul_tn(flat, grad_branch2))
    plane, _, core = place()
    width = grad_branch2.shape[1]
    block = width // 8
    columns = grad_branch2.reshape(-1, 4, 2, block)
    order = jnp.stack([flipped(plane, flip) for flip in range(4)])
    columns = jnp.take(columns, order, axis=1)
    terms = []
    for side in (1 - core, core):
        lhs = lax.dynamic_index_in_dim(columns, side, axis=2, keepdims=False).reshape(-1, width // 2)
        found = [matmul_tn(lhs, hidden[part]).reshape(4, block, -1) for part in range(4)]
        if len(terms) == 0:
            found = [value.astype(jnp.bfloat16) for value in found]
        terms.append(
            [
                [jnp.stack([found[2 * half][flip], found[2 * half + 1][flip]]) for flip in range(4)]
                for half in range(2)
            ]
        )
    total = scatter_terms(terms[0], terms[1])
    depth = total.shape[1] // 2
    cut = total.reshape(block, 2, depth).transpose(1, 0, 2)
    mine, theirs = pick(cut, core), pick(cut, 1 - core)
    arrived = swap(theirs, "core")
    whole = jnp.where(
        core == 0, jnp.concatenate([mine, arrived]), jnp.concatenate([arrived, mine])
    )
    return whole.T


def scatter_whole(gradient):
    part = lax.psum_scatter(
        gradient.astype(jnp.bfloat16), "dp", scatter_dimension=1, tiled=True
    ).astype(jnp.float32)
    return lax.psum_scatter(part, "fsdp", scatter_dimension=0, tiled=True)


def scatter_rows(pairs):
    if not on_box():
        return [
            scatter_whole(matmul_tn(left, right.transpose(1, 0, 2).reshape(left.shape[0], -1)))
            for left, right in pairs
        ]
    plane = place()[0]
    cut = [core_columns(left) for left, _ in pairs]
    terms = []
    for side in (1, 0):
        found = []
        for flip in range(4):
            products = [
                matmul_tn(left[side], pick(right, flipped(plane, flip)))
                for left, (_, right) in zip(cut, pairs)
            ]
            joined = jnp.concatenate(products, axis=1)
            if side:
                joined = joined.astype(jnp.bfloat16)
            found.append(joined.reshape(4, -1, joined.shape[1]))
        terms.append(halves(found))
    total = scatter_terms(terms[0], terms[1])
    results, begin = [], 0
    for _, right in pairs:
        results.append(total[:, begin : begin + right.shape[2]])
        begin += right.shape[2]
    return results


def trade(one_for_all, values, out, send_sems, recv_sems):
    planes, lines = lax.axis_size("dp"), lax.axis_size("fsdp")
    count = planes * lines
    me = lax.axis_index("dp") * lines + lax.axis_index("fsdp")

    def device(index):
        return (index // lines, index % lines)

    def chunk(index):
        return values if one_for_all else values.at[index]

    barrier = pltpu.get_barrier_semaphore()

    @pl.loop(1, count)
    def _(step):
        pl.semaphore_signal(
            barrier,
            inc=1,
            device_id=device((me + step) % count),
            device_id_type=pl.DeviceIdType.MESH,
        )

    pl.semaphore_wait(barrier, count - 1)

    @pl.loop(1, count)
    def _(step):
        peer = (me + step) % count
        pltpu.make_async_remote_copy(
            src_ref=chunk(peer),
            dst_ref=out.at[me],
            send_sem=send_sems.at[step],
            recv_sem=recv_sems.at[step],
            device_id=device(peer),
            device_id_type=pl.DeviceIdType.MESH,
        ).start()

    if one_for_all:
        out[me] = values[...]
    else:
        out[me] = values[me]

    @pl.loop(1, count)
    def _(step):
        peer = (me + step) % count
        copy = pltpu.make_async_remote_copy(
            src_ref=chunk(peer),
            dst_ref=out.at[(me + count - step) % count],
            send_sem=send_sems.at[step],
            recv_sem=recv_sems.at[step],
            device_id=device(peer),
            device_id_type=pl.DeviceIdType.MESH,
        )
        copy.wait()


def exchange(values, collective_id, one_for_all=False):
    count = lax.axis_size("dp") * lax.axis_size("fsdp")
    chunk = values.shape[-2:]
    size = count * chunk[0] * chunk[1] * values.dtype.itemsize
    return pl.pallas_call(
        partial(trade, one_for_all),
        out_shape=jax.ShapeDtypeStruct((count,) + chunk, values.dtype),
        in_specs=[pl.BlockSpec(memory_space=pltpu.VMEM)],
        out_specs=pl.BlockSpec(memory_space=pltpu.VMEM),
        scratch_shapes=[pltpu.SemaphoreType.DMA((count,)), pltpu.SemaphoreType.DMA((count,))],
        compiler_params=pltpu.CompilerParams(
            collective_id=collective_id,
            has_side_effects=True,
            vmem_limit_bytes=3 * size + 4 * 2**20,
        ),
        cost_estimate=pl.CostEstimate(flops=0, bytes_accessed=8 * size, transcendentals=0),
    )(values)


def gather_small(silu_bf, vectors):
    flat = jnp.concatenate([silu_bf.reshape(-1), *vectors])
    width = -(-flat.shape[0] // 2048) * 128
    flat = jnp.pad(flat, (0, 16 * width - flat.shape[0])).reshape(16, width)
    everyone = exchange(flat, 0, one_for_all=True)
    everyone = everyone.reshape(everyone.shape[0], -1)
    begin = silu_bf.size
    silu_all = everyone[:, :begin].reshape(-1, silu_bf.shape[1])
    found = []
    for vector in vectors:
        found.append(everyone[:, begin : begin + vector.shape[0]].reshape(-1))
        begin += vector.shape[0]
    return silu_all, found


def modulate_slots(silu_all, ada_weight, ada_bias):
    planes, lines = lax.axis_size("dp"), lax.axis_size("fsdp")
    rows, columns = ada_weight.shape
    devices = planes * lines
    slots = silu_all.shape[0] // devices
    silu_part = lax.dynamic_slice_in_dim(silu_all, lax.axis_index("fsdp") * rows, rows, axis=1)
    term = jnp.dot(silu_part, ada_weight, preferred_element_type=jnp.float32)
    term = exchange(term.reshape(devices, slots, columns), 1)
    term = jnp.sum(term.reshape(planes, lines, slots, columns), axis=1)
    modulation = term.transpose(1, 0, 2).reshape(slots, planes * columns)
    return modulation + ada_bias.astype(jnp.float32), silu_part


def modulation_back(modulation_grad, silu_part, ada_weight, terms):
    planes, lines = lax.axis_size("dp"), lax.axis_size("fsdp")
    devices = planes * lines
    slots = modulation_grad.shape[0]
    rows, columns = ada_weight.shape
    cut = modulation_grad.reshape(slots, planes, columns).transpose(1, 0, 2)
    cut = cut.reshape(planes, 1, 16, slots * columns // 16)
    cut = jnp.broadcast_to(cut, (planes, lines) + cut.shape[2:])
    cut = exchange(cut.reshape((devices,) + cut.shape[2:]), 2)
    cut = cut.reshape(devices * slots, columns)
    ada_grad = matmul_tn(silu_part, cut)
    sums = jnp.sum(cut, axis=0, dtype=jnp.float32)
    bias_width = columns // lines
    ada_bias_grad = lax.dynamic_slice_in_dim(sums, lax.axis_index("fsdp") * bias_width, bias_width)
    silu_grad = matmul_nt(cut, ada_weight).reshape(devices, slots * rows)
    flat = jnp.concatenate([silu_grad] + [term.reshape(devices, -1) for term in terms], axis=1)
    width = -(-flat.shape[1] // 1024) * 128
    flat = jnp.pad(flat, ((0, 0), (0, 8 * width - flat.shape[1])))
    flat = exchange(flat.reshape(devices, 8, width), 3).reshape(devices, -1)
    shared = jnp.sum(flat[:, slots * rows :], axis=0)
    silu_grad = flat[:, : slots * rows].reshape(planes, lines, slots, rows).sum(axis=0)
    silu_grad = silu_grad.transpose(1, 0, 2).reshape(slots, lines * rows)
    found, begin = [], 0
    for term in terms:
        found.append(shared[begin : begin + term.shape[0] // devices])
        begin += term.shape[0] // devices
    return ada_grad, ada_bias_grad, silu_grad, found


def by_columns(values, parts):
    rows, columns = values.shape
    return values.reshape(rows, parts, columns // parts).transpose(1, 0, 2)


def per_device(
    tokens,
    condition,
    kept_index,
    segment,
    grid_side,
    ada_weight,
    ada_bias,
    attn_weight,
    attn_bias,
    proj_weight,
    out_bias,
    up_weight,
    up_bias,
    down_weight,
    grad_out,
):
    model_width = tokens.shape[1]
    slot_count = condition.shape[0]
    planes = lax.axis_size("dp")
    joined_w, up_w, down_w = gather_blocks(attn_weight, proj_weight, up_weight, down_weight)
    attn_columns = attn_weight.shape[1]
    slot_ids = jnp.arange(slot_count, dtype=jnp.int32)
    same_slot = segment[:, None] == slot_ids[None, :]
    slot_table = same_slot.astype(jnp.float32)
    side_rows = jnp.sum(jnp.where(same_slot, grid_side[None, :], 0), axis=1)
    start = tokens.astype(jnp.float32) + position_code(kept_index, side_rows, model_width)
    condition_f = condition.astype(jnp.float32)
    silu_cond, silu_back = jax.vjp(jax.nn.silu, condition_f)
    silu_bf = silu_cond.astype(jnp.bfloat16)
    silu_all, (ada_bfull, attn_bfull, out_bfull, up_bfull) = gather_small(
        silu_bf, (ada_bias, attn_bias, out_bias, up_bias)
    )
    modulation, silu_part = modulate_slots(silu_all, ada_weight, ada_bfull)
    mod_rows = jnp.dot(
        slot_table, modulation, precision=lax.Precision.HIGHEST, preferred_element_type=jnp.float32
    )
    shift_one, scale_one, gate_one, shift_two, scale_two, gate_two = jnp.split(mod_rows, 6, axis=1)
    normed1, norm1_back = jax.vjp(norm_modulate, start, shift_one, scale_one)
    normed1_bf = normed1.astype(jnp.bfloat16)
    projected = jnp.concatenate(
        [
            jnp.dot(normed1_bf, joined_w[part, :, :attn_columns], preferred_element_type=jnp.float32)
            for part in range(planes)
        ],
        axis=1,
    )
    proj_full = joined_w[:, :, attn_columns:].transpose(1, 0, 2).reshape(model_width, model_width)
    attn_bias_f = attn_bfull.astype(jnp.float32)
    query_bf = (projected[:, :model_width] + attn_bias_f[:model_width]).astype(jnp.bfloat16)
    key_bf = projected[:, model_width : 2 * model_width].astype(jnp.bfloat16)
    value_bf = (projected[:, 2 * model_width :] + attn_bias_f[model_width:]).astype(jnp.bfloat16)
    attended, log_totals = attend_forward(query_bf, key_bf, value_bf, segment, HEADS)
    attended_bf = attended.astype(jnp.bfloat16)
    out_bias_f = out_bfull.astype(jnp.float32)
    branch1 = (
        jnp.dot(attended_bf, proj_full, preferred_element_type=jnp.float32)
        + out_bias_f[:model_width]
    )
    middle = start + gate_one * branch1
    normed2, norm2_back = jax.vjp(norm_modulate, middle, shift_two, scale_two)
    normed2_bf = normed2.astype(jnp.bfloat16)
    hidden_parts, gelu_parts = [], []
    up_bias_f = up_bfull.astype(jnp.float32).reshape(planes, -1)
    branch2 = out_bias_f[model_width:]
    for part in range(planes):
        hidden_pre = (
            jnp.dot(normed2_bf, up_w[part], preferred_element_type=jnp.float32) + up_bias_f[part]
        )
        hidden_act, gelu_back = jax.vjp(partial(jax.nn.gelu, approximate=True), hidden_pre)
        hidden_parts.append(hidden_act.astype(jnp.bfloat16))
        gelu_parts.append(gelu_back)
        branch2 = branch2 + matmul_nt(hidden_parts[part], down_w[part])
    mixed = (middle + gate_two * branch2).astype(jnp.bfloat16)
    out_grad = grad_out.astype(jnp.float32)
    grad_gate_two = out_grad * branch2
    grad_branch2 = (out_grad * gate_two).astype(jnp.bfloat16)
    down_weight_grad = scatter_down(jnp.stack(hidden_parts), grad_branch2)
    pre_parts = []
    for part in range(planes):
        hidden_grad = jnp.dot(grad_branch2, down_w[part], preferred_element_type=jnp.float32)
        pre_parts.append(gelu_parts[part](hidden_grad)[0].astype(jnp.bfloat16))
    pre_grad = jnp.stack(pre_parts)
    (up_weight_grad,) = scatter_rows([(normed2_bf, pre_grad)])
    up_bias_term = jnp.sum(pre_grad, axis=1, dtype=jnp.float32).reshape(-1)
    normed2_grad = sum(matmul_nt(pre_parts[part], up_w[part]) for part in range(planes))
    middle_part, grad_shift_two, grad_scale_two = norm2_back(normed2_grad)
    middle_grad = out_grad + middle_part
    grad_gate_one = middle_grad * branch1
    grad_branch1 = (middle_grad * gate_one).astype(jnp.bfloat16)
    attended_grad = matmul_nt(grad_branch1, proj_full).astype(jnp.bfloat16)
    query_grad, key_grad, value_grad = attend_backward(
        query_bf, key_bf, value_bf, attended_grad, segment, log_totals, HEADS
    )
    query_grad_bf = query_grad.astype(jnp.bfloat16)
    value_grad_bf = value_grad.astype(jnp.bfloat16)
    joined_grad = jnp.concatenate(
        [query_grad_bf, key_grad.astype(jnp.bfloat16), value_grad_bf], axis=1
    )
    joined_parts = by_columns(joined_grad, planes)
    attn_weight_grad, proj_weight_grad = scatter_rows(
        [(normed1_bf, joined_parts), (attended_bf, by_columns(grad_branch1, planes))]
    )
    attn_bias_term = jnp.concatenate(
        [
            jnp.sum(query_grad_bf, axis=0, dtype=jnp.float32),
            jnp.sum(value_grad_bf, axis=0, dtype=jnp.float32),
        ]
    )
    normed1_grad = sum(
        matmul_nt(joined_parts[part], joined_w[part, :, :attn_columns]) for part in range(planes)
    )
    start_part, grad_shift_one, grad_scale_one = norm1_back(normed1_grad)
    tokens_grad = middle_grad + start_part
    mod_rows_grad = jnp.concatenate(
        [
            grad_shift_one,
            grad_scale_one,
            grad_gate_one,
            grad_shift_two,
            grad_scale_two,
            grad_gate_two,
        ],
        axis=1,
    )
    modulation_grad = lax.dot_general(
        slot_table,
        mod_rows_grad,
        (((0,), (0,)), ((), ())),
        precision=lax.Precision.HIGHEST,
        preferred_element_type=jnp.float32,
    ).astype(jnp.bfloat16)
    out_bias_term = jnp.concatenate(
        [
            jnp.sum(grad_branch1, axis=0, dtype=jnp.float32),
            jnp.sum(grad_branch2, axis=0, dtype=jnp.float32),
        ]
    )
    ada_weight_grad, ada_bias_grad, silu_grad, bias_grads = modulation_back(
        modulation_grad, silu_part, ada_weight, (attn_bias_term, out_bias_term, up_bias_term)
    )
    attn_bias_grad, out_bias_grad, up_bias_grad = bias_grads
    condition_grad = silu_back(silu_grad)[0]
    return (
        mixed,
        tokens_grad,
        condition_grad,
        ada_weight_grad,
        ada_bias_grad,
        attn_weight_grad,
        attn_bias_grad,
        proj_weight_grad,
        out_bias_grad,
        up_weight_grad,
        up_bias_grad,
        down_weight_grad,
    )


def solution(mesh):
    return jax.shard_map(
        per_device,
        mesh=mesh,
        in_specs=(
            P(("dp", "fsdp"), None),
            P(("dp", "fsdp"), None),
            P(("dp", "fsdp")),
            P(("dp", "fsdp")),
            P(("dp", "fsdp")),
            P("fsdp", "dp"),
            P(("dp", "fsdp")),
            P("fsdp", "dp"),
            P(("dp", "fsdp")),
            P("fsdp", "dp"),
            P(("dp", "fsdp")),
            P("fsdp", "dp"),
            P(("dp", "fsdp")),
            P("fsdp", "dp"),
            P(("dp", "fsdp"), None),
        ),
        out_specs=(
            P(("dp", "fsdp"), None),
            P(("dp", "fsdp"), None),
            P(("dp", "fsdp"), None),
            P("fsdp", "dp"),
            P(("dp", "fsdp")),
            P("fsdp", "dp"),
            P(("dp", "fsdp")),
            P("fsdp", "dp"),
            P(("dp", "fsdp")),
            P("fsdp", "dp"),
            P(("dp", "fsdp")),
            P("fsdp", "dp"),
        ),
        check_vma=False,
    )
```

```python
from functools import partial
import math

import jax
import jax.numpy as jnp
from jax import lax
from jax.experimental import pallas as pl
from jax.experimental.pallas import tpu as pltpu
from jax.sharding import PartitionSpec as P

HEADS = 16
AXES = ("dp", "fsdp")


def position_code(kept_index, side_rows, model_width):
    quarter = model_width // 4
    exponent = jnp.arange(quarter, dtype=jnp.float32) / quarter
    frequency = 1.0 / 10000.0**exponent
    column = (kept_index % side_rows).astype(jnp.float32)[:, None] * frequency[None, :]
    line_pos = (kept_index // side_rows).astype(jnp.float32)[:, None] * frequency[None, :]
    return jnp.concatenate(
        [jnp.sin(column), jnp.cos(column), jnp.sin(line_pos), jnp.cos(line_pos)], axis=1
    )


def layer_norm(values):
    center = values - jnp.mean(values, axis=-1, keepdims=True)
    return center * lax.rsqrt(jnp.mean(center * center, axis=-1, keepdims=True) + 1e-06)


def norm_modulate(values, shift_rows, scale_rows):
    return layer_norm(values) * (1.0 + scale_rows) + shift_rows


def matmul_nt(first_matrix, second_matrix):
    return lax.dot_general(
        first_matrix, second_matrix, (((1,), (1,)), ((), ())), preferred_element_type=jnp.float32
    )


def matmul_tn(first_matrix, second_matrix):
    return lax.dot_general(
        first_matrix, second_matrix, (((0,), (0,)), ((), ())), preferred_element_type=jnp.float32
    )


def attend_forward(query_bf, key_bf, value_bf, segment, head_count):
    row_count, model_width = query_bf.shape
    head_size = model_width // head_count
    block_rows = min(row_count, 512)
    block_count = row_count // block_rows
    score_scale = 1.0 / math.sqrt(head_size)
    key_heads = key_bf.reshape(row_count, head_count, head_size)
    value_heads = value_bf.reshape(row_count, head_count, head_size)

    def forward_block(block_index):
        query_rows = query_bf.reshape(block_rows, head_count, head_size)
        same_image = segment[:, None] == segment[None, :]
        scores = (
            jnp.einsum("qhd,khd->hqk", query_rows, key_heads, preferred_element_type=jnp.float32)
            * score_scale
        )
        scores = jnp.where(same_image[None], scores, -1e30)
        highest = jnp.max(scores, axis=2, keepdims=True)
        powers = jnp.exp(scores - highest)
        totals = jnp.sum(powers, axis=2, keepdims=True)
        probs_bf = (powers / totals).astype(jnp.bfloat16)
        attended = jnp.einsum(
            "hqk,khd->qhd", probs_bf, value_heads, preferred_element_type=jnp.float32
        )
        return (attended.reshape(block_rows, model_width), (highest + jnp.log(totals))[:, :, 0])

    attended, log_totals = lax.map(forward_block, jnp.arange(block_count, dtype=jnp.int32))
    return (attended.reshape(row_count, model_width), log_totals)


def attend_backward(query_bf, key_bf, value_bf, attended_grad, segment, log_totals, head_count):
    row_count, model_width = query_bf.shape
    head_size = model_width // head_count
    block_rows = min(row_count, 512)
    block_count = row_count // block_rows
    score_scale = 1.0 / math.sqrt(head_size)
    key_heads = key_bf.reshape(row_count, head_count, head_size)
    value_heads = value_bf.reshape(row_count, head_count, head_size)

    def backward_block(running, pieces):
        key_sum, value_sum = running
        block_index, log_rows = pieces
        query_rows = query_bf.reshape(block_rows, head_count, head_size)
        grad_rows = attended_grad.reshape(block_rows, head_count, head_size)
        same_image = segment[:, None] == segment[None, :]
        scores = (
            jnp.einsum("qhd,khd->hqk", query_rows, key_heads, preferred_element_type=jnp.float32)
            * score_scale
        )
        scores = jnp.where(same_image[None], scores, -1e30)
        probs = jnp.exp(scores - log_rows[:, :, None])
        probs_bf = probs.astype(jnp.bfloat16)
        prob_grad = jnp.einsum(
            "qhd,khd->hqk", grad_rows, value_heads, preferred_element_type=jnp.float32
        )
        row_inner = jnp.sum(probs * prob_grad, axis=2, keepdims=True)
        score_grad = (probs * (prob_grad - row_inner)).astype(jnp.bfloat16)
        query_grad = (
            jnp.einsum("hqk,khd->qhd", score_grad, key_heads, preferred_element_type=jnp.float32)
            * score_scale
        )
        key_sum = (
            key_sum
            + jnp.einsum("hqk,qhd->khd", score_grad, query_rows, preferred_element_type=jnp.float32)
            * score_scale
        )
        value_sum = value_sum + jnp.einsum(
            "hqk,qhd->khd", probs_bf, grad_rows, preferred_element_type=jnp.float32
        )
        return ((key_sum, value_sum), query_grad.reshape(block_rows, model_width))

    empty_sum = jnp.zeros((row_count, head_count, head_size), jnp.float32)
    sums, query_grad = lax.scan(
        backward_block,
        (empty_sum, empty_sum),
        (jnp.arange(block_count, dtype=jnp.int32), log_totals),
    )
    return (
        query_grad.reshape(row_count, model_width),
        sums[0].reshape(row_count, model_width),
        sums[1].reshape(row_count, model_width),
    )


def on_box():
    return lax.axis_size("dp") == 4 and lax.axis_size("fsdp") == 8


def neighbour(index, axis):
    plane, line = index // 8, index % 8
    if axis == "x":
        plane ^= 1
    elif axis == "y":
        plane ^= 2
    elif axis == "core":
        line ^= 1
    else:
        line = (line - 2 * axis) % 8
    return plane * 8 + line


def swap(values, axis):
    return lax.ppermute(values, AXES, [(index, neighbour(index, axis)) for index in range(32)])


HALF_ORDERS = (("x", 1, "y", 2), ("y", 2, "x", 1))


def place():
    plane, line = lax.axis_index("dp"), lax.axis_index("fsdp")
    return plane, line // 2, line % 2


def flipped(plane, flip):
    if flip % 2:
        plane = plane + 1 - 2 * (plane % 2)
    if flip // 2:
        plane = plane + 2 - 4 * (plane // 2)
    return plane


def gather_line(shard):
    return [shard] + [swap(shard, turn) for turn in (1, 2, 3)]


def gather_plane(line):
    depth = place()[1]
    ring = jnp.stack(line + line)
    begin = (4 - depth) % 4
    own = []
    for half, (first, first_flip, second, second_flip) in enumerate(HALF_ORDERS):
        piece = lax.dynamic_slice_in_dim(ring, begin + 2 * half, 2, axis=0)
        beside = swap(piece, first)
        across = [swap(piece, second), swap(beside, second)]
        found = [piece, None, None, across[1]]
        found[first_flip] = beside
        found[second_flip] = across[0]
        own.append(found)
    other = [[swap(piece, "core") for piece in found] for found in own]
    return (own, other)


def pick(values, index):
    return lax.dynamic_index_in_dim(values, index, axis=0, keepdims=False)


def gather_blocks(attn_weight, proj_weight, up_weight, down_weight):
    parts = lax.axis_size("dp")
    attn, proj, up, down = [
        lax.all_gather(lax.all_gather(weight, "dp", axis=1, tiled=True), "fsdp", axis=0, tiled=True)
        for weight in (attn_weight, proj_weight, up_weight, down_weight)
    ]
    width = attn.shape[0]

    def by_block(weight):
        return weight.reshape(weight.shape[0], parts, -1).transpose(1, 0, 2)

    joined = jnp.concatenate([by_block(attn), by_block(proj)], axis=2)
    return joined, by_block(up), by_block(down.T.reshape(width, -1))


def scatter_whole(gradient):
    part = lax.psum_scatter(
        gradient.astype(jnp.bfloat16), "dp", scatter_dimension=1, tiled=True
    ).astype(jnp.float32)
    return lax.psum_scatter(part, "fsdp", scatter_dimension=0, tiled=True)


def scatter_rows(pairs):
    return [
        scatter_whole(matmul_tn(left, right.transpose(1, 0, 2).reshape(left.shape[0], -1)))
        for left, right in pairs
    ]


def trade(one_for_all, values, out, send_sems, recv_sems):
    planes, lines = lax.axis_size("dp"), lax.axis_size("fsdp")
    count = planes * lines
    me = lax.axis_index("dp") * lines + lax.axis_index("fsdp")

    def device(index):
        return (index // lines, index % lines)

    def chunk(index):
        return values if one_for_all else values.at[index]

    barrier = pltpu.get_barrier_semaphore()

    @pl.loop(1, count)
    def _(step):
        pl.semaphore_signal(
            barrier,
            inc=1,
            device_id=device((me + step) % count),
            device_id_type=pl.DeviceIdType.MESH,
        )

    pl.semaphore_wait(barrier, count - 1)

    @pl.loop(1, count)
    def _(step):
        peer = (me + step) % count
        pltpu.make_async_remote_copy(
            src_ref=chunk(peer),
            dst_ref=out.at[me],
            send_sem=send_sems.at[step],
            recv_sem=recv_sems.at[step],
            device_id=device(peer),
            device_id_type=pl.DeviceIdType.MESH,
        ).start()

    if one_for_all:
        out[me] = values[...]
    else:
        out[me] = values[me]

    @pl.loop(1, count)
    def _(step):
        peer = (me + step) % count
        copy = pltpu.make_async_remote_copy(
            src_ref=chunk(peer),
            dst_ref=out.at[(me + count - step) % count],
            send_sem=send_sems.at[step],
            recv_sem=recv_sems.at[step],
            device_id=device(peer),
            device_id_type=pl.DeviceIdType.MESH,
        )
        copy.wait()


def exchange(values, collective_id, one_for_all=False):
    count = lax.axis_size("dp") * lax.axis_size("fsdp")
    chunk = values.shape[-2:]
    size = count * chunk[0] * chunk[1] * values.dtype.itemsize
    return pl.pallas_call(
        partial(trade, one_for_all),
        out_shape=jax.ShapeDtypeStruct((count,) + chunk, values.dtype),
        in_specs=[pl.BlockSpec(memory_space=pltpu.VMEM)],
        out_specs=pl.BlockSpec(memory_space=pltpu.VMEM),
        scratch_shapes=[pltpu.SemaphoreType.DMA((count,)), pltpu.SemaphoreType.DMA((count,))],
        compiler_params=pltpu.CompilerParams(
            collective_id=collective_id,
            has_side_effects=True,
            vmem_limit_bytes=3 * size + 4 * 2**20,
        ),
        cost_estimate=pl.CostEstimate(flops=0, bytes_accessed=8 * size, transcendentals=0),
    )(values)


def gather_small(silu_bf, vectors):
    flat = jnp.concatenate([silu_bf.reshape(-1), *vectors])
    width = -(-flat.shape[0] // 2048) * 128
    flat = jnp.pad(flat, (0, 16 * width - flat.shape[0])).reshape(16, width)
    everyone = exchange(flat, 0, one_for_all=True)
    everyone = everyone.reshape(everyone.shape[0], -1)
    begin = silu_bf.size
    silu_all = everyone[:, :begin].reshape(-1, silu_bf.shape[1])
    found = []
    for vector in vectors:
        found.append(everyone[:, begin : begin + vector.shape[0]].reshape(-1))
        begin += vector.shape[0]
    return silu_all, found


def modulate_slots(silu_all, ada_weight, ada_bias):
    planes, lines = lax.axis_size("dp"), lax.axis_size("fsdp")
    rows, columns = ada_weight.shape
    devices = planes * lines
    slots = silu_all.shape[0] // devices
    silu_part = lax.dynamic_slice_in_dim(silu_all, lax.axis_index("fsdp") * rows, rows, axis=1)
    term = jnp.dot(silu_part, ada_weight, preferred_element_type=jnp.float32)
    term = exchange(term.reshape(devices, slots, columns), 1)
    term = jnp.sum(term.reshape(planes, lines, slots, columns), axis=1)
    modulation = term.transpose(1, 0, 2).reshape(slots, planes * columns)
    return modulation + ada_bias.astype(jnp.float32), silu_part


def modulation_back(modulation_grad, silu_part, ada_weight, terms):
    planes, lines = lax.axis_size("dp"), lax.axis_size("fsdp")
    devices = planes * lines
    slots = modulation_grad.shape[0]
    rows, columns = ada_weight.shape
    cut = modulation_grad.reshape(slots, planes, columns).transpose(1, 0, 2)
    cut = cut.reshape(planes, 1, 16, slots * columns // 16)
    cut = jnp.broadcast_to(cut, (planes, lines) + cut.shape[2:])
    cut = exchange(cut.reshape((devices,) + cut.shape[2:]), 2)
    cut = cut.reshape(devices * slots, columns)
    ada_grad = matmul_tn(silu_part, cut)
    sums = jnp.sum(cut, axis=0, dtype=jnp.float32)
    bias_width = columns // lines
    ada_bias_grad = lax.dynamic_slice_in_dim(sums, lax.axis_index("fsdp") * bias_width, bias_width)
    silu_grad = matmul_nt(cut, ada_weight).reshape(devices, slots * rows)
    flat = jnp.concatenate([silu_grad] + [term.reshape(devices, -1) for term in terms], axis=1)
    width = -(-flat.shape[1] // 1024) * 128
    flat = jnp.pad(flat, ((0, 0), (0, 8 * width - flat.shape[1])))
    flat = exchange(flat.reshape(devices, 8, width), 3).reshape(devices, -1)
    shared = jnp.sum(flat[:, slots * rows :], axis=0)
    silu_grad = flat[:, : slots * rows].reshape(planes, lines, slots, rows).sum(axis=0)
    silu_grad = silu_grad.transpose(1, 0, 2).reshape(slots, lines * rows)
    found, begin = [], 0
    for term in terms:
        found.append(shared[begin : begin + term.shape[0] // devices])
        begin += term.shape[0] // devices
    return ada_grad, ada_bias_grad, silu_grad, found


def by_columns(values, parts):
    rows, columns = values.shape
    return values.reshape(rows, parts, columns // parts).transpose(1, 0, 2)


SLOPE = math.sqrt(2.0 / math.pi)
WINDOW = 512


def mm(left, right):
    return jnp.dot(left, right, preferred_element_type=jnp.float32)


def local_call(kernel, outs, ins, anys, scratch, megabytes):
    return pl.pallas_call(
        kernel,
        out_shape=outs,
        in_specs=[pl.BlockSpec(memory_space=pltpu.VMEM)] * len(ins)
        + [pl.BlockSpec(memory_space=pl.ANY)] * len(anys),
        out_specs=[
            pl.BlockSpec(memory_space=pl.ANY if out.dtype == jnp.bfloat16 and out.ndim == 4 else pltpu.VMEM)
            for out in outs
        ],
        scratch_shapes=scratch,
        compiler_params=pltpu.CompilerParams(vmem_limit_bytes=megabytes * 2**20),
        cost_estimate=pl.CostEstimate(flops=0, bytes_accessed=0, transcendentals=0),
    )(*ins, *anys)


def shaped(dims, kind=jnp.float32):
    return jax.ShapeDtypeStruct(dims, kind)


def load_blocks(pieces, room, sems, plane_major, natural=False, lanes=None):
    plane, _, core = place()
    sides = (core, 1 - core)
    deep = pieces[0].shape[1]
    blocks = [[] for _ in range(4)]
    count = 0
    for flip in range(4):
        at = flipped(plane, flip)
        for turn in range(2):
            for depth in range(4):
                source = pieces[turn * 8 + depth // 2 * 4 + flip].at[depth % 2]
                if lanes is not None:
                    source = source.at[:, lanes[0] : lanes[1]]
                if plane_major:
                    block, row, held = flip, depth * 2 + sides[turn], at if natural else flip
                else:
                    block, row, held = depth, at * 2 + sides[turn], depth
                target = room.at[held, pl.ds(pl.multiple_of(row * deep, 16), deep)]
                blocks[block].append(pltpu.make_async_copy(source, target, sems.at[count]))
                count += 1
    for block in blocks:
        for copy in block:
            copy.start()
    return blocks


def wait_all(copies):
    for copy in copies:
        copy.wait()


def by_rows(count, step, body):
    @pl.loop(0, count // step)
    def _(index):
        body(pl.ds(pl.multiple_of(index * step, step), step))


def lane_index(rows, lanes):
    return lax.broadcasted_iota(jnp.int32, (rows, lanes), 1)


def window_of(block, width, total, span):
    begin = min(block * width // 128 * 128, total - span)
    return begin, block * width - begin


def slot_rows(slots, table, column, width):
    value = jnp.zeros((slots.shape[0], width), jnp.float32)
    for slot in range(4):
        value = value + jnp.where(slots == slot, table[slot : slot + 1, column * width : (column + 1) * width], 0.0)
    return value


def add_slots(out, slots, value):
    for slot in range(4):
        out[slot : slot + 1, :] += jnp.sum(jnp.where(slots == slot, value, 0.0), axis=0, keepdims=True)


def centred(value):
    center = value - jnp.mean(value, axis=-1, keepdims=True)
    scale = lax.rsqrt(jnp.mean(center * center, axis=-1, keepdims=True) + 1e-06)
    return center * scale, scale


def norm_back(normed, scale, grad):
    return scale * (
        grad
        - jnp.mean(grad, axis=-1, keepdims=True)
        - normed * jnp.mean(grad * normed, axis=-1, keepdims=True)
    )


def project_kernel(normed, bias, *refs):
    pieces, out, room, product, wide, sems = refs[:16], refs[16], refs[17], refs[18], refs[19], refs[20]
    rows, width = normed.shape
    columns = out.shape[1] // 4
    for block in load_blocks(pieces, room, sems, True, natural=True):
        wait_all(block)
    span = product.shape[1]
    for block in range(4):
        product[...] = mm(normed[...], room[block, :, :span])
        begin, offset = window_of(block, columns, out.shape[1], span)

        def put(at):
            moved = product[at, :]
            if offset:
                moved = pltpu.roll(moved, offset, 1)
            lane = lane_index(moved.shape[0], span)
            inside = (lane >= offset) & (lane < offset + columns)
            wide[at, begin : begin + span] = jnp.where(inside, moved, wide[at, begin : begin + span])

        by_rows(rows, 64, put)

    def finish(at):
        out[at, :] = (wide[at, :] + bias[...]).astype(jnp.bfloat16)

    by_rows(rows, 64, finish)


def project(normed, bias, pieces):
    rows, width = normed.shape
    total = bias.shape[1]
    span = -(-total // 4 // 128) * 128 + 128
    return local_call(
        project_kernel,
        [shaped((rows, total), jnp.bfloat16)],
        [normed, bias],
        pieces,
        [
            pltpu.VMEM((4, width, width), jnp.bfloat16),
            pltpu.VMEM((rows, span), jnp.float32),
            pltpu.VMEM((rows, total), jnp.float32),
            pltpu.SemaphoreType.DMA((32,)),
        ],
        56,
    )[0]


def head_window(head, size, total):
    begin = jnp.minimum(head * size // 128 * 128, total - 256)
    begin = pl.multiple_of(begin, 128)
    lane = lane_index(1, 256)
    offset = head * size - begin
    return begin, (lane >= offset) & (lane < offset + size)


def attend_kernel(joined, slots, slot_line, out, stats, bar, wide):
    rows, width = out.shape
    size = width // HEADS
    bar[...] = jnp.where(slots[...] == slot_line[...], 0.0, -1e30)
    scale = 1.0 / math.sqrt(size)
    stats[...] = jnp.zeros_like(stats)

    @pl.loop(0, HEADS)
    def _(head):
        begin, inside = head_window(head, size, width)
        query = jnp.where(inside, joined[:, pl.ds(begin, 256)], 0.0)
        key = joined[:, pl.ds(pl.multiple_of(begin + width, 128), 256)]
        value = joined[:, pl.ds(pl.multiple_of(begin + 2 * width, 128), 256)]
        scores = matmul_nt(query, key) * scale + bar[...]
        highest = jnp.max(scores, axis=1, keepdims=True)
        powers = jnp.exp(scores - highest)
        totals = jnp.sum(powers, axis=1, keepdims=True)
        probs = (powers * (1.0 / totals)).astype(jnp.bfloat16)
        found = mm(probs, value)
        wide[:, pl.ds(begin, 256)] = jnp.where(inside, found, wide[:, pl.ds(begin, 256)])
        lane = lane_index(rows, 128)
        stats[...] = jnp.where(lane == head, highest + jnp.log(totals), stats[...])

    out[...] = wide[...].astype(jnp.bfloat16)


def attend(joined, slots):
    rows, total = joined.shape
    width = total // 3
    return local_call(
        attend_kernel,
        [shaped((rows, width), jnp.bfloat16), shaped((rows, 128))],
        [joined, slots.reshape(rows, 1), slots.reshape(1, rows)],
        [],
        [pltpu.VMEM((rows, rows), jnp.float32), pltpu.VMEM((rows, width), jnp.float32)],
        40,
    )


def attend_back_kernel(joined, grad, stats, slots, slot_line, blocks, sums, bar, wide):
    rows, width = grad.shape
    size = width // HEADS
    scale = 1.0 / math.sqrt(size)
    bar[...] = jnp.where(slots[...] == slot_line[...], 0.0, -1e30)

    @pl.loop(0, HEADS)
    def _(head):
        begin, inside = head_window(head, size, width)
        columns = [pl.ds(pl.multiple_of(begin + part * width, 128), 256) for part in range(3)]
        query = jnp.where(inside, joined[:, columns[0]], 0.0)
        key = joined[:, columns[1]]
        value = joined[:, columns[2]]
        out_grad = jnp.where(inside, grad[:, columns[0]], 0.0)
        lane = lane_index(rows, 128)
        stat = jnp.sum(jnp.where(lane == head, stats[...], 0.0), axis=1, keepdims=True)
        probs = jnp.exp(matmul_nt(query, key) * scale + bar[...] - stat)
        prob_grad = matmul_nt(out_grad, value)
        inner = jnp.sum(probs * prob_grad, axis=1, keepdims=True)
        score_grad = (probs * (prob_grad - inner)).astype(jnp.bfloat16)
        found = (
            mm(score_grad, key) * scale,
            matmul_tn(score_grad, query) * scale,
            matmul_tn(probs.astype(jnp.bfloat16), out_grad),
        )
        for part in range(3):
            wide[:, columns[part]] = jnp.where(inside, found[part], wide[:, columns[part]])

    span = blocks.shape[2]
    block_width = 3 * width // 4

    def total(at):
        sums[...] += jnp.sum(wide[at, :].astype(jnp.bfloat16).astype(jnp.float32), axis=0, keepdims=True)

    sums[...] = jnp.zeros_like(sums)
    by_rows(rows, 64, total)
    for block in range(4):
        begin, offset = window_of(block, block_width, 3 * width, span)

        def cut(at):
            moved = wide[at, begin : begin + span]
            if offset:
                moved = pltpu.roll(moved, span - offset, 1)
            lane = lane_index(moved.shape[0], span)
            blocks[block, at, :] = jnp.where(lane < block_width, moved, 0.0).astype(jnp.bfloat16)

        by_rows(rows, 64, cut)


def attend_back(joined, grad, stats, slots):
    rows, total = joined.shape
    span = -(-total // 4 // 128) * 128 + 128
    return pl.pallas_call(
        attend_back_kernel,
        out_shape=[shaped((4, rows, span), jnp.bfloat16), shaped((1, total))],
        scratch_shapes=[pltpu.VMEM((rows, rows), jnp.float32), pltpu.VMEM((rows, total), jnp.float32)],
        compiler_params=pltpu.CompilerParams(vmem_limit_bytes=48 * 2**20),
        cost_estimate=pl.CostEstimate(flops=0, bytes_accessed=0, transcendentals=0),
    )(joined, grad, stats, slots.reshape(rows, 1), slots.reshape(1, rows))


def branch_kernel(attended, start, slots, table, bias, *refs):
    pieces, (branch, middle, normed, room, product, sems) = refs[:16], refs[16:]
    rows, width = start.shape
    columns = width // 4
    for block in load_blocks(pieces, room, sems, True, natural=True, lanes=(width - WINDOW, width)):
        wait_all(block)
    for block in range(4):
        product[...] = mm(attended[...], room[block])
        begin, offset = window_of(block, columns, width, WINDOW)

        def put(at):
            moved = product[at, :]
            if offset != WINDOW - columns:
                moved = pltpu.roll(moved, columns + offset, 1)
            lane = lane_index(moved.shape[0], WINDOW)
            inside = (lane >= offset) & (lane < offset + columns)
            branch[at, begin : begin + WINDOW] = jnp.where(
                inside, moved, branch[at, begin : begin + WINDOW]
            )

        by_rows(rows, 64, put)

    def finish(at):
        slot = slots[at, :]
        value = branch[at, :] + bias[...]
        branch[at, :] = value
        value = start[at, :] + slot_rows(slot, table, 2, width) * value
        middle[at, :] = value
        hat, _ = centred(value)
        value = hat * (1.0 + slot_rows(slot, table, 4, width)) + slot_rows(slot, table, 3, width)
        normed[at, :] = value.astype(jnp.bfloat16)

    by_rows(rows, 64, finish)


def branch_one(attended, start, slots, table, bias, pieces):
    rows, width = start.shape
    return local_call(
        branch_kernel,
        [shaped((rows, width)), shaped((rows, width)), shaped((rows, width), jnp.bfloat16)],
        [attended, start, slots.reshape(rows, 1), table, bias],
        pieces,
        [
            pltpu.VMEM((4, width, WINDOW), jnp.bfloat16),
            pltpu.VMEM((rows, WINDOW), jnp.float32),
            pltpu.SemaphoreType.DMA((32,)),
        ],
        48,
    )


def widen_kernel(normed, bias, *refs):
    pieces, (hidden, before, room, sems) = refs[:16], refs[16:]
    plane = place()[0]
    rows = normed.shape[0]
    blocks = load_blocks(pieces, room, sems, True)
    for flip in range(4):
        at = flipped(plane, flip)
        wait_all(blocks[flip])
        before[at] = mm(normed[...], room[flip]) + bias[at]

        def act(some):
            value = before[at, some, :]
            bend = 1.0 + jnp.tanh(SLOPE * (value + 0.044715 * (value * value * value)))
            hidden[at, some, :] = (value * (0.5 * bend)).astype(jnp.bfloat16)

        by_rows(rows, 64, act)


def widen(normed, bias, pieces):
    rows, width = normed.shape
    return pl.pallas_call(
        widen_kernel,
        out_shape=[shaped((4, rows, width), jnp.bfloat16), shaped((4, rows, width))],
        in_specs=[pl.BlockSpec(memory_space=pltpu.VMEM)] * 2 + [pl.BlockSpec(memory_space=pl.ANY)] * 16,
        scratch_shapes=[pltpu.VMEM((4, width, width), jnp.bfloat16), pltpu.SemaphoreType.DMA((32,))],
        compiler_params=pltpu.CompilerParams(vmem_limit_bytes=56 * 2**20),
        cost_estimate=pl.CostEstimate(flops=0, bytes_accessed=0, transcendentals=0),
    )(normed, bias, *pieces)


def narrow_kernel(hidden, middle, out_grad, slots, table, bias, before_all, *refs):
    pieces, (mixed, branch_grad, pre_grad, sums, gate_sums, pre_sums, room, total, before, sems, more) = (
        refs[:16],
        refs[16:],
    )
    rows, width = middle.shape
    blocks = load_blocks(pieces, room, sems, False)
    copies = [pltpu.make_async_copy(before_all.at[part], before.at[part], more.at[part]) for part in range(4)]
    for copy in copies:
        copy.start()
    for part in range(4):
        wait_all(blocks[part])
        term = matmul_nt(hidden[part], room[part])
        if part == 0:
            total[...] = term + bias[...]
        else:
            total[...] += term
    sums[...] = jnp.zeros_like(sums)
    gate_sums[...] = jnp.zeros_like(gate_sums)
    pre_sums[...] = jnp.zeros_like(pre_sums)

    def finish(at):
        slot = slots[at, :]
        gate = slot_rows(slot, table, 5, width)
        branch = total[at, :]
        grad = out_grad[at, :].astype(jnp.float32)
        mixed[at, :] = (middle[at, :] + gate * branch).astype(jnp.bfloat16)
        add_slots(gate_sums, slot, grad * branch)
        value = (grad * gate).astype(jnp.bfloat16)
        branch_grad[at, :] = value
        sums[...] += jnp.sum(value.astype(jnp.float32), axis=0, keepdims=True)

    by_rows(rows, 64, finish)
    for part in range(4):
        copies[part].wait()
        total[...] = mm(branch_grad[...], room[part])

        def act(at):
            value = before[part, at, :]
            square = value * value
            bend = jnp.tanh(SLOPE * (value + 0.044715 * (square * value)))
            slope = 0.5 * (1.0 + bend) + 0.5 * value * (1.0 - bend * bend) * (
                SLOPE * (1.0 + 3.0 * 0.044715 * square)
            )
            value = (total[at, :] * slope).astype(jnp.bfloat16)
            pre_grad[part, at, :] = value
            pre_sums[part : part + 1, :] += jnp.sum(value.astype(jnp.float32), axis=0, keepdims=True)

        by_rows(rows, 64, act)


def narrow(hidden, before, middle, out_grad, slots, table, bias, pieces):
    rows, width = middle.shape
    return pl.pallas_call(
        narrow_kernel,
        out_shape=[
            shaped((rows, width), jnp.bfloat16),
            shaped((rows, width), jnp.bfloat16),
            shaped((4, rows, width), jnp.bfloat16),
            shaped((1, width)),
            shaped((8, width)),
            shaped((8, width)),
        ],
        in_specs=[pl.BlockSpec(memory_space=pltpu.VMEM)] * 6 + [pl.BlockSpec(memory_space=pl.ANY)] * 17,
        scratch_shapes=[
            pltpu.VMEM((4, width, width), jnp.bfloat16),
            pltpu.VMEM((rows, width), jnp.float32),
            pltpu.VMEM((4, rows, width), jnp.float32),
            pltpu.SemaphoreType.DMA((32,)),
            pltpu.SemaphoreType.DMA((4,)),
        ],
        compiler_params=pltpu.CompilerParams(vmem_limit_bytes=58 * 2**20),
        cost_estimate=pl.CostEstimate(flops=0, bytes_accessed=0, transcendentals=0),
    )(hidden, middle, out_grad, slots.reshape(rows, 1), table, bias, before, *pieces)


def middle_kernel(pre_grad, middle, out_grad, branch, slots, table, *refs):
    wide_pieces, joined_pieces = refs[:16], refs[16:32]
    middle_grad, attended_grad, windows, slot_sums, sums, room, side, total, sems, more = refs[32:]
    plane = place()[0]
    rows, width = middle.shape
    columns = width // 4
    blocks = load_blocks(wide_pieces, room, sems, True)
    side_blocks = load_blocks(
        joined_pieces, side, more, True, natural=True, lanes=(width - WINDOW, width)
    )
    for flip in range(4):
        wait_all(blocks[flip])
        term = matmul_nt(pre_grad[flipped(plane, flip)], room[flip])
        if flip == 0:
            total[...] = term
        else:
            total[...] += term
    slot_sums[...] = jnp.zeros_like(slot_sums)
    sums[...] = jnp.zeros_like(sums)

    def finish(at):
        slot = slots[at, :]
        grad = total[at, :]
        hat, scale = centred(middle[at, :])
        add_slots(slot_sums.at[1], slot, grad)
        add_slots(slot_sums.at[2], slot, grad * hat)
        grad = grad * (1.0 + slot_rows(slot, table, 4, width))
        grad = out_grad[at, :].astype(jnp.float32) + norm_back(hat, scale, grad)
        middle_grad[at, :] = grad
        add_slots(slot_sums.at[0], slot, grad * branch[at, :])
        value = (grad * slot_rows(slot, table, 2, width)).astype(jnp.bfloat16).astype(jnp.float32)
        total[at, :] = value
        sums[...] += jnp.sum(value, axis=0, keepdims=True)

    by_rows(rows, 64, finish)
    for block in range(4):
        begin, offset = window_of(block, columns, width, WINDOW)

        def cut(at):
            moved = total[at, begin : begin + WINDOW]
            if offset != WINDOW - columns:
                moved = pltpu.roll(moved, (2 * WINDOW - columns - offset) % WINDOW, 1)
            lane = lane_index(moved.shape[0], WINDOW)
            moved = jnp.where(lane >= WINDOW - columns, moved, 0.0)
            windows[block, at, :] = moved.astype(jnp.bfloat16)

        by_rows(rows, 64, cut)
    for block in side_blocks:
        wait_all(block)
    value = matmul_nt(windows[0], side[0])
    for block in range(1, 4):
        value = value + matmul_nt(windows[block], side[block])
    attended_grad[...] = value.astype(jnp.bfloat16)


def middle_back(pre_grad, middle, out_grad, branch, slots, table, wide_pieces, joined_pieces):
    rows, width = middle.shape
    return pl.pallas_call(
        middle_kernel,
        out_shape=[
            shaped((rows, width)),
            shaped((rows, width), jnp.bfloat16),
            shaped((4, rows, WINDOW), jnp.bfloat16),
            shaped((3, 8, width)),
            shaped((1, width)),
        ],
        in_specs=[pl.BlockSpec(memory_space=pltpu.VMEM)] * 6 + [pl.BlockSpec(memory_space=pl.ANY)] * 32,
        scratch_shapes=[
            pltpu.VMEM((4, width, width), jnp.bfloat16),
            pltpu.VMEM((4, width, WINDOW), jnp.bfloat16),
            pltpu.VMEM((rows, width), jnp.float32),
            pltpu.SemaphoreType.DMA((32,)),
            pltpu.SemaphoreType.DMA((32,)),
        ],
        compiler_params=pltpu.CompilerParams(vmem_limit_bytes=58 * 2**20),
        cost_estimate=pl.CostEstimate(flops=0, bytes_accessed=0, transcendentals=0),
    )(pre_grad, middle, out_grad, branch, slots.reshape(rows, 1), table, *wide_pieces, *joined_pieces)


def start_kernel(blocks, start, middle_grad, slots, table, *refs):
    pieces, (grad_out, slot_sums, room, total, sems) = refs[:16], refs[16:]
    plane = place()[0]
    rows, width = start.shape
    span = blocks.shape[2]
    loads = load_blocks(pieces, room, sems, True, lanes=(0, span))
    for flip in range(4):
        wait_all(loads[flip])
        term = matmul_nt(blocks[flipped(plane, flip)], room[flip])
        if flip == 0:
            total[...] = term
        else:
            total[...] += term
    slot_sums[...] = jnp.zeros_like(slot_sums)

    def finish(at):
        slot = slots[at, :]
        grad = total[at, :]
        hat, scale = centred(start[at, :])
        add_slots(slot_sums.at[0], slot, grad)
        add_slots(slot_sums.at[1], slot, grad * hat)
        grad = grad * (1.0 + slot_rows(slot, table, 1, width))
        grad_out[at, :] = middle_grad[at, :] + norm_back(hat, scale, grad)

    by_rows(rows, 64, finish)


def start_back(blocks, start, middle_grad, slots, table, pieces):
    rows, width = start.shape
    return local_call(
        start_kernel,
        [shaped((rows, width)), shaped((2, 8, width))],
        [blocks, start, middle_grad, slots.reshape(rows, 1), table],
        pieces,
        [
            pltpu.VMEM((4, width, blocks.shape[2]), jnp.bfloat16),
            pltpu.VMEM((rows, width), jnp.float32),
            pltpu.SemaphoreType.DMA((32,)),
        ],
        48,
    )


SENT = ((0, (1, 3)), (0, (0, 2)), (1, (2, 3)), (1, (0, 1)))


def outer_kernel(plane_major, lefts, spans, *refs):
    left, right = refs[:lefts], refs[lefts : 2 * lefts]
    outs, (room, sems) = refs[2 * lefts : 2 * lefts + 8], refs[2 * lefts + 8 :]
    plane, _, core = place()
    sides = (1 - core, core)
    width = room.shape[1]
    deep = width // 8
    draining = [[], []]
    for block in range(4):
        slot = block % 2
        wait_all(draining[slot])
        index = flipped(plane, block) if plane_major else block
        if lefts == 1:
            room[slot] = mm(left[0][...], right[0][index]).astype(jnp.bfloat16)
        else:
            low, high = spans
            head = mm(left[0][...], right[0][index])
            tail = mm(left[1][...], right[1][index])
            room[slot, :, :high] = head[:, :high].astype(jnp.bfloat16)
            room[slot, :, high:low] = (head[:, high:low] + tail[:, : low - high]).astype(jnp.bfloat16)
            room[slot, :, low:] = tail[:, low - high :].astype(jnp.bfloat16)
        copies = []
        for kind in range(2):
            for number, (half, flips) in enumerate(SENT):
                target = outs[4 * kind + number]
                for place_in, flip in enumerate(flips):
                    for step in range(2):
                        depth = 2 * half + step
                        if plane_major:
                            if flip != block:
                                continue
                            row = depth * 2 + sides[kind]
                        else:
                            if depth != block:
                                continue
                            row = flipped(plane, flip) * 2 + sides[kind]
                        source = room.at[slot, pl.ds(pl.multiple_of(row * deep, 16), deep)]
                        copies.append(
                            pltpu.make_async_copy(
                                source, target.at[place_in, step], sems.at[slot, len(copies)]
                            )
                        )
        for copy in copies:
            copy.start()
        draining[slot] = copies
    wait_all(draining[0])
    wait_all(draining[1])


def outer(plane_major, lefts, rights, spans=None):
    width = lefts[0].shape[0]
    deep = width // 8
    return pl.pallas_call(
        partial(outer_kernel, plane_major, len(lefts), spans),
        out_shape=[shaped((2, 2, deep, width), jnp.bfloat16)] * 8,
        in_specs=[pl.BlockSpec(memory_space=pltpu.VMEM)] * (2 * len(lefts)),
        out_specs=[pl.BlockSpec(memory_space=pl.ANY)] * 8,
        scratch_shapes=[
            pltpu.VMEM((2, width, width), jnp.bfloat16),
            pltpu.SemaphoreType.DMA((2, 8)),
        ],
        compiler_params=pltpu.CompilerParams(vmem_limit_bytes=48 * 2**20),
        cost_estimate=pl.CostEstimate(flops=0, bytes_accessed=0, transcendentals=0),
    )(*lefts, *rights)


def low_bits(value):
    return value.astype(jnp.bfloat16)


def wide(value):
    return value.astype(jnp.float32)


def scatter_pieces(pieces):
    depth = place()[1]
    summed = [wide(own) + wide(swap(other, "core")) for other, own in zip(pieces[:4], pieces[4:])]
    totals = []
    for half, (first, _, second, _) in enumerate(HALF_ORDERS):
        sent, kept = summed[2 * half], summed[2 * half + 1]
        arrived = wide(swap(low_bits(sent), first))
        across = swap(low_bits(kept[1] + arrived[1]), second)
        totals.append(kept[0] + arrived[0] + wide(across))
    total = jnp.concatenate(totals)
    result = pick(total, depth)
    for turn in (1, 2, 3):
        result = result + wide(swap(low_bits(pick(total, (depth - turn) % 4)), turn))
    return result


def box_device(
    tokens,
    condition,
    kept_index,
    segment,
    grid_side,
    ada_weight,
    ada_bias,
    attn_weight,
    attn_bias,
    proj_weight,
    out_bias,
    up_weight,
    up_bias,
    down_weight,
    grad_out,
):
    rows, width = tokens.shape
    slot_count = condition.shape[0]
    core = place()[2]
    columns = attn_weight.shape[1]
    joined_line = gather_line(jnp.concatenate([attn_weight, proj_weight], axis=1))
    turned = down_weight.T.reshape(2, up_weight.shape[0], down_weight.shape[0])
    mine, theirs = pick(turned, core), pick(turned, 1 - core)
    arrived = swap(theirs, "core")
    down_shard = jnp.where(
        core == 0,
        jnp.concatenate([mine, arrived], axis=1),
        jnp.concatenate([arrived, mine], axis=1),
    )
    up_shard, _ = lax.optimization_barrier((up_weight, joined_line[1:]))
    up_line = gather_line(up_shard)
    down_shard, _ = lax.optimization_barrier((down_shard, up_line[1:]))
    down_line = gather_line(down_shard)

    def flat(pieces):
        return [piece for side in pieces for found in side for piece in found]

    joined_pieces = flat(gather_plane(joined_line))
    up_pieces = flat(gather_plane(up_line))
    down_pieces = flat(gather_plane(down_line))

    slot_ids = jnp.arange(slot_count, dtype=jnp.int32)
    side_rows = jnp.sum(jnp.where(segment[:, None] == slot_ids[None, :], grid_side[None, :], 0), axis=1)
    start = tokens.astype(jnp.float32) + position_code(kept_index, side_rows, width)
    silu_cond, silu_back = jax.vjp(jax.nn.silu, condition.astype(jnp.float32))
    silu_bf = silu_cond.astype(jnp.bfloat16)
    silu_all, (ada_bfull, attn_bfull, out_bfull, up_bfull) = gather_small(
        silu_bf, (ada_bias, attn_bias, out_bias, up_bias)
    )
    modulation, silu_part = modulate_slots(silu_all, ada_weight, ada_bfull)
    table = jnp.pad(modulation, ((0, 8 - slot_count), (0, 0)))

    def own_rows(part):
        return sum(
            jnp.where(segment[:, None] == slot, modulation[slot, part * width : (part + 1) * width], 0.0)
            for slot in range(slot_count)
        )

    normed1 = norm_modulate(start, own_rows(0), own_rows(1)).astype(jnp.bfloat16)
    zeros = jnp.zeros((width,), jnp.bfloat16)
    joined_bias = jnp.concatenate([attn_bfull[:width], zeros, attn_bfull[width:]])
    joined = project(normed1, joined_bias.astype(jnp.float32)[None], joined_pieces)
    attended, stats = attend(joined, segment)
    out_bias_f = out_bfull.astype(jnp.float32)
    branch1, middle, normed2 = branch_one(
        attended, start, segment, table, out_bias_f[None, :width], joined_pieces
    )
    hidden, before = widen(normed2, up_bfull.astype(jnp.float32).reshape(4, 1, -1), up_pieces)
    mixed, grad_branch2, pre_grad, branch2_sums, gate2_sums, pre_sums = narrow(
        hidden, before, middle, grad_out, segment, table, out_bias_f[None, width:], down_pieces
    )
    down_total = scatter_pieces(outer(False, [grad_branch2.T], [hidden]))
    up_weight_grad = scatter_pieces(outer(True, [normed2.T], [pre_grad]))
    half = down_total.shape[1] // 2
    cut = down_total.reshape(-1, 2, half).transpose(1, 0, 2)
    mine, theirs = pick(cut, core), pick(cut, 1 - core)
    arrived = swap(theirs, "core")
    down_weight_grad = jnp.where(
        core == 0, jnp.concatenate([mine, arrived]), jnp.concatenate([arrived, mine])
    ).T
    middle_grad, attended_grad, windows, slot_sums2, branch1_sums = middle_back(
        pre_grad, middle, grad_out, branch1, segment, table, up_pieces, joined_pieces
    )
    blocks, joined_sums = attend_back(joined, attended_grad, stats, segment)
    joined_total = scatter_pieces(
        outer(
            True,
            [normed1.T, attended.T],
            [blocks, windows],
            (blocks.shape[2], width - WINDOW),
        )
    )
    tokens_grad, slot_sums1 = start_back(blocks, start, middle_grad, segment, table, joined_pieces)
    modulation_grad = jnp.concatenate(
        [slot_sums1[0], slot_sums1[1], slot_sums2[0], slot_sums2[1], slot_sums2[2], gate2_sums], axis=1
    )[:slot_count].astype(jnp.bfloat16)
    joined_sums = joined_sums[0]
    terms = (
        jnp.concatenate([joined_sums[:width], joined_sums[2 * width :]]),
        jnp.concatenate([branch1_sums[0], branch2_sums[0]]),
        pre_sums[:4].reshape(-1),
    )
    ada_weight_grad, ada_bias_grad, silu_grad, bias_grads = modulation_back(
        modulation_grad, silu_part, ada_weight, terms
    )
    attn_bias_grad, out_bias_grad, up_bias_grad = bias_grads
    return (
        mixed,
        tokens_grad,
        silu_back(silu_grad)[0],
        ada_weight_grad,
        ada_bias_grad,
        joined_total[:, :columns],
        attn_bias_grad,
        joined_total[:, columns:],
        out_bias_grad,
        up_weight_grad,
        up_bias_grad,
        down_weight_grad,
    )


def per_device(
    tokens,
    condition,
    kept_index,
    segment,
    grid_side,
    ada_weight,
    ada_bias,
    attn_weight,
    attn_bias,
    proj_weight,
    out_bias,
    up_weight,
    up_bias,
    down_weight,
    grad_out,
):
    if on_box():
        return box_device(
            tokens,
            condition,
            kept_index,
            segment,
            grid_side,
            ada_weight,
            ada_bias,
            attn_weight,
            attn_bias,
            proj_weight,
            out_bias,
            up_weight,
            up_bias,
            down_weight,
            grad_out,
        )
    model_width = tokens.shape[1]
    slot_count = condition.shape[0]
    planes = lax.axis_size("dp")
    joined_w, up_w, down_w = gather_blocks(attn_weight, proj_weight, up_weight, down_weight)
    attn_columns = attn_weight.shape[1]
    slot_ids = jnp.arange(slot_count, dtype=jnp.int32)
    same_slot = segment[:, None] == slot_ids[None, :]
    slot_table = same_slot.astype(jnp.float32)
    side_rows = jnp.sum(jnp.where(same_slot, grid_side[None, :], 0), axis=1)
    start = tokens.astype(jnp.float32) + position_code(kept_index, side_rows, model_width)
    condition_f = condition.astype(jnp.float32)
    silu_cond, silu_back = jax.vjp(jax.nn.silu, condition_f)
    silu_bf = silu_cond.astype(jnp.bfloat16)
    silu_all, (ada_bfull, attn_bfull, out_bfull, up_bfull) = gather_small(
        silu_bf, (ada_bias, attn_bias, out_bias, up_bias)
    )
    modulation, silu_part = modulate_slots(silu_all, ada_weight, ada_bfull)
    mod_rows = jnp.dot(
        slot_table, modulation, precision=lax.Precision.HIGHEST, preferred_element_type=jnp.float32
    )
    shift_one, scale_one, gate_one, shift_two, scale_two, gate_two = jnp.split(mod_rows, 6, axis=1)
    normed1, norm1_back = jax.vjp(norm_modulate, start, shift_one, scale_one)
    normed1_bf = normed1.astype(jnp.bfloat16)
    projected = jnp.concatenate(
        [
            jnp.dot(normed1_bf, joined_w[part, :, :attn_columns], preferred_element_type=jnp.float32)
            for part in range(planes)
        ],
        axis=1,
    )
    proj_full = joined_w[:, :, attn_columns:].transpose(1, 0, 2).reshape(model_width, model_width)
    attn_bias_f = attn_bfull.astype(jnp.float32)
    query_bf = (projected[:, :model_width] + attn_bias_f[:model_width]).astype(jnp.bfloat16)
    key_bf = projected[:, model_width : 2 * model_width].astype(jnp.bfloat16)
    value_bf = (projected[:, 2 * model_width :] + attn_bias_f[model_width:]).astype(jnp.bfloat16)
    attended, log_totals = attend_forward(query_bf, key_bf, value_bf, segment, HEADS)
    attended_bf = attended.astype(jnp.bfloat16)
    out_bias_f = out_bfull.astype(jnp.float32)
    branch1 = (
        jnp.dot(attended_bf, proj_full, preferred_element_type=jnp.float32)
        + out_bias_f[:model_width]
    )
    middle = start + gate_one * branch1
    normed2, norm2_back = jax.vjp(norm_modulate, middle, shift_two, scale_two)
    normed2_bf = normed2.astype(jnp.bfloat16)
    hidden_parts, gelu_parts = [], []
    up_bias_f = up_bfull.astype(jnp.float32).reshape(planes, -1)
    branch2 = out_bias_f[model_width:]
    for part in range(planes):
        hidden_pre = (
            jnp.dot(normed2_bf, up_w[part], preferred_element_type=jnp.float32) + up_bias_f[part]
        )
        hidden_act, gelu_back = jax.vjp(partial(jax.nn.gelu, approximate=True), hidden_pre)
        hidden_parts.append(hidden_act.astype(jnp.bfloat16))
        gelu_parts.append(gelu_back)
        branch2 = branch2 + matmul_nt(hidden_parts[part], down_w[part])
    mixed = (middle + gate_two * branch2).astype(jnp.bfloat16)
    out_grad = grad_out.astype(jnp.float32)
    grad_gate_two = out_grad * branch2
    grad_branch2 = (out_grad * gate_two).astype(jnp.bfloat16)
    down_weight_grad = scatter_whole(matmul_tn(jnp.concatenate(hidden_parts, axis=1), grad_branch2))
    pre_parts = []
    for part in range(planes):
        hidden_grad = jnp.dot(grad_branch2, down_w[part], preferred_element_type=jnp.float32)
        pre_parts.append(gelu_parts[part](hidden_grad)[0].astype(jnp.bfloat16))
    pre_grad = jnp.stack(pre_parts)
    (up_weight_grad,) = scatter_rows([(normed2_bf, pre_grad)])
    up_bias_term = jnp.sum(pre_grad, axis=1, dtype=jnp.float32).reshape(-1)
    normed2_grad = sum(matmul_nt(pre_parts[part], up_w[part]) for part in range(planes))
    middle_part, grad_shift_two, grad_scale_two = norm2_back(normed2_grad)
    middle_grad = out_grad + middle_part
    grad_gate_one = middle_grad * branch1
    grad_branch1 = (middle_grad * gate_one).astype(jnp.bfloat16)
    attended_grad = matmul_nt(grad_branch1, proj_full).astype(jnp.bfloat16)
    query_grad, key_grad, value_grad = attend_backward(
        query_bf, key_bf, value_bf, attended_grad, segment, log_totals, HEADS
    )
    query_grad_bf = query_grad.astype(jnp.bfloat16)
    value_grad_bf = value_grad.astype(jnp.bfloat16)
    joined_grad = jnp.concatenate(
        [query_grad_bf, key_grad.astype(jnp.bfloat16), value_grad_bf], axis=1
    )
    joined_parts = by_columns(joined_grad, planes)
    attn_weight_grad, proj_weight_grad = scatter_rows(
        [(normed1_bf, joined_parts), (attended_bf, by_columns(grad_branch1, planes))]
    )
    attn_bias_term = jnp.concatenate(
        [
            jnp.sum(query_grad_bf, axis=0, dtype=jnp.float32),
            jnp.sum(value_grad_bf, axis=0, dtype=jnp.float32),
        ]
    )
    normed1_grad = sum(
        matmul_nt(joined_parts[part], joined_w[part, :, :attn_columns]) for part in range(planes)
    )
    start_part, grad_shift_one, grad_scale_one = norm1_back(normed1_grad)
    tokens_grad = middle_grad + start_part
    mod_rows_grad = jnp.concatenate(
        [
            grad_shift_one,
            grad_scale_one,
            grad_gate_one,
            grad_shift_two,
            grad_scale_two,
            grad_gate_two,
        ],
        axis=1,
    )
    modulation_grad = lax.dot_general(
        slot_table,
        mod_rows_grad,
        (((0,), (0,)), ((), ())),
        precision=lax.Precision.HIGHEST,
        preferred_element_type=jnp.float32,
    ).astype(jnp.bfloat16)
    out_bias_term = jnp.concatenate(
        [
            jnp.sum(grad_branch1, axis=0, dtype=jnp.float32),
            jnp.sum(grad_branch2, axis=0, dtype=jnp.float32),
        ]
    )
    ada_weight_grad, ada_bias_grad, silu_grad, bias_grads = modulation_back(
        modulation_grad, silu_part, ada_weight, (attn_bias_term, out_bias_term, up_bias_term)
    )
    attn_bias_grad, out_bias_grad, up_bias_grad = bias_grads
    condition_grad = silu_back(silu_grad)[0]
    return (
        mixed,
        tokens_grad,
        condition_grad,
        ada_weight_grad,
        ada_bias_grad,
        attn_weight_grad,
        attn_bias_grad,
        proj_weight_grad,
        out_bias_grad,
        up_weight_grad,
        up_bias_grad,
        down_weight_grad,
    )


def solution(mesh):
    return jax.shard_map(
        per_device,
        mesh=mesh,
        in_specs=(
            P(("dp", "fsdp"), None),
            P(("dp", "fsdp"), None),
            P(("dp", "fsdp")),
            P(("dp", "fsdp")),
            P(("dp", "fsdp")),
            P("fsdp", "dp"),
            P(("dp", "fsdp")),
            P("fsdp", "dp"),
            P(("dp", "fsdp")),
            P("fsdp", "dp"),
            P(("dp", "fsdp")),
            P("fsdp", "dp"),
            P(("dp", "fsdp")),
            P("fsdp", "dp"),
            P(("dp", "fsdp"), None),
        ),
        out_specs=(
            P(("dp", "fsdp"), None),
            P(("dp", "fsdp"), None),
            P(("dp", "fsdp"), None),
            P("fsdp", "dp"),
            P(("dp", "fsdp")),
            P("fsdp", "dp"),
            P(("dp", "fsdp")),
            P("fsdp", "dp"),
            P(("dp", "fsdp")),
            P("fsdp", "dp"),
            P(("dp", "fsdp")),
            P("fsdp", "dp"),
        ),
        check_vma=False,
    )
```

```python
from functools import partial
import math

import jax
import jax.numpy as jnp
from jax import lax
from jax.experimental import pallas as pl
from jax.experimental.pallas import tpu as pltpu
from jax.sharding import PartitionSpec as P

HEADS = 16
AXES = ("dp", "fsdp")


def position_code(kept_index, side_rows, model_width):
    quarter = model_width // 4
    exponent = jnp.arange(quarter, dtype=jnp.float32) / quarter
    frequency = 1.0 / 10000.0**exponent
    column = (kept_index % side_rows).astype(jnp.float32)[:, None] * frequency[None, :]
    line_pos = (kept_index // side_rows).astype(jnp.float32)[:, None] * frequency[None, :]
    return jnp.concatenate(
        [jnp.sin(column), jnp.cos(column), jnp.sin(line_pos), jnp.cos(line_pos)], axis=1
    )


def layer_norm(values):
    center = values - jnp.mean(values, axis=-1, keepdims=True)
    return center * lax.rsqrt(jnp.mean(center * center, axis=-1, keepdims=True) + 1e-06)


def norm_modulate(values, shift_rows, scale_rows):
    return layer_norm(values) * (1.0 + scale_rows) + shift_rows


def matmul_nt(first_matrix, second_matrix):
    return lax.dot_general(
        first_matrix, second_matrix, (((1,), (1,)), ((), ())), preferred_element_type=jnp.float32
    )


def matmul_tn(first_matrix, second_matrix):
    return lax.dot_general(
        first_matrix, second_matrix, (((0,), (0,)), ((), ())), preferred_element_type=jnp.float32
    )


def attend_forward(query_bf, key_bf, value_bf, segment, head_count):
    row_count, model_width = query_bf.shape
    head_size = model_width // head_count
    block_rows = min(row_count, 512)
    block_count = row_count // block_rows
    score_scale = 1.0 / math.sqrt(head_size)
    key_heads = key_bf.reshape(row_count, head_count, head_size)
    value_heads = value_bf.reshape(row_count, head_count, head_size)

    def forward_block(block_index):
        query_rows = query_bf.reshape(block_rows, head_count, head_size)
        same_image = segment[:, None] == segment[None, :]
        scores = (
            jnp.einsum("qhd,khd->hqk", query_rows, key_heads, preferred_element_type=jnp.float32)
            * score_scale
        )
        scores = jnp.where(same_image[None], scores, -1e30)
        highest = jnp.max(scores, axis=2, keepdims=True)
        powers = jnp.exp(scores - highest)
        totals = jnp.sum(powers, axis=2, keepdims=True)
        probs_bf = (powers / totals).astype(jnp.bfloat16)
        attended = jnp.einsum(
            "hqk,khd->qhd", probs_bf, value_heads, preferred_element_type=jnp.float32
        )
        return (attended.reshape(block_rows, model_width), (highest + jnp.log(totals))[:, :, 0])

    attended, log_totals = lax.map(forward_block, jnp.arange(block_count, dtype=jnp.int32))
    return (attended.reshape(row_count, model_width), log_totals)


def attend_backward(query_bf, key_bf, value_bf, attended_grad, segment, log_totals, head_count):
    row_count, model_width = query_bf.shape
    head_size = model_width // head_count
    block_rows = min(row_count, 512)
    block_count = row_count // block_rows
    score_scale = 1.0 / math.sqrt(head_size)
    key_heads = key_bf.reshape(row_count, head_count, head_size)
    value_heads = value_bf.reshape(row_count, head_count, head_size)

    def backward_block(running, pieces):
        key_sum, value_sum = running
        block_index, log_rows = pieces
        query_rows = query_bf.reshape(block_rows, head_count, head_size)
        grad_rows = attended_grad.reshape(block_rows, head_count, head_size)
        same_image = segment[:, None] == segment[None, :]
        scores = (
            jnp.einsum("qhd,khd->hqk", query_rows, key_heads, preferred_element_type=jnp.float32)
            * score_scale
        )
        scores = jnp.where(same_image[None], scores, -1e30)
        probs = jnp.exp(scores - log_rows[:, :, None])
        probs_bf = probs.astype(jnp.bfloat16)
        prob_grad = jnp.einsum(
            "qhd,khd->hqk", grad_rows, value_heads, preferred_element_type=jnp.float32
        )
        row_inner = jnp.sum(probs * prob_grad, axis=2, keepdims=True)
        score_grad = (probs * (prob_grad - row_inner)).astype(jnp.bfloat16)
        query_grad = (
            jnp.einsum("hqk,khd->qhd", score_grad, key_heads, preferred_element_type=jnp.float32)
            * score_scale
        )
        key_sum = (
            key_sum
            + jnp.einsum("hqk,qhd->khd", score_grad, query_rows, preferred_element_type=jnp.float32)
            * score_scale
        )
        value_sum = value_sum + jnp.einsum(
            "hqk,qhd->khd", probs_bf, grad_rows, preferred_element_type=jnp.float32
        )
        return ((key_sum, value_sum), query_grad.reshape(block_rows, model_width))

    empty_sum = jnp.zeros((row_count, head_count, head_size), jnp.float32)
    sums, query_grad = lax.scan(
        backward_block,
        (empty_sum, empty_sum),
        (jnp.arange(block_count, dtype=jnp.int32), log_totals),
    )
    return (
        query_grad.reshape(row_count, model_width),
        sums[0].reshape(row_count, model_width),
        sums[1].reshape(row_count, model_width),
    )


def on_box():
    return lax.axis_size("dp") == 4 and lax.axis_size("fsdp") == 8


def neighbour(index, axis):
    plane, line = index // 8, index % 8
    if axis == "x":
        plane ^= 1
    elif axis == "y":
        plane ^= 2
    elif axis == "core":
        line ^= 1
    else:
        line = (line - 2 * axis) % 8
    return plane * 8 + line


def swap(values, axis):
    return lax.ppermute(values, AXES, [(index, neighbour(index, axis)) for index in range(32)])


HALF_ORDERS = (("x", 1, "y", 2), ("y", 2, "x", 1))


def place():
    plane, line = lax.axis_index("dp"), lax.axis_index("fsdp")
    return plane, line // 2, line % 2


def flipped(plane, flip):
    if flip % 2:
        plane = plane + 1 - 2 * (plane % 2)
    if flip // 2:
        plane = plane + 2 - 4 * (plane // 2)
    return plane


def pick(values, index):
    return lax.dynamic_index_in_dim(values, index, axis=0, keepdims=False)


def gather_blocks(attn_weight, proj_weight, up_weight, down_weight):
    parts = lax.axis_size("dp")
    attn, proj, up, down = [
        lax.all_gather(lax.all_gather(weight, "dp", axis=1, tiled=True), "fsdp", axis=0, tiled=True)
        for weight in (attn_weight, proj_weight, up_weight, down_weight)
    ]
    width = attn.shape[0]

    def by_block(weight):
        return weight.reshape(weight.shape[0], parts, -1).transpose(1, 0, 2)

    joined = jnp.concatenate([by_block(attn), by_block(proj)], axis=2)
    return joined, by_block(up), by_block(down.T.reshape(width, -1))


def scatter_whole(gradient):
    part = lax.psum_scatter(
        gradient.astype(jnp.bfloat16), "dp", scatter_dimension=1, tiled=True
    ).astype(jnp.float32)
    return lax.psum_scatter(part, "fsdp", scatter_dimension=0, tiled=True)


def scatter_rows(pairs):
    return [
        scatter_whole(matmul_tn(left, right.transpose(1, 0, 2).reshape(left.shape[0], -1)))
        for left, right in pairs
    ]


def trade(one_for_all, values, out, send_sems, recv_sems):
    planes, lines = lax.axis_size("dp"), lax.axis_size("fsdp")
    count = planes * lines
    me = lax.axis_index("dp") * lines + lax.axis_index("fsdp")

    def device(index):
        return (index // lines, index % lines)

    def chunk(index):
        return values if one_for_all else values.at[index]

    barrier = pltpu.get_barrier_semaphore()

    @pl.loop(1, count)
    def _(step):
        pl.semaphore_signal(
            barrier,
            inc=1,
            device_id=device((me + step) % count),
            device_id_type=pl.DeviceIdType.MESH,
        )

    pl.semaphore_wait(barrier, count - 1)

    @pl.loop(1, count)
    def _(step):
        peer = (me + step) % count
        pltpu.make_async_remote_copy(
            src_ref=chunk(peer),
            dst_ref=out.at[me],
            send_sem=send_sems.at[step],
            recv_sem=recv_sems.at[step],
            device_id=device(peer),
            device_id_type=pl.DeviceIdType.MESH,
        ).start()

    if one_for_all:
        out[me] = values[...]
    else:
        out[me] = values[me]

    @pl.loop(1, count)
    def _(step):
        peer = (me + step) % count
        copy = pltpu.make_async_remote_copy(
            src_ref=chunk(peer),
            dst_ref=out.at[(me + count - step) % count],
            send_sem=send_sems.at[step],
            recv_sem=recv_sems.at[step],
            device_id=device(peer),
            device_id_type=pl.DeviceIdType.MESH,
        )
        copy.wait()


def exchange(values, collective_id, one_for_all=False):
    count = lax.axis_size("dp") * lax.axis_size("fsdp")
    chunk = values.shape[-2:]
    size = count * chunk[0] * chunk[1] * values.dtype.itemsize
    return pl.pallas_call(
        partial(trade, one_for_all),
        out_shape=jax.ShapeDtypeStruct((count,) + chunk, values.dtype),
        in_specs=[pl.BlockSpec(memory_space=pltpu.VMEM)],
        out_specs=pl.BlockSpec(memory_space=pltpu.VMEM),
        scratch_shapes=[pltpu.SemaphoreType.DMA((count,)), pltpu.SemaphoreType.DMA((count,))],
        compiler_params=pltpu.CompilerParams(
            collective_id=collective_id,
            has_side_effects=True,
            vmem_limit_bytes=3 * size + 4 * 2**20,
        ),
        cost_estimate=pl.CostEstimate(flops=0, bytes_accessed=8 * size, transcendentals=0),
    )(values)


def gather_small(silu_bf, vectors):
    flat = jnp.concatenate([silu_bf.reshape(-1), *vectors])
    width = -(-flat.shape[0] // 2048) * 128
    flat = jnp.pad(flat, (0, 16 * width - flat.shape[0])).reshape(16, width)
    everyone = exchange(flat, 0, one_for_all=True)
    everyone = everyone.reshape(everyone.shape[0], -1)
    begin = silu_bf.size
    silu_all = everyone[:, :begin].reshape(-1, silu_bf.shape[1])
    found = []
    for vector in vectors:
        found.append(everyone[:, begin : begin + vector.shape[0]].reshape(-1))
        begin += vector.shape[0]
    return silu_all, found


def modulate_slots(silu_all, ada_weight, ada_bias):
    planes, lines = lax.axis_size("dp"), lax.axis_size("fsdp")
    rows, columns = ada_weight.shape
    devices = planes * lines
    slots = silu_all.shape[0] // devices
    silu_part = lax.dynamic_slice_in_dim(silu_all, lax.axis_index("fsdp") * rows, rows, axis=1)
    term = jnp.dot(silu_part, ada_weight, preferred_element_type=jnp.float32)
    term = exchange(term.reshape(devices, slots, columns), 1)
    term = jnp.sum(term.reshape(planes, lines, slots, columns), axis=1)
    modulation = term.transpose(1, 0, 2).reshape(slots, planes * columns)
    return modulation + ada_bias.astype(jnp.float32), silu_part


def modulation_back(modulation_grad, silu_part, ada_weight, terms):
    planes, lines = lax.axis_size("dp"), lax.axis_size("fsdp")
    devices = planes * lines
    slots = modulation_grad.shape[0]
    rows, columns = ada_weight.shape
    cut = modulation_grad.reshape(slots, planes, columns).transpose(1, 0, 2)
    cut = cut.reshape(planes, 1, 16, slots * columns // 16)
    cut = jnp.broadcast_to(cut, (planes, lines) + cut.shape[2:])
    cut = exchange(cut.reshape((devices,) + cut.shape[2:]), 2)
    cut = cut.reshape(devices * slots, columns)
    ada_grad = matmul_tn(silu_part, cut)
    sums = jnp.sum(cut, axis=0, dtype=jnp.float32)
    bias_width = columns // lines
    ada_bias_grad = lax.dynamic_slice_in_dim(sums, lax.axis_index("fsdp") * bias_width, bias_width)
    silu_grad = matmul_nt(cut, ada_weight).reshape(devices, slots * rows)
    flat = jnp.concatenate([silu_grad] + [term.reshape(devices, -1) for term in terms], axis=1)
    width = -(-flat.shape[1] // 1024) * 128
    flat = jnp.pad(flat, ((0, 0), (0, 8 * width - flat.shape[1])))
    flat = exchange(flat.reshape(devices, 8, width), 3).reshape(devices, -1)
    shared = jnp.sum(flat[:, slots * rows :], axis=0)
    silu_grad = flat[:, : slots * rows].reshape(planes, lines, slots, rows).sum(axis=0)
    silu_grad = silu_grad.transpose(1, 0, 2).reshape(slots, lines * rows)
    found, begin = [], 0
    for term in terms:
        found.append(shared[begin : begin + term.shape[0] // devices])
        begin += term.shape[0] // devices
    return ada_grad, ada_bias_grad, silu_grad, found


def by_columns(values, parts):
    rows, columns = values.shape
    return values.reshape(rows, parts, columns // parts).transpose(1, 0, 2)


SLOPE = math.sqrt(2.0 / math.pi)
WINDOW = 512


def mm(left, right):
    return jnp.dot(left, right, preferred_element_type=jnp.float32)


def local_call(kernel, outs, ins, anys, scratch, megabytes):
    return pl.pallas_call(
        kernel,
        out_shape=outs,
        in_specs=[pl.BlockSpec(memory_space=pltpu.VMEM)] * len(ins)
        + [pl.BlockSpec(memory_space=pl.ANY)] * len(anys),
        out_specs=[
            pl.BlockSpec(memory_space=pl.ANY if out.dtype == jnp.bfloat16 and out.ndim == 4 else pltpu.VMEM)
            for out in outs
        ],
        scratch_shapes=scratch,
        compiler_params=pltpu.CompilerParams(vmem_limit_bytes=megabytes * 2**20),
        cost_estimate=pl.CostEstimate(flops=0, bytes_accessed=0, transcendentals=0),
    )(*ins, *anys)


def shaped(dims, kind=jnp.float32):
    return jax.ShapeDtypeStruct(dims, kind)


def load_blocks(whole, room, sems, lanes=None):
    copies = []
    for block in range(4):
        source = whole.at[block]
        if lanes is not None:
            source = source.at[:, lanes[0] : lanes[1]]
        copies.append([pltpu.make_async_copy(source, room.at[block], sems.at[block])])
        copies[-1][0].start()
    return copies


def wait_all(copies):
    for copy in copies:
        copy.wait()


def by_rows(count, step, body):
    @pl.loop(0, count // step)
    def _(index):
        body(pl.ds(pl.multiple_of(index * step, step), step))


def lane_index(rows, lanes):
    return lax.broadcasted_iota(jnp.int32, (rows, lanes), 1)


def window_of(block, width, total, span):
    begin = min(block * width // 128 * 128, total - span)
    return begin, block * width - begin


def slot_rows(slots, table, column, width):
    value = jnp.zeros((slots.shape[0], width), jnp.float32)
    for slot in range(4):
        value = value + jnp.where(slots == slot, table[slot : slot + 1, column * width : (column + 1) * width], 0.0)
    return value


def add_slots(out, slots, value):
    for slot in range(4):
        out[slot : slot + 1, :] += jnp.sum(jnp.where(slots == slot, value, 0.0), axis=0, keepdims=True)


def centred(value):
    center = value - jnp.mean(value, axis=-1, keepdims=True)
    scale = lax.rsqrt(jnp.mean(center * center, axis=-1, keepdims=True) + 1e-06)
    return center * scale, scale


def norm_back(normed, scale, grad):
    return scale * (
        grad
        - jnp.mean(grad, axis=-1, keepdims=True)
        - normed * jnp.mean(grad * normed, axis=-1, keepdims=True)
    )


def head_window(head, size, total):
    begin = jnp.minimum(head * size // 128 * 128, total - 256)
    begin = pl.multiple_of(begin, 128)
    lane = lane_index(1, 256)
    offset = head * size - begin
    return begin, (lane >= offset) & (lane < offset + size)


def attend_back_kernel(joined, grad, stats, slots, slot_line, blocks, sums, bar, wide):
    rows, width = grad.shape
    size = width // HEADS
    scale = 1.0 / math.sqrt(size)
    bar[...] = jnp.where(slots[...] == slot_line[...], 0.0, -1e30)

    @pl.loop(0, HEADS)
    def _(head):
        begin, inside = head_window(head, size, width)
        columns = [pl.ds(pl.multiple_of(begin + part * width, 128), 256) for part in range(3)]
        query = jnp.where(inside, joined[:, columns[0]], 0.0)
        key = joined[:, columns[1]]
        value = joined[:, columns[2]]
        out_grad = jnp.where(inside, grad[:, columns[0]], 0.0)
        lane = lane_index(rows, 128)
        stat = jnp.sum(jnp.where(lane == head, stats[...], 0.0), axis=1, keepdims=True)
        probs = jnp.exp(matmul_nt(query, key) * scale + bar[...] - stat)
        prob_grad = matmul_nt(out_grad, value)
        inner = jnp.sum(probs * prob_grad, axis=1, keepdims=True)
        score_grad = (probs * (prob_grad - inner)).astype(jnp.bfloat16)
        found = (
            mm(score_grad, key) * scale,
            matmul_tn(score_grad, query) * scale,
            matmul_tn(probs.astype(jnp.bfloat16), out_grad),
        )
        for part in range(3):
            wide[:, columns[part]] = jnp.where(inside, found[part], wide[:, columns[part]])

    span = blocks.shape[2]
    block_width = 3 * width // 4

    def total(at):
        sums[...] += jnp.sum(wide[at, :].astype(jnp.bfloat16).astype(jnp.float32), axis=0, keepdims=True)

    sums[...] = jnp.zeros_like(sums)
    by_rows(rows, 64, total)
    for block in range(4):
        begin, offset = window_of(block, block_width, 3 * width, span)

        def cut(at):
            moved = wide[at, begin : begin + span]
            if offset:
                moved = pltpu.roll(moved, span - offset, 1)
            lane = lane_index(moved.shape[0], span)
            blocks[block, at, :] = jnp.where(lane < block_width, moved, 0.0).astype(jnp.bfloat16)

        by_rows(rows, 64, cut)


def attend_back(joined, grad, stats, slots):
    rows, total = joined.shape
    span = -(-total // 4 // 128) * 128 + 128
    return pl.pallas_call(
        attend_back_kernel,
        out_shape=[shaped((4, rows, span), jnp.bfloat16), shaped((1, total))],
        scratch_shapes=[pltpu.VMEM((rows, rows), jnp.float32), pltpu.VMEM((rows, total), jnp.float32)],
        compiler_params=pltpu.CompilerParams(vmem_limit_bytes=48 * 2**20),
        cost_estimate=pl.CostEstimate(flops=0, bytes_accessed=0, transcendentals=0),
    )(joined, grad, stats, slots.reshape(rows, 1), slots.reshape(1, rows))


def narrow_kernel(hidden, middle, out_grad, slots, table, bias, before_all, *refs):
    whole, mixed, branch_grad, pre_grad, sums, gate_sums, pre_sums, room, total, before, sems, more = refs
    rows, width = middle.shape
    blocks = load_blocks(whole, room, sems)
    copies = [pltpu.make_async_copy(before_all.at[part], before.at[part], more.at[part]) for part in range(4)]
    for copy in copies:
        copy.start()
    for part in range(4):
        wait_all(blocks[part])
        term = matmul_nt(hidden[part], room[part])
        if part == 0:
            total[...] = term + bias[...]
        else:
            total[...] += term
    sums[...] = jnp.zeros_like(sums)
    gate_sums[...] = jnp.zeros_like(gate_sums)
    pre_sums[...] = jnp.zeros_like(pre_sums)

    def finish(at):
        slot = slots[at, :]
        gate = slot_rows(slot, table, 5, width)
        branch = total[at, :]
        grad = out_grad[at, :].astype(jnp.float32)
        mixed[at, :] = (middle[at, :] + gate * branch).astype(jnp.bfloat16)
        add_slots(gate_sums, slot, grad * branch)
        value = (grad * gate).astype(jnp.bfloat16)
        branch_grad[at, :] = value
        sums[...] += jnp.sum(value.astype(jnp.float32), axis=0, keepdims=True)

    by_rows(rows, 64, finish)
    for part in range(4):
        copies[part].wait()
        total[...] = mm(branch_grad[...], room[part])

        def act(at):
            value = before[part, at, :]
            square = value * value
            bend = jnp.tanh(SLOPE * (value + 0.044715 * (square * value)))
            slope = 0.5 * (1.0 + bend) + 0.5 * value * (1.0 - bend * bend) * (
                SLOPE * (1.0 + 3.0 * 0.044715 * square)
            )
            value = (total[at, :] * slope).astype(jnp.bfloat16)
            pre_grad[part, at, :] = value
            pre_sums[part : part + 1, :] += jnp.sum(value.astype(jnp.float32), axis=0, keepdims=True)

        by_rows(rows, 64, act)


def narrow(hidden, before, middle, out_grad, slots, table, bias, whole):
    rows, width = middle.shape
    return pl.pallas_call(
        narrow_kernel,
        out_shape=[
            shaped((rows, width), jnp.bfloat16),
            shaped((rows, width), jnp.bfloat16),
            shaped((4, rows, width), jnp.bfloat16),
            shaped((1, width)),
            shaped((8, width)),
            shaped((8, width)),
        ],
        in_specs=[pl.BlockSpec(memory_space=pltpu.VMEM)] * 6 + [pl.BlockSpec(memory_space=pl.ANY)] * 2,
        scratch_shapes=[
            pltpu.VMEM((4, width, width), jnp.bfloat16),
            pltpu.VMEM((rows, width), jnp.float32),
            pltpu.VMEM((4, rows, width), jnp.float32),
            pltpu.SemaphoreType.DMA((32,)),
            pltpu.SemaphoreType.DMA((4,)),
        ],
        compiler_params=pltpu.CompilerParams(vmem_limit_bytes=58 * 2**20),
        cost_estimate=pl.CostEstimate(flops=0, bytes_accessed=0, transcendentals=0),
    )(hidden, middle, out_grad, slots.reshape(rows, 1), table, bias, before, whole)


def middle_kernel(pre_grad, middle, out_grad, branch, slots, table, *refs):
    up_whole, joined_whole, middle_grad, attended_grad, windows = refs[:5]
    slot_sums, sums, room, side, total, sems, more = refs[5:]
    rows, width = middle.shape
    columns = width // 4
    blocks = load_blocks(up_whole, room, sems)
    side_blocks = load_blocks(joined_whole, side, more, lanes=(width - WINDOW, width))
    for flip in range(4):
        wait_all(blocks[flip])
        term = matmul_nt(pre_grad[flip], room[flip])
        if flip == 0:
            total[...] = term
        else:
            total[...] += term
    slot_sums[...] = jnp.zeros_like(slot_sums)
    sums[...] = jnp.zeros_like(sums)

    def finish(at):
        slot = slots[at, :]
        grad = total[at, :]
        hat, scale = centred(middle[at, :])
        add_slots(slot_sums.at[1], slot, grad)
        add_slots(slot_sums.at[2], slot, grad * hat)
        grad = grad * (1.0 + slot_rows(slot, table, 4, width))
        grad = out_grad[at, :].astype(jnp.float32) + norm_back(hat, scale, grad)
        middle_grad[at, :] = grad
        add_slots(slot_sums.at[0], slot, grad * branch[at, :])
        value = (grad * slot_rows(slot, table, 2, width)).astype(jnp.bfloat16).astype(jnp.float32)
        total[at, :] = value
        sums[...] += jnp.sum(value, axis=0, keepdims=True)

    by_rows(rows, 64, finish)
    for block in range(4):
        begin, offset = window_of(block, columns, width, WINDOW)

        def cut(at):
            moved = total[at, begin : begin + WINDOW]
            if offset != WINDOW - columns:
                moved = pltpu.roll(moved, (2 * WINDOW - columns - offset) % WINDOW, 1)
            lane = lane_index(moved.shape[0], WINDOW)
            moved = jnp.where(lane >= WINDOW - columns, moved, 0.0)
            windows[block, at, :] = moved.astype(jnp.bfloat16)

        by_rows(rows, 64, cut)
    for block in side_blocks:
        wait_all(block)
    value = matmul_nt(windows[0], side[0])
    for block in range(1, 4):
        value = value + matmul_nt(windows[block], side[block])
    attended_grad[...] = value.astype(jnp.bfloat16)


def middle_back(pre_grad, middle, out_grad, branch, slots, table, up_whole, joined_whole):
    rows, width = middle.shape
    return pl.pallas_call(
        middle_kernel,
        out_shape=[
            shaped((rows, width)),
            shaped((rows, width), jnp.bfloat16),
            shaped((4, rows, WINDOW), jnp.bfloat16),
            shaped((3, 8, width)),
            shaped((1, width)),
        ],
        in_specs=[pl.BlockSpec(memory_space=pltpu.VMEM)] * 6 + [pl.BlockSpec(memory_space=pl.ANY)] * 2,
        scratch_shapes=[
            pltpu.VMEM((4, width, width), jnp.bfloat16),
            pltpu.VMEM((4, width, WINDOW), jnp.bfloat16),
            pltpu.VMEM((rows, width), jnp.float32),
            pltpu.SemaphoreType.DMA((32,)),
            pltpu.SemaphoreType.DMA((32,)),
        ],
        compiler_params=pltpu.CompilerParams(vmem_limit_bytes=58 * 2**20),
        cost_estimate=pl.CostEstimate(flops=0, bytes_accessed=0, transcendentals=0),
    )(pre_grad, middle, out_grad, branch, slots.reshape(rows, 1), table, up_whole, joined_whole)


def start_kernel(blocks, start, middle_grad, slots, table, *refs):
    whole, grad_out, slot_sums, room, total, sems = refs
    rows, width = start.shape
    span = blocks.shape[2]
    loads = load_blocks(whole, room, sems, lanes=(0, span))
    for flip in range(4):
        wait_all(loads[flip])
        term = matmul_nt(blocks[flip], room[flip])
        if flip == 0:
            total[...] = term
        else:
            total[...] += term
    slot_sums[...] = jnp.zeros_like(slot_sums)

    def finish(at):
        slot = slots[at, :]
        grad = total[at, :]
        hat, scale = centred(start[at, :])
        add_slots(slot_sums.at[0], slot, grad)
        add_slots(slot_sums.at[1], slot, grad * hat)
        grad = grad * (1.0 + slot_rows(slot, table, 1, width))
        grad_out[at, :] = middle_grad[at, :] + norm_back(hat, scale, grad)

    by_rows(rows, 64, finish)


def start_back(blocks, start, middle_grad, slots, table, whole):
    rows, width = start.shape
    return local_call(
        start_kernel,
        [shaped((rows, width)), shaped((2, 8, width))],
        [blocks, start, middle_grad, slots.reshape(rows, 1), table],
        [whole],
        [
            pltpu.VMEM((4, width, blocks.shape[2]), jnp.bfloat16),
            pltpu.VMEM((rows, width), jnp.float32),
            pltpu.SemaphoreType.DMA((32,)),
        ],
        48,
    )


def far_device(plane, depth, core):
    return (plane, depth * 2 + core)


class Gather:
    def __init__(self, shards, wholes, send_sems, recv_sems, local_sems):
        self.shards, self.wholes = shards, wholes
        self.send_sems, self.recv_sems, self.local_sems = send_sems, recv_sems, local_sems
        self.plane, self.depth, self.core = place()
        self.started = []
        self.kept = []
        self.counts = [0, 0, 0]

    def partners(self):
        found = [
            far_device(flipped(self.plane, 1), self.depth, self.core),
            far_device(flipped(self.plane, 2), self.depth, self.core),
            far_device(self.plane, self.depth, 1 - self.core),
        ]
        return found + [far_device(self.plane, (self.depth + d) % 4, self.core) for d in (1, 2, 3)]

    def spot(self, weight, flip, back, other=False):
        plane, depth = flipped(self.plane, flip), (self.depth + 4 - back) % 4
        core = 1 - self.core if other else self.core
        if weight < 2:
            return self.wholes[weight].at[plane, depth, core]
        return self.wholes[weight].at[depth, plane, core]

    def send(self, weight, source, target, partner, kind, entry):
        copy = pltpu.make_async_remote_copy(
            src_ref=source,
            dst_ref=target,
            send_sem=self.send_sems.at[weight, self.counts[weight]],
            recv_sem=self.recv_sems.at[weight, kind, entry],
            device_id=partner,
            device_id_type=pl.DeviceIdType.MESH,
        )
        self.counts[weight] += 1
        copy.start()
        self.started.append(copy)

    def arrive(self, weight, region, kind, entry):
        pltpu.make_async_remote_copy(
            src_ref=region,
            dst_ref=region,
            send_sem=self.send_sems.at[weight, 0],
            recv_sem=self.recv_sems.at[weight, kind, entry],
            device_id=self.partners()[2],
            device_id_type=pl.DeviceIdType.MESH,
        ).wait_recv()

    def pass_on(self, weight, source, flip, back):
        target = self.spot(weight, flip, back)
        beside = self.partners()
        if flip == 0 or (flip == 2 and back % 2 == 1):
            self.send(weight, source, target, beside[0], 1 if flip == 0 else 3, back)
        if flip == 0 or (flip == 1 and back % 2 == 0):
            self.send(weight, source, target, beside[1], 2 if flip == 0 else 3, back)
        self.send(weight, source, target, beside[2], 4 + flip, back)

    def open_plane(self, weight):
        keep = pltpu.make_async_copy(
            self.shards[weight], self.spot(weight, 0, 0), self.local_sems.at[weight]
        )
        keep.start()
        self.kept.append(keep)
        self.pass_on(weight, self.shards[weight], 0, 0)

    def open_line(self, weight):
        for d in (1, 3, 2):
            target = self.spot(weight, 0, 0)
            self.send(weight, self.shards[weight], target, self.partners()[2 + d], 0, d)

    def on_line(self, weight, back):
        region = self.spot(weight, 0, back)
        self.arrive(weight, region, 0, back)
        self.pass_on(weight, region, 0, back)

    def on_plane(self, weight, flip, back):
        region = self.spot(weight, flip, back)
        self.arrive(weight, region, flip, back)
        self.pass_on(weight, region, flip, back)

    def steps(self, weight):
        found = []
        for back in (0, 1, 3, 2):
            if back:
                found.append(partial(self.on_line, weight, back))
        for back in (0, 1, 3, 2):
            found.append(partial(self.on_plane, weight, 1, back))
            found.append(partial(self.on_plane, weight, 2, back))
        for back in (0, 1, 3, 2):
            found.append(partial(self.on_plane, weight, 3, back))
        return found

    def ready(self, weight):
        for flip in range(4):
            for back in (0, 1, 3, 2):
                self.arrive(weight, self.spot(weight, flip, back, True), 4 + flip, back)
        self.kept[weight].wait()

    def finish(self):
        for copy in self.started:
            copy.wait_send()


def greet(partners):
    barrier = pltpu.get_barrier_semaphore()
    for partner in partners:
        pl.semaphore_signal(
            barrier, inc=1, device_id=partner, device_id_type=pl.DeviceIdType.MESH
        )
    pl.semaphore_wait(barrier, len(partners))


def forward_kernel(
    normed,
    start,
    slots,
    slot_line,
    table,
    joined_bias,
    out_bias,
    up_bias,
    joined_shard,
    up_shard,
    down_shard,
    joined_whole,
    up_whole,
    down_whole,
    joined,
    attended,
    stats,
    branch,
    middle,
    normed2,
    hidden,
    before,
    room,
    product,
    wide_room,
    bar,
    before_room,
    send_sems,
    recv_sems,
    local_sems,
    load_sems,
    store_sems,
):
    gather = Gather(
        (joined_shard, up_shard, down_shard),
        (joined_whole, up_whole, down_whole),
        send_sems,
        recv_sems,
        local_sems,
    )
    greet(gather.partners())
    gather.open_line(0)
    for weight in range(3):
        gather.open_plane(weight)
    first = gather.steps(0)
    for step in first[:3]:
        step()
    gather.open_line(1)
    for step in first[3:]:
        step()
    later = gather.steps(1)[:3] + [partial(gather.open_line, 2)] + gather.steps(1)[3:]
    later += gather.steps(2)

    def tick(count=1):
        for _ in range(count):
            if later:
                later.pop(0)()

    rows, width = normed.shape
    columns = joined.shape[1] // 4
    size = room.shape[1]
    gather.ready(0)
    loads = [
        pltpu.make_async_copy(
            joined_whole.at[block], room.at[block], load_sems.at[block]
        )
        for block in range(4)
    ]
    for load in loads:
        load.start()
    tick(3)
    span = product.shape[1]
    for block in range(4):
        loads[block].wait()
        product[...] = mm(normed[...], room[block].reshape(width, width)[:, :span])
        begin, offset = window_of(block, columns, joined.shape[1], span)

        def put(at):
            moved = product[at, :]
            if offset:
                moved = pltpu.roll(moved, offset, 1)
            lane = lane_index(moved.shape[0], span)
            inside = (lane >= offset) & (lane < offset + columns)
            wide_room[at, begin : begin + span] = jnp.where(
                inside, moved, wide_room[at, begin : begin + span]
            )

        by_rows(rows, 64, put)
        tick()

    def settle(at):
        joined[at, :] = (wide_room[at, :] + joined_bias[...]).astype(jnp.bfloat16)

    by_rows(rows, 64, settle)
    bar[...] = jnp.where(slots[...] == slot_line[...], 0.0, -1e30)
    stats[...] = jnp.zeros_like(stats)
    head_size = width // HEADS
    scale = 1.0 / math.sqrt(head_size)
    for group in range(8):

        @pl.loop(2 * group, 2 * group + 2)
        def _(head):
            at, inside = head_window(head, head_size, width)
            query = jnp.where(inside, joined[:, pl.ds(at, 256)], 0.0)
            key = joined[:, pl.ds(pl.multiple_of(at + width, 128), 256)]
            value = joined[:, pl.ds(pl.multiple_of(at + 2 * width, 128), 256)]
            scores = matmul_nt(query, key) * scale + bar[...]
            highest = jnp.max(scores, axis=1, keepdims=True)
            powers = jnp.exp(scores - highest)
            totals = jnp.sum(powers, axis=1, keepdims=True)
            probs = (powers * (1.0 / totals)).astype(jnp.bfloat16)
            found = mm(probs, value)
            wide_room[:, pl.ds(at, 256)] = jnp.where(inside, found, wide_room[:, pl.ds(at, 256)])
            lane = lane_index(rows, 128)
            stats[...] = jnp.where(lane == head, highest + jnp.log(totals), stats[...])

        tick(2)

    attended[...] = wide_room[:, :width].astype(jnp.bfloat16)
    columns = width // 4
    for block in range(4):
        product[:, :WINDOW] = mm(attended[...], room[block].reshape(width, width)[:, width - WINDOW :])
        begin, offset = window_of(block, columns, width, WINDOW)

        def put(at):
            moved = product[at, :WINDOW]
            if offset != WINDOW - columns:
                moved = pltpu.roll(moved, columns + offset, 1)
            lane = lane_index(moved.shape[0], WINDOW)
            inside = (lane >= offset) & (lane < offset + columns)
            branch[at, begin : begin + WINDOW] = jnp.where(
                inside, moved, branch[at, begin : begin + WINDOW]
            )

        by_rows(rows, 64, put)
        tick()

    def combine(at):
        slot = slots[at, :]
        value = branch[at, :] + out_bias[...]
        branch[at, :] = value
        value = start[at, :] + slot_rows(slot, table, 2, width) * value
        middle[at, :] = value
        hat, _ = centred(value)
        value = hat * (1.0 + slot_rows(slot, table, 4, width)) + slot_rows(slot, table, 3, width)
        normed2[at, :] = value.astype(jnp.bfloat16)

    by_rows(rows, 64, combine)
    while len(later) > 15:
        tick()
    gather.ready(1)
    loads = [
        pltpu.make_async_copy(up_whole.at[block], room.at[block], load_sems.at[block])
        for block in range(4)
    ]
    for load in loads:
        load.start()
    stores = [None, None]
    for block in range(4):
        loads[block].wait()
        slot = block % 2
        if stores[slot] is not None:
            stores[slot].wait()
        before_room[slot] = mm(normed2[...], room[block].reshape(width, width)) + up_bias[block]
        stores[slot] = pltpu.make_async_copy(
            before_room.at[slot], before.at[block], store_sems.at[slot]
        )
        stores[slot].start()

        def act(some):
            value = before_room[slot, some, :]
            bend = 1.0 + jnp.tanh(SLOPE * (value + 0.044715 * (value * value * value)))
            hidden[block, some, :] = (value * (0.5 * bend)).astype(jnp.bfloat16)

        by_rows(rows, 64, act)
        tick(3)
    while later:
        tick()
    for store in stores:
        store.wait()
    gather.ready(2)
    gather.finish()


def forward(normed, start, slots, table, joined_bias, out_bias, up_bias, shards):
    rows, width = normed.shape
    deep = width // 8
    whole = shaped((4, 4, 2, deep, width), jnp.bfloat16)
    vmem, away = pl.BlockSpec(memory_space=pltpu.VMEM), pl.BlockSpec(memory_space=pl.ANY)
    return pl.pallas_call(
        forward_kernel,
        out_shape=[
            whole,
            whole,
            whole,
            shaped((rows, 3 * width), jnp.bfloat16),
            shaped((rows, width), jnp.bfloat16),
            shaped((rows, 128)),
            shaped((rows, width)),
            shaped((rows, width)),
            shaped((rows, width), jnp.bfloat16),
            shaped((4, rows, width), jnp.bfloat16),
            shaped((4, rows, width)),
        ],
        in_specs=[vmem] * 8 + [away] * 3,
        out_specs=[away] * 3 + [vmem] * 7 + [away],
        scratch_shapes=[
            pltpu.VMEM((4, 4, 2, deep, width), jnp.bfloat16),
            pltpu.VMEM((rows, 1024), jnp.float32),
            pltpu.VMEM((rows, 3 * width), jnp.float32),
            pltpu.VMEM((rows, rows), jnp.float32),
            pltpu.VMEM((2, rows, width), jnp.float32),
            pltpu.SemaphoreType.DMA((3, 32)),
            pltpu.SemaphoreType.DMA((3, 8, 4)),
            pltpu.SemaphoreType.DMA((3,)),
            pltpu.SemaphoreType.DMA((4,)),
            pltpu.SemaphoreType.DMA((2,)),
        ],
        compiler_params=pltpu.CompilerParams(
            collective_id=4, has_side_effects=True, vmem_limit_bytes=60 * 2**20
        ),
        cost_estimate=pl.CostEstimate(
            flops=2 * 10 * rows * width * width, bytes_accessed=10**8, transcendentals=0
        ),
    )(
        normed,
        start,
        slots.reshape(rows, 1),
        slots.reshape(1, rows),
        table,
        joined_bias,
        out_bias,
        up_bias,
        *shards,
    )


SENT = ((0, (1, 3)), (0, (0, 2)), (1, (2, 3)), (1, (0, 1)))


def outer_kernel(plane_major, lefts, spans, *refs):
    left, right = refs[:lefts], refs[lefts : 2 * lefts]
    outs, (room, sems) = refs[2 * lefts : 2 * lefts + 8], refs[2 * lefts + 8 :]
    plane, _, core = place()
    sides = (1 - core, core)
    width = room.shape[1]
    deep = width // 8
    draining = [[], []]
    for block in range(4):
        slot = block % 2
        wait_all(draining[slot])
        index = flipped(plane, block) if plane_major else block
        if lefts == 1:
            room[slot] = mm(left[0][...], right[0][index]).astype(jnp.bfloat16)
        else:
            low, high = spans
            head = mm(left[0][...], right[0][index])
            tail = mm(left[1][...], right[1][index])
            room[slot, :, :high] = head[:, :high].astype(jnp.bfloat16)
            room[slot, :, high:low] = (head[:, high:low] + tail[:, : low - high]).astype(jnp.bfloat16)
            room[slot, :, low:] = tail[:, low - high :].astype(jnp.bfloat16)
        copies = []
        for kind in range(2):
            for number, (half, flips) in enumerate(SENT):
                target = outs[4 * kind + number]
                for place_in, flip in enumerate(flips):
                    for step in range(2):
                        depth = 2 * half + step
                        if plane_major:
                            if flip != block:
                                continue
                            row = depth * 2 + sides[kind]
                        else:
                            if depth != block:
                                continue
                            row = flipped(plane, flip) * 2 + sides[kind]
                        source = room.at[slot, pl.ds(pl.multiple_of(row * deep, 16), deep)]
                        copies.append(
                            pltpu.make_async_copy(
                                source, target.at[place_in, step], sems.at[slot, len(copies)]
                            )
                        )
        for copy in copies:
            copy.start()
        draining[slot] = copies
    wait_all(draining[0])
    wait_all(draining[1])


def outer(plane_major, lefts, rights, spans=None):
    width = lefts[0].shape[0]
    deep = width // 8
    return pl.pallas_call(
        partial(outer_kernel, plane_major, len(lefts), spans),
        out_shape=[shaped((2, 2, deep, width), jnp.bfloat16)] * 8,
        in_specs=[pl.BlockSpec(memory_space=pltpu.VMEM)] * (2 * len(lefts)),
        out_specs=[pl.BlockSpec(memory_space=pl.ANY)] * 8,
        scratch_shapes=[
            pltpu.VMEM((2, width, width), jnp.bfloat16),
            pltpu.SemaphoreType.DMA((2, 8)),
        ],
        compiler_params=pltpu.CompilerParams(vmem_limit_bytes=48 * 2**20),
        cost_estimate=pl.CostEstimate(flops=0, bytes_accessed=0, transcendentals=0),
    )(*lefts, *rights)


def low_bits(value):
    return value.astype(jnp.bfloat16)


def wide(value):
    return value.astype(jnp.float32)


def scatter_pieces(pieces):
    depth = place()[1]
    summed = [wide(own) + wide(swap(other, "core")) for other, own in zip(pieces[:4], pieces[4:])]
    totals = []
    for half, (first, _, second, _) in enumerate(HALF_ORDERS):
        sent, kept = summed[2 * half], summed[2 * half + 1]
        arrived = wide(swap(low_bits(sent), first))
        across = swap(low_bits(kept[1] + arrived[1]), second)
        totals.append(kept[0] + arrived[0] + wide(across))
    total = jnp.concatenate(totals)
    result = pick(total, depth)
    for turn in (1, 2, 3):
        result = result + wide(swap(low_bits(pick(total, (depth - turn) % 4)), turn))
    return result


def box_device(
    tokens,
    condition,
    kept_index,
    segment,
    grid_side,
    ada_weight,
    ada_bias,
    attn_weight,
    attn_bias,
    proj_weight,
    out_bias,
    up_weight,
    up_bias,
    down_weight,
    grad_out,
):
    rows, width = tokens.shape
    slot_count = condition.shape[0]
    core = place()[2]
    columns = attn_weight.shape[1]
    turned = down_weight.T.reshape(2, up_weight.shape[0], down_weight.shape[0])
    mine, theirs = pick(turned, core), pick(turned, 1 - core)
    arrived = swap(theirs, "core")
    down_shard = jnp.where(
        core == 0,
        jnp.concatenate([mine, arrived], axis=1),
        jnp.concatenate([arrived, mine], axis=1),
    )
    slot_ids = jnp.arange(slot_count, dtype=jnp.int32)
    side_rows = jnp.sum(jnp.where(segment[:, None] == slot_ids[None, :], grid_side[None, :], 0), axis=1)
    start = tokens.astype(jnp.float32) + position_code(kept_index, side_rows, width)
    silu_cond, silu_back = jax.vjp(jax.nn.silu, condition.astype(jnp.float32))
    silu_bf = silu_cond.astype(jnp.bfloat16)
    silu_all, (ada_bfull, attn_bfull, out_bfull, up_bfull) = gather_small(
        silu_bf, (ada_bias, attn_bias, out_bias, up_bias)
    )
    modulation, silu_part = modulate_slots(silu_all, ada_weight, ada_bfull)
    table = jnp.pad(modulation, ((0, 8 - slot_count), (0, 0)))

    def own_rows(part):
        return sum(
            jnp.where(segment[:, None] == slot, modulation[slot, part * width : (part + 1) * width], 0.0)
            for slot in range(slot_count)
        )

    normed1 = norm_modulate(start, own_rows(0), own_rows(1)).astype(jnp.bfloat16)
    zeros = jnp.zeros((width,), jnp.bfloat16)
    joined_bias = jnp.concatenate([attn_bfull[:width], zeros, attn_bfull[width:]])
    out_bias_f = out_bfull.astype(jnp.float32)
    (
        joined_whole,
        up_whole,
        down_whole,
        joined,
        attended,
        stats,
        branch1,
        middle,
        normed2,
        hidden,
        before,
    ) = forward(
        normed1,
        start,
        segment,
        table,
        joined_bias.astype(jnp.float32)[None],
        out_bias_f[None, :width],
        up_bfull.astype(jnp.float32).reshape(4, 1, -1),
        (jnp.concatenate([attn_weight, proj_weight], axis=1), up_weight, down_shard),
    )
    joined_whole, up_whole, down_whole = [
        whole.reshape(4, width, width) for whole in (joined_whole, up_whole, down_whole)
    ]
    mixed, grad_branch2, pre_grad, branch2_sums, gate2_sums, pre_sums = narrow(
        hidden, before, middle, grad_out, segment, table, out_bias_f[None, width:], down_whole
    )
    down_total = scatter_pieces(outer(False, [grad_branch2.T], [hidden]))
    up_weight_grad = scatter_pieces(outer(True, [normed2.T], [pre_grad]))
    half = down_total.shape[1] // 2
    cut = down_total.reshape(-1, 2, half).transpose(1, 0, 2)
    mine, theirs = pick(cut, core), pick(cut, 1 - core)
    arrived = swap(theirs, "core")
    down_weight_grad = jnp.where(
        core == 0, jnp.concatenate([mine, arrived]), jnp.concatenate([arrived, mine])
    ).T
    middle_grad, attended_grad, windows, slot_sums2, branch1_sums = middle_back(
        pre_grad, middle, grad_out, branch1, segment, table, up_whole, joined_whole
    )
    blocks, joined_sums = attend_back(joined, attended_grad, stats, segment)
    joined_total = scatter_pieces(
        outer(
            True,
            [normed1.T, attended.T],
            [blocks, windows],
            (blocks.shape[2], width - WINDOW),
        )
    )
    tokens_grad, slot_sums1 = start_back(blocks, start, middle_grad, segment, table, joined_whole)
    modulation_grad = jnp.concatenate(
        [slot_sums1[0], slot_sums1[1], slot_sums2[0], slot_sums2[1], slot_sums2[2], gate2_sums], axis=1
    )[:slot_count].astype(jnp.bfloat16)
    joined_sums = joined_sums[0]
    terms = (
        jnp.concatenate([joined_sums[:width], joined_sums[2 * width :]]),
        jnp.concatenate([branch1_sums[0], branch2_sums[0]]),
        pre_sums[:4].reshape(-1),
    )
    ada_weight_grad, ada_bias_grad, silu_grad, bias_grads = modulation_back(
        modulation_grad, silu_part, ada_weight, terms
    )
    attn_bias_grad, out_bias_grad, up_bias_grad = bias_grads
    return (
        mixed,
        tokens_grad,
        silu_back(silu_grad)[0],
        ada_weight_grad,
        ada_bias_grad,
        joined_total[:, :columns],
        attn_bias_grad,
        joined_total[:, columns:],
        out_bias_grad,
        up_weight_grad,
        up_bias_grad,
        down_weight_grad,
    )


def per_device(
    tokens,
    condition,
    kept_index,
    segment,
    grid_side,
    ada_weight,
    ada_bias,
    attn_weight,
    attn_bias,
    proj_weight,
    out_bias,
    up_weight,
    up_bias,
    down_weight,
    grad_out,
):
    if on_box():
        return box_device(
            tokens,
            condition,
            kept_index,
            segment,
            grid_side,
            ada_weight,
            ada_bias,
            attn_weight,
            attn_bias,
            proj_weight,
            out_bias,
            up_weight,
            up_bias,
            down_weight,
            grad_out,
        )
    model_width = tokens.shape[1]
    slot_count = condition.shape[0]
    planes = lax.axis_size("dp")
    joined_w, up_w, down_w = gather_blocks(attn_weight, proj_weight, up_weight, down_weight)
    attn_columns = attn_weight.shape[1]
    slot_ids = jnp.arange(slot_count, dtype=jnp.int32)
    same_slot = segment[:, None] == slot_ids[None, :]
    slot_table = same_slot.astype(jnp.float32)
    side_rows = jnp.sum(jnp.where(same_slot, grid_side[None, :], 0), axis=1)
    start = tokens.astype(jnp.float32) + position_code(kept_index, side_rows, model_width)
    condition_f = condition.astype(jnp.float32)
    silu_cond, silu_back = jax.vjp(jax.nn.silu, condition_f)
    silu_bf = silu_cond.astype(jnp.bfloat16)
    silu_all, (ada_bfull, attn_bfull, out_bfull, up_bfull) = gather_small(
        silu_bf, (ada_bias, attn_bias, out_bias, up_bias)
    )
    modulation, silu_part = modulate_slots(silu_all, ada_weight, ada_bfull)
    mod_rows = jnp.dot(
        slot_table, modulation, precision=lax.Precision.HIGHEST, preferred_element_type=jnp.float32
    )
    shift_one, scale_one, gate_one, shift_two, scale_two, gate_two = jnp.split(mod_rows, 6, axis=1)
    normed1, norm1_back = jax.vjp(norm_modulate, start, shift_one, scale_one)
    normed1_bf = normed1.astype(jnp.bfloat16)
    projected = jnp.concatenate(
        [
            jnp.dot(normed1_bf, joined_w[part, :, :attn_columns], preferred_element_type=jnp.float32)
            for part in range(planes)
        ],
        axis=1,
    )
    proj_full = joined_w[:, :, attn_columns:].transpose(1, 0, 2).reshape(model_width, model_width)
    attn_bias_f = attn_bfull.astype(jnp.float32)
    query_bf = (projected[:, :model_width] + attn_bias_f[:model_width]).astype(jnp.bfloat16)
    key_bf = projected[:, model_width : 2 * model_width].astype(jnp.bfloat16)
    value_bf = (projected[:, 2 * model_width :] + attn_bias_f[model_width:]).astype(jnp.bfloat16)
    attended, log_totals = attend_forward(query_bf, key_bf, value_bf, segment, HEADS)
    attended_bf = attended.astype(jnp.bfloat16)
    out_bias_f = out_bfull.astype(jnp.float32)
    branch1 = (
        jnp.dot(attended_bf, proj_full, preferred_element_type=jnp.float32)
        + out_bias_f[:model_width]
    )
    middle = start + gate_one * branch1
    normed2, norm2_back = jax.vjp(norm_modulate, middle, shift_two, scale_two)
    normed2_bf = normed2.astype(jnp.bfloat16)
    hidden_parts, gelu_parts = [], []
    up_bias_f = up_bfull.astype(jnp.float32).reshape(planes, -1)
    branch2 = out_bias_f[model_width:]
    for part in range(planes):
        hidden_pre = (
            jnp.dot(normed2_bf, up_w[part], preferred_element_type=jnp.float32) + up_bias_f[part]
        )
        hidden_act, gelu_back = jax.vjp(partial(jax.nn.gelu, approximate=True), hidden_pre)
        hidden_parts.append(hidden_act.astype(jnp.bfloat16))
        gelu_parts.append(gelu_back)
        branch2 = branch2 + matmul_nt(hidden_parts[part], down_w[part])
    mixed = (middle + gate_two * branch2).astype(jnp.bfloat16)
    out_grad = grad_out.astype(jnp.float32)
    grad_gate_two = out_grad * branch2
    grad_branch2 = (out_grad * gate_two).astype(jnp.bfloat16)
    down_weight_grad = scatter_whole(matmul_tn(jnp.concatenate(hidden_parts, axis=1), grad_branch2))
    pre_parts = []
    for part in range(planes):
        hidden_grad = jnp.dot(grad_branch2, down_w[part], preferred_element_type=jnp.float32)
        pre_parts.append(gelu_parts[part](hidden_grad)[0].astype(jnp.bfloat16))
    pre_grad = jnp.stack(pre_parts)
    (up_weight_grad,) = scatter_rows([(normed2_bf, pre_grad)])
    up_bias_term = jnp.sum(pre_grad, axis=1, dtype=jnp.float32).reshape(-1)
    normed2_grad = sum(matmul_nt(pre_parts[part], up_w[part]) for part in range(planes))
    middle_part, grad_shift_two, grad_scale_two = norm2_back(normed2_grad)
    middle_grad = out_grad + middle_part
    grad_gate_one = middle_grad * branch1
    grad_branch1 = (middle_grad * gate_one).astype(jnp.bfloat16)
    attended_grad = matmul_nt(grad_branch1, proj_full).astype(jnp.bfloat16)
    query_grad, key_grad, value_grad = attend_backward(
        query_bf, key_bf, value_bf, attended_grad, segment, log_totals, HEADS
    )
    query_grad_bf = query_grad.astype(jnp.bfloat16)
    value_grad_bf = value_grad.astype(jnp.bfloat16)
    joined_grad = jnp.concatenate(
        [query_grad_bf, key_grad.astype(jnp.bfloat16), value_grad_bf], axis=1
    )
    joined_parts = by_columns(joined_grad, planes)
    attn_weight_grad, proj_weight_grad = scatter_rows(
        [(normed1_bf, joined_parts), (attended_bf, by_columns(grad_branch1, planes))]
    )
    attn_bias_term = jnp.concatenate(
        [
            jnp.sum(query_grad_bf, axis=0, dtype=jnp.float32),
            jnp.sum(value_grad_bf, axis=0, dtype=jnp.float32),
        ]
    )
    normed1_grad = sum(
        matmul_nt(joined_parts[part], joined_w[part, :, :attn_columns]) for part in range(planes)
    )
    start_part, grad_shift_one, grad_scale_one = norm1_back(normed1_grad)
    tokens_grad = middle_grad + start_part
    mod_rows_grad = jnp.concatenate(
        [
            grad_shift_one,
            grad_scale_one,
            grad_gate_one,
            grad_shift_two,
            grad_scale_two,
            grad_gate_two,
        ],
        axis=1,
    )
    modulation_grad = lax.dot_general(
        slot_table,
        mod_rows_grad,
        (((0,), (0,)), ((), ())),
        precision=lax.Precision.HIGHEST,
        preferred_element_type=jnp.float32,
    ).astype(jnp.bfloat16)
    out_bias_term = jnp.concatenate(
        [
            jnp.sum(grad_branch1, axis=0, dtype=jnp.float32),
            jnp.sum(grad_branch2, axis=0, dtype=jnp.float32),
        ]
    )
    ada_weight_grad, ada_bias_grad, silu_grad, bias_grads = modulation_back(
        modulation_grad, silu_part, ada_weight, (attn_bias_term, out_bias_term, up_bias_term)
    )
    attn_bias_grad, out_bias_grad, up_bias_grad = bias_grads
    condition_grad = silu_back(silu_grad)[0]
    return (
        mixed,
        tokens_grad,
        condition_grad,
        ada_weight_grad,
        ada_bias_grad,
        attn_weight_grad,
        attn_bias_grad,
        proj_weight_grad,
        out_bias_grad,
        up_weight_grad,
        up_bias_grad,
        down_weight_grad,
    )


def solution(mesh):
    return jax.shard_map(
        per_device,
        mesh=mesh,
        in_specs=(
            P(("dp", "fsdp"), None),
            P(("dp", "fsdp"), None),
            P(("dp", "fsdp")),
            P(("dp", "fsdp")),
            P(("dp", "fsdp")),
            P("fsdp", "dp"),
            P(("dp", "fsdp")),
            P("fsdp", "dp"),
            P(("dp", "fsdp")),
            P("fsdp", "dp"),
            P(("dp", "fsdp")),
            P("fsdp", "dp"),
            P(("dp", "fsdp")),
            P("fsdp", "dp"),
            P(("dp", "fsdp"), None),
        ),
        out_specs=(
            P(("dp", "fsdp"), None),
            P(("dp", "fsdp"), None),
            P(("dp", "fsdp"), None),
            P("fsdp", "dp"),
            P(("dp", "fsdp")),
            P("fsdp", "dp"),
            P(("dp", "fsdp")),
            P("fsdp", "dp"),
            P(("dp", "fsdp")),
            P("fsdp", "dp"),
            P(("dp", "fsdp")),
            P("fsdp", "dp"),
        ),
        check_vma=False,
    )
```

```python
from functools import partial
import math

import jax
import jax.numpy as jnp
from jax import lax
from jax.experimental import pallas as pl
from jax.experimental.pallas import tpu as pltpu
from jax.sharding import PartitionSpec as P

HEADS = 16
AXES = ("dp", "fsdp")


def position_code(kept_index, side_rows, model_width):
    quarter = model_width // 4
    exponent = jnp.arange(quarter, dtype=jnp.float32) / quarter
    frequency = 1.0 / 10000.0**exponent
    column = (kept_index % side_rows).astype(jnp.float32)[:, None] * frequency[None, :]
    line_pos = (kept_index // side_rows).astype(jnp.float32)[:, None] * frequency[None, :]
    return jnp.concatenate(
        [jnp.sin(column), jnp.cos(column), jnp.sin(line_pos), jnp.cos(line_pos)], axis=1
    )


def layer_norm(values):
    center = values - jnp.mean(values, axis=-1, keepdims=True)
    return center * lax.rsqrt(jnp.mean(center * center, axis=-1, keepdims=True) + 1e-06)


def norm_modulate(values, shift_rows, scale_rows):
    return layer_norm(values) * (1.0 + scale_rows) + shift_rows


def matmul_nt(first_matrix, second_matrix):
    return lax.dot_general(
        first_matrix, second_matrix, (((1,), (1,)), ((), ())), preferred_element_type=jnp.float32
    )


def matmul_tn(first_matrix, second_matrix):
    return lax.dot_general(
        first_matrix, second_matrix, (((0,), (0,)), ((), ())), preferred_element_type=jnp.float32
    )


def attend_forward(query_bf, key_bf, value_bf, segment, head_count):
    row_count, model_width = query_bf.shape
    head_size = model_width // head_count
    block_rows = min(row_count, 512)
    block_count = row_count // block_rows
    score_scale = 1.0 / math.sqrt(head_size)
    key_heads = key_bf.reshape(row_count, head_count, head_size)
    value_heads = value_bf.reshape(row_count, head_count, head_size)

    def forward_block(block_index):
        query_rows = query_bf.reshape(block_rows, head_count, head_size)
        same_image = segment[:, None] == segment[None, :]
        scores = (
            jnp.einsum("qhd,khd->hqk", query_rows, key_heads, preferred_element_type=jnp.float32)
            * score_scale
        )
        scores = jnp.where(same_image[None], scores, -1e30)
        highest = jnp.max(scores, axis=2, keepdims=True)
        powers = jnp.exp(scores - highest)
        totals = jnp.sum(powers, axis=2, keepdims=True)
        probs_bf = (powers / totals).astype(jnp.bfloat16)
        attended = jnp.einsum(
            "hqk,khd->qhd", probs_bf, value_heads, preferred_element_type=jnp.float32
        )
        return (attended.reshape(block_rows, model_width), (highest + jnp.log(totals))[:, :, 0])

    attended, log_totals = lax.map(forward_block, jnp.arange(block_count, dtype=jnp.int32))
    return (attended.reshape(row_count, model_width), log_totals)


def attend_backward(query_bf, key_bf, value_bf, attended_grad, segment, log_totals, head_count):
    row_count, model_width = query_bf.shape
    head_size = model_width // head_count
    block_rows = min(row_count, 512)
    block_count = row_count // block_rows
    score_scale = 1.0 / math.sqrt(head_size)
    key_heads = key_bf.reshape(row_count, head_count, head_size)
    value_heads = value_bf.reshape(row_count, head_count, head_size)

    def backward_block(running, pieces):
        key_sum, value_sum = running
        block_index, log_rows = pieces
        query_rows = query_bf.reshape(block_rows, head_count, head_size)
        grad_rows = attended_grad.reshape(block_rows, head_count, head_size)
        same_image = segment[:, None] == segment[None, :]
        scores = (
            jnp.einsum("qhd,khd->hqk", query_rows, key_heads, preferred_element_type=jnp.float32)
            * score_scale
        )
        scores = jnp.where(same_image[None], scores, -1e30)
        probs = jnp.exp(scores - log_rows[:, :, None])
        probs_bf = probs.astype(jnp.bfloat16)
        prob_grad = jnp.einsum(
            "qhd,khd->hqk", grad_rows, value_heads, preferred_element_type=jnp.float32
        )
        row_inner = jnp.sum(probs * prob_grad, axis=2, keepdims=True)
        score_grad = (probs * (prob_grad - row_inner)).astype(jnp.bfloat16)
        query_grad = (
            jnp.einsum("hqk,khd->qhd", score_grad, key_heads, preferred_element_type=jnp.float32)
            * score_scale
        )
        key_sum = (
            key_sum
            + jnp.einsum("hqk,qhd->khd", score_grad, query_rows, preferred_element_type=jnp.float32)
            * score_scale
        )
        value_sum = value_sum + jnp.einsum(
            "hqk,qhd->khd", probs_bf, grad_rows, preferred_element_type=jnp.float32
        )
        return ((key_sum, value_sum), query_grad.reshape(block_rows, model_width))

    empty_sum = jnp.zeros((row_count, head_count, head_size), jnp.float32)
    sums, query_grad = lax.scan(
        backward_block,
        (empty_sum, empty_sum),
        (jnp.arange(block_count, dtype=jnp.int32), log_totals),
    )
    return (
        query_grad.reshape(row_count, model_width),
        sums[0].reshape(row_count, model_width),
        sums[1].reshape(row_count, model_width),
    )


def on_box():
    return lax.axis_size("dp") == 4 and lax.axis_size("fsdp") == 8


def neighbour(index, axis):
    plane, line = index // 8, index % 8
    if axis == "x":
        plane ^= 1
    elif axis == "y":
        plane ^= 2
    elif axis == "core":
        line ^= 1
    else:
        line = (line - 2 * axis) % 8
    return plane * 8 + line


def swap(values, axis):
    return lax.ppermute(values, AXES, [(index, neighbour(index, axis)) for index in range(32)])


HALF_ORDERS = (("x", 1, "y", 2), ("y", 2, "x", 1))


def place():
    plane, line = lax.axis_index("dp"), lax.axis_index("fsdp")
    return plane, line // 2, line % 2


def flipped(plane, flip):
    if flip % 2:
        plane = plane + 1 - 2 * (plane % 2)
    if flip // 2:
        plane = plane + 2 - 4 * (plane // 2)
    return plane


def pick(values, index):
    return lax.dynamic_index_in_dim(values, index, axis=0, keepdims=False)


def gather_blocks(attn_weight, proj_weight, up_weight, down_weight):
    parts = lax.axis_size("dp")
    attn, proj, up, down = [
        lax.all_gather(lax.all_gather(weight, "dp", axis=1, tiled=True), "fsdp", axis=0, tiled=True)
        for weight in (attn_weight, proj_weight, up_weight, down_weight)
    ]
    width = attn.shape[0]

    def by_block(weight):
        return weight.reshape(weight.shape[0], parts, -1).transpose(1, 0, 2)

    joined = jnp.concatenate([by_block(attn), by_block(proj)], axis=2)
    return joined, by_block(up), by_block(down.T.reshape(width, -1))


def scatter_whole(gradient):
    part = lax.psum_scatter(
        gradient.astype(jnp.bfloat16), "dp", scatter_dimension=1, tiled=True
    ).astype(jnp.float32)
    return lax.psum_scatter(part, "fsdp", scatter_dimension=0, tiled=True)


def scatter_rows(pairs):
    return [
        scatter_whole(matmul_tn(left, right.transpose(1, 0, 2).reshape(left.shape[0], -1)))
        for left, right in pairs
    ]


def trade(one_for_all, values, out, send_sems, recv_sems):
    planes, lines = lax.axis_size("dp"), lax.axis_size("fsdp")
    count = planes * lines
    me = lax.axis_index("dp") * lines + lax.axis_index("fsdp")

    def device(index):
        return (index // lines, index % lines)

    def chunk(index):
        return values if one_for_all else values.at[index]

    barrier = pltpu.get_barrier_semaphore()

    @pl.loop(1, count)
    def _(step):
        pl.semaphore_signal(
            barrier,
            inc=1,
            device_id=device((me + step) % count),
            device_id_type=pl.DeviceIdType.MESH,
        )

    pl.semaphore_wait(barrier, count - 1)

    @pl.loop(1, count)
    def _(step):
        peer = (me + step) % count
        pltpu.make_async_remote_copy(
            src_ref=chunk(peer),
            dst_ref=out.at[me],
            send_sem=send_sems.at[step],
            recv_sem=recv_sems.at[step],
            device_id=device(peer),
            device_id_type=pl.DeviceIdType.MESH,
        ).start()

    if one_for_all:
        out[me] = values[...]
    else:
        out[me] = values[me]

    @pl.loop(1, count)
    def _(step):
        peer = (me + step) % count
        copy = pltpu.make_async_remote_copy(
            src_ref=chunk(peer),
            dst_ref=out.at[(me + count - step) % count],
            send_sem=send_sems.at[step],
            recv_sem=recv_sems.at[step],
            device_id=device(peer),
            device_id_type=pl.DeviceIdType.MESH,
        )
        copy.wait()


def exchange(values, collective_id, one_for_all=False):
    count = lax.axis_size("dp") * lax.axis_size("fsdp")
    chunk = values.shape[-2:]
    size = count * chunk[0] * chunk[1] * values.dtype.itemsize
    return pl.pallas_call(
        partial(trade, one_for_all),
        out_shape=jax.ShapeDtypeStruct((count,) + chunk, values.dtype),
        in_specs=[pl.BlockSpec(memory_space=pltpu.VMEM)],
        out_specs=pl.BlockSpec(memory_space=pltpu.VMEM),
        scratch_shapes=[pltpu.SemaphoreType.DMA((count,)), pltpu.SemaphoreType.DMA((count,))],
        compiler_params=pltpu.CompilerParams(
            collective_id=collective_id,
            has_side_effects=True,
            vmem_limit_bytes=3 * size + 4 * 2**20,
        ),
        cost_estimate=pl.CostEstimate(flops=0, bytes_accessed=8 * size, transcendentals=0),
    )(values)


def gather_small(silu_bf, vectors):
    flat = jnp.concatenate([silu_bf.reshape(-1), *vectors])
    width = -(-flat.shape[0] // 2048) * 128
    flat = jnp.pad(flat, (0, 16 * width - flat.shape[0])).reshape(16, width)
    everyone = exchange(flat, 0, one_for_all=True)
    everyone = everyone.reshape(everyone.shape[0], -1)
    begin = silu_bf.size
    silu_all = everyone[:, :begin].reshape(-1, silu_bf.shape[1])
    found = []
    for vector in vectors:
        found.append(everyone[:, begin : begin + vector.shape[0]].reshape(-1))
        begin += vector.shape[0]
    return silu_all, found


def modulate_slots(silu_all, ada_weight, ada_bias):
    planes, lines = lax.axis_size("dp"), lax.axis_size("fsdp")
    rows, columns = ada_weight.shape
    devices = planes * lines
    slots = silu_all.shape[0] // devices
    silu_part = lax.dynamic_slice_in_dim(silu_all, lax.axis_index("fsdp") * rows, rows, axis=1)
    term = jnp.dot(silu_part, ada_weight, preferred_element_type=jnp.float32)
    term = exchange(term.reshape(devices, slots, columns), 1)
    term = jnp.sum(term.reshape(planes, lines, slots, columns), axis=1)
    modulation = term.transpose(1, 0, 2).reshape(slots, planes * columns)
    return modulation + ada_bias.astype(jnp.float32), silu_part


def modulation_back(modulation_grad, silu_part, ada_weight, terms):
    planes, lines = lax.axis_size("dp"), lax.axis_size("fsdp")
    devices = planes * lines
    slots = modulation_grad.shape[0]
    rows, columns = ada_weight.shape
    cut = modulation_grad.reshape(slots, planes, columns).transpose(1, 0, 2)
    cut = cut.reshape(planes, 1, 16, slots * columns // 16)
    cut = jnp.broadcast_to(cut, (planes, lines) + cut.shape[2:])
    cut = exchange(cut.reshape((devices,) + cut.shape[2:]), 2)
    cut = cut.reshape(devices * slots, columns)
    ada_grad = matmul_tn(silu_part, cut)
    sums = jnp.sum(cut, axis=0, dtype=jnp.float32)
    bias_width = columns // lines
    ada_bias_grad = lax.dynamic_slice_in_dim(sums, lax.axis_index("fsdp") * bias_width, bias_width)
    silu_grad = matmul_nt(cut, ada_weight).reshape(devices, slots * rows)
    flat = jnp.concatenate([silu_grad] + [term.reshape(devices, -1) for term in terms], axis=1)
    width = -(-flat.shape[1] // 1024) * 128
    flat = jnp.pad(flat, ((0, 0), (0, 8 * width - flat.shape[1])))
    flat = exchange(flat.reshape(devices, 8, width), 3).reshape(devices, -1)
    shared = jnp.sum(flat[:, slots * rows :], axis=0)
    silu_grad = flat[:, : slots * rows].reshape(planes, lines, slots, rows).sum(axis=0)
    silu_grad = silu_grad.transpose(1, 0, 2).reshape(slots, lines * rows)
    found, begin = [], 0
    for term in terms:
        found.append(shared[begin : begin + term.shape[0] // devices])
        begin += term.shape[0] // devices
    return ada_grad, ada_bias_grad, silu_grad, found


def by_columns(values, parts):
    rows, columns = values.shape
    return values.reshape(rows, parts, columns // parts).transpose(1, 0, 2)


SLOPE = math.sqrt(2.0 / math.pi)
WINDOW = 512


def mm(left, right):
    return jnp.dot(left, right, preferred_element_type=jnp.float32)


def shaped(dims, kind=jnp.float32):
    return jax.ShapeDtypeStruct(dims, kind)


def by_rows(count, step, body):
    @pl.loop(0, count // step)
    def _(index):
        body(pl.ds(pl.multiple_of(index * step, step), step))


def lane_index(rows, lanes):
    return lax.broadcasted_iota(jnp.int32, (rows, lanes), 1)


def window_of(block, width, total, span):
    begin = min(block * width // 128 * 128, total - span)
    return begin, block * width - begin


def slot_rows(slots, table, column, width):
    value = jnp.zeros((slots.shape[0], width), jnp.float32)
    for slot in range(4):
        value = value + jnp.where(slots == slot, table[slot : slot + 1, column * width : (column + 1) * width], 0.0)
    return value


def add_slots(out, slots, value):
    for slot in range(4):
        out[slot : slot + 1, :] += jnp.sum(jnp.where(slots == slot, value, 0.0), axis=0, keepdims=True)


def centred(value):
    center = value - jnp.mean(value, axis=-1, keepdims=True)
    scale = lax.rsqrt(jnp.mean(center * center, axis=-1, keepdims=True) + 1e-06)
    return center * scale, scale


def norm_back(normed, scale, grad):
    return scale * (
        grad
        - jnp.mean(grad, axis=-1, keepdims=True)
        - normed * jnp.mean(grad * normed, axis=-1, keepdims=True)
    )


def head_window(head, size, total):
    begin = jnp.minimum(head * size // 128 * 128, total - 256)
    begin = pl.multiple_of(begin, 128)
    lane = lane_index(1, 256)
    offset = head * size - begin
    return begin, (lane >= offset) & (lane < offset + size)


def far_device(plane, depth, core):
    return (plane, depth * 2 + core)


class Gather:
    def __init__(self, shards, wholes, send_sems, recv_sems, local_sems):
        self.shards, self.wholes = shards, wholes
        self.send_sems, self.recv_sems, self.local_sems = send_sems, recv_sems, local_sems
        self.plane, self.depth, self.core = place()
        self.started = []
        self.kept = []
        self.counts = [0, 0, 0]

    def partners(self):
        found = [
            far_device(flipped(self.plane, 1), self.depth, self.core),
            far_device(flipped(self.plane, 2), self.depth, self.core),
            far_device(self.plane, self.depth, 1 - self.core),
        ]
        return found + [far_device(self.plane, (self.depth + d) % 4, self.core) for d in (1, 2, 3)]

    def spot(self, weight, flip, back, other=False):
        plane, depth = flipped(self.plane, flip), (self.depth + 4 - back) % 4
        core = 1 - self.core if other else self.core
        if weight < 2:
            return self.wholes[weight].at[plane, depth, core]
        return self.wholes[weight].at[depth, plane, core]

    def send(self, weight, source, target, partner, kind, entry):
        copy = pltpu.make_async_remote_copy(
            src_ref=source,
            dst_ref=target,
            send_sem=self.send_sems.at[weight, self.counts[weight]],
            recv_sem=self.recv_sems.at[weight, kind, entry],
            device_id=partner,
            device_id_type=pl.DeviceIdType.MESH,
        )
        self.counts[weight] += 1
        copy.start()
        self.started.append(copy)

    def arrive(self, weight, region, kind, entry):
        pltpu.make_async_remote_copy(
            src_ref=region,
            dst_ref=region,
            send_sem=self.send_sems.at[weight, 0],
            recv_sem=self.recv_sems.at[weight, kind, entry],
            device_id=self.partners()[2],
            device_id_type=pl.DeviceIdType.MESH,
        ).wait_recv()

    def pass_on(self, weight, source, flip, back):
        target = self.spot(weight, flip, back)
        beside = self.partners()
        if flip == 0 or (flip == 2 and back % 2 == 1):
            self.send(weight, source, target, beside[0], 1 if flip == 0 else 3, back)
        if flip == 0 or (flip == 1 and back % 2 == 0):
            self.send(weight, source, target, beside[1], 2 if flip == 0 else 3, back)
        self.send(weight, source, target, beside[2], 4 + flip, back)

    def open_plane(self, weight):
        keep = pltpu.make_async_copy(
            self.shards[weight], self.spot(weight, 0, 0), self.local_sems.at[weight]
        )
        keep.start()
        self.kept.append(keep)
        self.pass_on(weight, self.shards[weight], 0, 0)

    def open_line(self, weight):
        for d in (1, 3, 2):
            target = self.spot(weight, 0, 0)
            self.send(weight, self.shards[weight], target, self.partners()[2 + d], 0, d)

    def on_line(self, weight, back):
        region = self.spot(weight, 0, back)
        self.arrive(weight, region, 0, back)
        self.pass_on(weight, region, 0, back)

    def on_plane(self, weight, flip, back):
        region = self.spot(weight, flip, back)
        self.arrive(weight, region, flip, back)
        self.pass_on(weight, region, flip, back)

    def steps(self, weight):
        found = []
        for back in (0, 1, 3, 2):
            if back:
                found.append(partial(self.on_line, weight, back))
        for back in (0, 1, 3, 2):
            found.append(partial(self.on_plane, weight, 1, back))
            found.append(partial(self.on_plane, weight, 2, back))
        for back in (0, 1, 3, 2):
            found.append(partial(self.on_plane, weight, 3, back))
        return found

    def ready(self, weight):
        for flip in range(4):
            for back in (0, 1, 3, 2):
                self.arrive(weight, self.spot(weight, flip, back, True), 4 + flip, back)
        self.kept[weight].wait()

    def finish(self):
        for copy in self.started:
            copy.wait_send()


def greet(partners):
    barrier = pltpu.get_barrier_semaphore()
    for partner in partners:
        pl.semaphore_signal(
            barrier, inc=1, device_id=partner, device_id_type=pl.DeviceIdType.MESH
        )
    pl.semaphore_wait(barrier, len(partners))


def forward_kernel(
    normed,
    start,
    slots,
    slot_line,
    table,
    joined_bias,
    out_bias,
    up_bias,
    joined_shard,
    up_shard,
    down_shard,
    joined_whole,
    up_whole,
    down_whole,
    joined,
    attended,
    stats,
    branch,
    middle,
    normed2,
    hidden,
    before,
    room,
    product,
    wide_room,
    bar,
    before_room,
    send_sems,
    recv_sems,
    local_sems,
    load_sems,
    store_sems,
):
    gather = Gather(
        (joined_shard, up_shard, down_shard),
        (joined_whole, up_whole, down_whole),
        send_sems,
        recv_sems,
        local_sems,
    )
    greet(gather.partners())
    gather.open_line(0)
    for weight in range(3):
        gather.open_plane(weight)
    first = gather.steps(0)
    for step in first[:3]:
        step()
    gather.open_line(1)
    for step in first[3:]:
        step()
    later = gather.steps(1)[:3] + [partial(gather.open_line, 2)] + gather.steps(1)[3:]
    later += gather.steps(2)

    def tick(count=1):
        for _ in range(count):
            if later:
                later.pop(0)()

    rows, width = normed.shape
    columns = joined.shape[1] // 4
    size = room.shape[1]
    gather.ready(0)
    loads = [
        pltpu.make_async_copy(
            joined_whole.at[block], room.at[block], load_sems.at[block]
        )
        for block in range(4)
    ]
    for load in loads:
        load.start()
    tick(3)
    span = product.shape[1]
    for block in range(4):
        loads[block].wait()
        product[...] = mm(normed[...], room[block].reshape(width, width)[:, :span])
        begin, offset = window_of(block, columns, joined.shape[1], span)

        def put(at):
            moved = product[at, :]
            if offset:
                moved = pltpu.roll(moved, offset, 1)
            lane = lane_index(moved.shape[0], span)
            inside = (lane >= offset) & (lane < offset + columns)
            wide_room[at, begin : begin + span] = jnp.where(
                inside, moved, wide_room[at, begin : begin + span]
            )

        by_rows(rows, 64, put)
        tick()

    def settle(at):
        joined[at, :] = (wide_room[at, :] + joined_bias[...]).astype(jnp.bfloat16)

    by_rows(rows, 64, settle)
    bar[...] = jnp.where(slots[...] == slot_line[...], 0.0, -1e30)
    stats[...] = jnp.zeros_like(stats)
    head_size = width // HEADS
    scale = 1.0 / math.sqrt(head_size)
    for group in range(8):

        @pl.loop(2 * group, 2 * group + 2)
        def _(head):
            at, inside = head_window(head, head_size, width)
            query = jnp.where(inside, joined[:, pl.ds(at, 256)], 0.0)
            key = joined[:, pl.ds(pl.multiple_of(at + width, 128), 256)]
            value = joined[:, pl.ds(pl.multiple_of(at + 2 * width, 128), 256)]
            scores = matmul_nt(query, key) * scale + bar[...]
            highest = jnp.max(scores, axis=1, keepdims=True)
            powers = jnp.exp(scores - highest)
            totals = jnp.sum(powers, axis=1, keepdims=True)
            probs = (powers * (1.0 / totals)).astype(jnp.bfloat16)
            found = mm(probs, value)
            wide_room[:, pl.ds(at, 256)] = jnp.where(inside, found, wide_room[:, pl.ds(at, 256)])
            lane = lane_index(rows, 128)
            stats[...] = jnp.where(lane == head, highest + jnp.log(totals), stats[...])

        tick(2)

    attended[...] = wide_room[:, :width].astype(jnp.bfloat16)
    columns = width // 4
    for block in range(4):
        product[:, :WINDOW] = mm(attended[...], room[block].reshape(width, width)[:, width - WINDOW :])
        begin, offset = window_of(block, columns, width, WINDOW)

        def put(at):
            moved = product[at, :WINDOW]
            if offset != WINDOW - columns:
                moved = pltpu.roll(moved, columns + offset, 1)
            lane = lane_index(moved.shape[0], WINDOW)
            inside = (lane >= offset) & (lane < offset + columns)
            branch[at, begin : begin + WINDOW] = jnp.where(
                inside, moved, branch[at, begin : begin + WINDOW]
            )

        by_rows(rows, 64, put)
        tick()

    def combine(at):
        slot = slots[at, :]
        value = branch[at, :] + out_bias[...]
        branch[at, :] = value
        value = start[at, :] + slot_rows(slot, table, 2, width) * value
        middle[at, :] = value
        hat, _ = centred(value)
        value = hat * (1.0 + slot_rows(slot, table, 4, width)) + slot_rows(slot, table, 3, width)
        normed2[at, :] = value.astype(jnp.bfloat16)

    by_rows(rows, 64, combine)
    while len(later) > 15:
        tick()
    gather.ready(1)
    loads = [
        pltpu.make_async_copy(up_whole.at[block], room.at[block], load_sems.at[block])
        for block in range(4)
    ]
    for load in loads:
        load.start()
    stores = [None, None]
    for block in range(4):
        loads[block].wait()
        slot = block % 2
        if stores[slot] is not None:
            stores[slot].wait()
        before_room[slot] = mm(normed2[...], room[block].reshape(width, width)) + up_bias[block]
        stores[slot] = pltpu.make_async_copy(
            before_room.at[slot], before.at[block], store_sems.at[slot]
        )
        stores[slot].start()

        def act(some):
            value = before_room[slot, some, :]
            bend = 1.0 + jnp.tanh(SLOPE * (value + 0.044715 * (value * value * value)))
            hidden[block, some, :] = (value * (0.5 * bend)).astype(jnp.bfloat16)

        by_rows(rows, 64, act)
        tick(3)
    while later:
        tick()
    for store in stores:
        store.wait()
    gather.ready(2)
    gather.finish()


def forward(normed, start, slots, table, joined_bias, out_bias, up_bias, shards):
    rows, width = normed.shape
    deep = width // 8
    whole = shaped((4, 4, 2, deep, width), jnp.bfloat16)
    vmem, away = pl.BlockSpec(memory_space=pltpu.VMEM), pl.BlockSpec(memory_space=pl.ANY)
    return pl.pallas_call(
        forward_kernel,
        out_shape=[
            whole,
            whole,
            whole,
            shaped((rows, 3 * width), jnp.bfloat16),
            shaped((rows, width), jnp.bfloat16),
            shaped((rows, 128)),
            shaped((rows, width)),
            shaped((rows, width)),
            shaped((rows, width), jnp.bfloat16),
            shaped((4, rows, width), jnp.bfloat16),
            shaped((4, rows, width)),
        ],
        in_specs=[vmem] * 8 + [away] * 3,
        out_specs=[away] * 3 + [vmem] * 7 + [away],
        scratch_shapes=[
            pltpu.VMEM((4, 4, 2, deep, width), jnp.bfloat16),
            pltpu.VMEM((rows, 1024), jnp.float32),
            pltpu.VMEM((rows, 3 * width), jnp.float32),
            pltpu.VMEM((rows, rows), jnp.float32),
            pltpu.VMEM((2, rows, width), jnp.float32),
            pltpu.SemaphoreType.DMA((3, 32)),
            pltpu.SemaphoreType.DMA((3, 8, 4)),
            pltpu.SemaphoreType.DMA((3,)),
            pltpu.SemaphoreType.DMA((4,)),
            pltpu.SemaphoreType.DMA((2,)),
        ],
        compiler_params=pltpu.CompilerParams(
            collective_id=4, has_side_effects=True, vmem_limit_bytes=60 * 2**20
        ),
        cost_estimate=pl.CostEstimate(
            flops=2 * 10 * rows * width * width, bytes_accessed=10**8, transcendentals=0
        ),
    )(
        normed,
        start,
        slots.reshape(rows, 1),
        slots.reshape(1, rows),
        table,
        joined_bias,
        out_bias,
        up_bias,
        *shards,
    )


def low_bits(value):
    return value.astype(jnp.bfloat16)


def wide(value):
    return value.astype(jnp.float32)


class Scatter:
    def __init__(self, own, lands, stage, outs, send_sems, recv_sems, stage_sems):
        self.own, self.lands, self.stage, self.outs = own, lands, stage, outs
        self.send_sems, self.recv_sems, self.stage_sems = send_sems, recv_sems, stage_sems
        self.plane, self.depth, self.core = place()
        self.started = []
        self.counts = [0] * len(lands)
        self.queue, self.held, self.turn = [], [], 0

    def partners(self):
        found = [
            far_device(flipped(self.plane, 1), self.depth, self.core),
            far_device(flipped(self.plane, 2), self.depth, self.core),
            far_device(self.plane, self.depth, 1 - self.core),
        ]
        return found + [far_device(self.plane, (self.depth + d) % 4, self.core) for d in (1, 2, 3)]

    def sending(self, weight, source, index, partner, number):
        return pltpu.make_async_remote_copy(
            src_ref=source,
            dst_ref=self.lands[weight].at[index],
            send_sem=self.send_sems.at[weight, number],
            recv_sem=self.recv_sems.at[weight, index],
            device_id=self.partners()[partner],
            device_id_type=pl.DeviceIdType.MESH,
        )

    def send(self, weight, source, index, partner):
        copy = self.sending(weight, source, index, partner, self.counts[weight])
        self.counts[weight] += 1
        copy.start()
        return copy

    def term(self, weight, flip, back, rows_of, line_rows):
        plane, depth = flipped(self.plane, flip), (self.depth + 4 - back) % 4
        base = (depth if line_rows else plane) * 2
        self.own[weight, flip, back] = rows_of(base + self.core)[...]
        return self.send(weight, rows_of(base + 1 - self.core), flip * 4 + back, 2)

    def open(self, weight):
        order = (2, 1, 3, 0)
        near = {back: (1, 2) if back % 2 == 0 else (2, 1) for back in order}
        for back in order:
            for flip in (3, near[back][0]):
                goes = (flip, back, 16 + (4 if flip == 3 else 0) + back, 0 if back % 2 == 0 else 1)
                self.queue.append((weight, flip * 4 + back, flip, back, goes))
        for back in order:
            for flip in (near[back][1], 0):
                self.queue.append((weight, flip * 4 + back, flip, back, None))
        for back in order:
            flip = near[back][1]
            goes = (flip, back, 24 + back, 1 if back % 2 == 0 else 0)
            self.queue.append((weight, 20 + back, flip, back, goes))
            self.queue.append((weight, 16 + back, 0, back, None))
        for back in order:
            goes = (0, back, 28 + back, 2 + 4 - back) if back else None
            self.queue.append((weight, 24 + back, 0, back, goes))
        for back in (2, 1, 3):
            self.queue.append((weight, 28 + back, 0, 0, "last" if back == 3 else None))

    def fetch(self, job):
        weight, index = job[0], job[1]
        region = self.lands[weight].at[index]
        pltpu.make_async_remote_copy(
            src_ref=region,
            dst_ref=region,
            send_sem=self.send_sems.at[weight, 0],
            recv_sem=self.recv_sems.at[weight, index],
            device_id=self.partners()[2],
            device_id_type=pl.DeviceIdType.MESH,
        ).wait_recv()
        self.staging(weight, index, self.turn).start()
        self.held.append((job, self.turn))
        self.turn = (self.turn + 1) % 2

    def staging(self, weight, index, turn):
        return pltpu.make_async_copy(
            self.lands[weight].at[index], self.stage.at[turn], self.stage_sems.at[turn]
        )

    def merge(self):
        (weight, index, flip, back, goes), turn = self.held.pop(0)
        self.staging(weight, index, turn).wait()
        total = wide(self.own[weight, flip, back]) + wide(self.stage[turn])
        if index >= 28:
            if index == 30:
                self.outs[weight][...] = total
            else:
                self.outs[weight][...] += wide(self.stage[turn])
            return
        self.own[weight, flip, back] = low_bits(total)
        if goes is not None:
            self.started.append((weight, goes, self.counts[weight]))
            self.send(weight, self.own.at[weight, goes[0], goes[1]], goes[2], goes[3])

    def tick(self, count=1):
        for _ in range(count):
            if self.held:
                self.merge()
            if self.queue:
                self.fetch(self.queue.pop(0))

    def drain(self):
        while self.queue or self.held:
            self.tick()
        for weight, (flip, back, index, partner), number in self.started:
            source = self.own.at[weight, flip, back]
            self.sending(weight, source, index, partner, number).wait_send()


def multiply_rows(out, left, right, step=384):
    @pl.loop(0, left.shape[0] // step)
    def _(index):
        at = pl.ds(pl.multiple_of(index * step, step), step)
        out[at, :] = mm(left[at, :], right[...]).astype(jnp.bfloat16)


def deep_rows(room, slot, deep):
    def rows_of(row):
        return room.at[slot, pl.ds(pl.multiple_of(row * deep, 16), deep)]

    return rows_of


def backward_kernel(
    hidden_in,
    before_in,
    joined_in,
    joined_whole,
    up_whole,
    down_whole,
    middle,
    out_grad,
    branch,
    normed_t,
    stats,
    slots,
    slot_line,
    table,
    bias,
    down_land,
    up_land,
    blocks,
    mixed,
    middle_grad,
    windows,
    slot_sums,
    branch_sums,
    pre_sums,
    joined_sums,
    down_out,
    up_out,
    own,
    stage,
    room,
    acts,
    grads,
    grads_t,
    attended_grad,
    send_sems,
    recv_sems,
    stage_sems,
    load_sems,
    more_sems,
):
    rows, width = middle.shape
    deep = width // 8
    scatter = Scatter(
        own, (down_land, up_land), stage, (down_out, up_out), send_sems, recv_sems, stage_sems
    )
    greet(scatter.partners())
    slot_sums[...] = jnp.zeros_like(slot_sums)
    branch_sums[...] = jnp.zeros_like(branch_sums)
    pre_sums[...] = jnp.zeros_like(pre_sums)
    joined_sums[...] = jnp.zeros_like(joined_sums)

    def dense(weights, before, total):
        plan = [(down_whole, part) for part in range(4)] * 2 + [(up_whole, part) for part in range(4)]

        def load(step):
            whole, part = plan[step]
            copy = pltpu.make_async_copy(
                whole.at[part], weights.at[step % 2], load_sems.at[step % 2]
            )
            copy.start()
            return copy

        loads = {0: load(0)}
        acting = [
            pltpu.make_async_copy(hidden_in.at[part], acts.at[part], more_sems.at[part])
            for part in range(4)
        ]
        for copy in acting:
            copy.start()

        def next_weight(step):
            if step + 1 < len(plan):
                loads[step + 1] = load(step + 1)
            loads[step].wait()
            return weights.at[step % 2]

        for part in range(4):
            acting[part].wait()
            term = matmul_nt(acts[part], next_weight(part)[...])
            total[...] = term + bias[...] if part == 0 else total[...] + term

        def settle(at):
            slot = slots[at, :]
            gate = slot_rows(slot, table, 5, width)
            value = total[at, :]
            grad = wide(out_grad[at, :])
            mixed[at, :] = low_bits(middle[at, :] + gate * value)
            add_slots(slot_sums.at[3], slot, grad * value)
            value = low_bits(grad * gate)
            grads[at, :] = value
            branch_sums[1:2, :] += jnp.sum(wide(value), axis=0, keepdims=True)

        by_rows(rows, 64, settle)
        grads_t[...] = grads[...].T
        waits = [[], []]
        for number, back in enumerate((2, 1, 3, 0)):
            slot = number % 2
            for copy in waits[slot]:
                copy.wait_send()
            multiply_rows(room.at[slot], grads_t, acts.at[(scatter.depth + 4 - back) % 4])
            rows_of = deep_rows(room, slot, deep)
            waits[slot] = [scatter.term(0, flip, back, rows_of, False) for flip in (3, 1, 2, 0)]
        scatter.open(0)
        befores = [
            pltpu.make_async_copy(before_in.at[part], before.at[part % 2], more_sems.at[part])
            for part in range(4)
        ]
        befores[0].start()
        for part in range(4):
            if part < 3:
                befores[part + 1].start()
            total[...] = mm(grads[...], next_weight(4 + part)[...])
            befores[part].wait()

            def act(at):
                value = before[part % 2, at, :]
                square = value * value
                bend = jnp.tanh(SLOPE * (value + 0.044715 * (square * value)))
                slope = 0.5 * (1.0 + bend) + 0.5 * value * (1.0 - bend * bend) * (
                    SLOPE * (1.0 + 3.0 * 0.044715 * square)
                )
                value = low_bits(total[at, :] * slope)
                acts[part, at, :] = value
                pre_sums[part : part + 1, :] += jnp.sum(wide(value), axis=0, keepdims=True)

            by_rows(rows, 64, act)
            scatter.tick(3)
        for number, flip in enumerate((3, 1, 2, 0)):
            slot = number % 2
            for copy in waits[slot]:
                copy.wait_send()
            multiply_rows(room.at[slot], normed_t, acts.at[flipped(scatter.plane, flip)])
            rows_of = deep_rows(room, slot, deep)
            waits[slot] = [scatter.term(1, flip, back, rows_of, True) for back in (2, 1, 3, 0)]
            scatter.tick(3)
        scatter.open(1)
        for part in range(4):
            term = matmul_nt(acts[part], next_weight(8 + part)[...])
            total[...] = term if part == 0 else total[...] + term
            scatter.tick(1)

        def turn(at):
            slot = slots[at, :]
            grad = total[at, :]
            hat, scale = centred(middle[at, :])
            add_slots(slot_sums.at[1], slot, grad)
            add_slots(slot_sums.at[2], slot, grad * hat)
            grad = grad * (1.0 + slot_rows(slot, table, 4, width))
            grad = wide(out_grad[at, :]) + norm_back(hat, scale, grad)
            middle_grad[at, :] = grad
            add_slots(slot_sums.at[0], slot, grad * branch[at, :])
            value = wide(low_bits(grad * slot_rows(slot, table, 2, width)))
            total[at, :] = value
            branch_sums[0:1, :] += jnp.sum(value, axis=0, keepdims=True)

        by_rows(rows, 64, turn)
        scatter.tick(2)
        for slot in range(2):
            for copy in waits[slot]:
                copy.wait_send()
        columns = width // 4
        span = pl.ds(width - WINDOW, WINDOW)
        sides = []
        for block in range(4):
            copy = pltpu.make_async_copy(
                joined_whole.at[block, :, span],
                weights.at[block // 2, :, pl.ds(block % 2 * WINDOW, WINDOW)],
                more_sems.at[block],
            )
            copy.start()
            sides.append(copy)
        for block in range(4):
            begin, offset = window_of(block, columns, width, WINDOW)

            def cut(at):
                moved = total[at, begin : begin + WINDOW]
                if offset != WINDOW - columns:
                    moved = pltpu.roll(moved, (2 * WINDOW - columns - offset) % WINDOW, 1)
                lane = lane_index(moved.shape[0], WINDOW)
                moved = jnp.where(lane >= WINDOW - columns, moved, 0.0)
                windows[block, at, :] = low_bits(moved)

            by_rows(rows, 64, cut)
            scatter.tick(1)
        for block in range(4):
            sides[block].wait()
            side = weights[block // 2, :, block % 2 * WINDOW : (block % 2 + 1) * WINDOW]
            term = matmul_nt(windows[block], side)
            total[...] = term if block == 0 else total[...] + term
        attended_grad[...] = low_bits(total[...])
        scatter.tick(2)

    pl.run_scoped(
        dense,
        pltpu.VMEM((2, width, width), jnp.bfloat16),
        pltpu.VMEM((2, rows, width), jnp.float32),
        pltpu.VMEM((rows, width), jnp.float32),
    )

    def heads(joined, found_room, bar, cuts):
        load = pltpu.make_async_copy(joined_in, joined, load_sems.at[0])
        load.start()
        size = width // HEADS
        scale = 1.0 / math.sqrt(size)
        bar[...] = jnp.where(slots[...] == slot_line[...], 0.0, -1e30)
        load.wait()
        for head_static in range(0, HEADS, 2):

            @pl.loop(head_static, head_static + 2)
            def _(head):
                begin, inside = head_window(head, size, width)
                columns = [pl.ds(pl.multiple_of(begin + part * width, 128), 256) for part in range(3)]
                query = jnp.where(inside, joined[:, columns[0]], 0.0)
                key = joined[:, columns[1]]
                value = joined[:, columns[2]]
                out_part = jnp.where(inside, attended_grad[:, columns[0]], 0.0)
                lane = lane_index(rows, 128)
                stat = jnp.sum(jnp.where(lane == head, stats[...], 0.0), axis=1, keepdims=True)
                probs = jnp.exp(matmul_nt(query, key) * scale + bar[...] - stat)
                prob_grad = matmul_nt(out_part, value)
                inner = jnp.sum(probs * prob_grad, axis=1, keepdims=True)
                score_grad = low_bits(probs * (prob_grad - inner))
                found = (
                    mm(score_grad, key) * scale,
                    matmul_tn(score_grad, query) * scale,
                    matmul_tn(low_bits(probs), out_part),
                )
                for part in range(3):
                    found_room[:, columns[part]] = jnp.where(
                        inside, found[part], found_room[:, columns[part]]
                    )

            scatter.tick(4)

        span = cuts.shape[2]
        block_width = 3 * width // 4

        def add_up(at):
            joined_sums[...] += jnp.sum(wide(low_bits(found_room[at, :])), axis=0, keepdims=True)

        by_rows(rows, 64, add_up)
        stores = []
        for block in range(4):
            begin, offset = window_of(block, block_width, 3 * width, span)
            if block >= 2:
                stores[block - 2].wait()

            def cut(at):
                moved = found_room[at, begin : begin + span]
                if offset:
                    moved = pltpu.roll(moved, span - offset, 1)
                lane = lane_index(moved.shape[0], span)
                cuts[block % 2, at, :] = low_bits(jnp.where(lane < block_width, moved, 0.0))

            by_rows(rows, 64, cut)
            stores.append(
                pltpu.make_async_copy(cuts.at[block % 2], blocks.at[block], more_sems.at[block])
            )
            stores[block].start()
            scatter.tick(1)
        stores[2].wait()
        stores[3].wait()

    pl.run_scoped(
        heads,
        pltpu.VMEM((rows, 3 * width), jnp.bfloat16),
        pltpu.VMEM((rows, 3 * width), jnp.float32),
        pltpu.VMEM((rows, rows), jnp.float32),
        pltpu.VMEM((2, rows, 1024), jnp.bfloat16),
    )
    scatter.drain()


def backward(hidden, before, joined, wholes, middle, out_grad, branch, normed_t, stats, slots, table, bias):
    rows, width = middle.shape
    deep = width // 8
    vmem, away = pl.BlockSpec(memory_space=pltpu.VMEM), pl.BlockSpec(memory_space=pl.ANY)
    land = shaped((32, deep, width), jnp.bfloat16)
    return pl.pallas_call(
        backward_kernel,
        out_shape=[
            land,
            land,
            shaped((4, rows, 1024), jnp.bfloat16),
            shaped((rows, width), jnp.bfloat16),
            shaped((rows, width)),
            shaped((4, rows, WINDOW), jnp.bfloat16),
            shaped((4, 8, width)),
            shaped((8, width)),
            shaped((8, width)),
            shaped((1, 3 * width)),
            shaped((deep, width)),
            shaped((deep, width)),
        ],
        in_specs=[away] * 6 + [vmem] * 9,
        out_specs=[away] * 3 + [vmem] * 9,
        scratch_shapes=[
            pltpu.VMEM((2, 4, 4, deep, width), jnp.bfloat16),
            pltpu.VMEM((2, deep, width), jnp.bfloat16),
            pltpu.VMEM((2, width, width), jnp.bfloat16),
            pltpu.VMEM((4, rows, width), jnp.bfloat16),
            pltpu.VMEM((rows, width), jnp.bfloat16),
            pltpu.VMEM((width, rows), jnp.bfloat16),
            pltpu.VMEM((rows, width), jnp.bfloat16),
            pltpu.SemaphoreType.DMA((2, 32)),
            pltpu.SemaphoreType.DMA((2, 32)),
            pltpu.SemaphoreType.DMA((2,)),
            pltpu.SemaphoreType.DMA((2,)),
            pltpu.SemaphoreType.DMA((4,)),
        ],
        compiler_params=pltpu.CompilerParams(
            collective_id=5, has_side_effects=True, vmem_limit_bytes=62 * 2**20
        ),
        cost_estimate=pl.CostEstimate(
            flops=2 * 22 * rows * width * width, bytes_accessed=10**8, transcendentals=0
        ),
    )(
        hidden,
        before,
        joined,
        *wholes,
        middle,
        out_grad,
        branch,
        normed_t,
        stats,
        slots.reshape(rows, 1),
        slots.reshape(1, rows),
        table,
        bias,
    )


def ending_kernel(
    joined_whole,
    blocks,
    windows,
    normed_t,
    attended_t,
    start,
    middle_grad,
    slots,
    table,
    land,
    grad_out,
    slot_sums,
    joined_out,
    own,
    stage,
    room,
    weights,
    total,
    send_sems,
    recv_sems,
    stage_sems,
    load_sems,
):
    rows, width = start.shape
    deep = width // 8
    span = blocks.shape[2]
    scatter = Scatter(own, (land,), stage, (joined_out,), send_sems, recv_sems, stage_sems)
    greet(scatter.partners())
    low, high = span, width - WINDOW
    loads = [
        pltpu.make_async_copy(joined_whole.at[part, :, pl.ds(0, span)], weights.at[part], load_sems.at[part])
        for part in range(4)
    ]
    for load in loads:
        load.start()
    waits = [[], []]
    for number, flip in enumerate((3, 1, 2, 0)):
        slot = number % 2
        for copy in waits[slot]:
            copy.wait_send()
        at = flipped(scatter.plane, flip)

        @pl.loop(0, 3)
        def _(index):
            some = pl.ds(pl.multiple_of(index * (width // 3), width // 3), width // 3)
            head = mm(normed_t[some, :], blocks[at])
            tail = mm(attended_t[some, :], windows[at])
            room[slot, some, :high] = low_bits(head[:, :high])
            room[slot, some, high:low] = low_bits(head[:, high:low] + tail[:, : low - high])
            room[slot, some, low:] = low_bits(tail[:, low - high :])

        rows_of = deep_rows(room, slot, deep)
        waits[slot] = [scatter.term(0, flip, back, rows_of, True) for back in (2, 1, 3, 0)]
    scatter.open(0)
    slot_sums[...] = jnp.zeros_like(slot_sums)
    for part in range(4):
        loads[part].wait()
        term = matmul_nt(blocks[part], weights[part])
        total[...] = term if part == 0 else total[...] + term
        scatter.tick(3)

    def turn(at):
        slot = slots[at, :]
        grad = total[at, :]
        hat, scale = centred(start[at, :])
        add_slots(slot_sums.at[0], slot, grad)
        add_slots(slot_sums.at[1], slot, grad * hat)
        grad = grad * (1.0 + slot_rows(slot, table, 1, width))
        grad_out[at, :] = middle_grad[at, :] + norm_back(hat, scale, grad)

    for part in range(4):

        @pl.loop(0, rows // 256)
        def _(index):
            begin = part * (rows // 4) + index * 64
            turn(pl.ds(pl.multiple_of(begin, 64), 64))

        scatter.tick(3)
    for slot in range(2):
        for copy in waits[slot]:
            copy.wait_send()
    scatter.drain()


def ending(joined_whole, blocks, windows, normed_t, attended_t, start, middle_grad, slots, table):
    rows, width = start.shape
    deep = width // 8
    vmem, away = pl.BlockSpec(memory_space=pltpu.VMEM), pl.BlockSpec(memory_space=pl.ANY)
    return pl.pallas_call(
        ending_kernel,
        out_shape=[
            shaped((32, deep, width), jnp.bfloat16),
            shaped((rows, width)),
            shaped((2, 8, width)),
            shaped((deep, width)),
        ],
        in_specs=[away] + [vmem] * 8,
        out_specs=[away] + [vmem] * 3,
        scratch_shapes=[
            pltpu.VMEM((1, 4, 4, deep, width), jnp.bfloat16),
            pltpu.VMEM((2, deep, width), jnp.bfloat16),
            pltpu.VMEM((2, width, width), jnp.bfloat16),
            pltpu.VMEM((4, width, blocks.shape[2]), jnp.bfloat16),
            pltpu.VMEM((rows, width), jnp.float32),
            pltpu.SemaphoreType.DMA((1, 32)),
            pltpu.SemaphoreType.DMA((1, 32)),
            pltpu.SemaphoreType.DMA((2,)),
            pltpu.SemaphoreType.DMA((4,)),
        ],
        compiler_params=pltpu.CompilerParams(
            collective_id=6, has_side_effects=True, vmem_limit_bytes=56 * 2**20
        ),
        cost_estimate=pl.CostEstimate(
            flops=2 * 7 * rows * width * width, bytes_accessed=3 * 10**7, transcendentals=0
        ),
    )(
        joined_whole,
        blocks,
        windows,
        normed_t,
        attended_t,
        start,
        middle_grad,
        slots.reshape(rows, 1),
        table,
    )


def box_device(
    tokens,
    condition,
    kept_index,
    segment,
    grid_side,
    ada_weight,
    ada_bias,
    attn_weight,
    attn_bias,
    proj_weight,
    out_bias,
    up_weight,
    up_bias,
    down_weight,
    grad_out,
):
    rows, width = tokens.shape
    slot_count = condition.shape[0]
    core = place()[2]
    columns = attn_weight.shape[1]
    turned = down_weight.T.reshape(2, up_weight.shape[0], down_weight.shape[0])
    mine, theirs = pick(turned, core), pick(turned, 1 - core)
    arrived = swap(theirs, "core")
    down_shard = jnp.where(
        core == 0,
        jnp.concatenate([mine, arrived], axis=1),
        jnp.concatenate([arrived, mine], axis=1),
    )
    slot_ids = jnp.arange(slot_count, dtype=jnp.int32)
    side_rows = jnp.sum(jnp.where(segment[:, None] == slot_ids[None, :], grid_side[None, :], 0), axis=1)
    start = tokens.astype(jnp.float32) + position_code(kept_index, side_rows, width)
    silu_cond, silu_back = jax.vjp(jax.nn.silu, condition.astype(jnp.float32))
    silu_bf = silu_cond.astype(jnp.bfloat16)
    silu_all, (ada_bfull, attn_bfull, out_bfull, up_bfull) = gather_small(
        silu_bf, (ada_bias, attn_bias, out_bias, up_bias)
    )
    modulation, silu_part = modulate_slots(silu_all, ada_weight, ada_bfull)
    table = jnp.pad(modulation, ((0, 8 - slot_count), (0, 0)))

    def own_rows(part):
        return sum(
            jnp.where(segment[:, None] == slot, modulation[slot, part * width : (part + 1) * width], 0.0)
            for slot in range(slot_count)
        )

    normed1 = norm_modulate(start, own_rows(0), own_rows(1)).astype(jnp.bfloat16)
    zeros = jnp.zeros((width,), jnp.bfloat16)
    joined_bias = jnp.concatenate([attn_bfull[:width], zeros, attn_bfull[width:]])
    out_bias_f = out_bfull.astype(jnp.float32)
    (
        joined_whole,
        up_whole,
        down_whole,
        joined,
        attended,
        stats,
        branch1,
        middle,
        normed2,
        hidden,
        before,
    ) = forward(
        normed1,
        start,
        segment,
        table,
        joined_bias.astype(jnp.float32)[None],
        out_bias_f[None, :width],
        up_bfull.astype(jnp.float32).reshape(4, 1, -1),
        (jnp.concatenate([attn_weight, proj_weight], axis=1), up_weight, down_shard),
    )
    wholes = [whole.reshape(4, width, width) for whole in (joined_whole, up_whole, down_whole)]
    (
        _,
        _,
        blocks,
        mixed,
        middle_grad,
        windows,
        slot_sums2,
        branch_sums,
        pre_sums,
        joined_sums,
        down_total,
        up_weight_grad,
    ) = backward(
        hidden,
        before,
        joined,
        wholes,
        middle,
        grad_out,
        branch1,
        normed2.T,
        stats,
        segment,
        table,
        out_bias_f[None, width:],
    )
    half = down_total.shape[1] // 2
    cut = down_total.reshape(-1, 2, half).transpose(1, 0, 2)
    mine, theirs = pick(cut, core), pick(cut, 1 - core)
    arrived = swap(theirs, "core")
    down_weight_grad = jnp.where(
        core == 0, jnp.concatenate([mine, arrived]), jnp.concatenate([arrived, mine])
    ).T
    _, tokens_grad, slot_sums1, joined_total = ending(
        wholes[0], blocks, windows, normed1.T, attended.T, start, middle_grad, segment, table
    )
    modulation_grad = jnp.concatenate(
        [slot_sums1[0], slot_sums1[1]] + [slot_sums2[part] for part in range(4)], axis=1
    )[:slot_count].astype(jnp.bfloat16)
    joined_sums = joined_sums[0]
    terms = (
        jnp.concatenate([joined_sums[:width], joined_sums[2 * width :]]),
        branch_sums[:2].reshape(-1),
        pre_sums[:4].reshape(-1),
    )
    ada_weight_grad, ada_bias_grad, silu_grad, bias_grads = modulation_back(
        modulation_grad, silu_part, ada_weight, terms
    )
    attn_bias_grad, out_bias_grad, up_bias_grad = bias_grads
    return (
        mixed,
        tokens_grad,
        silu_back(silu_grad)[0],
        ada_weight_grad,
        ada_bias_grad,
        joined_total[:, :columns],
        attn_bias_grad,
        joined_total[:, columns:],
        out_bias_grad,
        up_weight_grad,
        up_bias_grad,
        down_weight_grad,
    )


def per_device(
    tokens,
    condition,
    kept_index,
    segment,
    grid_side,
    ada_weight,
    ada_bias,
    attn_weight,
    attn_bias,
    proj_weight,
    out_bias,
    up_weight,
    up_bias,
    down_weight,
    grad_out,
):
    if on_box():
        return box_device(
            tokens,
            condition,
            kept_index,
            segment,
            grid_side,
            ada_weight,
            ada_bias,
            attn_weight,
            attn_bias,
            proj_weight,
            out_bias,
            up_weight,
            up_bias,
            down_weight,
            grad_out,
        )
    model_width = tokens.shape[1]
    slot_count = condition.shape[0]
    planes = lax.axis_size("dp")
    joined_w, up_w, down_w = gather_blocks(attn_weight, proj_weight, up_weight, down_weight)
    attn_columns = attn_weight.shape[1]
    slot_ids = jnp.arange(slot_count, dtype=jnp.int32)
    same_slot = segment[:, None] == slot_ids[None, :]
    slot_table = same_slot.astype(jnp.float32)
    side_rows = jnp.sum(jnp.where(same_slot, grid_side[None, :], 0), axis=1)
    start = tokens.astype(jnp.float32) + position_code(kept_index, side_rows, model_width)
    condition_f = condition.astype(jnp.float32)
    silu_cond, silu_back = jax.vjp(jax.nn.silu, condition_f)
    silu_bf = silu_cond.astype(jnp.bfloat16)
    silu_all, (ada_bfull, attn_bfull, out_bfull, up_bfull) = gather_small(
        silu_bf, (ada_bias, attn_bias, out_bias, up_bias)
    )
    modulation, silu_part = modulate_slots(silu_all, ada_weight, ada_bfull)
    mod_rows = jnp.dot(
        slot_table, modulation, precision=lax.Precision.HIGHEST, preferred_element_type=jnp.float32
    )
    shift_one, scale_one, gate_one, shift_two, scale_two, gate_two = jnp.split(mod_rows, 6, axis=1)
    normed1, norm1_back = jax.vjp(norm_modulate, start, shift_one, scale_one)
    normed1_bf = normed1.astype(jnp.bfloat16)
    projected = jnp.concatenate(
        [
            jnp.dot(normed1_bf, joined_w[part, :, :attn_columns], preferred_element_type=jnp.float32)
            for part in range(planes)
        ],
        axis=1,
    )
    proj_full = joined_w[:, :, attn_columns:].transpose(1, 0, 2).reshape(model_width, model_width)
    attn_bias_f = attn_bfull.astype(jnp.float32)
    query_bf = (projected[:, :model_width] + attn_bias_f[:model_width]).astype(jnp.bfloat16)
    key_bf = projected[:, model_width : 2 * model_width].astype(jnp.bfloat16)
    value_bf = (projected[:, 2 * model_width :] + attn_bias_f[model_width:]).astype(jnp.bfloat16)
    attended, log_totals = attend_forward(query_bf, key_bf, value_bf, segment, HEADS)
    attended_bf = attended.astype(jnp.bfloat16)
    out_bias_f = out_bfull.astype(jnp.float32)
    branch1 = (
        jnp.dot(attended_bf, proj_full, preferred_element_type=jnp.float32)
        + out_bias_f[:model_width]
    )
    middle = start + gate_one * branch1
    normed2, norm2_back = jax.vjp(norm_modulate, middle, shift_two, scale_two)
    normed2_bf = normed2.astype(jnp.bfloat16)
    hidden_parts, gelu_parts = [], []
    up_bias_f = up_bfull.astype(jnp.float32).reshape(planes, -1)
    branch2 = out_bias_f[model_width:]
    for part in range(planes):
        hidden_pre = (
            jnp.dot(normed2_bf, up_w[part], preferred_element_type=jnp.float32) + up_bias_f[part]
        )
        hidden_act, gelu_back = jax.vjp(partial(jax.nn.gelu, approximate=True), hidden_pre)
        hidden_parts.append(hidden_act.astype(jnp.bfloat16))
        gelu_parts.append(gelu_back)
        branch2 = branch2 + matmul_nt(hidden_parts[part], down_w[part])
    mixed = (middle + gate_two * branch2).astype(jnp.bfloat16)
    out_grad = grad_out.astype(jnp.float32)
    grad_gate_two = out_grad * branch2
    grad_branch2 = (out_grad * gate_two).astype(jnp.bfloat16)
    down_weight_grad = scatter_whole(matmul_tn(jnp.concatenate(hidden_parts, axis=1), grad_branch2))
    pre_parts = []
    for part in range(planes):
        hidden_grad = jnp.dot(grad_branch2, down_w[part], preferred_element_type=jnp.float32)
        pre_parts.append(gelu_parts[part](hidden_grad)[0].astype(jnp.bfloat16))
    pre_grad = jnp.stack(pre_parts)
    (up_weight_grad,) = scatter_rows([(normed2_bf, pre_grad)])
    up_bias_term = jnp.sum(pre_grad, axis=1, dtype=jnp.float32).reshape(-1)
    normed2_grad = sum(matmul_nt(pre_parts[part], up_w[part]) for part in range(planes))
    middle_part, grad_shift_two, grad_scale_two = norm2_back(normed2_grad)
    middle_grad = out_grad + middle_part
    grad_gate_one = middle_grad * branch1
    grad_branch1 = (middle_grad * gate_one).astype(jnp.bfloat16)
    attended_grad = matmul_nt(grad_branch1, proj_full).astype(jnp.bfloat16)
    query_grad, key_grad, value_grad = attend_backward(
        query_bf, key_bf, value_bf, attended_grad, segment, log_totals, HEADS
    )
    query_grad_bf = query_grad.astype(jnp.bfloat16)
    value_grad_bf = value_grad.astype(jnp.bfloat16)
    joined_grad = jnp.concatenate(
        [query_grad_bf, key_grad.astype(jnp.bfloat16), value_grad_bf], axis=1
    )
    joined_parts = by_columns(joined_grad, planes)
    attn_weight_grad, proj_weight_grad = scatter_rows(
        [(normed1_bf, joined_parts), (attended_bf, by_columns(grad_branch1, planes))]
    )
    attn_bias_term = jnp.concatenate(
        [
            jnp.sum(query_grad_bf, axis=0, dtype=jnp.float32),
            jnp.sum(value_grad_bf, axis=0, dtype=jnp.float32),
        ]
    )
    normed1_grad = sum(
        matmul_nt(joined_parts[part], joined_w[part, :, :attn_columns]) for part in range(planes)
    )
    start_part, grad_shift_one, grad_scale_one = norm1_back(normed1_grad)
    tokens_grad = middle_grad + start_part
    mod_rows_grad = jnp.concatenate(
        [
            grad_shift_one,
            grad_scale_one,
            grad_gate_one,
            grad_shift_two,
            grad_scale_two,
            grad_gate_two,
        ],
        axis=1,
    )
    modulation_grad = lax.dot_general(
        slot_table,
        mod_rows_grad,
        (((0,), (0,)), ((), ())),
        precision=lax.Precision.HIGHEST,
        preferred_element_type=jnp.float32,
    ).astype(jnp.bfloat16)
    out_bias_term = jnp.concatenate(
        [
            jnp.sum(grad_branch1, axis=0, dtype=jnp.float32),
            jnp.sum(grad_branch2, axis=0, dtype=jnp.float32),
        ]
    )
    ada_weight_grad, ada_bias_grad, silu_grad, bias_grads = modulation_back(
        modulation_grad, silu_part, ada_weight, (attn_bias_term, out_bias_term, up_bias_term)
    )
    attn_bias_grad, out_bias_grad, up_bias_grad = bias_grads
    condition_grad = silu_back(silu_grad)[0]
    return (
        mixed,
        tokens_grad,
        condition_grad,
        ada_weight_grad,
        ada_bias_grad,
        attn_weight_grad,
        attn_bias_grad,
        proj_weight_grad,
        out_bias_grad,
        up_weight_grad,
        up_bias_grad,
        down_weight_grad,
    )


def solution(mesh):
    return jax.shard_map(
        per_device,
        mesh=mesh,
        in_specs=(
            P(("dp", "fsdp"), None),
            P(("dp", "fsdp"), None),
            P(("dp", "fsdp")),
            P(("dp", "fsdp")),
            P(("dp", "fsdp")),
            P("fsdp", "dp"),
            P(("dp", "fsdp")),
            P("fsdp", "dp"),
            P(("dp", "fsdp")),
            P("fsdp", "dp"),
            P(("dp", "fsdp")),
            P("fsdp", "dp"),
            P(("dp", "fsdp")),
            P("fsdp", "dp"),
            P(("dp", "fsdp"), None),
        ),
        out_specs=(
            P(("dp", "fsdp"), None),
            P(("dp", "fsdp"), None),
            P(("dp", "fsdp"), None),
            P("fsdp", "dp"),
            P(("dp", "fsdp")),
            P("fsdp", "dp"),
            P(("dp", "fsdp")),
            P("fsdp", "dp"),
            P(("dp", "fsdp")),
            P("fsdp", "dp"),
            P(("dp", "fsdp")),
            P("fsdp", "dp"),
        ),
        check_vma=False,
    )
```

```python
from functools import partial
import math

import jax
import jax.numpy as jnp
from jax import lax
from jax.experimental import pallas as pl
from jax.experimental.pallas import tpu as pltpu
from jax.sharding import PartitionSpec as P

HEADS = 16
AXES = ("dp", "fsdp")


def position_code(kept_index, side_rows, model_width):
    quarter = model_width // 4
    exponent = jnp.arange(quarter, dtype=jnp.float32) / quarter
    frequency = 1.0 / 10000.0**exponent
    column = (kept_index % side_rows).astype(jnp.float32)[:, None] * frequency[None, :]
    line_pos = (kept_index // side_rows).astype(jnp.float32)[:, None] * frequency[None, :]
    return jnp.concatenate(
        [jnp.sin(column), jnp.cos(column), jnp.sin(line_pos), jnp.cos(line_pos)], axis=1
    )


def layer_norm(values):
    center = values - jnp.mean(values, axis=-1, keepdims=True)
    return center * lax.rsqrt(jnp.mean(center * center, axis=-1, keepdims=True) + 1e-06)


def norm_modulate(values, shift_rows, scale_rows):
    return layer_norm(values) * (1.0 + scale_rows) + shift_rows


def matmul_nt(first_matrix, second_matrix):
    return lax.dot_general(
        first_matrix, second_matrix, (((1,), (1,)), ((), ())), preferred_element_type=jnp.float32
    )


def matmul_tn(first_matrix, second_matrix):
    return lax.dot_general(
        first_matrix, second_matrix, (((0,), (0,)), ((), ())), preferred_element_type=jnp.float32
    )


def attend_forward(query_bf, key_bf, value_bf, segment, head_count):
    row_count, model_width = query_bf.shape
    head_size = model_width // head_count
    block_rows = min(row_count, 512)
    block_count = row_count // block_rows
    score_scale = 1.0 / math.sqrt(head_size)
    key_heads = key_bf.reshape(row_count, head_count, head_size)
    value_heads = value_bf.reshape(row_count, head_count, head_size)

    def forward_block(block_index):
        query_rows = query_bf.reshape(block_rows, head_count, head_size)
        same_image = segment[:, None] == segment[None, :]
        scores = (
            jnp.einsum("qhd,khd->hqk", query_rows, key_heads, preferred_element_type=jnp.float32)
            * score_scale
        )
        scores = jnp.where(same_image[None], scores, -1e30)
        highest = jnp.max(scores, axis=2, keepdims=True)
        powers = jnp.exp(scores - highest)
        totals = jnp.sum(powers, axis=2, keepdims=True)
        probs_bf = (powers / totals).astype(jnp.bfloat16)
        attended = jnp.einsum(
            "hqk,khd->qhd", probs_bf, value_heads, preferred_element_type=jnp.float32
        )
        return (attended.reshape(block_rows, model_width), (highest + jnp.log(totals))[:, :, 0])

    attended, log_totals = lax.map(forward_block, jnp.arange(block_count, dtype=jnp.int32))
    return (attended.reshape(row_count, model_width), log_totals)


def attend_backward(query_bf, key_bf, value_bf, attended_grad, segment, log_totals, head_count):
    row_count, model_width = query_bf.shape
    head_size = model_width // head_count
    block_rows = min(row_count, 512)
    block_count = row_count // block_rows
    score_scale = 1.0 / math.sqrt(head_size)
    key_heads = key_bf.reshape(row_count, head_count, head_size)
    value_heads = value_bf.reshape(row_count, head_count, head_size)

    def backward_block(running, pieces):
        key_sum, value_sum = running
        block_index, log_rows = pieces
        query_rows = query_bf.reshape(block_rows, head_count, head_size)
        grad_rows = attended_grad.reshape(block_rows, head_count, head_size)
        same_image = segment[:, None] == segment[None, :]
        scores = (
            jnp.einsum("qhd,khd->hqk", query_rows, key_heads, preferred_element_type=jnp.float32)
            * score_scale
        )
        scores = jnp.where(same_image[None], scores, -1e30)
        probs = jnp.exp(scores - log_rows[:, :, None])
        probs_bf = probs.astype(jnp.bfloat16)
        prob_grad = jnp.einsum(
            "qhd,khd->hqk", grad_rows, value_heads, preferred_element_type=jnp.float32
        )
        row_inner = jnp.sum(probs * prob_grad, axis=2, keepdims=True)
        score_grad = (probs * (prob_grad - row_inner)).astype(jnp.bfloat16)
        query_grad = (
            jnp.einsum("hqk,khd->qhd", score_grad, key_heads, preferred_element_type=jnp.float32)
            * score_scale
        )
        key_sum = (
            key_sum
            + jnp.einsum("hqk,qhd->khd", score_grad, query_rows, preferred_element_type=jnp.float32)
            * score_scale
        )
        value_sum = value_sum + jnp.einsum(
            "hqk,qhd->khd", probs_bf, grad_rows, preferred_element_type=jnp.float32
        )
        return ((key_sum, value_sum), query_grad.reshape(block_rows, model_width))

    empty_sum = jnp.zeros((row_count, head_count, head_size), jnp.float32)
    sums, query_grad = lax.scan(
        backward_block,
        (empty_sum, empty_sum),
        (jnp.arange(block_count, dtype=jnp.int32), log_totals),
    )
    return (
        query_grad.reshape(row_count, model_width),
        sums[0].reshape(row_count, model_width),
        sums[1].reshape(row_count, model_width),
    )


def on_box():
    return lax.axis_size("dp") == 4 and lax.axis_size("fsdp") == 8


def neighbour(index, axis):
    plane, line = index // 8, index % 8
    if axis == "x":
        plane ^= 1
    elif axis == "y":
        plane ^= 2
    elif axis == "core":
        line ^= 1
    else:
        line = (line - 2 * axis) % 8
    return plane * 8 + line


def swap(values, axis):
    return lax.ppermute(values, AXES, [(index, neighbour(index, axis)) for index in range(32)])


HALF_ORDERS = (("x", 1, "y", 2), ("y", 2, "x", 1))


def place():
    plane, line = lax.axis_index("dp"), lax.axis_index("fsdp")
    return plane, line // 2, line % 2


def flipped(plane, flip):
    if flip % 2:
        plane = plane + 1 - 2 * (plane % 2)
    if flip // 2:
        plane = plane + 2 - 4 * (plane // 2)
    return plane


def pick(values, index):
    return lax.dynamic_index_in_dim(values, index, axis=0, keepdims=False)


def gather_blocks(attn_weight, proj_weight, up_weight, down_weight):
    parts = lax.axis_size("dp")
    attn, proj, up, down = [
        lax.all_gather(lax.all_gather(weight, "dp", axis=1, tiled=True), "fsdp", axis=0, tiled=True)
        for weight in (attn_weight, proj_weight, up_weight, down_weight)
    ]
    width = attn.shape[0]

    def by_block(weight):
        return weight.reshape(weight.shape[0], parts, -1).transpose(1, 0, 2)

    joined = jnp.concatenate([by_block(attn), by_block(proj)], axis=2)
    return joined, by_block(up), by_block(down.T.reshape(width, -1))


def scatter_whole(gradient):
    part = lax.psum_scatter(
        gradient.astype(jnp.bfloat16), "dp", scatter_dimension=1, tiled=True
    ).astype(jnp.float32)
    return lax.psum_scatter(part, "fsdp", scatter_dimension=0, tiled=True)


def scatter_rows(pairs):
    return [
        scatter_whole(matmul_tn(left, right.transpose(1, 0, 2).reshape(left.shape[0], -1)))
        for left, right in pairs
    ]


def trade(one_for_all, values, out, send_sems, recv_sems):
    planes, lines = lax.axis_size("dp"), lax.axis_size("fsdp")
    count = planes * lines
    me = lax.axis_index("dp") * lines + lax.axis_index("fsdp")

    def device(index):
        return (index // lines, index % lines)

    def chunk(index):
        return values if one_for_all else values.at[index]

    barrier = pltpu.get_barrier_semaphore()

    @pl.loop(1, count)
    def _(step):
        pl.semaphore_signal(
            barrier,
            inc=1,
            device_id=device((me + step) % count),
            device_id_type=pl.DeviceIdType.MESH,
        )

    pl.semaphore_wait(barrier, count - 1)

    @pl.loop(1, count)
    def _(step):
        peer = (me + step) % count
        pltpu.make_async_remote_copy(
            src_ref=chunk(peer),
            dst_ref=out.at[me],
            send_sem=send_sems.at[step],
            recv_sem=recv_sems.at[step],
            device_id=device(peer),
            device_id_type=pl.DeviceIdType.MESH,
        ).start()

    if one_for_all:
        out[me] = values[...]
    else:
        out[me] = values[me]

    @pl.loop(1, count)
    def _(step):
        peer = (me + step) % count
        copy = pltpu.make_async_remote_copy(
            src_ref=chunk(peer),
            dst_ref=out.at[(me + count - step) % count],
            send_sem=send_sems.at[step],
            recv_sem=recv_sems.at[step],
            device_id=device(peer),
            device_id_type=pl.DeviceIdType.MESH,
        )
        copy.wait()


def exchange(values, collective_id, one_for_all=False):
    count = lax.axis_size("dp") * lax.axis_size("fsdp")
    chunk = values.shape[-2:]
    size = count * chunk[0] * chunk[1] * values.dtype.itemsize
    return pl.pallas_call(
        partial(trade, one_for_all),
        out_shape=jax.ShapeDtypeStruct((count,) + chunk, values.dtype),
        in_specs=[pl.BlockSpec(memory_space=pltpu.VMEM)],
        out_specs=pl.BlockSpec(memory_space=pltpu.VMEM),
        scratch_shapes=[pltpu.SemaphoreType.DMA((count,)), pltpu.SemaphoreType.DMA((count,))],
        compiler_params=pltpu.CompilerParams(
            collective_id=collective_id,
            has_side_effects=True,
            vmem_limit_bytes=3 * size + 4 * 2**20,
        ),
        cost_estimate=pl.CostEstimate(flops=0, bytes_accessed=8 * size, transcendentals=0),
    )(values)


def gather_small(silu_bf, vectors):
    flat = jnp.concatenate([silu_bf.reshape(-1), *vectors])
    width = -(-flat.shape[0] // 2048) * 128
    flat = jnp.pad(flat, (0, 16 * width - flat.shape[0])).reshape(16, width)
    everyone = exchange(flat, 0, one_for_all=True)
    everyone = everyone.reshape(everyone.shape[0], -1)
    begin = silu_bf.size
    silu_all = everyone[:, :begin].reshape(-1, silu_bf.shape[1])
    found = []
    for vector in vectors:
        found.append(everyone[:, begin : begin + vector.shape[0]].reshape(-1))
        begin += vector.shape[0]
    return silu_all, found


def silu_columns(silu_all, ada_weight):
    rows = ada_weight.shape[0]
    return lax.dynamic_slice_in_dim(silu_all, lax.axis_index("fsdp") * rows, rows, axis=1)


def modulate_slots(silu_all, ada_weight, ada_bias):
    planes, lines = lax.axis_size("dp"), lax.axis_size("fsdp")
    columns = ada_weight.shape[1]
    slots = silu_all.shape[0] // (planes * lines)
    silu_part = silu_columns(silu_all, ada_weight)
    term = jnp.dot(silu_part, ada_weight, preferred_element_type=jnp.float32)
    term = exchange(term.reshape(planes * lines, slots, columns), 1)
    term = jnp.sum(term.reshape(planes, lines, slots, columns), axis=1)
    modulation = term.transpose(1, 0, 2).reshape(slots, planes * columns)
    return modulation + ada_bias.astype(jnp.float32), silu_part


def modulation_back(modulation_grad, silu_part, ada_weight, terms):
    planes, lines = lax.axis_size("dp"), lax.axis_size("fsdp")
    devices = planes * lines
    slots = modulation_grad.shape[0]
    rows, columns = ada_weight.shape
    cut = modulation_grad.reshape(slots, planes, columns).transpose(1, 0, 2)
    cut = cut.reshape(planes, 1, 16, slots * columns // 16)
    cut = jnp.broadcast_to(cut, (planes, lines) + cut.shape[2:])
    cut = exchange(cut.reshape((devices,) + cut.shape[2:]), 2)
    cut = cut.reshape(devices * slots, columns)
    ada_grad = matmul_tn(silu_part, cut)
    sums = jnp.sum(cut, axis=0, dtype=jnp.float32)
    bias_width = columns // lines
    ada_bias_grad = lax.dynamic_slice_in_dim(sums, lax.axis_index("fsdp") * bias_width, bias_width)
    silu_grad = matmul_nt(cut, ada_weight).reshape(devices, slots * rows)
    flat = jnp.concatenate([silu_grad] + [term.reshape(devices, -1) for term in terms], axis=1)
    width = -(-flat.shape[1] // 1024) * 128
    flat = jnp.pad(flat, ((0, 0), (0, 8 * width - flat.shape[1])))
    flat = exchange(flat.reshape(devices, 8, width), 3).reshape(devices, -1)
    shared = jnp.sum(flat[:, slots * rows :], axis=0)
    silu_grad = flat[:, : slots * rows].reshape(planes, lines, slots, rows).sum(axis=0)
    silu_grad = silu_grad.transpose(1, 0, 2).reshape(slots, lines * rows)
    found, begin = [], 0
    for term in terms:
        found.append(shared[begin : begin + term.shape[0] // devices])
        begin += term.shape[0] // devices
    return ada_grad, ada_bias_grad, silu_grad, found


def by_columns(values, parts):
    rows, columns = values.shape
    return values.reshape(rows, parts, columns // parts).transpose(1, 0, 2)


SLOPE = math.sqrt(2.0 / math.pi)
WINDOW = 512


def mm(left, right):
    return jnp.dot(left, right, preferred_element_type=jnp.float32)


def shaped(dims, kind=jnp.float32):
    return jax.ShapeDtypeStruct(dims, kind)


def by_rows(count, step, body):
    @pl.loop(0, count // step)
    def _(index):
        body(pl.ds(pl.multiple_of(index * step, step), step))


def by_groups(count, step, body):
    @pl.loop(0, count // step)
    def _(index):
        body(pl.ds(pl.multiple_of(index * step, step), step), index * step // 128)


def lane_index(rows, lanes):
    return lax.broadcasted_iota(jnp.int32, (rows, lanes), 1)


def window_of(block, width, total, span):
    begin = min(block * width // 128 * 128, total - span)
    return begin, block * width - begin


def group_row(table, group, column, width):
    return table[pl.ds(group, 1), column * width : (column + 1) * width]


def add_group(out, group, value):
    out[pl.ds(group, 1), :] += jnp.sum(value, axis=0, keepdims=True)


def centred(value):
    center = value - jnp.mean(value, axis=-1, keepdims=True)
    scale = lax.rsqrt(jnp.mean(center * center, axis=-1, keepdims=True) + 1e-06)
    return center * scale, scale


def norm_back(normed, scale, grad):
    return scale * (
        grad
        - jnp.mean(grad, axis=-1, keepdims=True)
        - normed * jnp.mean(grad * normed, axis=-1, keepdims=True)
    )


def head_window(head, size, total):
    begin = jnp.minimum(head * size // 128 * 128, total - 256)
    begin = pl.multiple_of(begin, 128)
    lane = lane_index(1, 256)
    offset = head * size - begin
    return begin, (lane >= offset) & (lane < offset + size)


def far_device(plane, depth, core):
    return (plane, depth * 2 + core)


class Gather:
    def __init__(self, shards, wholes, send_sems, recv_sems, local_sems):
        self.shards, self.wholes = shards, wholes
        self.send_sems, self.recv_sems, self.local_sems = send_sems, recv_sems, local_sems
        self.plane, self.depth, self.core = place()
        self.started = []
        self.kept = []
        self.counts = [0, 0, 0]

    def partners(self):
        return [
            far_device(flipped(self.plane, 1), self.depth, self.core),
            far_device(flipped(self.plane, 2), self.depth, self.core),
            far_device(self.plane, self.depth, 1 - self.core),
        ]

    def back(self, entry):
        low, high = (3 - self.depth) // 3, self.depth // 3
        return (0, 1 + 2 * low, 3 - low - high, 2 - low + high)[entry]

    def spot(self, weight, flip, back, other=False):
        plane, depth = flipped(self.plane, flip), (self.depth + 4 - back) % 4
        core = 1 - self.core if other else self.core
        if weight < 2:
            return self.wholes[weight].at[plane, depth, core]
        return self.wholes[weight].at[depth, plane, core]

    def send(self, weight, source, target, partner, kind, entry):
        copy = pltpu.make_async_remote_copy(
            src_ref=source,
            dst_ref=target,
            send_sem=self.send_sems.at[weight, self.counts[weight]],
            recv_sem=self.recv_sems.at[weight, kind, entry],
            device_id=partner,
            device_id_type=pl.DeviceIdType.MESH,
        )
        self.counts[weight] += 1
        copy.start()
        self.started.append(copy)

    def arrive(self, weight, region, kind, entry):
        pltpu.make_async_remote_copy(
            src_ref=region,
            dst_ref=region,
            send_sem=self.send_sems.at[weight, 0],
            recv_sem=self.recv_sems.at[weight, kind, entry],
            device_id=self.partners()[2],
            device_id_type=pl.DeviceIdType.MESH,
        ).wait_recv()

    def pass_on(self, weight, source, flip, entry):
        back = self.back(entry)
        target = self.spot(weight, flip, back)
        beside = self.partners()
        if flip == 0 or (flip == 2 and entry % 2 == 1):
            self.send(weight, source, target, beside[0], 1 if flip == 0 else 3, back)
        if flip == 0 or (flip == 1 and entry % 2 == 0):
            self.send(weight, source, target, beside[1], 2 if flip == 0 else 3, back)
        self.send(weight, source, target, beside[2], 4 + flip, back)

    def open_plane(self, weight):
        keep = pltpu.make_async_copy(
            self.shards[weight], self.spot(weight, 0, 0), self.local_sems.at[weight]
        )
        keep.start()
        self.kept.append(keep)
        self.pass_on(weight, self.shards[weight], 0, 0)

    def along(self, weight, source, back, step, number, start):
        beyond = self.depth + step

        @pl.when((beyond >= 0) & (beyond <= 3))
        def _():
            copy = pltpu.make_async_remote_copy(
                src_ref=source,
                dst_ref=self.spot(weight, 0, back),
                send_sem=self.send_sems.at[weight, number],
                recv_sem=self.recv_sems.at[weight, 0, (back + step + 4) % 4],
                device_id=far_device(self.plane, (beyond + 4) % 4, self.core),
                device_id_type=pl.DeviceIdType.MESH,
            )
            if start:
                copy.start()
            else:
                copy.wait_send()

    def line_sends(self, weight, entry, start):
        back = self.back(entry)
        if entry == 0:
            for number, step in enumerate((1, -1)):
                self.along(weight, self.shards[weight], 0, step, 32 + number, start)
        else:
            step = 2 * ((self.depth - back + 4) // 4) - 1
            self.along(weight, self.spot(weight, 0, back), back, step, 33 + entry, start)

    def open_line(self, weight):
        self.line_sends(weight, 0, True)

    def on_line(self, weight, entry):
        region = self.spot(weight, 0, self.back(entry))
        self.arrive(weight, region, 0, self.back(entry))
        self.line_sends(weight, entry, True)
        self.pass_on(weight, region, 0, entry)

    def on_plane(self, weight, flip, entry):
        back = self.back(entry)
        region = self.spot(weight, flip, back)
        self.arrive(weight, region, flip, back)
        self.pass_on(weight, region, flip, entry)

    def plane_steps(self, weight):
        found = []
        for entry in range(4):
            found.append(partial(self.on_plane, weight, 1, entry))
            found.append(partial(self.on_plane, weight, 2, entry))
            if entry:
                found.append(partial(self.on_plane, weight, 3, entry - 1))
        found.append(partial(self.on_plane, weight, 3, 3))
        return found

    def ready(self, weight):
        for flip in range(4):
            for back in range(4):
                self.arrive(weight, self.spot(weight, flip, back, True), 4 + flip, back)
        self.kept[weight].wait()

    def finish(self):
        for copy in self.started:
            copy.wait_send()
        for weight in range(3):
            for entry in range(4):
                self.line_sends(weight, entry, False)


def greet(partners):
    barrier = pltpu.get_barrier_semaphore()
    for partner in partners:
        pl.semaphore_signal(
            barrier, inc=1, device_id=partner, device_id_type=pl.DeviceIdType.MESH
        )
    pl.semaphore_wait(barrier, len(partners))


def trade_along(axis, values, land, send_sems, recv_sems, start):
    count, me = lax.axis_size(axis), lax.axis_index(axis)

    @pl.loop(1, count)
    def _(step):
        peer = (me + step) % count
        target = me if start else (me + count - step) % count
        if axis == "dp":
            device = (peer, lax.axis_index("fsdp"))
        else:
            device = (lax.axis_index("dp"), peer)
        copy = pltpu.make_async_remote_copy(
            src_ref=values.at[peer],
            dst_ref=land.at[target],
            send_sem=send_sems.at[step],
            recv_sem=recv_sems.at[step],
            device_id=device,
            device_id_type=pl.DeviceIdType.MESH,
        )
        if start:
            copy.start()
        else:
            copy.wait()

    if start:
        land[me] = values[me]


def greet_all():
    planes, lines = lax.axis_size("dp"), lax.axis_size("fsdp")
    count = planes * lines
    me = lax.axis_index("dp") * lines + lax.axis_index("fsdp")
    barrier = pltpu.get_barrier_semaphore()

    @pl.loop(1, count)
    def _(step):
        peer = (me + step) % count
        pl.semaphore_signal(
            barrier,
            inc=1,
            device_id=(peer // lines, peer % lines),
            device_id_type=pl.DeviceIdType.MESH,
        )

    pl.semaphore_wait(barrier, count - 1)


def forward_kernel(
    tokens,
    places,
    codes,
    slots,
    slot_line,
    group_slots,
    term,
    ada_bias,
    joined_bias,
    out_bias,
    up_bias,
    joined_shard,
    up_shard,
    down_shard,
    joined_whole,
    up_whole,
    down_whole,
    joined,
    start,
    table,
    normed_t,
    attended_t,
    normed2_t,
    stats,
    branch,
    middle,
    hidden,
    before,
    room,
    product,
    wide_room,
    bar,
    before_room,
    normed,
    attended,
    normed2,
    term_land,
    plane_term,
    plane_land,
    strip,
    all_modulation,
    send_sems,
    recv_sems,
    local_sems,
    load_sems,
    store_sems,
    term_send_sems,
    term_recv_sems,
    plane_send_sems,
    plane_recv_sems,
):
    gather = Gather(
        (joined_shard, up_shard, down_shard),
        (joined_whole, up_whole, down_whole),
        send_sems,
        recv_sems,
        local_sems,
    )
    greet_all()
    gather.open_line(0)
    gather.open_plane(0)
    line_trade = (term, term_land, term_send_sems, term_recv_sems)
    plane_trade = (plane_term, plane_land, plane_send_sems, plane_recv_sems)
    trade_along("fsdp", *line_trade, True)
    rows, width = tokens.shape
    lane = lane_index(rows, codes.shape[0])
    spot = jnp.where(lane % 64 < 32, places[:, 0:1], places[:, 1:2])
    hot = jnp.where(lane % 32 == spot, 1.0, 0.0).astype(jnp.bfloat16)
    start[...] = mm(hot, codes[...]) + wide(tokens[...])
    first = gather.plane_steps(0)
    for entry in (1, 2, 3):
        gather.on_line(0, entry)
    gather.open_line(1)
    trade_along("fsdp", *line_trade, False)
    total = term_land[0]
    for line in range(1, term_land.shape[0]):
        total = total + term_land[line]
    plane_term[...] = total
    trade_along("dp", *plane_trade, True)
    for step in first[:2]:
        step()
    gather.on_line(1, 1)
    trade_along("dp", *plane_trade, False)
    strip[...] = jnp.zeros_like(strip)
    slot_count, part = plane_land.shape[1:]
    for plane in range(4):
        strip[:slot_count, :part] = plane_land[plane]
        shift = plane * part % 128
        begin = plane * part - shift
        moved = pltpu.roll(strip[...], shift, 1) if shift else strip[...]
        lane = lane_index(8, strip.shape[1])
        span = pl.ds(begin, strip.shape[1])
        inside = (lane >= shift) & (lane < shift + part)
        all_modulation[:, span] = jnp.where(inside, moved, all_modulation[:, span])
    total = jnp.zeros(table.shape, jnp.float32)
    for slot in range(slot_count):
        row = all_modulation[slot : slot + 1, : table.shape[1]] + ada_bias[...]
        total = total + jnp.where(group_slots[...] == slot, row, 0.0)
    table[...] = total

    def norm_first(at, group):
        hat, _ = centred(start[at, :])
        value = hat * (1.0 + group_row(table, group, 1, width)) + group_row(table, group, 0, width)
        normed[at, :] = low_bits(value)

    by_groups(rows, 64, norm_first)
    gather.open_plane(1)
    for step in first[2:5]:
        step()
    gather.on_line(1, 2)
    for step in first[5:8]:
        step()
    gather.on_line(1, 3)
    gather.open_line(2)
    for step in first[8:]:
        step()
    second = gather.plane_steps(1)
    later = [partial(gather.on_line, 2, 1)] + second[:2] + [partial(gather.on_line, 2, 2)]
    later += second[2:5] + [partial(gather.on_line, 2, 3), partial(gather.open_plane, 2)]
    later += second[5:] + gather.plane_steps(2)

    def tick(count=1):
        for _ in range(count):
            if later:
                later.pop(0)()

    normed_t[...] = normed[...].T
    columns = joined.shape[1] // 4
    gather.ready(0)
    loads = [
        pltpu.make_async_copy(
            joined_whole.at[block], room.at[block], load_sems.at[block]
        )
        for block in range(4)
    ]
    for load in loads:
        load.start()
    tick(3)
    span = product.shape[1]
    for block in range(4):
        loads[block].wait()
        product[...] = mm(normed[...], room[block].reshape(width, width)[:, :span])
        begin, offset = window_of(block, columns, joined.shape[1], span)

        def put(at):
            moved = product[at, :]
            if offset:
                moved = pltpu.roll(moved, offset, 1)
            lane = lane_index(moved.shape[0], span)
            inside = (lane >= offset) & (lane < offset + columns)
            wide_room[at, begin : begin + span] = jnp.where(
                inside, moved, wide_room[at, begin : begin + span]
            )

        by_rows(rows, 64, put)
        tick()

    def settle(at):
        joined[at, :] = (wide_room[at, :] + joined_bias[...]).astype(jnp.bfloat16)

    by_rows(rows, 64, settle)
    bar[...] = jnp.where(slots[...] == slot_line[...], 0.0, -1e30)
    stats[...] = jnp.zeros_like(stats)
    head_size = width // HEADS
    scale = 1.0 / math.sqrt(head_size)
    for group in range(8):

        @pl.loop(2 * group, 2 * group + 2)
        def _(head):
            at, inside = head_window(head, head_size, width)
            query = jnp.where(inside, joined[:, pl.ds(at, 256)], 0.0)
            key = joined[:, pl.ds(pl.multiple_of(at + width, 128), 256)]
            value = joined[:, pl.ds(pl.multiple_of(at + 2 * width, 128), 256)]
            scores = matmul_nt(query, key) * scale + bar[...]
            highest = jnp.max(scores, axis=1, keepdims=True)
            powers = jnp.exp(scores - highest)
            totals = jnp.sum(powers, axis=1, keepdims=True)
            probs = (powers * (1.0 / totals)).astype(jnp.bfloat16)
            found = mm(probs, value)
            wide_room[:, pl.ds(at, 256)] = jnp.where(inside, found, wide_room[:, pl.ds(at, 256)])
            lane = lane_index(rows, 128)
            stats[...] = jnp.where(lane == head, highest + jnp.log(totals), stats[...])

        tick(1)

    attended[...] = wide_room[:, :width].astype(jnp.bfloat16)
    columns = width // 4
    for block in range(4):
        product[:, :WINDOW] = mm(attended[...], room[block].reshape(width, width)[:, width - WINDOW :])
        begin, offset = window_of(block, columns, width, WINDOW)

        def put(at):
            moved = product[at, :WINDOW]
            if offset != WINDOW - columns:
                moved = pltpu.roll(moved, columns + offset, 1)
            lane = lane_index(moved.shape[0], WINDOW)
            inside = (lane >= offset) & (lane < offset + columns)
            branch[at, begin : begin + WINDOW] = jnp.where(
                inside, moved, branch[at, begin : begin + WINDOW]
            )

        by_rows(rows, 64, put)
        tick()

    def combine(at, group):
        value = branch[at, :] + out_bias[...]
        branch[at, :] = value
        value = start[at, :] + group_row(table, group, 2, width) * value
        middle[at, :] = value
        hat, _ = centred(value)
        value = hat * (1.0 + group_row(table, group, 4, width)) + group_row(table, group, 3, width)
        normed2[at, :] = value.astype(jnp.bfloat16)

    by_groups(rows, 64, combine)
    normed2_t[...] = normed2[...].T
    attended_t[...] = attended[...].T
    while len(later) > 12:
        tick()
    gather.ready(1)
    loads = [
        pltpu.make_async_copy(up_whole.at[block], room.at[block], load_sems.at[block])
        for block in range(4)
    ]
    for load in loads:
        load.start()
    stores = [None, None]
    for block in range(4):
        loads[block].wait()
        slot = block % 2
        if stores[slot] is not None:
            stores[slot].wait()
        before_room[slot] = mm(normed2[...], room[block].reshape(width, width)) + up_bias[block]
        stores[slot] = pltpu.make_async_copy(
            before_room.at[slot], before.at[block], store_sems.at[slot]
        )
        stores[slot].start()

        def act(some):
            value = before_room[slot, some, :]
            bend = 1.0 + jnp.tanh(SLOPE * (value + 0.044715 * (value * value * value)))
            hidden[block, some, :] = (value * (0.5 * bend)).astype(jnp.bfloat16)

        by_rows(rows, 64, act)
        tick(3)
    while later:
        tick()
    for store in stores:
        store.wait()
    gather.ready(2)
    gather.finish()


def forward(tokens, places, codes, slots, group_slots, term, ada_bias, biases, shards):
    rows, width = tokens.shape
    deep = width // 8
    whole = shaped((4, 4, 2, deep, width), jnp.bfloat16)
    vmem, away = pl.BlockSpec(memory_space=pltpu.VMEM), pl.BlockSpec(memory_space=pl.ANY)
    part = term.shape[3]
    return pl.pallas_call(
        forward_kernel,
        out_shape=[
            whole,
            whole,
            whole,
            shaped((rows, 3 * width), jnp.bfloat16),
            shaped((rows, width)),
            shaped((8, 4 * part)),
            shaped((width, rows), jnp.bfloat16),
            shaped((width, rows), jnp.bfloat16),
            shaped((width, rows), jnp.bfloat16),
            shaped((rows, 128)),
            shaped((rows, width)),
            shaped((rows, width)),
            shaped((4, rows, width), jnp.bfloat16),
            shaped((4, rows, width)),
        ],
        in_specs=[vmem] * 11 + [away] * 3,
        out_specs=[away] * 3 + [vmem] * 10 + [away],
        scratch_shapes=[
            pltpu.VMEM((4, 4, 2, deep, width), jnp.bfloat16),
            pltpu.VMEM((rows, 1024), jnp.float32),
            pltpu.VMEM((rows, 3 * width), jnp.float32),
            pltpu.VMEM((rows, rows), jnp.float32),
            pltpu.VMEM((2, rows, width), jnp.float32),
            pltpu.VMEM((rows, width), jnp.bfloat16),
            pltpu.VMEM((rows, width), jnp.bfloat16),
            pltpu.VMEM((rows, width), jnp.bfloat16),
            pltpu.VMEM(term.shape, jnp.float32),
            pltpu.VMEM(term.shape[1:], jnp.float32),
            pltpu.VMEM(term.shape[1:], jnp.float32),
            pltpu.VMEM((8, -(-part // 128) * 128), jnp.float32),
            pltpu.VMEM((8, 4 * part + 128), jnp.float32),
            pltpu.SemaphoreType.DMA((3, 40)),
            pltpu.SemaphoreType.DMA((3, 8, 4)),
            pltpu.SemaphoreType.DMA((3,)),
            pltpu.SemaphoreType.DMA((4,)),
            pltpu.SemaphoreType.DMA((2,)),
            pltpu.SemaphoreType.DMA((8,)),
            pltpu.SemaphoreType.DMA((8,)),
            pltpu.SemaphoreType.DMA((4,)),
            pltpu.SemaphoreType.DMA((4,)),
        ],
        compiler_params=pltpu.CompilerParams(
            collective_id=4, has_side_effects=True, vmem_limit_bytes=62 * 2**20
        ),
        cost_estimate=pl.CostEstimate(
            flops=2 * 10 * rows * width * width, bytes_accessed=10**8, transcendentals=0
        ),
    )(
        tokens,
        places,
        codes,
        slots.reshape(rows, 1),
        slots.reshape(1, rows),
        group_slots,
        term,
        ada_bias,
        *biases,
        *shards,
    )


def low_bits(value):
    return value.astype(jnp.bfloat16)


def wide(value):
    return value.astype(jnp.float32)


class Scatter:
    def __init__(self, own, lands, stage, outs, send_sems, recv_sems, stage_sems):
        self.own, self.lands, self.stage, self.outs = own, lands, stage, outs
        self.send_sems, self.recv_sems, self.stage_sems = send_sems, recv_sems, stage_sems
        self.plane, self.depth, self.core = place()
        self.started = []
        self.counts = [0] * len(lands)
        self.queue, self.held, self.turn = [], [], 0

    def partners(self):
        found = [
            far_device(flipped(self.plane, 1), self.depth, self.core),
            far_device(flipped(self.plane, 2), self.depth, self.core),
            far_device(self.plane, self.depth, 1 - self.core),
        ]
        return found + [far_device(self.plane, (self.depth + d) % 4, self.core) for d in (1, 2, 3)]

    def sending(self, weight, source, index, partner, number):
        return pltpu.make_async_remote_copy(
            src_ref=source,
            dst_ref=self.lands[weight].at[index],
            send_sem=self.send_sems.at[weight, number],
            recv_sem=self.recv_sems.at[weight, index],
            device_id=self.partners()[partner],
            device_id_type=pl.DeviceIdType.MESH,
        )

    def send(self, weight, source, index, partner):
        copy = self.sending(weight, source, index, partner, self.counts[weight])
        self.counts[weight] += 1
        copy.start()
        return copy

    def term(self, weight, flip, back, rows_of, line_rows):
        plane, depth = flipped(self.plane, flip), (self.depth + 4 - back) % 4
        base = (depth if line_rows else plane) * 2
        self.own[weight % 2, flip, back] = rows_of(base + self.core)[...]
        return self.send(weight, rows_of(base + 1 - self.core), flip * 4 + back, 2)

    def open(self, weight, *parts):
        order = (2, 1, 3, 0)
        near = {back: (1, 2) if back % 2 == 0 else (2, 1) for back in order}
        if "core" in parts:
            for back in order:
                for flip in (3, near[back][0]):
                    land = 16 + (4 if flip == 3 else 0) + back
                    goes = (flip, back, land, 0 if back % 2 == 0 else 1)
                    self.queue.append((weight, flip * 4 + back, flip, back, goes))
            for back in order:
                for flip in (near[back][1], 0):
                    self.queue.append((weight, flip * 4 + back, flip, back, None))
        if "first" in parts:
            for back in order:
                flip = near[back][1]
                goes = (flip, back, 24 + back, 1 if back % 2 == 0 else 0)
                self.queue.append((weight, 20 + back, flip, back, goes))
                self.queue.append((weight, 16 + back, 0, back, None))
        if "second" in parts:
            for back in order:
                goes = (0, back, 28 + back, 2 + 4 - back) if back else None
                self.queue.append((weight, 24 + back, 0, back, goes))
        if "line" in parts:
            for back in (2, 1, 3):
                self.queue.append((weight, 28 + back, 0, 0, None))

    def fetch(self, job):
        weight, index = job[0], job[1]
        region = self.lands[weight].at[index]
        pltpu.make_async_remote_copy(
            src_ref=region,
            dst_ref=region,
            send_sem=self.send_sems.at[weight, 0],
            recv_sem=self.recv_sems.at[weight, index],
            device_id=self.partners()[2],
            device_id_type=pl.DeviceIdType.MESH,
        ).wait_recv()
        if self.stage is not None:
            self.staging(weight, index, self.turn).start()
        self.held.append((job, self.turn))
        self.turn = (self.turn + 1) % 2

    def staging(self, weight, index, turn):
        return pltpu.make_async_copy(
            self.lands[weight].at[index], self.stage.at[turn], self.stage_sems.at[turn]
        )

    def merge(self):
        (weight, index, flip, back, goes), turn = self.held.pop(0)
        if self.stage is None:
            arrived = self.lands[weight][index]
        else:
            self.staging(weight, index, turn).wait()
            arrived = self.stage[turn]
        if index >= 28:
            self.outs[weight][...] += wide(arrived)
            return
        if index == 24:
            self.outs[weight][...] = wide(self.own[weight % 2, flip, back]) + wide(arrived)
            return
        self.own[weight % 2, flip, back] = self.own[weight % 2, flip, back] + arrived
        if goes is not None:
            self.started.append((weight, goes, self.counts[weight]))
            self.send(weight, self.own.at[weight % 2, goes[0], goes[1]], goes[2], goes[3])

    def tick(self, count=1):
        for _ in range(count):
            if self.held:
                self.merge()
            if self.queue:
                self.fetch(self.queue.pop(0))
                if self.stage is None:
                    self.merge()

    def clear(self, weight, flip):
        while any(job[0] == weight and flip == 0 for job in self.queue) or any(
            held[0][0] == weight and held[0][2] == flip for held in self.held
        ):
            self.tick()
        for entry in [entry for entry in self.started if entry[0] == weight and entry[1][0] == flip]:
            self.started.remove(entry)
            self.sent(entry)

    def sent(self, entry):
        weight, (flip, back, index, partner), number = entry
        source = self.own.at[weight % 2, flip, back]
        self.sending(weight, source, index, partner, number).wait_send()

    def drain(self):
        while self.queue or self.held:
            self.tick()
        for entry in self.started:
            self.sent(entry)


def multiply_rows(out, left, right, step=384):
    @pl.loop(0, left.shape[0] // step)
    def _(index):
        at = pl.ds(pl.multiple_of(index * step, step), step)
        out[at, :] = mm(left[at, :], right[...]).astype(jnp.bfloat16)


def deep_rows(room, slot, deep):
    def rows_of(row):
        return room.at[slot, pl.ds(pl.multiple_of(row * deep, 16), deep)]

    return rows_of


def backward_kernel(
    hidden_in,
    before_in,
    joined_in,
    joined_whole,
    up_whole,
    down_whole,
    normed_in,
    attended_in,
    start_in,
    middle,
    out_grad,
    branch,
    normed_t,
    stats,
    slots,
    slot_line,
    table,
    bias,
    down_land,
    up_land,
    joined_land,
    mixed,
    middle_grad,
    slot_sums,
    branch_sums,
    pre_sums,
    joined_sums,
    down_out,
    up_out,
    joined_out,
    windows,
    own,
    stage,
    room,
    acts,
    grads,
    grads_t,
    attended_grad,
    send_sems,
    recv_sems,
    stage_sems,
    load_sems,
    more_sems,
):
    rows, width = middle.shape
    deep = width // 8
    scatter = Scatter(
        own,
        (down_land, up_land, joined_land),
        stage,
        (down_out, up_out, joined_out),
        send_sems,
        recv_sems,
        stage_sems,
    )
    greet(scatter.partners())
    slot_sums[...] = jnp.zeros_like(slot_sums)
    branch_sums[...] = jnp.zeros_like(branch_sums)
    pre_sums[...] = jnp.zeros_like(pre_sums)
    joined_sums[...] = jnp.zeros_like(joined_sums)

    def dense(weights, before, total):
        plan = [(down_whole, part) for part in range(4)] * 2 + [(up_whole, part) for part in range(4)]

        def load(step):
            whole, part = plan[step]
            copy = pltpu.make_async_copy(
                whole.at[part], weights.at[step % 2], load_sems.at[step % 2]
            )
            copy.start()
            return copy

        loads = {0: load(0)}
        acting = [
            pltpu.make_async_copy(hidden_in.at[part], acts.at[part], more_sems.at[part])
            for part in range(4)
        ]
        for copy in acting:
            copy.start()

        def next_weight(step):
            if step + 1 < len(plan):
                loads[step + 1] = load(step + 1)
            loads[step].wait()
            return weights.at[step % 2]

        for part in range(4):
            acting[part].wait()
            term = matmul_nt(acts[part], next_weight(part)[...])
            total[...] = term + bias[...] if part == 0 else total[...] + term

        def settle(at, group):
            gate = group_row(table, group, 5, width)
            value = total[at, :]
            grad = wide(out_grad[at, :])
            mixed[at, :] = low_bits(middle[at, :] + gate * value)
            add_group(slot_sums.at[3], group, grad * value)
            value = low_bits(grad * gate)
            grads[at, :] = value
            branch_sums[1:2, :] += jnp.sum(wide(value), axis=0, keepdims=True)

        by_groups(rows, 64, settle)
        grads_t[...] = grads[...].T
        waits = [[], []]
        for number, back in enumerate((2, 1, 3, 0)):
            slot = number % 2
            for copy in waits[slot]:
                copy.wait_send()
            multiply_rows(room.at[slot], grads_t, acts.at[(scatter.depth + 4 - back) % 4])
            rows_of = deep_rows(room, slot, deep)
            waits[slot] = [scatter.term(0, flip, back, rows_of, False) for flip in (3, 1, 2, 0)]
        scatter.open(0, "core")
        befores = [
            pltpu.make_async_copy(before_in.at[part], before.at[part % 2], more_sems.at[part])
            for part in range(4)
        ]
        befores[0].start()
        for part in range(4):
            if part < 3:
                befores[part + 1].start()
            total[...] = mm(grads[...], next_weight(4 + part)[...])
            befores[part].wait()

            def act(at):
                value = before[part % 2, at, :]
                square = value * value
                bend = jnp.tanh(SLOPE * (value + 0.044715 * (square * value)))
                slope = 0.5 * (1.0 + bend) + 0.5 * value * (1.0 - bend * bend) * (
                    SLOPE * (1.0 + 3.0 * 0.044715 * square)
                )
                value = low_bits(total[at, :] * slope)
                acts[part, at, :] = value
                pre_sums[part : part + 1, :] += jnp.sum(wide(value), axis=0, keepdims=True)

            by_rows(rows, 64, act)
            scatter.tick(4)
        scatter.open(0, "first")
        for number, flip in enumerate((3, 1, 2, 0)):
            slot = number % 2
            for copy in waits[slot]:
                copy.wait_send()
            multiply_rows(room.at[slot], normed_t, acts.at[flipped(scatter.plane, flip)])
            rows_of = deep_rows(room, slot, deep)
            waits[slot] = [scatter.term(1, flip, back, rows_of, True) for back in (2, 1, 3, 0)]
            scatter.tick(1)
        scatter.open(1, "core")
        scatter.open(0, "second")
        scatter.open(1, "first", "second")
        for part in range(4):
            term = matmul_nt(acts[part], next_weight(8 + part)[...])
            total[...] = term if part == 0 else total[...] + term
            scatter.tick(4)

        def turn(at, group):
            grad = total[at, :]
            hat, scale = centred(middle[at, :])
            add_group(slot_sums.at[1], group, grad)
            add_group(slot_sums.at[2], group, grad * hat)
            grad = grad * (1.0 + group_row(table, group, 4, width))
            grad = wide(out_grad[at, :]) + norm_back(hat, scale, grad)
            middle_grad[at, :] = grad
            add_group(slot_sums.at[0], group, grad * branch[at, :])
            value = wide(low_bits(grad * group_row(table, group, 2, width)))
            total[at, :] = value
            branch_sums[0:1, :] += jnp.sum(value, axis=0, keepdims=True)

        by_groups(rows, 64, turn)
        scatter.tick(2)
        for slot in range(2):
            for copy in waits[slot]:
                copy.wait_send()
        columns = width // 4
        span = pl.ds(width - WINDOW, WINDOW)
        sides = []
        for block in range(4):
            copy = pltpu.make_async_copy(
                joined_whole.at[block, :, span],
                weights.at[block // 2, :, pl.ds(block % 2 * WINDOW, WINDOW)],
                more_sems.at[block],
            )
            copy.start()
            sides.append(copy)
        for block in range(4):
            begin, offset = window_of(block, columns, width, WINDOW)

            def cut(at):
                moved = total[at, begin : begin + WINDOW]
                if offset != WINDOW - columns:
                    moved = pltpu.roll(moved, (2 * WINDOW - columns - offset) % WINDOW, 1)
                lane = lane_index(moved.shape[0], WINDOW)
                moved = jnp.where(lane >= WINDOW - columns, moved, 0.0)
                windows[block, at, :] = low_bits(moved)

            by_rows(rows, 64, cut)
            scatter.tick(2)
        for block in range(4):
            sides[block].wait()
            side = weights[block // 2, :, block % 2 * WINDOW : (block % 2 + 1) * WINDOW]
            term = matmul_nt(windows[block], side)
            total[...] = term if block == 0 else total[...] + term
        attended_grad[...] = low_bits(total[...])
        scatter.tick(2)

    pl.run_scoped(
        dense,
        pltpu.VMEM((2, width, width), jnp.bfloat16),
        pltpu.VMEM((2, rows, width), jnp.float32),
        pltpu.VMEM((rows, width), jnp.float32),
    )

    def heads(joined, found_room, bar):
        load = pltpu.make_async_copy(joined_in, joined, load_sems.at[0])
        load.start()
        size = width // HEADS
        scale = 1.0 / math.sqrt(size)
        bar[...] = jnp.where(slots[...] == slot_line[...], 0.0, -1e30)
        load.wait()
        for head_static in range(0, HEADS, 2):

            @pl.loop(head_static, head_static + 2)
            def _(head):
                begin, inside = head_window(head, size, width)
                columns = [pl.ds(pl.multiple_of(begin + part * width, 128), 256) for part in range(3)]
                query = jnp.where(inside, joined[:, columns[0]], 0.0)
                key = joined[:, columns[1]]
                value = joined[:, columns[2]]
                out_part = jnp.where(inside, attended_grad[:, columns[0]], 0.0)
                lane = lane_index(rows, 128)
                stat = jnp.sum(jnp.where(lane == head, stats[...], 0.0), axis=1, keepdims=True)
                probs = jnp.exp(matmul_nt(query, key) * scale + bar[...] - stat)
                prob_grad = matmul_nt(out_part, value)
                inner = jnp.sum(probs * prob_grad, axis=1, keepdims=True)
                score_grad = low_bits(probs * (prob_grad - inner))
                found = (
                    mm(score_grad, key) * scale,
                    matmul_tn(score_grad, query) * scale,
                    matmul_tn(low_bits(probs), out_part),
                )
                for part in range(3):
                    found_room[:, columns[part]] = jnp.where(
                        inside, found[part], found_room[:, columns[part]]
                    )

            scatter.tick(2)

        span = 1024
        block_width = 3 * width // 4

        def add_up(at):
            joined_sums[...] += jnp.sum(wide(low_bits(found_room[at, :])), axis=0, keepdims=True)

        by_rows(rows, 64, add_up)
        for block in range(4):
            begin, offset = window_of(block, block_width, 3 * width, span)

            def cut(at):
                moved = found_room[at, begin : begin + span]
                if offset:
                    moved = pltpu.roll(moved, span - offset, 1)
                lane = lane_index(moved.shape[0], span)
                acts[block, at, :span] = low_bits(jnp.where(lane < block_width, moved, 0.0))

            by_rows(rows, 64, cut)

    pl.run_scoped(
        heads,
        pltpu.VMEM((rows, 3 * width), jnp.bfloat16),
        pltpu.VMEM((rows, 3 * width), jnp.float32),
        pltpu.VMEM((rows, rows), jnp.float32),
    )
    span = 1024

    def last(weights, attended_t, start, total):
        left = pltpu.make_async_copy(normed_in, grads_t, more_sems.at[0])
        other = pltpu.make_async_copy(attended_in, attended_t, more_sems.at[1])
        begin_copy = pltpu.make_async_copy(start_in, start, more_sems.at[2])
        for copy in (left, other, begin_copy):
            copy.start()

        def load(part):
            copy = pltpu.make_async_copy(
                joined_whole.at[part, :, pl.ds(0, span)], weights.at[part % 2], load_sems.at[part % 2]
            )
            copy.start()
            return copy

        loads = [load(0), load(1)]
        left.wait()
        other.wait()
        low, high = span, width - WINDOW
        waits = [[], []]
        for number, flip in enumerate((3, 1, 2, 0)):
            slot = number % 2
            for copy in waits[slot]:
                copy.wait_send()
            at = flipped(scatter.plane, flip)

            @pl.loop(0, 3)
            def _(index):
                some = pl.ds(pl.multiple_of(index * (width // 3), width // 3), width // 3)
                head = mm(grads_t[some, :], acts[at, :, :span])
                tail = mm(attended_t[some, :], windows[at])
                room[slot, some, :high] = low_bits(head[:, :high])
                room[slot, some, high:low] = low_bits(head[:, high:low] + tail[:, : low - high])
                room[slot, some, low:] = low_bits(tail[:, low - high :])

            scatter.clear(0, flip)
            rows_of = deep_rows(room, slot, deep)
            waits[slot] = [scatter.term(2, flip, back, rows_of, True) for back in (2, 1, 3, 0)]
        scatter.open(2, "core")
        scatter.open(0, "line")
        scatter.open(1, "line")
        scatter.open(2, "first", "second", "line")
        for part in range(4):
            loads[part].wait()
            term = matmul_nt(acts[part, :, :span], weights[part % 2])
            total[...] = term if part == 0 else total[...] + term
            if part < 2:
                loads.append(load(part + 2))
            scatter.tick(4)
        begin_copy.wait()

        def turn(at, group):
            grad = total[at, :]
            hat, scale = centred(start[at, :])
            add_group(slot_sums.at[4], group, grad)
            add_group(slot_sums.at[5], group, grad * hat)
            grad = grad * (1.0 + group_row(table, group, 1, width))
            middle_grad[at, :] = middle_grad[at, :] + norm_back(hat, scale, grad)

        for part in range(4):

            @pl.loop(0, rows // 256)
            def _(index):
                begin = part * (rows // 4) + index * 64
                turn(pl.ds(pl.multiple_of(begin, 64), 64), begin // 128)

            scatter.tick(2)
        for slot in range(2):
            for copy in waits[slot]:
                copy.wait_send()

    pl.run_scoped(
        last,
        pltpu.VMEM((2, width, span), jnp.bfloat16),
        pltpu.VMEM((width, rows), jnp.bfloat16),
        pltpu.VMEM((rows, width), jnp.float32),
        pltpu.VMEM((rows, width), jnp.float32),
    )
    scatter.drain()


def backward(away_ins, near_ins, slots, table, bias):
    middle = near_ins[0]
    rows, width = middle.shape
    deep = width // 8
    vmem, away = pl.BlockSpec(memory_space=pltpu.VMEM), pl.BlockSpec(memory_space=pl.ANY)
    land = shaped((32, deep, width), jnp.bfloat16)
    return pl.pallas_call(
        backward_kernel,
        out_shape=[
            land,
            land,
            land,
            shaped((rows, width), jnp.bfloat16),
            shaped((rows, width)),
            shaped((6, 8, width)),
            shaped((8, width)),
            shaped((8, width)),
            shaped((1, 3 * width)),
            shaped((deep, width)),
            shaped((deep, width)),
            shaped((deep, width)),
        ],
        in_specs=[away] * 9 + [vmem] * 9,
        out_specs=[away] * 3 + [vmem] * 9,
        scratch_shapes=[
            pltpu.VMEM((4, rows, WINDOW), jnp.bfloat16),
            pltpu.VMEM((2, 4, 4, deep, width), jnp.bfloat16),
            pltpu.VMEM((2, deep, width), jnp.bfloat16),
            pltpu.VMEM((2, width, width), jnp.bfloat16),
            pltpu.VMEM((4, rows, width), jnp.bfloat16),
            pltpu.VMEM((rows, width), jnp.bfloat16),
            pltpu.VMEM((width, rows), jnp.bfloat16),
            pltpu.VMEM((rows, width), jnp.bfloat16),
            pltpu.SemaphoreType.DMA((3, 32)),
            pltpu.SemaphoreType.DMA((3, 32)),
            pltpu.SemaphoreType.DMA((2,)),
            pltpu.SemaphoreType.DMA((2,)),
            pltpu.SemaphoreType.DMA((4,)),
        ],
        compiler_params=pltpu.CompilerParams(
            collective_id=5, has_side_effects=True, vmem_limit_bytes=62 * 2**20
        ),
        cost_estimate=pl.CostEstimate(
            flops=2 * 30 * rows * width * width, bytes_accessed=10**8, transcendentals=0
        ),
    )(
        *away_ins,
        *near_ins,
        slots.reshape(rows, 1),
        slots.reshape(1, rows),
        table,
        bias,
    )


def code_parts(width):
    quarter = width // 4
    exponent = jnp.arange(quarter, dtype=jnp.float32) / quarter
    frequency = 1.0 / 10000.0**exponent
    angle = jnp.arange(32, dtype=jnp.float32)[:, None] * frequency[None, :]
    half = jnp.concatenate([jnp.sin(angle), jnp.cos(angle)], axis=1)
    none = jnp.zeros_like(half)
    left = jnp.concatenate(
        [jnp.concatenate([half, none], axis=1), jnp.concatenate([none, half], axis=1)], axis=0
    )
    parts = []
    for _ in range(3):
        part = lax.reduce_precision(left, 8, 7)
        parts.append(part.astype(jnp.bfloat16))
        left = left - part
    return jnp.concatenate(parts, axis=0)


def box_device(
    tokens,
    condition,
    kept_index,
    segment,
    grid_side,
    ada_weight,
    ada_bias,
    attn_weight,
    attn_bias,
    proj_weight,
    out_bias,
    up_weight,
    up_bias,
    down_weight,
    grad_out,
):
    rows, width = tokens.shape
    slot_count = condition.shape[0]
    core = place()[2]
    columns = attn_weight.shape[1]
    turned = down_weight.T.reshape(2, up_weight.shape[0], down_weight.shape[0])
    mine, theirs = pick(turned, core), pick(turned, 1 - core)
    arrived = swap(theirs, "core")
    down_shard = jnp.where(
        core == 0,
        jnp.concatenate([mine, arrived], axis=1),
        jnp.concatenate([arrived, mine], axis=1),
    )
    silu_cond, silu_back = jax.vjp(jax.nn.silu, condition.astype(jnp.float32))
    silu_bf = silu_cond.astype(jnp.bfloat16)
    silu_all, (ada_bfull, attn_bfull, out_bfull, up_bfull) = gather_small(
        silu_bf, (ada_bias, attn_bias, out_bias, up_bias)
    )
    silu_part = silu_columns(silu_all, ada_weight)
    by_line = silu_part.reshape(4, 8, slot_count, -1).transpose(1, 0, 2, 3).reshape(silu_part.shape)
    term = jnp.dot(by_line, ada_weight, preferred_element_type=jnp.float32)
    term = term.reshape(8, 4, slot_count, -1)
    group_slots = segment.reshape(rows // 128, 128)[:, 0]
    group_sides = jnp.sum(
        jnp.where(group_slots[:, None] == jnp.arange(slot_count)[None, :], grid_side[None, :], 0), axis=1
    )
    side_rows = jnp.repeat(group_sides, 128)
    places = jnp.stack([kept_index % side_rows, kept_index // side_rows], axis=1)
    zeros = jnp.zeros((width,), jnp.bfloat16)
    joined_bias = jnp.concatenate([attn_bfull[:width], zeros, attn_bfull[width:]])
    out_bias_f = out_bfull.astype(jnp.float32)
    (
        joined_whole,
        up_whole,
        down_whole,
        joined,
        start,
        table,
        normed_t,
        attended_t,
        normed2_t,
        stats,
        branch1,
        middle,
        hidden,
        before,
    ) = forward(
        tokens,
        places,
        code_parts(width),
        segment,
        jnp.pad(group_slots, (0, 8 - rows // 128), constant_values=-1)[:, None],
        term,
        ada_bfull.astype(jnp.float32)[None],
        (
            joined_bias.astype(jnp.float32)[None],
            out_bias_f[None, :width],
            up_bfull.astype(jnp.float32).reshape(4, 1, -1),
        ),
        (jnp.concatenate([attn_weight, proj_weight], axis=1), up_weight, down_shard),
    )
    wholes = [whole.reshape(4, width, width) for whole in (joined_whole, up_whole, down_whole)]
    (
        _,
        _,
        _,
        mixed,
        tokens_grad,
        slot_sums,
        branch_sums,
        pre_sums,
        joined_sums,
        down_total,
        up_weight_grad,
        joined_total,
    ) = backward(
        (hidden, before, joined, *wholes, normed_t, attended_t, start),
        (middle, grad_out, branch1, normed2_t, stats),
        segment,
        table,
        out_bias_f[None, width:],
    )
    half = down_total.shape[1] // 2
    cut = down_total.reshape(-1, 2, half).transpose(1, 0, 2)
    mine, theirs = pick(cut, core), pick(cut, 1 - core)
    arrived = swap(theirs, "core")
    down_weight_grad = jnp.where(
        core == 0, jnp.concatenate([mine, arrived]), jnp.concatenate([arrived, mine])
    ).T
    group_grad = jnp.concatenate(
        [slot_sums[part] for part in (4, 5, 0, 1, 2, 3)], axis=1
    )
    modulation_grad = jnp.stack(
        [
            sum(
                jnp.where(group_slots[group] == slot, group_grad[group], 0.0)
                for group in range(rows // 128)
            )
            for slot in range(slot_count)
        ]
    ).astype(jnp.bfloat16)
    joined_sums = joined_sums[0]
    terms = (
        jnp.concatenate([joined_sums[:width], joined_sums[2 * width :]]),
        branch_sums[:2].reshape(-1),
        pre_sums[:4].reshape(-1),
    )
    ada_weight_grad, ada_bias_grad, silu_grad, bias_grads = modulation_back(
        modulation_grad, silu_part, ada_weight, terms
    )
    attn_bias_grad, out_bias_grad, up_bias_grad = bias_grads
    return (
        mixed,
        tokens_grad,
        silu_back(silu_grad)[0],
        ada_weight_grad,
        ada_bias_grad,
        joined_total[:, :columns],
        attn_bias_grad,
        joined_total[:, columns:],
        out_bias_grad,
        up_weight_grad,
        up_bias_grad,
        down_weight_grad,
    )


def per_device(
    tokens,
    condition,
    kept_index,
    segment,
    grid_side,
    ada_weight,
    ada_bias,
    attn_weight,
    attn_bias,
    proj_weight,
    out_bias,
    up_weight,
    up_bias,
    down_weight,
    grad_out,
):
    if on_box():
        return box_device(
            tokens,
            condition,
            kept_index,
            segment,
            grid_side,
            ada_weight,
            ada_bias,
            attn_weight,
            attn_bias,
            proj_weight,
            out_bias,
            up_weight,
            up_bias,
            down_weight,
            grad_out,
        )
    model_width = tokens.shape[1]
    slot_count = condition.shape[0]
    planes = lax.axis_size("dp")
    joined_w, up_w, down_w = gather_blocks(attn_weight, proj_weight, up_weight, down_weight)
    attn_columns = attn_weight.shape[1]
    slot_ids = jnp.arange(slot_count, dtype=jnp.int32)
    same_slot = segment[:, None] == slot_ids[None, :]
    slot_table = same_slot.astype(jnp.float32)
    side_rows = jnp.sum(jnp.where(same_slot, grid_side[None, :], 0), axis=1)
    start = tokens.astype(jnp.float32) + position_code(kept_index, side_rows, model_width)
    condition_f = condition.astype(jnp.float32)
    silu_cond, silu_back = jax.vjp(jax.nn.silu, condition_f)
    silu_bf = silu_cond.astype(jnp.bfloat16)
    silu_all, (ada_bfull, attn_bfull, out_bfull, up_bfull) = gather_small(
        silu_bf, (ada_bias, attn_bias, out_bias, up_bias)
    )
    modulation, silu_part = modulate_slots(silu_all, ada_weight, ada_bfull)
    mod_rows = jnp.dot(
        slot_table, modulation, precision=lax.Precision.HIGHEST, preferred_element_type=jnp.float32
    )
    shift_one, scale_one, gate_one, shift_two, scale_two, gate_two = jnp.split(mod_rows, 6, axis=1)
    normed1, norm1_back = jax.vjp(norm_modulate, start, shift_one, scale_one)
    normed1_bf = normed1.astype(jnp.bfloat16)
    projected = jnp.concatenate(
        [
            jnp.dot(normed1_bf, joined_w[part, :, :attn_columns], preferred_element_type=jnp.float32)
            for part in range(planes)
        ],
        axis=1,
    )
    proj_full = joined_w[:, :, attn_columns:].transpose(1, 0, 2).reshape(model_width, model_width)
    attn_bias_f = attn_bfull.astype(jnp.float32)
    query_bf = (projected[:, :model_width] + attn_bias_f[:model_width]).astype(jnp.bfloat16)
    key_bf = projected[:, model_width : 2 * model_width].astype(jnp.bfloat16)
    value_bf = (projected[:, 2 * model_width :] + attn_bias_f[model_width:]).astype(jnp.bfloat16)
    attended, log_totals = attend_forward(query_bf, key_bf, value_bf, segment, HEADS)
    attended_bf = attended.astype(jnp.bfloat16)
    out_bias_f = out_bfull.astype(jnp.float32)
    branch1 = (
        jnp.dot(attended_bf, proj_full, preferred_element_type=jnp.float32)
        + out_bias_f[:model_width]
    )
    middle = start + gate_one * branch1
    normed2, norm2_back = jax.vjp(norm_modulate, middle, shift_two, scale_two)
    normed2_bf = normed2.astype(jnp.bfloat16)
    hidden_parts, gelu_parts = [], []
    up_bias_f = up_bfull.astype(jnp.float32).reshape(planes, -1)
    branch2 = out_bias_f[model_width:]
    for part in range(planes):
        hidden_pre = (
            jnp.dot(normed2_bf, up_w[part], preferred_element_type=jnp.float32) + up_bias_f[part]
        )
        hidden_act, gelu_back = jax.vjp(partial(jax.nn.gelu, approximate=True), hidden_pre)
        hidden_parts.append(hidden_act.astype(jnp.bfloat16))
        gelu_parts.append(gelu_back)
        branch2 = branch2 + matmul_nt(hidden_parts[part], down_w[part])
    mixed = (middle + gate_two * branch2).astype(jnp.bfloat16)
    out_grad = grad_out.astype(jnp.float32)
    grad_gate_two = out_grad * branch2
    grad_branch2 = (out_grad * gate_two).astype(jnp.bfloat16)
    down_weight_grad = scatter_whole(matmul_tn(jnp.concatenate(hidden_parts, axis=1), grad_branch2))
    pre_parts = []
    for part in range(planes):
        hidden_grad = jnp.dot(grad_branch2, down_w[part], preferred_element_type=jnp.float32)
        pre_parts.append(gelu_parts[part](hidden_grad)[0].astype(jnp.bfloat16))
    pre_grad = jnp.stack(pre_parts)
    (up_weight_grad,) = scatter_rows([(normed2_bf, pre_grad)])
    up_bias_term = jnp.sum(pre_grad, axis=1, dtype=jnp.float32).reshape(-1)
    normed2_grad = sum(matmul_nt(pre_parts[part], up_w[part]) for part in range(planes))
    middle_part, grad_shift_two, grad_scale_two = norm2_back(normed2_grad)
    middle_grad = out_grad + middle_part
    grad_gate_one = middle_grad * branch1
    grad_branch1 = (middle_grad * gate_one).astype(jnp.bfloat16)
    attended_grad = matmul_nt(grad_branch1, proj_full).astype(jnp.bfloat16)
    query_grad, key_grad, value_grad = attend_backward(
        query_bf, key_bf, value_bf, attended_grad, segment, log_totals, HEADS
    )
    query_grad_bf = query_grad.astype(jnp.bfloat16)
    value_grad_bf = value_grad.astype(jnp.bfloat16)
    joined_grad = jnp.concatenate(
        [query_grad_bf, key_grad.astype(jnp.bfloat16), value_grad_bf], axis=1
    )
    joined_parts = by_columns(joined_grad, planes)
    attn_weight_grad, proj_weight_grad = scatter_rows(
        [(normed1_bf, joined_parts), (attended_bf, by_columns(grad_branch1, planes))]
    )
    attn_bias_term = jnp.concatenate(
        [
            jnp.sum(query_grad_bf, axis=0, dtype=jnp.float32),
            jnp.sum(value_grad_bf, axis=0, dtype=jnp.float32),
        ]
    )
    normed1_grad = sum(
        matmul_nt(joined_parts[part], joined_w[part, :, :attn_columns]) for part in range(planes)
    )
    start_part, grad_shift_one, grad_scale_one = norm1_back(normed1_grad)
    tokens_grad = middle_grad + start_part
    mod_rows_grad = jnp.concatenate(
        [
            grad_shift_one,
            grad_scale_one,
            grad_gate_one,
            grad_shift_two,
            grad_scale_two,
            grad_gate_two,
        ],
        axis=1,
    )
    modulation_grad = lax.dot_general(
        slot_table,
        mod_rows_grad,
        (((0,), (0,)), ((), ())),
        precision=lax.Precision.HIGHEST,
        preferred_element_type=jnp.float32,
    ).astype(jnp.bfloat16)
    out_bias_term = jnp.concatenate(
        [
            jnp.sum(grad_branch1, axis=0, dtype=jnp.float32),
            jnp.sum(grad_branch2, axis=0, dtype=jnp.float32),
        ]
    )
    ada_weight_grad, ada_bias_grad, silu_grad, bias_grads = modulation_back(
        modulation_grad, silu_part, ada_weight, (attn_bias_term, out_bias_term, up_bias_term)
    )
    attn_bias_grad, out_bias_grad, up_bias_grad = bias_grads
    condition_grad = silu_back(silu_grad)[0]
    return (
        mixed,
        tokens_grad,
        condition_grad,
        ada_weight_grad,
        ada_bias_grad,
        attn_weight_grad,
        attn_bias_grad,
        proj_weight_grad,
        out_bias_grad,
        up_weight_grad,
        up_bias_grad,
        down_weight_grad,
    )


def solution(mesh):
    return jax.shard_map(
        per_device,
        mesh=mesh,
        in_specs=(
            P(("dp", "fsdp"), None),
            P(("dp", "fsdp"), None),
            P(("dp", "fsdp")),
            P(("dp", "fsdp")),
            P(("dp", "fsdp")),
            P("fsdp", "dp"),
            P(("dp", "fsdp")),
            P("fsdp", "dp"),
            P(("dp", "fsdp")),
            P("fsdp", "dp"),
            P(("dp", "fsdp")),
            P("fsdp", "dp"),
            P(("dp", "fsdp")),
            P("fsdp", "dp"),
            P(("dp", "fsdp"), None),
        ),
        out_specs=(
            P(("dp", "fsdp"), None),
            P(("dp", "fsdp"), None),
            P(("dp", "fsdp"), None),
            P("fsdp", "dp"),
            P(("dp", "fsdp")),
            P("fsdp", "dp"),
            P(("dp", "fsdp")),
            P("fsdp", "dp"),
            P(("dp", "fsdp")),
            P("fsdp", "dp"),
            P(("dp", "fsdp")),
            P("fsdp", "dp"),
        ),
        check_vma=False,
    )
```

```python
from functools import partial
import math

import jax
import jax.numpy as jnp
from jax import lax
from jax.experimental import pallas as pl
from jax.experimental.pallas import tpu as pltpu
from jax.sharding import PartitionSpec as P

HEADS = 16
AXES = ("dp", "fsdp")


def position_code(kept_index, side_rows, model_width):
    quarter = model_width // 4
    exponent = jnp.arange(quarter, dtype=jnp.float32) / quarter
    frequency = 1.0 / 10000.0**exponent
    column = (kept_index % side_rows).astype(jnp.float32)[:, None] * frequency[None, :]
    line_pos = (kept_index // side_rows).astype(jnp.float32)[:, None] * frequency[None, :]
    return jnp.concatenate(
        [jnp.sin(column), jnp.cos(column), jnp.sin(line_pos), jnp.cos(line_pos)], axis=1
    )


def layer_norm(values):
    center = values - jnp.mean(values, axis=-1, keepdims=True)
    return center * lax.rsqrt(jnp.mean(center * center, axis=-1, keepdims=True) + 1e-06)


def norm_modulate(values, shift_rows, scale_rows):
    return layer_norm(values) * (1.0 + scale_rows) + shift_rows


def matmul_nt(first_matrix, second_matrix):
    return lax.dot_general(
        first_matrix, second_matrix, (((1,), (1,)), ((), ())), preferred_element_type=jnp.float32
    )


def matmul_tn(first_matrix, second_matrix):
    return lax.dot_general(
        first_matrix, second_matrix, (((0,), (0,)), ((), ())), preferred_element_type=jnp.float32
    )


def attend_forward(query_bf, key_bf, value_bf, segment, head_count):
    row_count, model_width = query_bf.shape
    head_size = model_width // head_count
    block_rows = min(row_count, 512)
    block_count = row_count // block_rows
    score_scale = 1.0 / math.sqrt(head_size)
    key_heads = key_bf.reshape(row_count, head_count, head_size)
    value_heads = value_bf.reshape(row_count, head_count, head_size)

    def forward_block(block_index):
        query_rows = query_bf.reshape(block_rows, head_count, head_size)
        same_image = segment[:, None] == segment[None, :]
        scores = (
            jnp.einsum("qhd,khd->hqk", query_rows, key_heads, preferred_element_type=jnp.float32)
            * score_scale
        )
        scores = jnp.where(same_image[None], scores, -1e30)
        highest = jnp.max(scores, axis=2, keepdims=True)
        powers = jnp.exp(scores - highest)
        totals = jnp.sum(powers, axis=2, keepdims=True)
        probs_bf = (powers / totals).astype(jnp.bfloat16)
        attended = jnp.einsum(
            "hqk,khd->qhd", probs_bf, value_heads, preferred_element_type=jnp.float32
        )
        return (attended.reshape(block_rows, model_width), (highest + jnp.log(totals))[:, :, 0])

    attended, log_totals = lax.map(forward_block, jnp.arange(block_count, dtype=jnp.int32))
    return (attended.reshape(row_count, model_width), log_totals)


def attend_backward(query_bf, key_bf, value_bf, attended_grad, segment, log_totals, head_count):
    row_count, model_width = query_bf.shape
    head_size = model_width // head_count
    block_rows = min(row_count, 512)
    block_count = row_count // block_rows
    score_scale = 1.0 / math.sqrt(head_size)
    key_heads = key_bf.reshape(row_count, head_count, head_size)
    value_heads = value_bf.reshape(row_count, head_count, head_size)

    def backward_block(running, pieces):
        key_sum, value_sum = running
        block_index, log_rows = pieces
        query_rows = query_bf.reshape(block_rows, head_count, head_size)
        grad_rows = attended_grad.reshape(block_rows, head_count, head_size)
        same_image = segment[:, None] == segment[None, :]
        scores = (
            jnp.einsum("qhd,khd->hqk", query_rows, key_heads, preferred_element_type=jnp.float32)
            * score_scale
        )
        scores = jnp.where(same_image[None], scores, -1e30)
        probs = jnp.exp(scores - log_rows[:, :, None])
        probs_bf = probs.astype(jnp.bfloat16)
        prob_grad = jnp.einsum(
            "qhd,khd->hqk", grad_rows, value_heads, preferred_element_type=jnp.float32
        )
        row_inner = jnp.sum(probs * prob_grad, axis=2, keepdims=True)
        score_grad = (probs * (prob_grad - row_inner)).astype(jnp.bfloat16)
        query_grad = (
            jnp.einsum("hqk,khd->qhd", score_grad, key_heads, preferred_element_type=jnp.float32)
            * score_scale
        )
        key_sum = (
            key_sum
            + jnp.einsum("hqk,qhd->khd", score_grad, query_rows, preferred_element_type=jnp.float32)
            * score_scale
        )
        value_sum = value_sum + jnp.einsum(
            "hqk,qhd->khd", probs_bf, grad_rows, preferred_element_type=jnp.float32
        )
        return ((key_sum, value_sum), query_grad.reshape(block_rows, model_width))

    empty_sum = jnp.zeros((row_count, head_count, head_size), jnp.float32)
    sums, query_grad = lax.scan(
        backward_block,
        (empty_sum, empty_sum),
        (jnp.arange(block_count, dtype=jnp.int32), log_totals),
    )
    return (
        query_grad.reshape(row_count, model_width),
        sums[0].reshape(row_count, model_width),
        sums[1].reshape(row_count, model_width),
    )


def on_box():
    return lax.axis_size("dp") == 4 and lax.axis_size("fsdp") == 8


def neighbour(index, axis):
    plane, line = index // 8, index % 8
    if axis == "x":
        plane ^= 1
    elif axis == "y":
        plane ^= 2
    elif axis == "core":
        line ^= 1
    else:
        line = (line - 2 * axis) % 8
    return plane * 8 + line


def swap(values, axis):
    return lax.ppermute(values, AXES, [(index, neighbour(index, axis)) for index in range(32)])


HALF_ORDERS = (("x", 1, "y", 2), ("y", 2, "x", 1))


def place():
    plane, line = lax.axis_index("dp"), lax.axis_index("fsdp")
    return plane, line // 2, line % 2


def flipped(plane, flip):
    if flip % 2:
        plane = plane + 1 - 2 * (plane % 2)
    if flip // 2:
        plane = plane + 2 - 4 * (plane // 2)
    return plane


def pick(values, index):
    return lax.dynamic_index_in_dim(values, index, axis=0, keepdims=False)


def gather_blocks(attn_weight, proj_weight, up_weight, down_weight):
    parts = lax.axis_size("dp")
    attn, proj, up, down = [
        lax.all_gather(lax.all_gather(weight, "dp", axis=1, tiled=True), "fsdp", axis=0, tiled=True)
        for weight in (attn_weight, proj_weight, up_weight, down_weight)
    ]
    width = attn.shape[0]

    def by_block(weight):
        return weight.reshape(weight.shape[0], parts, -1).transpose(1, 0, 2)

    joined = jnp.concatenate([by_block(attn), by_block(proj)], axis=2)
    return joined, by_block(up), by_block(down.T.reshape(width, -1))


def scatter_whole(gradient):
    part = lax.psum_scatter(
        gradient.astype(jnp.bfloat16), "dp", scatter_dimension=1, tiled=True
    ).astype(jnp.float32)
    return lax.psum_scatter(part, "fsdp", scatter_dimension=0, tiled=True)


def scatter_rows(pairs):
    return [
        scatter_whole(matmul_tn(left, right.transpose(1, 0, 2).reshape(left.shape[0], -1)))
        for left, right in pairs
    ]


def trade(one_for_all, values, out, send_sems, recv_sems):
    planes, lines = lax.axis_size("dp"), lax.axis_size("fsdp")
    count = planes * lines
    me = lax.axis_index("dp") * lines + lax.axis_index("fsdp")

    def device(index):
        return (index // lines, index % lines)

    def chunk(index):
        return values if one_for_all else values.at[index]

    barrier = pltpu.get_barrier_semaphore()

    @pl.loop(1, count)
    def _(step):
        pl.semaphore_signal(
            barrier,
            inc=1,
            device_id=device((me + step) % count),
            device_id_type=pl.DeviceIdType.MESH,
        )

    pl.semaphore_wait(barrier, count - 1)

    @pl.loop(1, count)
    def _(step):
        peer = (me + step) % count
        pltpu.make_async_remote_copy(
            src_ref=chunk(peer),
            dst_ref=out.at[me],
            send_sem=send_sems.at[step],
            recv_sem=recv_sems.at[step],
            device_id=device(peer),
            device_id_type=pl.DeviceIdType.MESH,
        ).start()

    if one_for_all:
        out[me] = values[...]
    else:
        out[me] = values[me]

    @pl.loop(1, count)
    def _(step):
        peer = (me + step) % count
        copy = pltpu.make_async_remote_copy(
            src_ref=chunk(peer),
            dst_ref=out.at[(me + count - step) % count],
            send_sem=send_sems.at[step],
            recv_sem=recv_sems.at[step],
            device_id=device(peer),
            device_id_type=pl.DeviceIdType.MESH,
        )
        copy.wait()


def exchange(values, collective_id, one_for_all=False):
    count = lax.axis_size("dp") * lax.axis_size("fsdp")
    chunk = values.shape[-2:]
    size = count * chunk[0] * chunk[1] * values.dtype.itemsize
    return pl.pallas_call(
        partial(trade, one_for_all),
        out_shape=jax.ShapeDtypeStruct((count,) + chunk, values.dtype),
        in_specs=[pl.BlockSpec(memory_space=pltpu.VMEM)],
        out_specs=pl.BlockSpec(memory_space=pltpu.VMEM),
        scratch_shapes=[pltpu.SemaphoreType.DMA((count,)), pltpu.SemaphoreType.DMA((count,))],
        compiler_params=pltpu.CompilerParams(
            collective_id=collective_id,
            has_side_effects=True,
            vmem_limit_bytes=3 * size + 4 * 2**20,
        ),
        cost_estimate=pl.CostEstimate(flops=0, bytes_accessed=8 * size, transcendentals=0),
    )(values)


def gather_small(silu_bf, vectors):
    flat = jnp.concatenate([silu_bf.reshape(-1), *vectors])
    width = -(-flat.shape[0] // 2048) * 128
    flat = jnp.pad(flat, (0, 16 * width - flat.shape[0])).reshape(16, width)
    everyone = exchange(flat, 0, one_for_all=True)
    everyone = everyone.reshape(everyone.shape[0], -1)
    begin = silu_bf.size
    silu_all = everyone[:, :begin].reshape(-1, silu_bf.shape[1])
    found = []
    for vector in vectors:
        found.append(everyone[:, begin : begin + vector.shape[0]].reshape(-1))
        begin += vector.shape[0]
    return silu_all, found


def silu_columns(silu_all, ada_weight):
    rows = ada_weight.shape[0]
    return lax.dynamic_slice_in_dim(silu_all, lax.axis_index("fsdp") * rows, rows, axis=1)


def modulate_slots(silu_all, ada_weight, ada_bias):
    planes, lines = lax.axis_size("dp"), lax.axis_size("fsdp")
    columns = ada_weight.shape[1]
    slots = silu_all.shape[0] // (planes * lines)
    silu_part = silu_columns(silu_all, ada_weight)
    term = jnp.dot(silu_part, ada_weight, preferred_element_type=jnp.float32)
    term = exchange(term.reshape(planes * lines, slots, columns), 1)
    term = jnp.sum(term.reshape(planes, lines, slots, columns), axis=1)
    modulation = term.transpose(1, 0, 2).reshape(slots, planes * columns)
    return modulation + ada_bias.astype(jnp.float32), silu_part


def modulation_back(modulation_grad, silu_part, ada_weight, terms):
    planes, lines = lax.axis_size("dp"), lax.axis_size("fsdp")
    devices = planes * lines
    slots = modulation_grad.shape[0]
    rows, columns = ada_weight.shape
    cut = modulation_grad.reshape(slots, planes, columns).transpose(1, 0, 2)
    cut = cut.reshape(planes, 1, 16, slots * columns // 16)
    cut = jnp.broadcast_to(cut, (planes, lines) + cut.shape[2:])
    cut = exchange(cut.reshape((devices,) + cut.shape[2:]), 2)
    cut = cut.reshape(devices * slots, columns)
    ada_grad = matmul_tn(silu_part, cut)
    sums = jnp.sum(cut, axis=0, dtype=jnp.float32)
    bias_width = columns // lines
    ada_bias_grad = lax.dynamic_slice_in_dim(sums, lax.axis_index("fsdp") * bias_width, bias_width)
    silu_grad = matmul_nt(cut, ada_weight).reshape(devices, slots * rows)
    flat = jnp.concatenate([silu_grad] + [term.reshape(devices, -1) for term in terms], axis=1)
    width = -(-flat.shape[1] // 1024) * 128
    flat = jnp.pad(flat, ((0, 0), (0, 8 * width - flat.shape[1])))
    flat = exchange(flat.reshape(devices, 8, width), 3).reshape(devices, -1)
    shared = jnp.sum(flat[:, slots * rows :], axis=0)
    silu_grad = flat[:, : slots * rows].reshape(planes, lines, slots, rows).sum(axis=0)
    silu_grad = silu_grad.transpose(1, 0, 2).reshape(slots, lines * rows)
    found, begin = [], 0
    for term in terms:
        found.append(shared[begin : begin + term.shape[0] // devices])
        begin += term.shape[0] // devices
    return ada_grad, ada_bias_grad, silu_grad, found


def by_columns(values, parts):
    rows, columns = values.shape
    return values.reshape(rows, parts, columns // parts).transpose(1, 0, 2)


SLOPE = math.sqrt(2.0 / math.pi)
WINDOW = 512


def mm(left, right):
    return jnp.dot(left, right, preferred_element_type=jnp.float32)


def shaped(dims, kind=jnp.float32):
    return jax.ShapeDtypeStruct(dims, kind)


def by_rows(count, step, body):
    @pl.loop(0, count // step)
    def _(index):
        body(pl.ds(pl.multiple_of(index * step, step), step))


def by_groups(count, step, body):
    @pl.loop(0, count // step)
    def _(index):
        body(pl.ds(pl.multiple_of(index * step, step), step), index * step // 128)


def lane_index(rows, lanes):
    return lax.broadcasted_iota(jnp.int32, (rows, lanes), 1)


def window_of(block, width, total, span):
    begin = min(block * width // 128 * 128, total - span)
    return begin, block * width - begin


def group_row(table, group, column, width):
    return table[pl.ds(group, 1), column * width : (column + 1) * width]


def add_group(out, group, value):
    out[pl.ds(group, 1), :] += jnp.sum(value, axis=0, keepdims=True)


def centred(value):
    center = value - jnp.mean(value, axis=-1, keepdims=True)
    scale = lax.rsqrt(jnp.mean(center * center, axis=-1, keepdims=True) + 1e-06)
    return center * scale, scale


def norm_back(normed, scale, grad):
    return scale * (
        grad
        - jnp.mean(grad, axis=-1, keepdims=True)
        - normed * jnp.mean(grad * normed, axis=-1, keepdims=True)
    )


def head_window(head, size, total):
    begin = jnp.minimum(head * size // 128 * 128, total - 256)
    begin = pl.multiple_of(begin, 128)
    lane = lane_index(1, 256)
    offset = head * size - begin
    return begin, (lane >= offset) & (lane < offset + size)


def far_device(plane, depth, core):
    return (plane, depth * 2 + core)


class Gather:
    def __init__(self, shards, wholes, send_sems, recv_sems, local_sems):
        self.shards, self.wholes = shards, wholes
        self.send_sems, self.recv_sems, self.local_sems = send_sems, recv_sems, local_sems
        self.plane, self.depth, self.core = place()
        self.started = []
        self.kept = []
        self.counts = [0, 0, 0]

    def partners(self):
        return [
            far_device(flipped(self.plane, 1), self.depth, self.core),
            far_device(flipped(self.plane, 2), self.depth, self.core),
            far_device(self.plane, self.depth, 1 - self.core),
        ]

    def back(self, entry):
        low, high = (3 - self.depth) // 3, self.depth // 3
        return (0, 1 + 2 * low, 3 - low - high, 2 - low + high)[entry]

    def spot(self, weight, flip, back, other=False):
        plane, depth = flipped(self.plane, flip), (self.depth + 4 - back) % 4
        core = 1 - self.core if other else self.core
        if weight < 2:
            return self.wholes[weight].at[plane, depth, core]
        return self.wholes[weight].at[depth, plane, core]

    def send(self, weight, source, target, partner, kind, entry):
        copy = pltpu.make_async_remote_copy(
            src_ref=source,
            dst_ref=target,
            send_sem=self.send_sems.at[weight, self.counts[weight]],
            recv_sem=self.recv_sems.at[weight, kind, entry],
            device_id=partner,
            device_id_type=pl.DeviceIdType.MESH,
        )
        self.counts[weight] += 1
        copy.start()
        self.started.append(copy)

    def arrive(self, weight, region, kind, entry):
        pltpu.make_async_remote_copy(
            src_ref=region,
            dst_ref=region,
            send_sem=self.send_sems.at[weight, 0],
            recv_sem=self.recv_sems.at[weight, kind, entry],
            device_id=self.partners()[2],
            device_id_type=pl.DeviceIdType.MESH,
        ).wait_recv()

    def pass_on(self, weight, source, flip, entry):
        back = self.back(entry)
        target = self.spot(weight, flip, back)
        beside = self.partners()
        if flip == 0 or (flip == 2 and entry % 2 == 1):
            self.send(weight, source, target, beside[0], 1 if flip == 0 else 3, back)
        if flip == 0 or (flip == 1 and entry % 2 == 0):
            self.send(weight, source, target, beside[1], 2 if flip == 0 else 3, back)
        self.send(weight, source, target, beside[2], 4 + flip, back)

    def keep(self, weight):
        keep = pltpu.make_async_copy(
            self.shards[weight], self.spot(weight, 0, 0), self.local_sems.at[weight]
        )
        keep.start()
        self.kept.append(keep)

    def open_plane(self, weight, entry):
        self.pass_on(weight, self.spot(weight, 0, self.back(entry)), 0, entry)

    def along(self, weight, source, back, step, number, start):
        beyond = self.depth + step

        @pl.when((beyond >= 0) & (beyond <= 3))
        def _():
            copy = pltpu.make_async_remote_copy(
                src_ref=source,
                dst_ref=self.spot(weight, 0, back),
                send_sem=self.send_sems.at[weight, number],
                recv_sem=self.recv_sems.at[weight, 0, (back + step + 4) % 4],
                device_id=far_device(self.plane, (beyond + 4) % 4, self.core),
                device_id_type=pl.DeviceIdType.MESH,
            )
            if start:
                copy.start()
            else:
                copy.wait_send()

    def line_sends(self, weight, entry, start):
        back = self.back(entry)
        if entry == 0:
            for number, step in enumerate((1, -1)):
                self.along(weight, self.spot(weight, 0, 0), 0, step, 32 + number, start)
        else:
            step = 2 * ((self.depth - back + 4) // 4) - 1
            self.along(weight, self.spot(weight, 0, back), back, step, 33 + entry, start)

    def open_line(self, weight):
        self.line_sends(weight, 0, True)

    def line_partners(self):
        return [far_device(self.plane, (self.depth + d) % 4, self.core) for d in (1, 2, 3)]

    def on_line(self, weight, entry):
        region = self.spot(weight, 0, self.back(entry))
        self.arrive(weight, region, 0, self.back(entry))
        self.line_sends(weight, entry, True)

    def on_plane(self, weight, flip, entry):
        back = self.back(entry)
        region = self.spot(weight, flip, back)
        self.arrive(weight, region, flip, back)
        self.pass_on(weight, region, flip, entry)

    def plane_steps(self, weight):
        found = []
        for entry in range(4):
            found.append(partial(self.on_plane, weight, 1, entry))
            found.append(partial(self.on_plane, weight, 2, entry))
            if entry:
                found.append(partial(self.on_plane, weight, 3, entry - 1))
        found.append(partial(self.on_plane, weight, 3, 3))
        return found

    def ready(self, weight, entries=(0, 1, 2, 3)):
        for flip in range(4):
            for back in [self.back(entry) for entry in entries]:
                self.arrive(weight, self.spot(weight, flip, back, True), 4 + flip, back)

    def finish(self):
        for copy in self.started:
            copy.wait_send()


def greet(partners):
    barrier = pltpu.get_barrier_semaphore()
    for partner in partners:
        pl.semaphore_signal(
            barrier, inc=1, device_id=partner, device_id_type=pl.DeviceIdType.MESH
        )
    pl.semaphore_wait(barrier, len(partners))


def trade_along(axis, values, land, send_sems, recv_sems, start):
    count, me = lax.axis_size(axis), lax.axis_index(axis)

    @pl.loop(1, count)
    def _(step):
        peer = (me + step) % count
        target = me if start else (me + count - step) % count
        if axis == "dp":
            device = (peer, lax.axis_index("fsdp"))
        else:
            device = (lax.axis_index("dp"), peer)
        copy = pltpu.make_async_remote_copy(
            src_ref=values.at[peer],
            dst_ref=land.at[target],
            send_sem=send_sems.at[step],
            recv_sem=recv_sems.at[step],
            device_id=device,
            device_id_type=pl.DeviceIdType.MESH,
        )
        if start:
            copy.start()
        else:
            copy.wait()

    if start:
        land[me] = values[me]


def greet_all():
    planes, lines = lax.axis_size("dp"), lax.axis_size("fsdp")
    count = planes * lines
    me = lax.axis_index("dp") * lines + lax.axis_index("fsdp")
    barrier = pltpu.get_barrier_semaphore()

    @pl.loop(1, count)
    def _(step):
        peer = (me + step) % count
        pl.semaphore_signal(
            barrier,
            inc=1,
            device_id=(peer // lines, peer % lines),
            device_id_type=pl.DeviceIdType.MESH,
        )

    pl.semaphore_wait(barrier, count - 1)


def spread(axis_peer, values, land, send_sems, recv_sems, start):
    planes, lines = lax.axis_size("dp"), lax.axis_size("fsdp")
    count = planes * lines
    me = lax.axis_index("dp") * lines + lax.axis_index("fsdp")

    @pl.loop(1, count)
    def _(step):
        peer = (me + step) % count
        target = me if start else (me + count - step) % count
        copy = pltpu.make_async_remote_copy(
            src_ref=values.at[peer % lines] if axis_peer else values,
            dst_ref=land.at[target],
            send_sem=send_sems.at[step],
            recv_sem=recv_sems.at[step],
            device_id=(peer // lines, peer % lines),
            device_id_type=pl.DeviceIdType.MESH,
        )
        if start:
            copy.start()
        else:
            copy.wait()

    if start:
        land[me] = values[me % lines] if axis_peer else values[...]


def opening_kernel(
    silu,
    flat,
    ada_weight,
    joined_shard,
    up_shard,
    down_shard,
    joined_whole,
    up_whole,
    down_whole,
    silu_land,
    flat_land,
    plane_land,
    product,
    term,
    term_land,
    plane_term,
    send_sems,
    recv_sems,
    local_sems,
    spread_sems,
    line_sems,
    plane_sems,
):
    gather = Gather(
        (joined_shard, up_shard, down_shard),
        (joined_whole, up_whole, down_whole),
        send_sems,
        recv_sems,
        local_sems,
    )
    for weight in range(3):
        gather.keep(weight)
    greet_all()
    silu_trade = (True, silu, silu_land, spread_sems.at[0], spread_sems.at[1])
    flat_trade = (False, flat, flat_land, spread_sems.at[2], spread_sems.at[3])
    line_trade = (term, term_land, line_sems.at[0], line_sems.at[1])
    plane_trade = (plane_term, plane_land, plane_sems.at[0], plane_sems.at[1])
    spread(*silu_trade, True)
    for copy in gather.kept:
        copy.wait()
    gather.open_line(0)
    gather.open_plane(0, 0)
    spread(*flat_trade, True)
    for entry in (1, 2, 3):
        gather.on_line(0, entry)
        gather.open_plane(0, entry)
    gather.open_line(1)
    gather.open_plane(1, 0)
    spread(*silu_trade, False)
    devices, tall, rows = silu_land.shape
    product[...] = mm(silu_land[...].reshape(devices * tall, rows), ada_weight[...])
    lines, planes, slots = term.shape[:3]
    for line in range(lines):
        for plane in range(planes):
            begin = (plane * lines + line) * tall
            term[line, plane] = product[begin : begin + slots, :]
    trade_along("fsdp", *line_trade, True)
    first, second = gather.plane_steps(0), gather.plane_steps(1)
    for step in first[:2]:
        step()
    gather.on_line(1, 1)
    for step in first[2:5]:
        step()
    gather.on_line(1, 2)
    gather.open_plane(1, 1)
    trade_along("fsdp", *line_trade, False)
    total = term_land[0]
    for line in range(1, lines):
        total = total + term_land[line]
    plane_term[...] = total
    trade_along("dp", *plane_trade, True)
    for step in first[5:8]:
        step()
    gather.on_line(1, 3)
    for step in first[8:] + second[:5]:
        step()
    gather.on_plane(1, 3, 1)
    spread(*flat_trade, False)
    trade_along("dp", *plane_trade, False)
    gather.ready(0)
    gather.ready(1, (0, 1))
    gather.finish()
    for weight in range(2):
        for entry in range(4):
            gather.line_sends(weight, entry, False)


def opening(silu, flat, ada_weight, shards):
    rows, width = shards[1].shape
    lines, tall, short = silu.shape
    slots, part = 4, ada_weight.shape[1]
    whole = shaped((4, 4, 2, rows, width), jnp.bfloat16)
    vmem, away = pl.BlockSpec(memory_space=pltpu.VMEM), pl.BlockSpec(memory_space=pl.ANY)
    return pl.pallas_call(
        opening_kernel,
        out_shape=[
            whole,
            whole,
            whole,
            shaped((4 * lines, tall, short), jnp.bfloat16),
            shaped((4 * lines,) + flat.shape, jnp.bfloat16),
            shaped((4, slots, part)),
        ],
        in_specs=[vmem] * 6,
        out_specs=[away] * 3 + [vmem] * 3,
        scratch_shapes=[
            pltpu.VMEM((4 * lines * tall, part), jnp.float32),
            pltpu.VMEM((lines, 4, slots, part), jnp.float32),
            pltpu.VMEM((lines, 4, slots, part), jnp.float32),
            pltpu.VMEM((4, slots, part), jnp.float32),
            pltpu.SemaphoreType.DMA((3, 40)),
            pltpu.SemaphoreType.DMA((3, 8, 4)),
            pltpu.SemaphoreType.DMA((3,)),
            pltpu.SemaphoreType.DMA((4, 32)),
            pltpu.SemaphoreType.DMA((2, 8)),
            pltpu.SemaphoreType.DMA((2, 4)),
        ],
        compiler_params=pltpu.CompilerParams(
            collective_id=7, has_side_effects=True, vmem_limit_bytes=32 * 2**20
        ),
        cost_estimate=pl.CostEstimate(flops=10**8, bytes_accessed=10**8, transcendentals=0),
    )(silu, flat, ada_weight, *shards)


def forward_kernel(
    tokens,
    places,
    codes,
    slots,
    slot_line,
    group_slots,
    plane_land,
    ada_bias,
    joined_bias,
    out_bias,
    up_bias,
    joined_whole,
    up_start,
    down_start,
    up_whole,
    down_whole,
    joined,
    start,
    table,
    normed_t,
    attended_t,
    normed2_t,
    stats,
    branch,
    middle,
    hidden,
    before,
    room,
    product,
    wide_room,
    bar,
    before_room,
    normed,
    attended,
    normed2,
    strip,
    all_modulation,
    send_sems,
    recv_sems,
    load_sems,
    store_sems,
):
    gather = Gather(
        (None, None, None), (None, up_whole, down_whole), send_sems, recv_sems, None
    )
    loads = [
        pltpu.make_async_copy(joined_whole.at[block], room.at[block], load_sems.at[block])
        for block in range(4)
    ]
    for load in loads:
        load.start()
    greet(gather.partners() + gather.line_partners())
    gather.open_line(2)
    for weight, entry in ((1, 2), (1, 3), (2, 0)):
        gather.open_plane(weight, entry)
    rows, width = tokens.shape
    lane = lane_index(rows, codes.shape[0])
    spot = jnp.where(lane % 64 < 32, places[:, 0:1], places[:, 1:2])
    hot = jnp.where(lane % 32 == spot, 1.0, 0.0).astype(jnp.bfloat16)
    start[...] = mm(hot, codes[...]) + wide(tokens[...])
    strip[...] = jnp.zeros_like(strip)
    slot_count, part = plane_land.shape[1:]
    for plane in range(4):
        strip[:slot_count, :part] = plane_land[plane]
        shift = plane * part % 128
        begin = plane * part - shift
        moved = pltpu.roll(strip[...], shift, 1) if shift else strip[...]
        lane = lane_index(8, strip.shape[1])
        span = pl.ds(begin, strip.shape[1])
        inside = (lane >= shift) & (lane < shift + part)
        all_modulation[:, span] = jnp.where(inside, moved, all_modulation[:, span])
    total = jnp.zeros(table.shape, jnp.float32)
    for slot in range(slot_count):
        row = all_modulation[slot : slot + 1, : table.shape[1]] + ada_bias[...]
        total = total + jnp.where(group_slots[...] == slot, row, 0.0)
    table[...] = total

    def norm_first(at, group):
        hat, _ = centred(start[at, :])
        value = hat * (1.0 + group_row(table, group, 1, width)) + group_row(table, group, 0, width)
        normed[at, :] = low_bits(value)

    by_groups(rows, 64, norm_first)
    line_step, plane_open, plane_step = (
        partial(partial, method) for method in (gather.on_line, gather.open_plane, gather.on_plane)
    )
    later = [line_step(2, 1), plane_step(1, 1, 2), plane_step(1, 2, 2), line_step(2, 2)]
    later += [plane_open(2, 1), plane_step(1, 1, 3), plane_step(1, 2, 3), plane_step(1, 3, 2)]
    later += [line_step(2, 3), plane_step(1, 3, 3), plane_open(2, 2), plane_open(2, 3)]
    later += gather.plane_steps(2)

    def tick(count=1):
        for _ in range(count):
            if later:
                later.pop(0)()

    normed_t[...] = normed[...].T
    columns = joined.shape[1] // 4
    tick(2)
    span = product.shape[1]
    for block in range(4):
        loads[block].wait()
        product[...] = mm(normed[...], room[block].reshape(width, width)[:, :span])
        begin, offset = window_of(block, columns, joined.shape[1], span)

        def put(at):
            moved = product[at, :]
            if offset:
                moved = pltpu.roll(moved, offset, 1)
            lane = lane_index(moved.shape[0], span)
            inside = (lane >= offset) & (lane < offset + columns)
            wide_room[at, begin : begin + span] = jnp.where(
                inside, moved, wide_room[at, begin : begin + span]
            )

        by_rows(rows, 64, put)
        tick(2)

    def settle(at):
        joined[at, :] = (wide_room[at, :] + joined_bias[...]).astype(jnp.bfloat16)

    by_rows(rows, 64, settle)
    bar[...] = jnp.where(slots[...] == slot_line[...], 0.0, -1e30)
    stats[...] = jnp.zeros_like(stats)
    head_size = width // HEADS
    scale = 1.0 / math.sqrt(head_size)
    for group in range(8):

        @pl.loop(2 * group, 2 * group + 2)
        def _(head):
            at, inside = head_window(head, head_size, width)
            query = jnp.where(inside, joined[:, pl.ds(at, 256)], 0.0)
            key = joined[:, pl.ds(pl.multiple_of(at + width, 128), 256)]
            value = joined[:, pl.ds(pl.multiple_of(at + 2 * width, 128), 256)]
            scores = matmul_nt(query, key) * scale + bar[...]
            highest = jnp.max(scores, axis=1, keepdims=True)
            powers = jnp.exp(scores - highest)
            totals = jnp.sum(powers, axis=1, keepdims=True)
            probs = (powers * (1.0 / totals)).astype(jnp.bfloat16)
            found = mm(probs, value)
            wide_room[:, pl.ds(at, 256)] = jnp.where(inside, found, wide_room[:, pl.ds(at, 256)])
            lane = lane_index(rows, 128)
            stats[...] = jnp.where(lane == head, highest + jnp.log(totals), stats[...])

        tick(1)

    attended[...] = wide_room[:, :width].astype(jnp.bfloat16)
    columns = width // 4
    for block in range(4):
        product[:, :WINDOW] = mm(attended[...], room[block].reshape(width, width)[:, width - WINDOW :])
        begin, offset = window_of(block, columns, width, WINDOW)

        def put(at):
            moved = product[at, :WINDOW]
            if offset != WINDOW - columns:
                moved = pltpu.roll(moved, columns + offset, 1)
            lane = lane_index(moved.shape[0], WINDOW)
            inside = (lane >= offset) & (lane < offset + columns)
            branch[at, begin : begin + WINDOW] = jnp.where(
                inside, moved, branch[at, begin : begin + WINDOW]
            )

        by_rows(rows, 64, put)
        tick()

    def combine(at, group):
        value = branch[at, :] + out_bias[...]
        branch[at, :] = value
        value = start[at, :] + group_row(table, group, 2, width) * value
        middle[at, :] = value
        hat, _ = centred(value)
        value = hat * (1.0 + group_row(table, group, 4, width)) + group_row(table, group, 3, width)
        normed2[at, :] = value.astype(jnp.bfloat16)

    by_groups(rows, 64, combine)
    normed2_t[...] = normed2[...].T
    attended_t[...] = attended[...].T
    while len(later) > 12:
        tick()
    gather.ready(1, (2, 3))
    loads = [
        pltpu.make_async_copy(up_whole.at[block], room.at[block], load_sems.at[block])
        for block in range(4)
    ]
    for load in loads:
        load.start()
    stores = [None, None]
    for block in range(4):
        loads[block].wait()
        slot = block % 2
        if stores[slot] is not None:
            stores[slot].wait()
        before_room[slot] = mm(normed2[...], room[block].reshape(width, width)) + up_bias[block]
        stores[slot] = pltpu.make_async_copy(
            before_room.at[slot], before.at[block], store_sems.at[slot]
        )
        stores[slot].start()

        def act(some):
            value = before_room[slot, some, :]
            bend = 1.0 + jnp.tanh(SLOPE * (value + 0.044715 * (value * value * value)))
            hidden[block, some, :] = (value * (0.5 * bend)).astype(jnp.bfloat16)

        by_rows(rows, 64, act)
        tick(3)
    while later:
        tick()
    for store in stores:
        store.wait()
    gather.ready(2)
    gather.finish()
    for entry in range(4):
        gather.line_sends(2, entry, False)


def forward(tokens, places, codes, slots, group_slots, modulation, ada_bias, biases, wholes):
    rows, width = tokens.shape
    deep = width // 8
    whole = shaped((4, 4, 2, deep, width), jnp.bfloat16)
    vmem, away = pl.BlockSpec(memory_space=pltpu.VMEM), pl.BlockSpec(memory_space=pl.ANY)
    part = modulation.shape[2]
    return pl.pallas_call(
        forward_kernel,
        out_shape=[
            whole,
            whole,
            shaped((rows, 3 * width), jnp.bfloat16),
            shaped((rows, width)),
            shaped((8, 4 * part)),
            shaped((width, rows), jnp.bfloat16),
            shaped((width, rows), jnp.bfloat16),
            shaped((width, rows), jnp.bfloat16),
            shaped((rows, 128)),
            shaped((rows, width)),
            shaped((rows, width)),
            shaped((4, rows, width), jnp.bfloat16),
            shaped((4, rows, width)),
        ],
        in_specs=[vmem] * 11 + [away] * 3,
        out_specs=[away] * 2 + [vmem] * 10 + [away],
        input_output_aliases={12: 0, 13: 1},
        scratch_shapes=[
            pltpu.VMEM((4, 4, 2, deep, width), jnp.bfloat16),
            pltpu.VMEM((rows, 1024), jnp.float32),
            pltpu.VMEM((rows, 3 * width), jnp.float32),
            pltpu.VMEM((rows, rows), jnp.float32),
            pltpu.VMEM((2, rows, width), jnp.float32),
            pltpu.VMEM((rows, width), jnp.bfloat16),
            pltpu.VMEM((rows, width), jnp.bfloat16),
            pltpu.VMEM((rows, width), jnp.bfloat16),
            pltpu.VMEM((8, -(-part // 128) * 128), jnp.float32),
            pltpu.VMEM((8, 4 * part + 128), jnp.float32),
            pltpu.SemaphoreType.DMA((3, 40)),
            pltpu.SemaphoreType.DMA((3, 8, 4)),
            pltpu.SemaphoreType.DMA((4,)),
            pltpu.SemaphoreType.DMA((2,)),
        ],
        compiler_params=pltpu.CompilerParams(
            collective_id=4, has_side_effects=True, vmem_limit_bytes=62 * 2**20
        ),
        cost_estimate=pl.CostEstimate(
            flops=2 * 10 * rows * width * width, bytes_accessed=10**8, transcendentals=0
        ),
    )(
        tokens,
        places,
        codes,
        slots.reshape(rows, 1),
        slots.reshape(1, rows),
        group_slots,
        modulation,
        ada_bias,
        *biases,
        *wholes,
    )


def low_bits(value):
    return value.astype(jnp.bfloat16)


def wide(value):
    return value.astype(jnp.float32)


class Scatter:
    def __init__(self, own, lands, stage, outs, send_sems, recv_sems, stage_sems):
        self.own, self.lands, self.stage, self.outs = own, lands, stage, outs
        self.send_sems, self.recv_sems, self.stage_sems = send_sems, recv_sems, stage_sems
        self.plane, self.depth, self.core = place()
        self.started = []
        self.counts = [0] * len(lands)
        self.queue, self.held, self.turn = [], [], 0

    def partners(self):
        found = [
            far_device(flipped(self.plane, 1), self.depth, self.core),
            far_device(flipped(self.plane, 2), self.depth, self.core),
            far_device(self.plane, self.depth, 1 - self.core),
        ]
        return found + [far_device(self.plane, (self.depth + d) % 4, self.core) for d in (1, 2, 3)]

    def sending(self, weight, source, index, partner, number):
        return pltpu.make_async_remote_copy(
            src_ref=source,
            dst_ref=self.lands[weight].at[index],
            send_sem=self.send_sems.at[weight, number],
            recv_sem=self.recv_sems.at[weight, index],
            device_id=self.partners()[partner],
            device_id_type=pl.DeviceIdType.MESH,
        )

    def send(self, weight, source, index, partner):
        copy = self.sending(weight, source, index, partner, self.counts[weight])
        self.counts[weight] += 1
        copy.start()
        return copy

    def term(self, weight, flip, back, rows_of, line_rows):
        plane, depth = flipped(self.plane, flip), (self.depth + 4 - back) % 4
        base = (depth if line_rows else plane) * 2
        self.own[weight % 2, flip, back] = rows_of(base + self.core)[...]
        return self.send(weight, rows_of(base + 1 - self.core), flip * 4 + back, 2)

    def open(self, weight, part, order=(2, 1, 3, 0)):
        for back in order:
            axis, near, far = (0, 1, 2) if back % 2 == 0 else (1, 2, 1)
            jobs = []
            if part == "sent":
                for flip in (3, near):
                    goes = (flip, back, 16 + (4 if flip == 3 else 0) + back, axis)
                    jobs.append((flip * 4 + back, flip, goes))
            elif part == "kept":
                jobs = [(flip * 4 + back, flip, None) for flip in (far, 0)]
            elif part == "first":
                jobs = [(20 + back, far, (far, back, 24 + back, 1 - axis)), (16 + back, 0, None)]
            elif part == "second":
                jobs = [(24 + back, 0, (0, back, 28 + back, 2 + 4 - back) if back else None)]
            elif back:
                self.queue.append((weight, 28 + back, 0, 0, None))
            for index, flip, goes in jobs:
                self.queue.append((weight, index, flip, back, goes))

    def fetch(self, job):
        weight, index = job[0], job[1]
        region = self.lands[weight].at[index]
        pltpu.make_async_remote_copy(
            src_ref=region,
            dst_ref=region,
            send_sem=self.send_sems.at[weight, 0],
            recv_sem=self.recv_sems.at[weight, index],
            device_id=self.partners()[2],
            device_id_type=pl.DeviceIdType.MESH,
        ).wait_recv()
        if self.stage is not None:
            self.staging(weight, index, self.turn).start()
        self.held.append((job, self.turn))
        self.turn = (self.turn + 1) % 2

    def staging(self, weight, index, turn):
        return pltpu.make_async_copy(
            self.lands[weight].at[index], self.stage.at[turn], self.stage_sems.at[turn]
        )

    def merge(self):
        (weight, index, flip, back, goes), turn = self.held.pop(0)
        if self.stage is None:
            arrived = self.lands[weight][index]
        else:
            self.staging(weight, index, turn).wait()
            arrived = self.stage[turn]
        if index >= 28:
            self.outs[weight][...] += wide(arrived)
            return
        if index == 24:
            self.outs[weight][...] = wide(self.own[weight % 2, flip, back]) + wide(arrived)
            return
        self.own[weight % 2, flip, back] = self.own[weight % 2, flip, back] + arrived
        if goes is not None:
            self.started.append((weight, goes, self.counts[weight]))
            self.send(weight, self.own.at[weight % 2, goes[0], goes[1]], goes[2], goes[3])

    def tick(self, count=1):
        for _ in range(count):
            if self.held:
                self.merge()
            if self.queue:
                self.fetch(self.queue.pop(0))
                if self.stage is None:
                    self.merge()

    def clear(self, weight, flip):
        while any(job[0] == weight and flip == 0 for job in self.queue) or any(
            held[0][0] == weight and held[0][2] == flip for held in self.held
        ):
            self.tick()
        for entry in [entry for entry in self.started if entry[0] == weight and entry[1][0] == flip]:
            self.started.remove(entry)
            self.sent(entry)

    def sent(self, entry):
        weight, (flip, back, index, partner), number = entry
        source = self.own.at[weight % 2, flip, back]
        self.sending(weight, source, index, partner, number).wait_send()

    def drain(self):
        while self.queue or self.held:
            self.tick()
        for entry in self.started:
            self.sent(entry)


def multiply_rows(out, left, right, step=384):
    @pl.loop(0, left.shape[0] // step)
    def _(index):
        at = pl.ds(pl.multiple_of(index * step, step), step)
        out[at, :] = mm(left[at, :], right[...]).astype(jnp.bfloat16)


def deep_rows(room, slot, deep):
    def rows_of(row):
        return room.at[slot, pl.ds(pl.multiple_of(row * deep, 16), deep)]

    return rows_of


def backward_kernel(
    hidden_in,
    before_in,
    joined_in,
    joined_whole,
    up_whole,
    down_whole,
    normed_in,
    attended_in,
    start_in,
    middle,
    out_grad,
    branch,
    normed_t,
    stats,
    slots,
    slot_line,
    table,
    bias,
    down_land,
    up_land,
    joined_land,
    mixed,
    middle_grad,
    slot_sums,
    branch_sums,
    pre_sums,
    joined_sums,
    down_out,
    up_out,
    joined_out,
    windows,
    own,
    stage,
    room,
    acts,
    grads,
    grads_t,
    attended_grad,
    send_sems,
    recv_sems,
    stage_sems,
    load_sems,
    more_sems,
):
    rows, width = middle.shape
    deep = width // 8
    scatter = Scatter(
        own,
        (down_land, up_land, joined_land),
        stage,
        (down_out, up_out, joined_out),
        send_sems,
        recv_sems,
        stage_sems,
    )
    greet(scatter.partners())
    slot_sums[...] = jnp.zeros_like(slot_sums)
    branch_sums[...] = jnp.zeros_like(branch_sums)
    pre_sums[...] = jnp.zeros_like(pre_sums)
    joined_sums[...] = jnp.zeros_like(joined_sums)

    def dense(weights, before, total):
        plan = [(down_whole, part) for part in range(4)] * 2 + [(up_whole, part) for part in range(4)]

        def load(step):
            whole, part = plan[step]
            copy = pltpu.make_async_copy(
                whole.at[part], weights.at[step % 2], load_sems.at[step % 2]
            )
            copy.start()
            return copy

        loads = {0: load(0)}
        acting = [
            pltpu.make_async_copy(hidden_in.at[part], acts.at[part], more_sems.at[part])
            for part in range(4)
        ]
        for copy in acting:
            copy.start()

        def next_weight(step):
            if step + 1 < len(plan):
                loads[step + 1] = load(step + 1)
            loads[step].wait()
            return weights.at[step % 2]

        for part in range(4):
            acting[part].wait()
            term = matmul_nt(acts[part], next_weight(part)[...])
            total[...] = term + bias[...] if part == 0 else total[...] + term

        def settle(at, group):
            gate = group_row(table, group, 5, width)
            value = total[at, :]
            grad = wide(out_grad[at, :])
            mixed[at, :] = low_bits(middle[at, :] + gate * value)
            add_group(slot_sums.at[3], group, grad * value)
            value = low_bits(grad * gate)
            grads[at, :] = value
            branch_sums[1:2, :] += jnp.sum(wide(value), axis=0, keepdims=True)

        by_groups(rows, 64, settle)
        grads_t[...] = grads[...].T
        waits = [[], []]
        for number, back in enumerate((2, 1, 3, 0)):
            slot = number % 2
            for copy in waits[slot]:
                copy.wait_send()
            multiply_rows(room.at[slot], grads_t, acts.at[(scatter.depth + 4 - back) % 4])
            rows_of = deep_rows(room, slot, deep)
            waits[slot] = [scatter.term(0, flip, back, rows_of, False) for flip in (3, 1, 2, 0)]
        scatter.open(0, "sent")
        scatter.open(0, "kept")
        befores = [
            pltpu.make_async_copy(before_in.at[part], before.at[part % 2], more_sems.at[part])
            for part in range(4)
        ]
        befores[0].start()
        for part in range(4):
            if part < 3:
                befores[part + 1].start()
            total[...] = mm(grads[...], next_weight(4 + part)[...])
            befores[part].wait()

            def act(at):
                value = before[part % 2, at, :]
                square = value * value
                bend = jnp.tanh(SLOPE * (value + 0.044715 * (square * value)))
                slope = 0.5 * (1.0 + bend) + 0.5 * value * (1.0 - bend * bend) * (
                    SLOPE * (1.0 + 3.0 * 0.044715 * square)
                )
                value = low_bits(total[at, :] * slope)
                acts[part, at, :] = value
                pre_sums[part : part + 1, :] += jnp.sum(wide(value), axis=0, keepdims=True)

            by_rows(rows, 64, act)
            scatter.tick(4 if part else 6)
        for number, flip in enumerate((3, 1, 2, 0)):
            slot = number % 2
            for copy in waits[slot]:
                copy.wait_send()
            multiply_rows(room.at[slot], normed_t, acts.at[flipped(scatter.plane, flip)])
            rows_of = deep_rows(room, slot, deep)
            waits[slot] = [scatter.term(1, flip, back, rows_of, True) for back in (2, 1, 3, 0)]
        scatter.open(1, "sent")
        scatter.open(1, "kept")
        scatter.open(0, "first")
        scatter.open(0, "second")
        scatter.open(1, "first")
        scatter.open(1, "second")
        for part in range(4):
            term = matmul_nt(acts[part], next_weight(8 + part)[...])
            total[...] = term if part == 0 else total[...] + term
            scatter.tick(4)

        def turn(at, group):
            grad = total[at, :]
            hat, scale = centred(middle[at, :])
            add_group(slot_sums.at[1], group, grad)
            add_group(slot_sums.at[2], group, grad * hat)
            grad = grad * (1.0 + group_row(table, group, 4, width))
            grad = wide(out_grad[at, :]) + norm_back(hat, scale, grad)
            middle_grad[at, :] = grad
            add_group(slot_sums.at[0], group, grad * branch[at, :])
            value = wide(low_bits(grad * group_row(table, group, 2, width)))
            total[at, :] = value
            branch_sums[0:1, :] += jnp.sum(value, axis=0, keepdims=True)

        by_groups(rows, 64, turn)
        scatter.tick(8)
        for slot in range(2):
            for copy in waits[slot]:
                copy.wait_send()
        columns = width // 4
        span = pl.ds(width - WINDOW, WINDOW)
        sides = []
        for block in range(4):
            copy = pltpu.make_async_copy(
                joined_whole.at[block, :, span],
                weights.at[block // 2, :, pl.ds(block % 2 * WINDOW, WINDOW)],
                more_sems.at[block],
            )
            copy.start()
            sides.append(copy)
        for block in range(4):
            begin, offset = window_of(block, columns, width, WINDOW)

            def cut(at):
                moved = total[at, begin : begin + WINDOW]
                if offset != WINDOW - columns:
                    moved = pltpu.roll(moved, (2 * WINDOW - columns - offset) % WINDOW, 1)
                lane = lane_index(moved.shape[0], WINDOW)
                moved = jnp.where(lane >= WINDOW - columns, moved, 0.0)
                windows[block, at, :] = low_bits(moved)

            by_rows(rows, 64, cut)
        for block in range(4):
            sides[block].wait()
            side = weights[block // 2, :, block % 2 * WINDOW : (block % 2 + 1) * WINDOW]
            term = matmul_nt(windows[block], side)
            total[...] = term if block == 0 else total[...] + term
        attended_grad[...] = low_bits(total[...])

    pl.run_scoped(
        dense,
        pltpu.VMEM((2, width, width), jnp.bfloat16),
        pltpu.VMEM((2, rows, width), jnp.float32),
        pltpu.VMEM((rows, width), jnp.float32),
    )

    def heads(joined, found_room, bar):
        load = pltpu.make_async_copy(joined_in, joined, load_sems.at[0])
        load.start()
        size = width // HEADS
        scale = 1.0 / math.sqrt(size)
        bar[...] = jnp.where(slots[...] == slot_line[...], 0.0, -1e30)
        load.wait()
        for head_static in range(0, HEADS, 2):

            @pl.loop(head_static, head_static + 2)
            def _(head):
                begin, inside = head_window(head, size, width)
                columns = [pl.ds(pl.multiple_of(begin + part * width, 128), 256) for part in range(3)]
                query = jnp.where(inside, joined[:, columns[0]], 0.0)
                key = joined[:, columns[1]]
                value = joined[:, columns[2]]
                out_part = jnp.where(inside, attended_grad[:, columns[0]], 0.0)
                lane = lane_index(rows, 128)
                stat = jnp.sum(jnp.where(lane == head, stats[...], 0.0), axis=1, keepdims=True)
                probs = jnp.exp(matmul_nt(query, key) * scale + bar[...] - stat)
                prob_grad = matmul_nt(out_part, value)
                inner = jnp.sum(probs * prob_grad, axis=1, keepdims=True)
                score_grad = low_bits(probs * (prob_grad - inner))
                found = (
                    mm(score_grad, key) * scale,
                    matmul_tn(score_grad, query) * scale,
                    matmul_tn(low_bits(probs), out_part),
                )
                for part in range(3):
                    found_room[:, columns[part]] = jnp.where(
                        inside, found[part], found_room[:, columns[part]]
                    )

            scatter.tick((0, 0, 0, 2, 2, 2, 3, 3)[head_static // 2])

        span = 1024
        block_width = 3 * width // 4

        def add_up(at):
            joined_sums[...] += jnp.sum(wide(low_bits(found_room[at, :])), axis=0, keepdims=True)

        by_rows(rows, 64, add_up)
        for block in range(4):
            begin, offset = window_of(block, block_width, 3 * width, span)

            def cut(at):
                moved = found_room[at, begin : begin + span]
                if offset:
                    moved = pltpu.roll(moved, span - offset, 1)
                lane = lane_index(moved.shape[0], span)
                acts[block, at, :span] = low_bits(jnp.where(lane < block_width, moved, 0.0))

            by_rows(rows, 64, cut)

    pl.run_scoped(
        heads,
        pltpu.VMEM((rows, 3 * width), jnp.bfloat16),
        pltpu.VMEM((rows, 3 * width), jnp.float32),
        pltpu.VMEM((rows, rows), jnp.float32),
    )
    span = 1024

    def last(weights, attended_t, start, total):
        left = pltpu.make_async_copy(normed_in, grads_t, more_sems.at[0])
        other = pltpu.make_async_copy(attended_in, attended_t, more_sems.at[1])
        begin_copy = pltpu.make_async_copy(start_in, start, more_sems.at[2])
        for copy in (left, other, begin_copy):
            copy.start()

        def load(part):
            copy = pltpu.make_async_copy(
                joined_whole.at[part, :, pl.ds(0, span)], weights.at[part % 2], load_sems.at[part % 2]
            )
            copy.start()
            return copy

        loads = [load(0), load(1)]
        left.wait()
        other.wait()
        low, high = span, width - WINDOW
        waits = [[], []]
        for number, flip in enumerate((3, 1, 2, 0)):
            slot = number % 2
            for copy in waits[slot]:
                copy.wait_send()
            at = flipped(scatter.plane, flip)

            @pl.loop(0, 3)
            def _(index):
                some = pl.ds(pl.multiple_of(index * (width // 3), width // 3), width // 3)
                head = mm(grads_t[some, :], acts[at, :, :span])
                tail = mm(attended_t[some, :], windows[at])
                room[slot, some, :high] = low_bits(head[:, :high])
                room[slot, some, high:low] = low_bits(head[:, high:low] + tail[:, : low - high])
                room[slot, some, low:] = low_bits(tail[:, low - high :])

            scatter.clear(0, flip)
            rows_of = deep_rows(room, slot, deep)
            waits[slot] = [scatter.term(2, flip, back, rows_of, True) for back in (2, 1, 3, 0)]
            scatter.tick(1)
        early, late = (2, 1), (3, 0)
        scatter.open(2, "sent", early)
        scatter.open(2, "kept", early)
        scatter.open(2, "kept", late)
        scatter.open(0, "line")
        scatter.open(2, "first", early)
        scatter.open(2, "sent", late)
        scatter.open(2, "second", early)
        scatter.open(1, "line")
        scatter.open(2, "first", late)
        scatter.open(2, "second", late)
        scatter.open(2, "line")
        for part in range(4):
            loads[part].wait()
            term = matmul_nt(acts[part, :, :span], weights[part % 2])
            total[...] = term if part == 0 else total[...] + term
            if part < 2:
                loads.append(load(part + 2))
            scatter.tick(4)
        begin_copy.wait()

        def turn(at, group):
            grad = total[at, :]
            hat, scale = centred(start[at, :])
            add_group(slot_sums.at[4], group, grad)
            add_group(slot_sums.at[5], group, grad * hat)
            grad = grad * (1.0 + group_row(table, group, 1, width))
            middle_grad[at, :] = middle_grad[at, :] + norm_back(hat, scale, grad)

        for part in range(4):

            @pl.loop(0, rows // 256)
            def _(index):
                begin = part * (rows // 4) + index * 64
                turn(pl.ds(pl.multiple_of(begin, 64), 64), begin // 128)

            scatter.tick(2)
        for slot in range(2):
            for copy in waits[slot]:
                copy.wait_send()

    pl.run_scoped(
        last,
        pltpu.VMEM((2, width, span), jnp.bfloat16),
        pltpu.VMEM((width, rows), jnp.bfloat16),
        pltpu.VMEM((rows, width), jnp.float32),
        pltpu.VMEM((rows, width), jnp.float32),
    )
    scatter.drain()


def backward(away_ins, near_ins, slots, table, bias):
    middle = near_ins[0]
    rows, width = middle.shape
    deep = width // 8
    vmem, away = pl.BlockSpec(memory_space=pltpu.VMEM), pl.BlockSpec(memory_space=pl.ANY)
    land = shaped((32, deep, width), jnp.bfloat16)
    return pl.pallas_call(
        backward_kernel,
        out_shape=[
            land,
            land,
            land,
            shaped((rows, width), jnp.bfloat16),
            shaped((rows, width)),
            shaped((6, 8, width)),
            shaped((8, width)),
            shaped((8, width)),
            shaped((1, 3 * width)),
            shaped((deep, width)),
            shaped((deep, width)),
            shaped((deep, width)),
        ],
        in_specs=[away] * 9 + [vmem] * 9,
        out_specs=[away] * 3 + [vmem] * 9,
        scratch_shapes=[
            pltpu.VMEM((4, rows, WINDOW), jnp.bfloat16),
            pltpu.VMEM((2, 4, 4, deep, width), jnp.bfloat16),
            pltpu.VMEM((2, deep, width), jnp.bfloat16),
            pltpu.VMEM((2, width, width), jnp.bfloat16),
            pltpu.VMEM((4, rows, width), jnp.bfloat16),
            pltpu.VMEM((rows, width), jnp.bfloat16),
            pltpu.VMEM((width, rows), jnp.bfloat16),
            pltpu.VMEM((rows, width), jnp.bfloat16),
            pltpu.SemaphoreType.DMA((3, 32)),
            pltpu.SemaphoreType.DMA((3, 32)),
            pltpu.SemaphoreType.DMA((2,)),
            pltpu.SemaphoreType.DMA((2,)),
            pltpu.SemaphoreType.DMA((4,)),
        ],
        compiler_params=pltpu.CompilerParams(
            collective_id=5, has_side_effects=True, vmem_limit_bytes=62 * 2**20
        ),
        cost_estimate=pl.CostEstimate(
            flops=2 * 30 * rows * width * width, bytes_accessed=10**8, transcendentals=0
        ),
    )(
        *away_ins,
        *near_ins,
        slots.reshape(rows, 1),
        slots.reshape(1, rows),
        table,
        bias,
    )


def code_parts(width):
    quarter = width // 4
    exponent = jnp.arange(quarter, dtype=jnp.float32) / quarter
    frequency = 1.0 / 10000.0**exponent
    angle = jnp.arange(32, dtype=jnp.float32)[:, None] * frequency[None, :]
    half = jnp.concatenate([jnp.sin(angle), jnp.cos(angle)], axis=1)
    none = jnp.zeros_like(half)
    left = jnp.concatenate(
        [jnp.concatenate([half, none], axis=1), jnp.concatenate([none, half], axis=1)], axis=0
    )
    parts = []
    for _ in range(3):
        part = lax.reduce_precision(left, 8, 7)
        parts.append(part.astype(jnp.bfloat16))
        left = left - part
    return jnp.concatenate(parts, axis=0)


def box_device(
    tokens,
    condition,
    kept_index,
    segment,
    grid_side,
    ada_weight,
    ada_bias,
    attn_weight,
    attn_bias,
    proj_weight,
    out_bias,
    up_weight,
    up_bias,
    down_weight,
    grad_out,
):
    rows, width = tokens.shape
    slot_count = condition.shape[0]
    core = place()[2]
    columns = attn_weight.shape[1]
    turned = down_weight.T.reshape(2, up_weight.shape[0], down_weight.shape[0])
    mine, theirs = pick(turned, core), pick(turned, 1 - core)
    arrived = swap(theirs, "core")
    down_shard = jnp.where(
        core == 0,
        jnp.concatenate([mine, arrived], axis=1),
        jnp.concatenate([arrived, mine], axis=1),
    )
    silu_cond, silu_back = jax.vjp(jax.nn.silu, condition.astype(jnp.float32))
    silu_bf = silu_cond.astype(jnp.bfloat16)
    vectors = (ada_bias, attn_bias, out_bias, up_bias)
    flat = jnp.concatenate(vectors)
    flat = jnp.pad(flat, (0, 2048 - flat.shape[0])).reshape(16, 128)
    cut = silu_bf.reshape(slot_count, 8, -1).transpose(1, 0, 2)
    cut = jnp.pad(cut, ((0, 0), (0, 16 - slot_count), (0, 0)))
    joined_whole, up_start, down_start, silu_land, flat_land, modulation = opening(
        cut,
        flat,
        ada_weight,
        (jnp.concatenate([attn_weight, proj_weight], axis=1), up_weight, down_shard),
    )
    silu_part = silu_land[:, :slot_count].reshape(32 * slot_count, -1)
    flat_land = flat_land.reshape(32, -1)
    found, begin = [], 0
    for vector in vectors:
        found.append(flat_land[:, begin : begin + vector.shape[0]].reshape(-1))
        begin += vector.shape[0]
    ada_bfull, attn_bfull, out_bfull, up_bfull = found
    group_slots = segment.reshape(rows // 128, 128)[:, 0]
    group_sides = jnp.sum(
        jnp.where(group_slots[:, None] == jnp.arange(slot_count)[None, :], grid_side[None, :], 0), axis=1
    )
    side_rows = jnp.repeat(group_sides, 128)
    places = jnp.stack([kept_index % side_rows, kept_index // side_rows], axis=1)
    zeros = jnp.zeros((width,), jnp.bfloat16)
    joined_bias = jnp.concatenate([attn_bfull[:width], zeros, attn_bfull[width:]])
    out_bias_f = out_bfull.astype(jnp.float32)
    (
        up_whole,
        down_whole,
        joined,
        start,
        table,
        normed_t,
        attended_t,
        normed2_t,
        stats,
        branch1,
        middle,
        hidden,
        before,
    ) = forward(
        tokens,
        places,
        code_parts(width),
        segment,
        jnp.pad(group_slots, (0, 8 - rows // 128), constant_values=-1)[:, None],
        modulation,
        ada_bfull.astype(jnp.float32)[None],
        (
            joined_bias.astype(jnp.float32)[None],
            out_bias_f[None, :width],
            up_bfull.astype(jnp.float32).reshape(4, 1, -1),
        ),
        (joined_whole, up_start, down_start),
    )
    wholes = [whole.reshape(4, width, width) for whole in (joined_whole, up_whole, down_whole)]
    (
        _,
        _,
        _,
        mixed,
        tokens_grad,
        slot_sums,
        branch_sums,
        pre_sums,
        joined_sums,
        down_total,
        up_weight_grad,
        joined_total,
    ) = backward(
        (hidden, before, joined, *wholes, normed_t, attended_t, start),
        (middle, grad_out, branch1, normed2_t, stats),
        segment,
        table,
        out_bias_f[None, width:],
    )
    half = down_total.shape[1] // 2
    cut = down_total.reshape(-1, 2, half).transpose(1, 0, 2)
    mine, theirs = pick(cut, core), pick(cut, 1 - core)
    arrived = swap(theirs, "core")
    down_weight_grad = jnp.where(
        core == 0, jnp.concatenate([mine, arrived]), jnp.concatenate([arrived, mine])
    ).T
    group_grad = jnp.concatenate(
        [slot_sums[part] for part in (4, 5, 0, 1, 2, 3)], axis=1
    )
    modulation_grad = jnp.stack(
        [
            sum(
                jnp.where(group_slots[group] == slot, group_grad[group], 0.0)
                for group in range(rows // 128)
            )
            for slot in range(slot_count)
        ]
    ).astype(jnp.bfloat16)
    joined_sums = joined_sums[0]
    terms = (
        jnp.concatenate([joined_sums[:width], joined_sums[2 * width :]]),
        branch_sums[:2].reshape(-1),
        pre_sums[:4].reshape(-1),
    )
    ada_weight_grad, ada_bias_grad, silu_grad, bias_grads = modulation_back(
        modulation_grad, silu_part, ada_weight, terms
    )
    attn_bias_grad, out_bias_grad, up_bias_grad = bias_grads
    return (
        mixed,
        tokens_grad,
        silu_back(silu_grad)[0],
        ada_weight_grad,
        ada_bias_grad,
        joined_total[:, :columns],
        attn_bias_grad,
        joined_total[:, columns:],
        out_bias_grad,
        up_weight_grad,
        up_bias_grad,
        down_weight_grad,
    )


def per_device(
    tokens,
    condition,
    kept_index,
    segment,
    grid_side,
    ada_weight,
    ada_bias,
    attn_weight,
    attn_bias,
    proj_weight,
    out_bias,
    up_weight,
    up_bias,
    down_weight,
    grad_out,
):
    if on_box():
        return box_device(
            tokens,
            condition,
            kept_index,
            segment,
            grid_side,
            ada_weight,
            ada_bias,
            attn_weight,
            attn_bias,
            proj_weight,
            out_bias,
            up_weight,
            up_bias,
            down_weight,
            grad_out,
        )
    model_width = tokens.shape[1]
    slot_count = condition.shape[0]
    planes = lax.axis_size("dp")
    joined_w, up_w, down_w = gather_blocks(attn_weight, proj_weight, up_weight, down_weight)
    attn_columns = attn_weight.shape[1]
    slot_ids = jnp.arange(slot_count, dtype=jnp.int32)
    same_slot = segment[:, None] == slot_ids[None, :]
    slot_table = same_slot.astype(jnp.float32)
    side_rows = jnp.sum(jnp.where(same_slot, grid_side[None, :], 0), axis=1)
    start = tokens.astype(jnp.float32) + position_code(kept_index, side_rows, model_width)
    condition_f = condition.astype(jnp.float32)
    silu_cond, silu_back = jax.vjp(jax.nn.silu, condition_f)
    silu_bf = silu_cond.astype(jnp.bfloat16)
    silu_all, (ada_bfull, attn_bfull, out_bfull, up_bfull) = gather_small(
        silu_bf, (ada_bias, attn_bias, out_bias, up_bias)
    )
    modulation, silu_part = modulate_slots(silu_all, ada_weight, ada_bfull)
    mod_rows = jnp.dot(
        slot_table, modulation, precision=lax.Precision.HIGHEST, preferred_element_type=jnp.float32
    )
    shift_one, scale_one, gate_one, shift_two, scale_two, gate_two = jnp.split(mod_rows, 6, axis=1)
    normed1, norm1_back = jax.vjp(norm_modulate, start, shift_one, scale_one)
    normed1_bf = normed1.astype(jnp.bfloat16)
    projected = jnp.concatenate(
        [
            jnp.dot(normed1_bf, joined_w[part, :, :attn_columns], preferred_element_type=jnp.float32)
            for part in range(planes)
        ],
        axis=1,
    )
    proj_full = joined_w[:, :, attn_columns:].transpose(1, 0, 2).reshape(model_width, model_width)
    attn_bias_f = attn_bfull.astype(jnp.float32)
    query_bf = (projected[:, :model_width] + attn_bias_f[:model_width]).astype(jnp.bfloat16)
    key_bf = projected[:, model_width : 2 * model_width].astype(jnp.bfloat16)
    value_bf = (projected[:, 2 * model_width :] + attn_bias_f[model_width:]).astype(jnp.bfloat16)
    attended, log_totals = attend_forward(query_bf, key_bf, value_bf, segment, HEADS)
    attended_bf = attended.astype(jnp.bfloat16)
    out_bias_f = out_bfull.astype(jnp.float32)
    branch1 = (
        jnp.dot(attended_bf, proj_full, preferred_element_type=jnp.float32)
        + out_bias_f[:model_width]
    )
    middle = start + gate_one * branch1
    normed2, norm2_back = jax.vjp(norm_modulate, middle, shift_two, scale_two)
    normed2_bf = normed2.astype(jnp.bfloat16)
    hidden_parts, gelu_parts = [], []
    up_bias_f = up_bfull.astype(jnp.float32).reshape(planes, -1)
    branch2 = out_bias_f[model_width:]
    for part in range(planes):
        hidden_pre = (
            jnp.dot(normed2_bf, up_w[part], preferred_element_type=jnp.float32) + up_bias_f[part]
        )
        hidden_act, gelu_back = jax.vjp(partial(jax.nn.gelu, approximate=True), hidden_pre)
        hidden_parts.append(hidden_act.astype(jnp.bfloat16))
        gelu_parts.append(gelu_back)
        branch2 = branch2 + matmul_nt(hidden_parts[part], down_w[part])
    mixed = (middle + gate_two * branch2).astype(jnp.bfloat16)
    out_grad = grad_out.astype(jnp.float32)
    grad_gate_two = out_grad * branch2
    grad_branch2 = (out_grad * gate_two).astype(jnp.bfloat16)
    down_weight_grad = scatter_whole(matmul_tn(jnp.concatenate(hidden_parts, axis=1), grad_branch2))
    pre_parts = []
    for part in range(planes):
        hidden_grad = jnp.dot(grad_branch2, down_w[part], preferred_element_type=jnp.float32)
        pre_parts.append(gelu_parts[part](hidden_grad)[0].astype(jnp.bfloat16))
    pre_grad = jnp.stack(pre_parts)
    (up_weight_grad,) = scatter_rows([(normed2_bf, pre_grad)])
    up_bias_term = jnp.sum(pre_grad, axis=1, dtype=jnp.float32).reshape(-1)
    normed2_grad = sum(matmul_nt(pre_parts[part], up_w[part]) for part in range(planes))
    middle_part, grad_shift_two, grad_scale_two = norm2_back(normed2_grad)
    middle_grad = out_grad + middle_part
    grad_gate_one = middle_grad * branch1
    grad_branch1 = (middle_grad * gate_one).astype(jnp.bfloat16)
    attended_grad = matmul_nt(grad_branch1, proj_full).astype(jnp.bfloat16)
    query_grad, key_grad, value_grad = attend_backward(
        query_bf, key_bf, value_bf, attended_grad, segment, log_totals, HEADS
    )
    query_grad_bf = query_grad.astype(jnp.bfloat16)
    value_grad_bf = value_grad.astype(jnp.bfloat16)
    joined_grad = jnp.concatenate(
        [query_grad_bf, key_grad.astype(jnp.bfloat16), value_grad_bf], axis=1
    )
    joined_parts = by_columns(joined_grad, planes)
    attn_weight_grad, proj_weight_grad = scatter_rows(
        [(normed1_bf, joined_parts), (attended_bf, by_columns(grad_branch1, planes))]
    )
    attn_bias_term = jnp.concatenate(
        [
            jnp.sum(query_grad_bf, axis=0, dtype=jnp.float32),
            jnp.sum(value_grad_bf, axis=0, dtype=jnp.float32),
        ]
    )
    normed1_grad = sum(
        matmul_nt(joined_parts[part], joined_w[part, :, :attn_columns]) for part in range(planes)
    )
    start_part, grad_shift_one, grad_scale_one = norm1_back(normed1_grad)
    tokens_grad = middle_grad + start_part
    mod_rows_grad = jnp.concatenate(
        [
            grad_shift_one,
            grad_scale_one,
            grad_gate_one,
            grad_shift_two,
            grad_scale_two,
            grad_gate_two,
        ],
        axis=1,
    )
    modulation_grad = lax.dot_general(
        slot_table,
        mod_rows_grad,
        (((0,), (0,)), ((), ())),
        precision=lax.Precision.HIGHEST,
        preferred_element_type=jnp.float32,
    ).astype(jnp.bfloat16)
    out_bias_term = jnp.concatenate(
        [
            jnp.sum(grad_branch1, axis=0, dtype=jnp.float32),
            jnp.sum(grad_branch2, axis=0, dtype=jnp.float32),
        ]
    )
    ada_weight_grad, ada_bias_grad, silu_grad, bias_grads = modulation_back(
        modulation_grad, silu_part, ada_weight, (attn_bias_term, out_bias_term, up_bias_term)
    )
    attn_bias_grad, out_bias_grad, up_bias_grad = bias_grads
    condition_grad = silu_back(silu_grad)[0]
    return (
        mixed,
        tokens_grad,
        condition_grad,
        ada_weight_grad,
        ada_bias_grad,
        attn_weight_grad,
        attn_bias_grad,
        proj_weight_grad,
        out_bias_grad,
        up_weight_grad,
        up_bias_grad,
        down_weight_grad,
    )


def solution(mesh):
    return jax.shard_map(
        per_device,
        mesh=mesh,
        in_specs=(
            P(("dp", "fsdp"), None),
            P(("dp", "fsdp"), None),
            P(("dp", "fsdp")),
            P(("dp", "fsdp")),
            P(("dp", "fsdp")),
            P("fsdp", "dp"),
            P(("dp", "fsdp")),
            P("fsdp", "dp"),
            P(("dp", "fsdp")),
            P("fsdp", "dp"),
            P(("dp", "fsdp")),
            P("fsdp", "dp"),
            P(("dp", "fsdp")),
            P("fsdp", "dp"),
            P(("dp", "fsdp"), None),
        ),
        out_specs=(
            P(("dp", "fsdp"), None),
            P(("dp", "fsdp"), None),
            P(("dp", "fsdp"), None),
            P("fsdp", "dp"),
            P(("dp", "fsdp")),
            P("fsdp", "dp"),
            P(("dp", "fsdp")),
            P("fsdp", "dp"),
            P(("dp", "fsdp")),
            P("fsdp", "dp"),
            P(("dp", "fsdp")),
            P("fsdp", "dp"),
        ),
        check_vma=False,
    )
```

```python
from functools import partial
import math

import jax
import jax.numpy as jnp
from jax import lax
from jax.experimental import pallas as pl
from jax.experimental.pallas import tpu as pltpu
from jax.sharding import PartitionSpec as P

HEADS = 16
AXES = ("dp", "fsdp")


def position_code(kept_index, side_rows, model_width):
    quarter = model_width // 4
    exponent = jnp.arange(quarter, dtype=jnp.float32) / quarter
    frequency = 1.0 / 10000.0**exponent
    column = (kept_index % side_rows).astype(jnp.float32)[:, None] * frequency[None, :]
    line_pos = (kept_index // side_rows).astype(jnp.float32)[:, None] * frequency[None, :]
    return jnp.concatenate(
        [jnp.sin(column), jnp.cos(column), jnp.sin(line_pos), jnp.cos(line_pos)], axis=1
    )


def layer_norm(values):
    center = values - jnp.mean(values, axis=-1, keepdims=True)
    return center * lax.rsqrt(jnp.mean(center * center, axis=-1, keepdims=True) + 1e-06)


def norm_modulate(values, shift_rows, scale_rows):
    return layer_norm(values) * (1.0 + scale_rows) + shift_rows


def matmul_nt(first_matrix, second_matrix):
    return lax.dot_general(
        first_matrix, second_matrix, (((1,), (1,)), ((), ())), preferred_element_type=jnp.float32
    )


def matmul_tn(first_matrix, second_matrix):
    return lax.dot_general(
        first_matrix, second_matrix, (((0,), (0,)), ((), ())), preferred_element_type=jnp.float32
    )


def attend_forward(query_bf, key_bf, value_bf, segment, head_count):
    row_count, model_width = query_bf.shape
    head_size = model_width // head_count
    block_rows = min(row_count, 512)
    block_count = row_count // block_rows
    score_scale = 1.0 / math.sqrt(head_size)
    key_heads = key_bf.reshape(row_count, head_count, head_size)
    value_heads = value_bf.reshape(row_count, head_count, head_size)

    def forward_block(block_index):
        query_rows = query_bf.reshape(block_rows, head_count, head_size)
        same_image = segment[:, None] == segment[None, :]
        scores = (
            jnp.einsum("qhd,khd->hqk", query_rows, key_heads, preferred_element_type=jnp.float32)
            * score_scale
        )
        scores = jnp.where(same_image[None], scores, -1e30)
        highest = jnp.max(scores, axis=2, keepdims=True)
        powers = jnp.exp(scores - highest)
        totals = jnp.sum(powers, axis=2, keepdims=True)
        probs_bf = (powers / totals).astype(jnp.bfloat16)
        attended = jnp.einsum(
            "hqk,khd->qhd", probs_bf, value_heads, preferred_element_type=jnp.float32
        )
        return (attended.reshape(block_rows, model_width), (highest + jnp.log(totals))[:, :, 0])

    attended, log_totals = lax.map(forward_block, jnp.arange(block_count, dtype=jnp.int32))
    return (attended.reshape(row_count, model_width), log_totals)


def attend_backward(query_bf, key_bf, value_bf, attended_grad, segment, log_totals, head_count):
    row_count, model_width = query_bf.shape
    head_size = model_width // head_count
    block_rows = min(row_count, 512)
    block_count = row_count // block_rows
    score_scale = 1.0 / math.sqrt(head_size)
    key_heads = key_bf.reshape(row_count, head_count, head_size)
    value_heads = value_bf.reshape(row_count, head_count, head_size)

    def backward_block(running, pieces):
        key_sum, value_sum = running
        block_index, log_rows = pieces
        query_rows = query_bf.reshape(block_rows, head_count, head_size)
        grad_rows = attended_grad.reshape(block_rows, head_count, head_size)
        same_image = segment[:, None] == segment[None, :]
        scores = (
            jnp.einsum("qhd,khd->hqk", query_rows, key_heads, preferred_element_type=jnp.float32)
            * score_scale
        )
        scores = jnp.where(same_image[None], scores, -1e30)
        probs = jnp.exp(scores - log_rows[:, :, None])
        probs_bf = probs.astype(jnp.bfloat16)
        prob_grad = jnp.einsum(
            "qhd,khd->hqk", grad_rows, value_heads, preferred_element_type=jnp.float32
        )
        row_inner = jnp.sum(probs * prob_grad, axis=2, keepdims=True)
        score_grad = (probs * (prob_grad - row_inner)).astype(jnp.bfloat16)
        query_grad = (
            jnp.einsum("hqk,khd->qhd", score_grad, key_heads, preferred_element_type=jnp.float32)
            * score_scale
        )
        key_sum = (
            key_sum
            + jnp.einsum("hqk,qhd->khd", score_grad, query_rows, preferred_element_type=jnp.float32)
            * score_scale
        )
        value_sum = value_sum + jnp.einsum(
            "hqk,qhd->khd", probs_bf, grad_rows, preferred_element_type=jnp.float32
        )
        return ((key_sum, value_sum), query_grad.reshape(block_rows, model_width))

    empty_sum = jnp.zeros((row_count, head_count, head_size), jnp.float32)
    sums, query_grad = lax.scan(
        backward_block,
        (empty_sum, empty_sum),
        (jnp.arange(block_count, dtype=jnp.int32), log_totals),
    )
    return (
        query_grad.reshape(row_count, model_width),
        sums[0].reshape(row_count, model_width),
        sums[1].reshape(row_count, model_width),
    )


def on_box():
    return lax.axis_size("dp") == 4 and lax.axis_size("fsdp") == 8


def neighbour(index, axis):
    plane, line = index // 8, index % 8
    if axis == "x":
        plane ^= 1
    elif axis == "y":
        plane ^= 2
    elif axis == "core":
        line ^= 1
    else:
        line = (line - 2 * axis) % 8
    return plane * 8 + line


def swap(values, axis):
    return lax.ppermute(values, AXES, [(index, neighbour(index, axis)) for index in range(32)])


HALF_ORDERS = (("x", 1, "y", 2), ("y", 2, "x", 1))


def place():
    plane, line = lax.axis_index("dp"), lax.axis_index("fsdp")
    return plane, line // 2, line % 2


def flipped(plane, flip):
    if flip % 2:
        plane = plane + 1 - 2 * (plane % 2)
    if flip // 2:
        plane = plane + 2 - 4 * (plane // 2)
    return plane


def pick(values, index):
    return lax.dynamic_index_in_dim(values, index, axis=0, keepdims=False)


def gather_blocks(attn_weight, proj_weight, up_weight, down_weight):
    parts = lax.axis_size("dp")
    attn, proj, up, down = [
        lax.all_gather(lax.all_gather(weight, "dp", axis=1, tiled=True), "fsdp", axis=0, tiled=True)
        for weight in (attn_weight, proj_weight, up_weight, down_weight)
    ]
    width = attn.shape[0]

    def by_block(weight):
        return weight.reshape(weight.shape[0], parts, -1).transpose(1, 0, 2)

    joined = jnp.concatenate([by_block(attn), by_block(proj)], axis=2)
    return joined, by_block(up), by_block(down.T.reshape(width, -1))


def scatter_whole(gradient):
    part = lax.psum_scatter(
        gradient.astype(jnp.bfloat16), "dp", scatter_dimension=1, tiled=True
    ).astype(jnp.float32)
    return lax.psum_scatter(part, "fsdp", scatter_dimension=0, tiled=True)


def scatter_rows(pairs):
    return [
        scatter_whole(matmul_tn(left, right.transpose(1, 0, 2).reshape(left.shape[0], -1)))
        for left, right in pairs
    ]


def trade(one_for_all, values, out, send_sems, recv_sems):
    planes, lines = lax.axis_size("dp"), lax.axis_size("fsdp")
    count = planes * lines
    me = lax.axis_index("dp") * lines + lax.axis_index("fsdp")

    def device(index):
        return (index // lines, index % lines)

    def chunk(index):
        return values if one_for_all else values.at[index]

    barrier = pltpu.get_barrier_semaphore()

    @pl.loop(1, count)
    def _(step):
        pl.semaphore_signal(
            barrier,
            inc=1,
            device_id=device((me + step) % count),
            device_id_type=pl.DeviceIdType.MESH,
        )

    pl.semaphore_wait(barrier, count - 1)

    @pl.loop(1, count)
    def _(step):
        peer = (me + step) % count
        pltpu.make_async_remote_copy(
            src_ref=chunk(peer),
            dst_ref=out.at[me],
            send_sem=send_sems.at[step],
            recv_sem=recv_sems.at[step],
            device_id=device(peer),
            device_id_type=pl.DeviceIdType.MESH,
        ).start()

    if one_for_all:
        out[me] = values[...]
    else:
        out[me] = values[me]

    @pl.loop(1, count)
    def _(step):
        peer = (me + step) % count
        copy = pltpu.make_async_remote_copy(
            src_ref=chunk(peer),
            dst_ref=out.at[(me + count - step) % count],
            send_sem=send_sems.at[step],
            recv_sem=recv_sems.at[step],
            device_id=device(peer),
            device_id_type=pl.DeviceIdType.MESH,
        )
        copy.wait()


def exchange(values, collective_id, one_for_all=False):
    count = lax.axis_size("dp") * lax.axis_size("fsdp")
    chunk = values.shape[-2:]
    size = count * chunk[0] * chunk[1] * values.dtype.itemsize
    return pl.pallas_call(
        partial(trade, one_for_all),
        out_shape=jax.ShapeDtypeStruct((count,) + chunk, values.dtype),
        in_specs=[pl.BlockSpec(memory_space=pltpu.VMEM)],
        out_specs=pl.BlockSpec(memory_space=pltpu.VMEM),
        scratch_shapes=[pltpu.SemaphoreType.DMA((count,)), pltpu.SemaphoreType.DMA((count,))],
        compiler_params=pltpu.CompilerParams(
            collective_id=collective_id,
            has_side_effects=True,
            vmem_limit_bytes=3 * size + 4 * 2**20,
        ),
        cost_estimate=pl.CostEstimate(flops=0, bytes_accessed=8 * size, transcendentals=0),
    )(values)


def gather_small(silu_bf, vectors):
    flat = jnp.concatenate([silu_bf.reshape(-1), *vectors])
    width = -(-flat.shape[0] // 2048) * 128
    flat = jnp.pad(flat, (0, 16 * width - flat.shape[0])).reshape(16, width)
    everyone = exchange(flat, 0, one_for_all=True)
    everyone = everyone.reshape(everyone.shape[0], -1)
    begin = silu_bf.size
    silu_all = everyone[:, :begin].reshape(-1, silu_bf.shape[1])
    found = []
    for vector in vectors:
        found.append(everyone[:, begin : begin + vector.shape[0]].reshape(-1))
        begin += vector.shape[0]
    return silu_all, found


def silu_columns(silu_all, ada_weight):
    rows = ada_weight.shape[0]
    return lax.dynamic_slice_in_dim(silu_all, lax.axis_index("fsdp") * rows, rows, axis=1)


def modulate_slots(silu_all, ada_weight, ada_bias):
    planes, lines = lax.axis_size("dp"), lax.axis_size("fsdp")
    columns = ada_weight.shape[1]
    slots = silu_all.shape[0] // (planes * lines)
    silu_part = silu_columns(silu_all, ada_weight)
    term = jnp.dot(silu_part, ada_weight, preferred_element_type=jnp.float32)
    term = exchange(term.reshape(planes * lines, slots, columns), 1)
    term = jnp.sum(term.reshape(planes, lines, slots, columns), axis=1)
    modulation = term.transpose(1, 0, 2).reshape(slots, planes * columns)
    return modulation + ada_bias.astype(jnp.float32), silu_part


def modulation_back(modulation_grad, silu_part, ada_weight, terms):
    planes, lines = lax.axis_size("dp"), lax.axis_size("fsdp")
    devices = planes * lines
    slots = modulation_grad.shape[0]
    rows, columns = ada_weight.shape
    cut = modulation_grad.reshape(slots, planes, columns).transpose(1, 0, 2)
    cut = cut.reshape(planes, 1, 16, slots * columns // 16)
    cut = jnp.broadcast_to(cut, (planes, lines) + cut.shape[2:])
    cut = exchange(cut.reshape((devices,) + cut.shape[2:]), 2)
    return modulation_ends(cut.reshape(devices * slots, columns), silu_part, ada_weight, terms)


def modulation_ends(cut, silu_part, ada_weight, terms):
    planes, lines = lax.axis_size("dp"), lax.axis_size("fsdp")
    devices = planes * lines
    rows, columns = ada_weight.shape
    slots = cut.shape[0] // devices
    ada_grad = matmul_tn(silu_part, cut)
    sums = jnp.sum(cut, axis=0, dtype=jnp.float32)
    bias_width = columns // lines
    ada_bias_grad = lax.dynamic_slice_in_dim(sums, lax.axis_index("fsdp") * bias_width, bias_width)
    silu_grad = matmul_nt(cut, ada_weight).reshape(devices, slots * rows)
    flat = jnp.concatenate([silu_grad] + [term.reshape(devices, -1) for term in terms], axis=1)
    width = -(-flat.shape[1] // 1024) * 128
    flat = jnp.pad(flat, ((0, 0), (0, 8 * width - flat.shape[1])))
    flat = exchange(flat.reshape(devices, 8, width), 3).reshape(devices, -1)
    shared = jnp.sum(flat[:, slots * rows :], axis=0)
    silu_grad = flat[:, : slots * rows].reshape(planes, lines, slots, rows).sum(axis=0)
    silu_grad = silu_grad.transpose(1, 0, 2).reshape(slots, lines * rows)
    found, begin = [], 0
    for term in terms:
        found.append(shared[begin : begin + term.shape[0] // devices])
        begin += term.shape[0] // devices
    return ada_grad, ada_bias_grad, silu_grad, found


def by_columns(values, parts):
    rows, columns = values.shape
    return values.reshape(rows, parts, columns // parts).transpose(1, 0, 2)


SLOPE = math.sqrt(2.0 / math.pi)
WINDOW = 512


def mm(left, right):
    return jnp.dot(left, right, preferred_element_type=jnp.float32)


def shaped(dims, kind=jnp.float32):
    return jax.ShapeDtypeStruct(dims, kind)


def by_rows(count, step, body):
    @pl.loop(0, count // step)
    def _(index):
        body(pl.ds(pl.multiple_of(index * step, step), step))


def by_groups(count, step, body):
    @pl.loop(0, count // step)
    def _(index):
        body(pl.ds(pl.multiple_of(index * step, step), step), index * step // 128)


def lane_index(rows, lanes):
    return lax.broadcasted_iota(jnp.int32, (rows, lanes), 1)


def window_of(block, width, total, span):
    begin = min(block * width // 128 * 128, total - span)
    return begin, block * width - begin


def group_row(table, group, column, width):
    return table[pl.ds(group, 1), column * width : (column + 1) * width]


def add_group(out, group, value):
    out[pl.ds(group, 1), :] += jnp.sum(value, axis=0, keepdims=True)


def centred(value):
    center = value - jnp.mean(value, axis=-1, keepdims=True)
    scale = lax.rsqrt(jnp.mean(center * center, axis=-1, keepdims=True) + 1e-06)
    return center * scale, scale


def norm_back(normed, scale, grad):
    return scale * (
        grad
        - jnp.mean(grad, axis=-1, keepdims=True)
        - normed * jnp.mean(grad * normed, axis=-1, keepdims=True)
    )


def head_window(head, size, total):
    begin = jnp.minimum(head * size // 128 * 128, total - 256)
    begin = pl.multiple_of(begin, 128)
    lane = lane_index(1, 256)
    offset = head * size - begin
    return begin, (lane >= offset) & (lane < offset + size)


def far_device(plane, depth, core):
    return (plane, depth * 2 + core)


class Gather:
    def __init__(self, shards, wholes, send_sems, recv_sems, local_sems):
        self.shards, self.wholes = shards, wholes
        self.send_sems, self.recv_sems, self.local_sems = send_sems, recv_sems, local_sems
        self.plane, self.depth, self.core = place()
        self.started = []
        self.kept = []
        self.counts = [0, 0, 0]

    def partners(self):
        return [
            far_device(flipped(self.plane, 1), self.depth, self.core),
            far_device(flipped(self.plane, 2), self.depth, self.core),
            far_device(self.plane, self.depth, 1 - self.core),
        ]

    def back(self, entry):
        low, high = (3 - self.depth) // 3, self.depth // 3
        return (0, 1 + 2 * low, 3 - low - high, 2 - low + high)[entry]

    def spot(self, weight, flip, back, other=False):
        plane, depth = flipped(self.plane, flip), (self.depth + 4 - back) % 4
        core = 1 - self.core if other else self.core
        if weight < 2:
            return self.wholes[weight].at[plane, depth, core]
        return self.wholes[weight].at[depth, plane, core]

    def send(self, weight, source, target, partner, kind, entry):
        copy = pltpu.make_async_remote_copy(
            src_ref=source,
            dst_ref=target,
            send_sem=self.send_sems.at[weight, self.counts[weight]],
            recv_sem=self.recv_sems.at[weight, kind, entry],
            device_id=partner,
            device_id_type=pl.DeviceIdType.MESH,
        )
        self.counts[weight] += 1
        copy.start()
        self.started.append(copy)

    def arrive(self, weight, region, kind, entry):
        pltpu.make_async_remote_copy(
            src_ref=region,
            dst_ref=region,
            send_sem=self.send_sems.at[weight, 0],
            recv_sem=self.recv_sems.at[weight, kind, entry],
            device_id=self.partners()[2],
            device_id_type=pl.DeviceIdType.MESH,
        ).wait_recv()

    def pass_on(self, weight, source, flip, entry):
        back = self.back(entry)
        target = self.spot(weight, flip, back)
        beside = self.partners()
        if flip == 0 or (flip == 2 and entry % 2 == 1):
            self.send(weight, source, target, beside[0], 1 if flip == 0 else 3, back)
        if flip == 0 or (flip == 1 and entry % 2 == 0):
            self.send(weight, source, target, beside[1], 2 if flip == 0 else 3, back)
        self.send(weight, source, target, beside[2], 4 + flip, back)

    def keep(self, weight):
        keep = pltpu.make_async_copy(
            self.shards[weight], self.spot(weight, 0, 0), self.local_sems.at[weight]
        )
        keep.start()
        self.kept.append(keep)

    def open_plane(self, weight, entry):
        self.pass_on(weight, self.spot(weight, 0, self.back(entry)), 0, entry)

    def along(self, weight, source, back, step, number, start):
        beyond = self.depth + step

        @pl.when((beyond >= 0) & (beyond <= 3))
        def _():
            copy = pltpu.make_async_remote_copy(
                src_ref=source,
                dst_ref=self.spot(weight, 0, back),
                send_sem=self.send_sems.at[weight, number],
                recv_sem=self.recv_sems.at[weight, 0, (back + step + 4) % 4],
                device_id=far_device(self.plane, (beyond + 4) % 4, self.core),
                device_id_type=pl.DeviceIdType.MESH,
            )
            if start:
                copy.start()
            else:
                copy.wait_send()

    def line_sends(self, weight, entry, start):
        back = self.back(entry)
        if entry == 0:
            for number, step in enumerate((1, -1)):
                self.along(weight, self.spot(weight, 0, 0), 0, step, 32 + number, start)
        else:
            step = 2 * ((self.depth - back + 4) // 4) - 1
            self.along(weight, self.spot(weight, 0, back), back, step, 33 + entry, start)

    def open_line(self, weight):
        self.line_sends(weight, 0, True)

    def line_partners(self):
        return [far_device(self.plane, (self.depth + d) % 4, self.core) for d in (1, 2, 3)]

    def on_line(self, weight, entry):
        region = self.spot(weight, 0, self.back(entry))
        self.arrive(weight, region, 0, self.back(entry))
        self.line_sends(weight, entry, True)

    def on_plane(self, weight, flip, entry):
        back = self.back(entry)
        region = self.spot(weight, flip, back)
        self.arrive(weight, region, flip, back)
        self.pass_on(weight, region, flip, entry)

    def plane_steps(self, weight):
        found = []
        for entry in range(4):
            found.append(partial(self.on_plane, weight, 1, entry))
            found.append(partial(self.on_plane, weight, 2, entry))
            if entry:
                found.append(partial(self.on_plane, weight, 3, entry - 1))
        found.append(partial(self.on_plane, weight, 3, 3))
        return found

    def ready(self, weight, entries=(0, 1, 2, 3)):
        for flip in range(4):
            for back in [self.back(entry) for entry in entries]:
                self.arrive(weight, self.spot(weight, flip, back, True), 4 + flip, back)

    def finish(self):
        for copy in self.started:
            copy.wait_send()


def greet(partners):
    barrier = pltpu.get_barrier_semaphore()
    for partner in partners:
        pl.semaphore_signal(
            barrier, inc=1, device_id=partner, device_id_type=pl.DeviceIdType.MESH
        )
    pl.semaphore_wait(barrier, len(partners))


def trade_along(axis, values, land, send_sems, recv_sems, start, same=False):
    count, me = lax.axis_size(axis), lax.axis_index(axis)

    @pl.loop(1, count)
    def _(step):
        peer = (me + step) % count
        target = me if start else (me + count - step) % count
        if axis == "dp":
            device = (peer, lax.axis_index("fsdp"))
        else:
            device = (lax.axis_index("dp"), peer)
        copy = pltpu.make_async_remote_copy(
            src_ref=values if same else values.at[peer],
            dst_ref=land.at[target],
            send_sem=send_sems.at[step],
            recv_sem=recv_sems.at[step],
            device_id=device,
            device_id_type=pl.DeviceIdType.MESH,
        )
        if start:
            copy.start()
        else:
            copy.wait()

    if start:
        land[me] = values[...] if same else values[me]


def greet_all():
    planes, lines = lax.axis_size("dp"), lax.axis_size("fsdp")
    count = planes * lines
    me = lax.axis_index("dp") * lines + lax.axis_index("fsdp")
    barrier = pltpu.get_barrier_semaphore()

    @pl.loop(1, count)
    def _(step):
        peer = (me + step) % count
        pl.semaphore_signal(
            barrier,
            inc=1,
            device_id=(peer // lines, peer % lines),
            device_id_type=pl.DeviceIdType.MESH,
        )

    pl.semaphore_wait(barrier, count - 1)


def spread(axis_peer, values, land, send_sems, recv_sems, start):
    planes, lines = lax.axis_size("dp"), lax.axis_size("fsdp")
    count = planes * lines
    me = lax.axis_index("dp") * lines + lax.axis_index("fsdp")

    @pl.loop(1, count)
    def _(step):
        peer = (me + step) % count
        target = me if start else (me + count - step) % count
        copy = pltpu.make_async_remote_copy(
            src_ref=values.at[peer % lines] if axis_peer else values,
            dst_ref=land.at[target],
            send_sem=send_sems.at[step],
            recv_sem=recv_sems.at[step],
            device_id=(peer // lines, peer % lines),
            device_id_type=pl.DeviceIdType.MESH,
        )
        if start:
            copy.start()
        else:
            copy.wait()

    if start:
        land[me] = values[me % lines] if axis_peer else values[...]


def opening_kernel(
    silu,
    flat,
    ada_weight,
    joined_shard,
    up_shard,
    down_shard,
    joined_whole,
    up_whole,
    down_whole,
    silu_land,
    flat_land,
    plane_land,
    product,
    term,
    term_land,
    plane_term,
    send_sems,
    recv_sems,
    local_sems,
    spread_sems,
    line_sems,
    plane_sems,
):
    gather = Gather(
        (joined_shard, up_shard, down_shard),
        (joined_whole, up_whole, down_whole),
        send_sems,
        recv_sems,
        local_sems,
    )
    for weight in range(3):
        gather.keep(weight)
    greet_all()
    silu_trade = (True, silu, silu_land, spread_sems.at[0], spread_sems.at[1])
    flat_trade = (False, flat, flat_land, spread_sems.at[2], spread_sems.at[3])
    line_trade = (term, term_land, line_sems.at[0], line_sems.at[1])
    plane_trade = (plane_term, plane_land, plane_sems.at[0], plane_sems.at[1])
    spread(*silu_trade, True)
    for copy in gather.kept:
        copy.wait()
    gather.open_line(0)
    gather.open_plane(0, 0)
    spread(*flat_trade, True)
    for entry in (1, 2, 3):
        gather.on_line(0, entry)
        gather.open_plane(0, entry)
    gather.open_line(1)
    gather.open_plane(1, 0)
    spread(*silu_trade, False)
    devices, tall, rows = silu_land.shape
    product[...] = mm(silu_land[...].reshape(devices * tall, rows), ada_weight[...])
    lines, planes, slots = term.shape[:3]
    for line in range(lines):
        for plane in range(planes):
            begin = (plane * lines + line) * tall
            term[line, plane] = product[begin : begin + slots, :]
    trade_along("fsdp", *line_trade, True)
    first, second = gather.plane_steps(0), gather.plane_steps(1)
    for step in first[:2]:
        step()
    gather.on_line(1, 1)
    for step in first[2:5]:
        step()
    gather.on_line(1, 2)
    gather.open_plane(1, 1)
    trade_along("fsdp", *line_trade, False)
    total = term_land[0]
    for line in range(1, lines):
        total = total + term_land[line]
    plane_term[...] = total
    trade_along("dp", *plane_trade, True)
    for step in first[5:8]:
        step()
    gather.on_line(1, 3)
    for step in first[8:] + second[:5]:
        step()
    gather.on_plane(1, 3, 1)
    spread(*flat_trade, False)
    trade_along("dp", *plane_trade, False)
    gather.ready(0)
    gather.ready(1, (0, 1))
    gather.finish()
    for weight in range(2):
        for entry in range(4):
            gather.line_sends(weight, entry, False)


def opening(silu, flat, ada_weight, shards):
    rows, width = shards[1].shape
    lines, tall, short = silu.shape
    slots, part = 4, ada_weight.shape[1]
    whole = shaped((4, 4, 2, rows, width), jnp.bfloat16)
    vmem, away = pl.BlockSpec(memory_space=pltpu.VMEM), pl.BlockSpec(memory_space=pl.ANY)
    return pl.pallas_call(
        opening_kernel,
        out_shape=[
            whole,
            whole,
            whole,
            shaped((4 * lines, tall, short), jnp.bfloat16),
            shaped((4 * lines,) + flat.shape, jnp.bfloat16),
            shaped((4, slots, part)),
        ],
        in_specs=[vmem] * 6,
        out_specs=[away] * 3 + [vmem] * 3,
        scratch_shapes=[
            pltpu.VMEM((4 * lines * tall, part), jnp.float32),
            pltpu.VMEM((lines, 4, slots, part), jnp.float32),
            pltpu.VMEM((lines, 4, slots, part), jnp.float32),
            pltpu.VMEM((4, slots, part), jnp.float32),
            pltpu.SemaphoreType.DMA((3, 40)),
            pltpu.SemaphoreType.DMA((3, 8, 4)),
            pltpu.SemaphoreType.DMA((3,)),
            pltpu.SemaphoreType.DMA((4, 32)),
            pltpu.SemaphoreType.DMA((2, 8)),
            pltpu.SemaphoreType.DMA((2, 4)),
        ],
        compiler_params=pltpu.CompilerParams(
            collective_id=7, has_side_effects=True, vmem_limit_bytes=32 * 2**20
        ),
        cost_estimate=pl.CostEstimate(flops=10**8, bytes_accessed=10**8, transcendentals=0),
    )(silu, flat, ada_weight, *shards)


def forward_kernel(
    tokens,
    places,
    codes,
    slots,
    slot_line,
    group_slots,
    plane_land,
    ada_bias,
    joined_bias,
    out_bias,
    up_bias,
    joined_whole,
    up_start,
    down_start,
    up_whole,
    down_whole,
    joined,
    start,
    table,
    normed_t,
    attended_t,
    normed2_t,
    stats,
    branch,
    middle,
    hidden,
    before,
    room,
    product,
    wide_room,
    bar,
    before_room,
    normed,
    attended,
    normed2,
    strip,
    all_modulation,
    send_sems,
    recv_sems,
    load_sems,
    store_sems,
):
    gather = Gather(
        (None, None, None), (None, up_whole, down_whole), send_sems, recv_sems, None
    )
    loads = [
        pltpu.make_async_copy(joined_whole.at[block], room.at[block], load_sems.at[block])
        for block in range(4)
    ]
    for load in loads:
        load.start()
    greet(gather.partners() + gather.line_partners())
    gather.open_line(2)
    for weight, entry in ((1, 2), (1, 3), (2, 0)):
        gather.open_plane(weight, entry)
    rows, width = tokens.shape
    lane = lane_index(rows, codes.shape[0])
    spot = jnp.where(lane % 64 < 32, places[:, 0:1], places[:, 1:2])
    hot = jnp.where(lane % 32 == spot, 1.0, 0.0).astype(jnp.bfloat16)
    start[...] = mm(hot, codes[...]) + wide(tokens[...])
    strip[...] = jnp.zeros_like(strip)
    slot_count, part = plane_land.shape[1:]
    for plane in range(4):
        strip[:slot_count, :part] = plane_land[plane]
        shift = plane * part % 128
        begin = plane * part - shift
        moved = pltpu.roll(strip[...], shift, 1) if shift else strip[...]
        lane = lane_index(8, strip.shape[1])
        span = pl.ds(begin, strip.shape[1])
        inside = (lane >= shift) & (lane < shift + part)
        all_modulation[:, span] = jnp.where(inside, moved, all_modulation[:, span])
    total = jnp.zeros(table.shape, jnp.float32)
    for slot in range(slot_count):
        row = all_modulation[slot : slot + 1, : table.shape[1]] + ada_bias[...]
        total = total + jnp.where(group_slots[...] == slot, row, 0.0)
    table[...] = total

    def norm_first(at, group):
        hat, _ = centred(start[at, :])
        value = hat * (1.0 + group_row(table, group, 1, width)) + group_row(table, group, 0, width)
        normed[at, :] = low_bits(value)

    by_groups(rows, 64, norm_first)
    line_step, plane_open, plane_step = (
        partial(partial, method) for method in (gather.on_line, gather.open_plane, gather.on_plane)
    )
    later = [line_step(2, 1), plane_step(1, 1, 2), plane_step(1, 2, 2), line_step(2, 2)]
    later += [plane_open(2, 1), plane_step(1, 1, 3), plane_step(1, 2, 3), plane_step(1, 3, 2)]
    later += [line_step(2, 3), plane_step(1, 3, 3), plane_open(2, 2), plane_open(2, 3)]
    later += gather.plane_steps(2)

    def tick(count=1):
        for _ in range(count):
            if later:
                later.pop(0)()

    normed_t[...] = normed[...].T
    columns = joined.shape[1] // 4
    tick(2)
    span = product.shape[1]
    for block in range(4):
        loads[block].wait()
        product[...] = mm(normed[...], room[block].reshape(width, width)[:, :span])
        begin, offset = window_of(block, columns, joined.shape[1], span)

        def put(at):
            moved = product[at, :]
            if offset:
                moved = pltpu.roll(moved, offset, 1)
            lane = lane_index(moved.shape[0], span)
            inside = (lane >= offset) & (lane < offset + columns)
            wide_room[at, begin : begin + span] = jnp.where(
                inside, moved, wide_room[at, begin : begin + span]
            )

        by_rows(rows, 64, put)
        tick(2)

    def settle(at):
        joined[at, :] = (wide_room[at, :] + joined_bias[...]).astype(jnp.bfloat16)

    by_rows(rows, 64, settle)
    bar[...] = jnp.where(slots[...] == slot_line[...], 0.0, -1e30)
    stats[...] = jnp.zeros_like(stats)
    head_size = width // HEADS
    scale = 1.0 / math.sqrt(head_size)
    for group in range(8):

        @pl.loop(2 * group, 2 * group + 2)
        def _(head):
            at, inside = head_window(head, head_size, width)
            query = jnp.where(inside, joined[:, pl.ds(at, 256)], 0.0)
            key = joined[:, pl.ds(pl.multiple_of(at + width, 128), 256)]
            value = joined[:, pl.ds(pl.multiple_of(at + 2 * width, 128), 256)]
            scores = matmul_nt(query, key) * scale + bar[...]
            highest = jnp.max(scores, axis=1, keepdims=True)
            powers = jnp.exp(scores - highest)
            totals = jnp.sum(powers, axis=1, keepdims=True)
            probs = (powers * (1.0 / totals)).astype(jnp.bfloat16)
            found = mm(probs, value)
            wide_room[:, pl.ds(at, 256)] = jnp.where(inside, found, wide_room[:, pl.ds(at, 256)])
            lane = lane_index(rows, 128)
            stats[...] = jnp.where(lane == head, highest + jnp.log(totals), stats[...])

        tick(1)

    attended[...] = wide_room[:, :width].astype(jnp.bfloat16)
    columns = width // 4
    for block in range(4):
        product[:, :WINDOW] = mm(attended[...], room[block].reshape(width, width)[:, width - WINDOW :])
        begin, offset = window_of(block, columns, width, WINDOW)

        def put(at):
            moved = product[at, :WINDOW]
            if offset != WINDOW - columns:
                moved = pltpu.roll(moved, columns + offset, 1)
            lane = lane_index(moved.shape[0], WINDOW)
            inside = (lane >= offset) & (lane < offset + columns)
            branch[at, begin : begin + WINDOW] = jnp.where(
                inside, moved, branch[at, begin : begin + WINDOW]
            )

        by_rows(rows, 64, put)
        tick()

    def combine(at, group):
        value = branch[at, :] + out_bias[...]
        branch[at, :] = value
        value = start[at, :] + group_row(table, group, 2, width) * value
        middle[at, :] = value
        hat, _ = centred(value)
        value = hat * (1.0 + group_row(table, group, 4, width)) + group_row(table, group, 3, width)
        normed2[at, :] = value.astype(jnp.bfloat16)

    by_groups(rows, 64, combine)
    normed2_t[...] = normed2[...].T
    attended_t[...] = attended[...].T
    while len(later) > 12:
        tick()
    gather.ready(1, (2, 3))
    loads = [
        pltpu.make_async_copy(up_whole.at[block], room.at[block], load_sems.at[block])
        for block in range(4)
    ]
    for load in loads:
        load.start()
    stores = [None, None]
    for block in range(4):
        loads[block].wait()
        slot = block % 2
        if stores[slot] is not None:
            stores[slot].wait()
        before_room[slot] = mm(normed2[...], room[block].reshape(width, width)) + up_bias[block]
        stores[slot] = pltpu.make_async_copy(
            before_room.at[slot], before.at[block], store_sems.at[slot]
        )
        stores[slot].start()

        def act(some):
            value = before_room[slot, some, :]
            bend = 1.0 + jnp.tanh(SLOPE * (value + 0.044715 * (value * value * value)))
            hidden[block, some, :] = (value * (0.5 * bend)).astype(jnp.bfloat16)

        by_rows(rows, 64, act)
        tick(3)
    while later:
        tick()
    for store in stores:
        store.wait()
    gather.ready(2)
    gather.finish()
    for entry in range(4):
        gather.line_sends(2, entry, False)


def forward(tokens, places, codes, slots, group_slots, modulation, ada_bias, biases, wholes):
    rows, width = tokens.shape
    deep = width // 8
    whole = shaped((4, 4, 2, deep, width), jnp.bfloat16)
    vmem, away = pl.BlockSpec(memory_space=pltpu.VMEM), pl.BlockSpec(memory_space=pl.ANY)
    part = modulation.shape[2]
    return pl.pallas_call(
        forward_kernel,
        out_shape=[
            whole,
            whole,
            shaped((rows, 3 * width), jnp.bfloat16),
            shaped((rows, width)),
            shaped((8, 4 * part)),
            shaped((width, rows), jnp.bfloat16),
            shaped((width, rows), jnp.bfloat16),
            shaped((width, rows), jnp.bfloat16),
            shaped((rows, 128)),
            shaped((rows, width)),
            shaped((rows, width)),
            shaped((4, rows, width), jnp.bfloat16),
            shaped((4, rows, width)),
        ],
        in_specs=[vmem] * 11 + [away] * 3,
        out_specs=[away] * 2 + [vmem] * 10 + [away],
        input_output_aliases={12: 0, 13: 1},
        scratch_shapes=[
            pltpu.VMEM((4, 4, 2, deep, width), jnp.bfloat16),
            pltpu.VMEM((rows, 1024), jnp.float32),
            pltpu.VMEM((rows, 3 * width), jnp.float32),
            pltpu.VMEM((rows, rows), jnp.float32),
            pltpu.VMEM((2, rows, width), jnp.float32),
            pltpu.VMEM((rows, width), jnp.bfloat16),
            pltpu.VMEM((rows, width), jnp.bfloat16),
            pltpu.VMEM((rows, width), jnp.bfloat16),
            pltpu.VMEM((8, -(-part // 128) * 128), jnp.float32),
            pltpu.VMEM((8, 4 * part + 128), jnp.float32),
            pltpu.SemaphoreType.DMA((3, 40)),
            pltpu.SemaphoreType.DMA((3, 8, 4)),
            pltpu.SemaphoreType.DMA((4,)),
            pltpu.SemaphoreType.DMA((2,)),
        ],
        compiler_params=pltpu.CompilerParams(
            collective_id=4, has_side_effects=True, vmem_limit_bytes=62 * 2**20
        ),
        cost_estimate=pl.CostEstimate(
            flops=2 * 10 * rows * width * width, bytes_accessed=10**8, transcendentals=0
        ),
    )(
        tokens,
        places,
        codes,
        slots.reshape(rows, 1),
        slots.reshape(1, rows),
        group_slots,
        modulation,
        ada_bias,
        *biases,
        *wholes,
    )


def low_bits(value):
    return value.astype(jnp.bfloat16)


def wide(value):
    return value.astype(jnp.float32)


class Scatter:
    def __init__(self, own, lands, stage, outs, send_sems, recv_sems, stage_sems):
        self.own, self.lands, self.stage, self.outs = own, lands, stage, outs
        self.send_sems, self.recv_sems, self.stage_sems = send_sems, recv_sems, stage_sems
        self.plane, self.depth, self.core = place()
        self.started = []
        self.counts = [0] * len(lands)
        self.queue, self.held, self.turn = [], [], 0

    def partners(self):
        found = [
            far_device(flipped(self.plane, 1), self.depth, self.core),
            far_device(flipped(self.plane, 2), self.depth, self.core),
            far_device(self.plane, self.depth, 1 - self.core),
        ]
        return found + [far_device(self.plane, (self.depth + d) % 4, self.core) for d in (1, 2, 3)]

    def sending(self, weight, source, index, partner, number):
        return pltpu.make_async_remote_copy(
            src_ref=source,
            dst_ref=self.lands[weight].at[index],
            send_sem=self.send_sems.at[weight, number],
            recv_sem=self.recv_sems.at[weight, index],
            device_id=self.partners()[partner],
            device_id_type=pl.DeviceIdType.MESH,
        )

    def send(self, weight, source, index, partner):
        copy = self.sending(weight, source, index, partner, self.counts[weight])
        self.counts[weight] += 1
        copy.start()
        return copy

    def term(self, weight, flip, back, rows_of, line_rows):
        plane, depth = flipped(self.plane, flip), (self.depth + 4 - back) % 4
        base = (depth if line_rows else plane) * 2
        self.own[weight % 2, flip, back] = rows_of(base + self.core)[...]
        return self.send(weight, rows_of(base + 1 - self.core), flip * 4 + back, 2)

    def open(self, weight, part, order=(2, 1, 3, 0)):
        for back in order:
            axis, near, far = (0, 1, 2) if back % 2 == 0 else (1, 2, 1)
            jobs = []
            if part == "sent":
                for flip in (3, near):
                    goes = (flip, back, 16 + (4 if flip == 3 else 0) + back, axis)
                    jobs.append((flip * 4 + back, flip, goes))
            elif part == "kept":
                jobs = [(flip * 4 + back, flip, None) for flip in (far, 0)]
            elif part == "first":
                jobs = [(20 + back, far, (far, back, 24 + back, 1 - axis)), (16 + back, 0, None)]
            elif part == "second":
                jobs = [(24 + back, 0, (0, back, 28 + back, 2 + 4 - back) if back else None)]
            elif back:
                self.queue.append((weight, 28 + back, 0, 0, None))
            for index, flip, goes in jobs:
                self.queue.append((weight, index, flip, back, goes))

    def fetch(self, job):
        weight, index = job[0], job[1]
        region = self.lands[weight].at[index]
        pltpu.make_async_remote_copy(
            src_ref=region,
            dst_ref=region,
            send_sem=self.send_sems.at[weight, 0],
            recv_sem=self.recv_sems.at[weight, index],
            device_id=self.partners()[2],
            device_id_type=pl.DeviceIdType.MESH,
        ).wait_recv()
        if self.stage is not None:
            self.staging(weight, index, self.turn).start()
        self.held.append((job, self.turn))
        self.turn = (self.turn + 1) % 2

    def staging(self, weight, index, turn):
        return pltpu.make_async_copy(
            self.lands[weight].at[index], self.stage.at[turn], self.stage_sems.at[turn]
        )

    def merge(self):
        (weight, index, flip, back, goes), turn = self.held.pop(0)
        if self.stage is None:
            arrived = self.lands[weight][index]
        else:
            self.staging(weight, index, turn).wait()
            arrived = self.stage[turn]
        if index >= 28:
            self.outs[weight][...] += wide(arrived)
            return
        if index == 24:
            self.outs[weight][...] = wide(self.own[weight % 2, flip, back]) + wide(arrived)
            return
        self.own[weight % 2, flip, back] = self.own[weight % 2, flip, back] + arrived
        if goes is not None:
            self.started.append((weight, goes, self.counts[weight]))
            self.send(weight, self.own.at[weight % 2, goes[0], goes[1]], goes[2], goes[3])

    def tick(self, count=1):
        for _ in range(count):
            if self.held:
                self.merge()
            if self.queue:
                self.fetch(self.queue.pop(0))
                if self.stage is None:
                    self.merge()

    def clear(self, weight, flip):
        while any(job[0] == weight and flip == 0 for job in self.queue) or any(
            held[0][0] == weight and held[0][2] == flip for held in self.held
        ):
            self.tick()
        for entry in [entry for entry in self.started if entry[0] == weight and entry[1][0] == flip]:
            self.started.remove(entry)
            self.sent(entry)

    def sent(self, entry):
        weight, (flip, back, index, partner), number = entry
        source = self.own.at[weight % 2, flip, back]
        self.sending(weight, source, index, partner, number).wait_send()

    def drain(self):
        while self.queue or self.held:
            self.tick()
        for entry in self.started:
            self.sent(entry)


def multiply_rows(out, left, right, step=384):
    @pl.loop(0, left.shape[0] // step)
    def _(index):
        at = pl.ds(pl.multiple_of(index * step, step), step)
        out[at, :] = mm(left[at, :], right[...]).astype(jnp.bfloat16)


def deep_rows(room, slot, deep):
    def rows_of(row):
        return room.at[slot, pl.ds(pl.multiple_of(row * deep, 16), deep)]

    return rows_of


def backward_kernel(
    hidden_in,
    before_in,
    joined_in,
    joined_whole,
    up_whole,
    down_whole,
    normed_in,
    attended_in,
    start_in,
    middle,
    out_grad,
    branch,
    normed_t,
    stats,
    slots,
    slot_line,
    table,
    bias,
    group_slots,
    down_land,
    up_land,
    joined_land,
    mixed,
    middle_grad,
    slot_sums,
    branch_sums,
    pre_sums,
    joined_sums,
    down_out,
    up_out,
    joined_out,
    line_land,
    windows,
    own,
    stage,
    room,
    acts,
    grads,
    grads_t,
    attended_grad,
    send_sems,
    recv_sems,
    stage_sems,
    load_sems,
    more_sems,
    mod_room,
    strip,
    plane_out,
    plane_land,
    plane_sems,
    line_sems,
):
    rows, width = middle.shape
    deep = width // 8
    scatter = Scatter(
        own,
        (down_land, up_land, joined_land),
        stage,
        (down_out, up_out, joined_out),
        send_sems,
        recv_sems,
        stage_sems,
    )
    others = [far_device(flipped(scatter.plane, flip), scatter.depth, scatter.core) for flip in (1, 2, 3)]
    others.append(scatter.partners()[2])
    for far in (1, 2, 3):
        for core in range(2):
            others.append(far_device(scatter.plane, (scatter.depth + far) % 4, core))
    greet(others)
    slot_sums[...] = jnp.zeros_like(slot_sums)
    branch_sums[...] = jnp.zeros_like(branch_sums)
    pre_sums[...] = jnp.zeros_like(pre_sums)
    joined_sums[...] = jnp.zeros_like(joined_sums)

    def dense(weights, before, total):
        plan = [(down_whole, part) for part in range(4)] * 2 + [(up_whole, part) for part in range(4)]

        def load(step):
            whole, part = plan[step]
            copy = pltpu.make_async_copy(
                whole.at[part], weights.at[step % 2], load_sems.at[step % 2]
            )
            copy.start()
            return copy

        loads = {0: load(0)}
        acting = [
            pltpu.make_async_copy(hidden_in.at[part], acts.at[part], more_sems.at[part])
            for part in range(4)
        ]
        for copy in acting:
            copy.start()

        def next_weight(step):
            if step + 1 < len(plan):
                loads[step + 1] = load(step + 1)
            loads[step].wait()
            return weights.at[step % 2]

        for part in range(4):
            acting[part].wait()
            term = matmul_nt(acts[part], next_weight(part)[...])
            total[...] = term + bias[...] if part == 0 else total[...] + term

        def settle(at, group):
            gate = group_row(table, group, 5, width)
            value = total[at, :]
            grad = wide(out_grad[at, :])
            mixed[at, :] = low_bits(middle[at, :] + gate * value)
            add_group(slot_sums.at[3], group, grad * value)
            value = low_bits(grad * gate)
            grads[at, :] = value
            branch_sums[1:2, :] += jnp.sum(wide(value), axis=0, keepdims=True)

        by_groups(rows, 64, settle)
        grads_t[...] = grads[...].T
        waits = [[], []]
        for number, back in enumerate((2, 1, 3, 0)):
            slot = number % 2
            for copy in waits[slot]:
                copy.wait_send()
            multiply_rows(room.at[slot], grads_t, acts.at[(scatter.depth + 4 - back) % 4])
            rows_of = deep_rows(room, slot, deep)
            waits[slot] = [scatter.term(0, flip, back, rows_of, False) for flip in (3, 1, 2, 0)]
        scatter.open(0, "sent")
        scatter.open(0, "kept")
        befores = [
            pltpu.make_async_copy(before_in.at[part], before.at[part % 2], more_sems.at[part])
            for part in range(4)
        ]
        befores[0].start()
        for part in range(4):
            if part < 3:
                befores[part + 1].start()
            total[...] = mm(grads[...], next_weight(4 + part)[...])
            befores[part].wait()

            def act(at):
                value = before[part % 2, at, :]
                square = value * value
                bend = jnp.tanh(SLOPE * (value + 0.044715 * (square * value)))
                slope = 0.5 * (1.0 + bend) + 0.5 * value * (1.0 - bend * bend) * (
                    SLOPE * (1.0 + 3.0 * 0.044715 * square)
                )
                value = low_bits(total[at, :] * slope)
                acts[part, at, :] = value
                pre_sums[part : part + 1, :] += jnp.sum(wide(value), axis=0, keepdims=True)

            by_rows(rows, 64, act)
            scatter.tick(4 if part else 6)
        for number, flip in enumerate((3, 1, 2, 0)):
            slot = number % 2
            for copy in waits[slot]:
                copy.wait_send()
            multiply_rows(room.at[slot], normed_t, acts.at[flipped(scatter.plane, flip)])
            rows_of = deep_rows(room, slot, deep)
            waits[slot] = [scatter.term(1, flip, back, rows_of, True) for back in (2, 1, 3, 0)]
        scatter.open(1, "sent")
        scatter.open(1, "kept")
        scatter.open(0, "first")
        scatter.open(0, "second")
        scatter.open(1, "first")
        scatter.open(1, "second")
        for part in range(4):
            term = matmul_nt(acts[part], next_weight(8 + part)[...])
            total[...] = term if part == 0 else total[...] + term
            scatter.tick(4)

        def turn(at, group):
            grad = total[at, :]
            hat, scale = centred(middle[at, :])
            add_group(slot_sums.at[1], group, grad)
            add_group(slot_sums.at[2], group, grad * hat)
            grad = grad * (1.0 + group_row(table, group, 4, width))
            grad = wide(out_grad[at, :]) + norm_back(hat, scale, grad)
            middle_grad[at, :] = grad
            add_group(slot_sums.at[0], group, grad * branch[at, :])
            value = wide(low_bits(grad * group_row(table, group, 2, width)))
            total[at, :] = value
            branch_sums[0:1, :] += jnp.sum(value, axis=0, keepdims=True)

        by_groups(rows, 64, turn)
        scatter.tick(8)
        for slot in range(2):
            for copy in waits[slot]:
                copy.wait_send()
        columns = width // 4
        span = pl.ds(width - WINDOW, WINDOW)
        sides = []
        for block in range(4):
            copy = pltpu.make_async_copy(
                joined_whole.at[block, :, span],
                weights.at[block // 2, :, pl.ds(block % 2 * WINDOW, WINDOW)],
                more_sems.at[block],
            )
            copy.start()
            sides.append(copy)
        for block in range(4):
            begin, offset = window_of(block, columns, width, WINDOW)

            def cut(at):
                moved = total[at, begin : begin + WINDOW]
                if offset != WINDOW - columns:
                    moved = pltpu.roll(moved, (2 * WINDOW - columns - offset) % WINDOW, 1)
                lane = lane_index(moved.shape[0], WINDOW)
                moved = jnp.where(lane >= WINDOW - columns, moved, 0.0)
                windows[block, at, :] = low_bits(moved)

            by_rows(rows, 64, cut)
        for block in range(4):
            sides[block].wait()
            side = weights[block // 2, :, block % 2 * WINDOW : (block % 2 + 1) * WINDOW]
            term = matmul_nt(windows[block], side)
            total[...] = term if block == 0 else total[...] + term
        attended_grad[...] = low_bits(total[...])

    pl.run_scoped(
        dense,
        pltpu.VMEM((2, width, width), jnp.bfloat16),
        pltpu.VMEM((2, rows, width), jnp.float32),
        pltpu.VMEM((rows, width), jnp.float32),
    )

    def heads(joined, found_room, bar):
        load = pltpu.make_async_copy(joined_in, joined, load_sems.at[0])
        load.start()
        size = width // HEADS
        scale = 1.0 / math.sqrt(size)
        bar[...] = jnp.where(slots[...] == slot_line[...], 0.0, -1e30)
        load.wait()
        for head_static in range(0, HEADS, 2):

            @pl.loop(head_static, head_static + 2)
            def _(head):
                begin, inside = head_window(head, size, width)
                columns = [pl.ds(pl.multiple_of(begin + part * width, 128), 256) for part in range(3)]
                query = jnp.where(inside, joined[:, columns[0]], 0.0)
                key = joined[:, columns[1]]
                value = joined[:, columns[2]]
                out_part = jnp.where(inside, attended_grad[:, columns[0]], 0.0)
                lane = lane_index(rows, 128)
                stat = jnp.sum(jnp.where(lane == head, stats[...], 0.0), axis=1, keepdims=True)
                probs = jnp.exp(matmul_nt(query, key) * scale + bar[...] - stat)
                prob_grad = matmul_nt(out_part, value)
                inner = jnp.sum(probs * prob_grad, axis=1, keepdims=True)
                score_grad = low_bits(probs * (prob_grad - inner))
                found = (
                    mm(score_grad, key) * scale,
                    matmul_tn(score_grad, query) * scale,
                    matmul_tn(low_bits(probs), out_part),
                )
                for part in range(3):
                    found_room[:, columns[part]] = jnp.where(
                        inside, found[part], found_room[:, columns[part]]
                    )

            scatter.tick((0, 0, 0, 2, 2, 2, 3, 3)[head_static // 2])

        span = 1024
        block_width = 3 * width // 4

        def add_up(at):
            joined_sums[...] += jnp.sum(wide(low_bits(found_room[at, :])), axis=0, keepdims=True)

        by_rows(rows, 64, add_up)
        for block in range(4):
            begin, offset = window_of(block, block_width, 3 * width, span)

            def cut(at):
                moved = found_room[at, begin : begin + span]
                if offset:
                    moved = pltpu.roll(moved, span - offset, 1)
                lane = lane_index(moved.shape[0], span)
                acts[block, at, :span] = low_bits(jnp.where(lane < block_width, moved, 0.0))

            by_rows(rows, 64, cut)

    pl.run_scoped(
        heads,
        pltpu.VMEM((rows, 3 * width), jnp.bfloat16),
        pltpu.VMEM((rows, 3 * width), jnp.float32),
        pltpu.VMEM((rows, rows), jnp.float32),
    )
    span = 1024

    def last(weights, attended_t, start, total):
        left = pltpu.make_async_copy(normed_in, grads_t, more_sems.at[0])
        other = pltpu.make_async_copy(attended_in, attended_t, more_sems.at[1])
        begin_copy = pltpu.make_async_copy(start_in, start, more_sems.at[2])
        for copy in (left, other, begin_copy):
            copy.start()

        def load(part):
            copy = pltpu.make_async_copy(
                joined_whole.at[part, :, pl.ds(0, span)], weights.at[part % 2], load_sems.at[part % 2]
            )
            copy.start()
            return copy

        loads = [load(0), load(1)]
        left.wait()
        other.wait()
        low, high = span, width - WINDOW
        waits = [[], []]
        for number, flip in enumerate((3, 1, 2, 0)):
            slot = number % 2
            for copy in waits[slot]:
                copy.wait_send()
            at = flipped(scatter.plane, flip)

            @pl.loop(0, 3)
            def _(index):
                some = pl.ds(pl.multiple_of(index * (width // 3), width // 3), width // 3)
                head = mm(grads_t[some, :], acts[at, :, :span])
                tail = mm(attended_t[some, :], windows[at])
                room[slot, some, :high] = low_bits(head[:, :high])
                room[slot, some, high:low] = low_bits(head[:, high:low] + tail[:, : low - high])
                room[slot, some, low:] = low_bits(tail[:, low - high :])

            scatter.clear(0, flip)
            rows_of = deep_rows(room, slot, deep)
            waits[slot] = [scatter.term(2, flip, back, rows_of, True) for back in (2, 1, 3, 0)]
            scatter.tick(1)
        early, late = (2, 1), (3, 0)
        scatter.open(2, "sent", early)
        scatter.open(2, "kept", early)
        scatter.open(2, "kept", late)
        scatter.open(0, "line")
        scatter.open(2, "first", early)
        scatter.open(2, "sent", late)
        scatter.open(2, "second", early)
        scatter.open(1, "line")
        scatter.open(2, "first", late)
        scatter.open(2, "second", late)
        scatter.open(2, "line")
        for part in range(4):
            loads[part].wait()
            term = matmul_nt(acts[part, :, :span], weights[part % 2])
            total[...] = term if part == 0 else total[...] + term
            if part < 2:
                loads.append(load(part + 2))
            scatter.tick(4)
        begin_copy.wait()

        def turn(at, group):
            grad = total[at, :]
            hat, scale = centred(start[at, :])
            add_group(slot_sums.at[4], group, grad)
            add_group(slot_sums.at[5], group, grad * hat)
            grad = grad * (1.0 + group_row(table, group, 1, width))
            middle_grad[at, :] = middle_grad[at, :] + norm_back(hat, scale, grad)

        for part in range(4):

            @pl.loop(0, rows // 256)
            def _(index):
                begin = part * (rows // 4) + index * 64
                turn(pl.ds(pl.multiple_of(begin, 64), 64), begin // 128)

            if part == 1:
                scatter.tick(2)
        for slot in range(2):
            for copy in waits[slot]:
                copy.wait_send()

    pl.run_scoped(
        last,
        pltpu.VMEM((2, width, span), jnp.bfloat16),
        pltpu.VMEM((width, rows), jnp.bfloat16),
        pltpu.VMEM((rows, width), jnp.float32),
        pltpu.VMEM((rows, width), jnp.float32),
    )
    mod_room[...] = jnp.zeros_like(mod_room)
    slot_count, part = plane_out.shape[1:]
    for slot in range(slot_count):
        for number, kind in enumerate((4, 5, 0, 1, 2, 3)):
            value = jnp.where(group_slots[...] == slot, slot_sums[kind], 0.0)
            value = wide(low_bits(jnp.sum(value, axis=0, keepdims=True)))
            mod_room[slot : slot + 1, number * width : (number + 1) * width] = value
    reach = strip.shape[1]
    for plane in range(4):
        shift = plane * part % 128
        begin = plane * part - shift
        moved = mod_room[:, begin : begin + reach]
        strip[...] = pltpu.roll(moved, reach - shift, 1) if shift else moved
        plane_out[plane] = strip[:slot_count, :part]
    plane_trade = (plane_out, plane_land, plane_sems.at[0], plane_sems.at[1])
    line_trade = (plane_land, line_land, line_sems.at[0], line_sems.at[1])
    trade_along("dp", *plane_trade, True)
    while len(scatter.queue) > 12:
        scatter.tick()
    trade_along("dp", *plane_trade, False)
    trade_along("fsdp", *line_trade, True, True)
    scatter.drain()
    trade_along("fsdp", *line_trade, False, True)


def backward(away_ins, near_ins, slots, table, bias, group_slots):
    middle = near_ins[0]
    rows, width = middle.shape
    deep = width // 8
    part = 6 * width // 4
    vmem, away = pl.BlockSpec(memory_space=pltpu.VMEM), pl.BlockSpec(memory_space=pl.ANY)
    land = shaped((32, deep, width), jnp.bfloat16)
    return pl.pallas_call(
        backward_kernel,
        out_shape=[
            land,
            land,
            land,
            shaped((rows, width), jnp.bfloat16),
            shaped((rows, width)),
            shaped((6, 8, width)),
            shaped((8, width)),
            shaped((8, width)),
            shaped((1, 3 * width)),
            shaped((deep, width)),
            shaped((deep, width)),
            shaped((deep, width)),
            shaped((8, 4, 4, part)),
        ],
        in_specs=[away] * 9 + [vmem] * 10,
        out_specs=[away] * 3 + [vmem] * 10,
        scratch_shapes=[
            pltpu.VMEM((4, rows, WINDOW), jnp.bfloat16),
            pltpu.VMEM((2, 4, 4, deep, width), jnp.bfloat16),
            pltpu.VMEM((2, deep, width), jnp.bfloat16),
            pltpu.VMEM((2, width, width), jnp.bfloat16),
            pltpu.VMEM((4, rows, width), jnp.bfloat16),
            pltpu.VMEM((rows, width), jnp.bfloat16),
            pltpu.VMEM((width, rows), jnp.bfloat16),
            pltpu.VMEM((rows, width), jnp.bfloat16),
            pltpu.SemaphoreType.DMA((3, 32)),
            pltpu.SemaphoreType.DMA((3, 32)),
            pltpu.SemaphoreType.DMA((2,)),
            pltpu.SemaphoreType.DMA((2,)),
            pltpu.SemaphoreType.DMA((4,)),
            pltpu.VMEM((8, 4 * part), jnp.float32),
            pltpu.VMEM((8, -(-part // 128) * 128), jnp.float32),
            pltpu.VMEM((4, 4, part), jnp.float32),
            pltpu.VMEM((4, 4, part), jnp.float32),
            pltpu.SemaphoreType.DMA((2, 4)),
            pltpu.SemaphoreType.DMA((2, 8)),
        ],
        compiler_params=pltpu.CompilerParams(
            collective_id=5, has_side_effects=True, vmem_limit_bytes=62 * 2**20
        ),
        cost_estimate=pl.CostEstimate(
            flops=2 * 30 * rows * width * width, bytes_accessed=10**8, transcendentals=0
        ),
    )(
        *away_ins,
        *near_ins,
        slots.reshape(rows, 1),
        slots.reshape(1, rows),
        table,
        bias,
        group_slots,
    )


def code_parts(width):
    quarter = width // 4
    exponent = jnp.arange(quarter, dtype=jnp.float32) / quarter
    frequency = 1.0 / 10000.0**exponent
    angle = jnp.arange(32, dtype=jnp.float32)[:, None] * frequency[None, :]
    half = jnp.concatenate([jnp.sin(angle), jnp.cos(angle)], axis=1)
    none = jnp.zeros_like(half)
    left = jnp.concatenate(
        [jnp.concatenate([half, none], axis=1), jnp.concatenate([none, half], axis=1)], axis=0
    )
    parts = []
    for _ in range(3):
        part = lax.reduce_precision(left, 8, 7)
        parts.append(part.astype(jnp.bfloat16))
        left = left - part
    return jnp.concatenate(parts, axis=0)


def box_device(
    tokens,
    condition,
    kept_index,
    segment,
    grid_side,
    ada_weight,
    ada_bias,
    attn_weight,
    attn_bias,
    proj_weight,
    out_bias,
    up_weight,
    up_bias,
    down_weight,
    grad_out,
):
    rows, width = tokens.shape
    slot_count = condition.shape[0]
    core = place()[2]
    columns = attn_weight.shape[1]
    turned = down_weight.T.reshape(2, up_weight.shape[0], down_weight.shape[0])
    mine, theirs = pick(turned, core), pick(turned, 1 - core)
    arrived = swap(theirs, "core")
    down_shard = jnp.where(
        core == 0,
        jnp.concatenate([mine, arrived], axis=1),
        jnp.concatenate([arrived, mine], axis=1),
    )
    silu_cond, silu_back = jax.vjp(jax.nn.silu, condition.astype(jnp.float32))
    silu_bf = silu_cond.astype(jnp.bfloat16)
    vectors = (ada_bias, attn_bias, out_bias, up_bias)
    flat = jnp.concatenate(vectors)
    flat = jnp.pad(flat, (0, 2048 - flat.shape[0])).reshape(16, 128)
    cut = silu_bf.reshape(slot_count, 8, -1).transpose(1, 0, 2)
    cut = jnp.pad(cut, ((0, 0), (0, 16 - slot_count), (0, 0)))
    joined_whole, up_start, down_start, silu_land, flat_land, modulation = opening(
        cut,
        flat,
        ada_weight,
        (jnp.concatenate([attn_weight, proj_weight], axis=1), up_weight, down_shard),
    )
    silu_part = silu_land[:, :slot_count].reshape(32 * slot_count, -1)
    flat_land = flat_land.reshape(32, -1)
    found, begin = [], 0
    for vector in vectors:
        found.append(flat_land[:, begin : begin + vector.shape[0]].reshape(-1))
        begin += vector.shape[0]
    ada_bfull, attn_bfull, out_bfull, up_bfull = found
    group_slots = segment.reshape(rows // 128, 128)[:, 0]
    group_column = jnp.pad(group_slots, (0, 8 - rows // 128), constant_values=-1)[:, None]
    group_sides = jnp.sum(
        jnp.where(group_slots[:, None] == jnp.arange(slot_count)[None, :], grid_side[None, :], 0), axis=1
    )
    side_rows = jnp.repeat(group_sides, 128)
    places = jnp.stack([kept_index % side_rows, kept_index // side_rows], axis=1)
    zeros = jnp.zeros((width,), jnp.bfloat16)
    joined_bias = jnp.concatenate([attn_bfull[:width], zeros, attn_bfull[width:]])
    out_bias_f = out_bfull.astype(jnp.float32)
    (
        up_whole,
        down_whole,
        joined,
        start,
        table,
        normed_t,
        attended_t,
        normed2_t,
        stats,
        branch1,
        middle,
        hidden,
        before,
    ) = forward(
        tokens,
        places,
        code_parts(width),
        segment,
        group_column,
        modulation,
        ada_bfull.astype(jnp.float32)[None],
        (
            joined_bias.astype(jnp.float32)[None],
            out_bias_f[None, :width],
            up_bfull.astype(jnp.float32).reshape(4, 1, -1),
        ),
        (joined_whole, up_start, down_start),
    )
    wholes = [whole.reshape(4, width, width) for whole in (joined_whole, up_whole, down_whole)]
    (
        _,
        _,
        _,
        mixed,
        tokens_grad,
        slot_sums,
        branch_sums,
        pre_sums,
        joined_sums,
        down_total,
        up_weight_grad,
        joined_total,
        line_land,
    ) = backward(
        (hidden, before, joined, *wholes, normed_t, attended_t, start),
        (middle, grad_out, branch1, normed2_t, stats),
        segment,
        table,
        out_bias_f[None, width:],
        group_column,
    )
    half = down_total.shape[1] // 2
    cut = down_total.reshape(-1, 2, half).transpose(1, 0, 2)
    mine, theirs = pick(cut, core), pick(cut, 1 - core)
    arrived = swap(theirs, "core")
    down_weight_grad = jnp.where(
        core == 0, jnp.concatenate([mine, arrived]), jnp.concatenate([arrived, mine])
    ).T
    cut = line_land.transpose(1, 0, 2, 3).reshape(32 * slot_count, -1).astype(jnp.bfloat16)
    joined_sums = joined_sums[0]
    terms = (
        jnp.concatenate([joined_sums[:width], joined_sums[2 * width :]]),
        branch_sums[:2].reshape(-1),
        pre_sums[:4].reshape(-1),
    )
    ada_weight_grad, ada_bias_grad, silu_grad, bias_grads = modulation_ends(cut, silu_part, ada_weight, terms)
    attn_bias_grad, out_bias_grad, up_bias_grad = bias_grads
    return (
        mixed,
        tokens_grad,
        silu_back(silu_grad)[0],
        ada_weight_grad,
        ada_bias_grad,
        joined_total[:, :columns],
        attn_bias_grad,
        joined_total[:, columns:],
        out_bias_grad,
        up_weight_grad,
        up_bias_grad,
        down_weight_grad,
    )


def per_device(
    tokens,
    condition,
    kept_index,
    segment,
    grid_side,
    ada_weight,
    ada_bias,
    attn_weight,
    attn_bias,
    proj_weight,
    out_bias,
    up_weight,
    up_bias,
    down_weight,
    grad_out,
):
    if on_box():
        return box_device(
            tokens,
            condition,
            kept_index,
            segment,
            grid_side,
            ada_weight,
            ada_bias,
            attn_weight,
            attn_bias,
            proj_weight,
            out_bias,
            up_weight,
            up_bias,
            down_weight,
            grad_out,
        )
    model_width = tokens.shape[1]
    slot_count = condition.shape[0]
    planes = lax.axis_size("dp")
    joined_w, up_w, down_w = gather_blocks(attn_weight, proj_weight, up_weight, down_weight)
    attn_columns = attn_weight.shape[1]
    slot_ids = jnp.arange(slot_count, dtype=jnp.int32)
    same_slot = segment[:, None] == slot_ids[None, :]
    slot_table = same_slot.astype(jnp.float32)
    side_rows = jnp.sum(jnp.where(same_slot, grid_side[None, :], 0), axis=1)
    start = tokens.astype(jnp.float32) + position_code(kept_index, side_rows, model_width)
    condition_f = condition.astype(jnp.float32)
    silu_cond, silu_back = jax.vjp(jax.nn.silu, condition_f)
    silu_bf = silu_cond.astype(jnp.bfloat16)
    silu_all, (ada_bfull, attn_bfull, out_bfull, up_bfull) = gather_small(
        silu_bf, (ada_bias, attn_bias, out_bias, up_bias)
    )
    modulation, silu_part = modulate_slots(silu_all, ada_weight, ada_bfull)
    mod_rows = jnp.dot(
        slot_table, modulation, precision=lax.Precision.HIGHEST, preferred_element_type=jnp.float32
    )
    shift_one, scale_one, gate_one, shift_two, scale_two, gate_two = jnp.split(mod_rows, 6, axis=1)
    normed1, norm1_back = jax.vjp(norm_modulate, start, shift_one, scale_one)
    normed1_bf = normed1.astype(jnp.bfloat16)
    projected = jnp.concatenate(
        [
            jnp.dot(normed1_bf, joined_w[part, :, :attn_columns], preferred_element_type=jnp.float32)
            for part in range(planes)
        ],
        axis=1,
    )
    proj_full = joined_w[:, :, attn_columns:].transpose(1, 0, 2).reshape(model_width, model_width)
    attn_bias_f = attn_bfull.astype(jnp.float32)
    query_bf = (projected[:, :model_width] + attn_bias_f[:model_width]).astype(jnp.bfloat16)
    key_bf = projected[:, model_width : 2 * model_width].astype(jnp.bfloat16)
    value_bf = (projected[:, 2 * model_width :] + attn_bias_f[model_width:]).astype(jnp.bfloat16)
    attended, log_totals = attend_forward(query_bf, key_bf, value_bf, segment, HEADS)
    attended_bf = attended.astype(jnp.bfloat16)
    out_bias_f = out_bfull.astype(jnp.float32)
    branch1 = (
        jnp.dot(attended_bf, proj_full, preferred_element_type=jnp.float32)
        + out_bias_f[:model_width]
    )
    middle = start + gate_one * branch1
    normed2, norm2_back = jax.vjp(norm_modulate, middle, shift_two, scale_two)
    normed2_bf = normed2.astype(jnp.bfloat16)
    hidden_parts, gelu_parts = [], []
    up_bias_f = up_bfull.astype(jnp.float32).reshape(planes, -1)
    branch2 = out_bias_f[model_width:]
    for part in range(planes):
        hidden_pre = (
            jnp.dot(normed2_bf, up_w[part], preferred_element_type=jnp.float32) + up_bias_f[part]
        )
        hidden_act, gelu_back = jax.vjp(partial(jax.nn.gelu, approximate=True), hidden_pre)
        hidden_parts.append(hidden_act.astype(jnp.bfloat16))
        gelu_parts.append(gelu_back)
        branch2 = branch2 + matmul_nt(hidden_parts[part], down_w[part])
    mixed = (middle + gate_two * branch2).astype(jnp.bfloat16)
    out_grad = grad_out.astype(jnp.float32)
    grad_gate_two = out_grad * branch2
    grad_branch2 = (out_grad * gate_two).astype(jnp.bfloat16)
    down_weight_grad = scatter_whole(matmul_tn(jnp.concatenate(hidden_parts, axis=1), grad_branch2))
    pre_parts = []
    for part in range(planes):
        hidden_grad = jnp.dot(grad_branch2, down_w[part], preferred_element_type=jnp.float32)
        pre_parts.append(gelu_parts[part](hidden_grad)[0].astype(jnp.bfloat16))
    pre_grad = jnp.stack(pre_parts)
    (up_weight_grad,) = scatter_rows([(normed2_bf, pre_grad)])
    up_bias_term = jnp.sum(pre_grad, axis=1, dtype=jnp.float32).reshape(-1)
    normed2_grad = sum(matmul_nt(pre_parts[part], up_w[part]) for part in range(planes))
    middle_part, grad_shift_two, grad_scale_two = norm2_back(normed2_grad)
    middle_grad = out_grad + middle_part
    grad_gate_one = middle_grad * branch1
    grad_branch1 = (middle_grad * gate_one).astype(jnp.bfloat16)
    attended_grad = matmul_nt(grad_branch1, proj_full).astype(jnp.bfloat16)
    query_grad, key_grad, value_grad = attend_backward(
        query_bf, key_bf, value_bf, attended_grad, segment, log_totals, HEADS
    )
    query_grad_bf = query_grad.astype(jnp.bfloat16)
    value_grad_bf = value_grad.astype(jnp.bfloat16)
    joined_grad = jnp.concatenate(
        [query_grad_bf, key_grad.astype(jnp.bfloat16), value_grad_bf], axis=1
    )
    joined_parts = by_columns(joined_grad, planes)
    attn_weight_grad, proj_weight_grad = scatter_rows(
        [(normed1_bf, joined_parts), (attended_bf, by_columns(grad_branch1, planes))]
    )
    attn_bias_term = jnp.concatenate(
        [
            jnp.sum(query_grad_bf, axis=0, dtype=jnp.float32),
            jnp.sum(value_grad_bf, axis=0, dtype=jnp.float32),
        ]
    )
    normed1_grad = sum(
        matmul_nt(joined_parts[part], joined_w[part, :, :attn_columns]) for part in range(planes)
    )
    start_part, grad_shift_one, grad_scale_one = norm1_back(normed1_grad)
    tokens_grad = middle_grad + start_part
    mod_rows_grad = jnp.concatenate(
        [
            grad_shift_one,
            grad_scale_one,
            grad_gate_one,
            grad_shift_two,
            grad_scale_two,
            grad_gate_two,
        ],
        axis=1,
    )
    modulation_grad = lax.dot_general(
        slot_table,
        mod_rows_grad,
        (((0,), (0,)), ((), ())),
        precision=lax.Precision.HIGHEST,
        preferred_element_type=jnp.float32,
    ).astype(jnp.bfloat16)
    out_bias_term = jnp.concatenate(
        [
            jnp.sum(grad_branch1, axis=0, dtype=jnp.float32),
            jnp.sum(grad_branch2, axis=0, dtype=jnp.float32),
        ]
    )
    ada_weight_grad, ada_bias_grad, silu_grad, bias_grads = modulation_back(
        modulation_grad, silu_part, ada_weight, (attn_bias_term, out_bias_term, up_bias_term)
    )
    attn_bias_grad, out_bias_grad, up_bias_grad = bias_grads
    condition_grad = silu_back(silu_grad)[0]
    return (
        mixed,
        tokens_grad,
        condition_grad,
        ada_weight_grad,
        ada_bias_grad,
        attn_weight_grad,
        attn_bias_grad,
        proj_weight_grad,
        out_bias_grad,
        up_weight_grad,
        up_bias_grad,
        down_weight_grad,
    )


def solution(mesh):
    return jax.shard_map(
        per_device,
        mesh=mesh,
        in_specs=(
            P(("dp", "fsdp"), None),
            P(("dp", "fsdp"), None),
            P(("dp", "fsdp")),
            P(("dp", "fsdp")),
            P(("dp", "fsdp")),
            P("fsdp", "dp"),
            P(("dp", "fsdp")),
            P("fsdp", "dp"),
            P(("dp", "fsdp")),
            P("fsdp", "dp"),
            P(("dp", "fsdp")),
            P("fsdp", "dp"),
            P(("dp", "fsdp")),
            P("fsdp", "dp"),
            P(("dp", "fsdp"), None),
        ),
        out_specs=(
            P(("dp", "fsdp"), None),
            P(("dp", "fsdp"), None),
            P(("dp", "fsdp"), None),
            P("fsdp", "dp"),
            P(("dp", "fsdp")),
            P("fsdp", "dp"),
            P(("dp", "fsdp")),
            P("fsdp", "dp"),
            P(("dp", "fsdp")),
            P("fsdp", "dp"),
            P(("dp", "fsdp")),
            P("fsdp", "dp"),
        ),
        check_vma=False,
    )
```

```python
from functools import partial
import math

import jax
import jax.numpy as jnp
from jax import lax
from jax.experimental import pallas as pl
from jax.experimental.pallas import tpu as pltpu
from jax.sharding import PartitionSpec as P

HEADS = 16
AXES = ("dp", "fsdp")


def position_code(kept_index, side_rows, model_width):
    quarter = model_width // 4
    exponent = jnp.arange(quarter, dtype=jnp.float32) / quarter
    frequency = 1.0 / 10000.0**exponent
    column = (kept_index % side_rows).astype(jnp.float32)[:, None] * frequency[None, :]
    line_pos = (kept_index // side_rows).astype(jnp.float32)[:, None] * frequency[None, :]
    return jnp.concatenate(
        [jnp.sin(column), jnp.cos(column), jnp.sin(line_pos), jnp.cos(line_pos)], axis=1
    )


def layer_norm(values):
    center = values - jnp.mean(values, axis=-1, keepdims=True)
    return center * lax.rsqrt(jnp.mean(center * center, axis=-1, keepdims=True) + 1e-06)


def norm_modulate(values, shift_rows, scale_rows):
    return layer_norm(values) * (1.0 + scale_rows) + shift_rows


def matmul_nt(first_matrix, second_matrix):
    return lax.dot_general(
        first_matrix, second_matrix, (((1,), (1,)), ((), ())), preferred_element_type=jnp.float32
    )


def matmul_tn(first_matrix, second_matrix):
    return lax.dot_general(
        first_matrix, second_matrix, (((0,), (0,)), ((), ())), preferred_element_type=jnp.float32
    )


def attend_forward(query_bf, key_bf, value_bf, segment, head_count):
    row_count, model_width = query_bf.shape
    head_size = model_width // head_count
    block_rows = min(row_count, 512)
    block_count = row_count // block_rows
    score_scale = 1.0 / math.sqrt(head_size)
    key_heads = key_bf.reshape(row_count, head_count, head_size)
    value_heads = value_bf.reshape(row_count, head_count, head_size)

    def forward_block(block_index):
        query_rows = query_bf.reshape(block_rows, head_count, head_size)
        same_image = segment[:, None] == segment[None, :]
        scores = (
            jnp.einsum("qhd,khd->hqk", query_rows, key_heads, preferred_element_type=jnp.float32)
            * score_scale
        )
        scores = jnp.where(same_image[None], scores, -1e30)
        highest = jnp.max(scores, axis=2, keepdims=True)
        powers = jnp.exp(scores - highest)
        totals = jnp.sum(powers, axis=2, keepdims=True)
        probs_bf = (powers / totals).astype(jnp.bfloat16)
        attended = jnp.einsum(
            "hqk,khd->qhd", probs_bf, value_heads, preferred_element_type=jnp.float32
        )
        return (attended.reshape(block_rows, model_width), (highest + jnp.log(totals))[:, :, 0])

    attended, log_totals = lax.map(forward_block, jnp.arange(block_count, dtype=jnp.int32))
    return (attended.reshape(row_count, model_width), log_totals)


def attend_backward(query_bf, key_bf, value_bf, attended_grad, segment, log_totals, head_count):
    row_count, model_width = query_bf.shape
    head_size = model_width // head_count
    block_rows = min(row_count, 512)
    block_count = row_count // block_rows
    score_scale = 1.0 / math.sqrt(head_size)
    key_heads = key_bf.reshape(row_count, head_count, head_size)
    value_heads = value_bf.reshape(row_count, head_count, head_size)

    def backward_block(running, pieces):
        key_sum, value_sum = running
        block_index, log_rows = pieces
        query_rows = query_bf.reshape(block_rows, head_count, head_size)
        grad_rows = attended_grad.reshape(block_rows, head_count, head_size)
        same_image = segment[:, None] == segment[None, :]
        scores = (
            jnp.einsum("qhd,khd->hqk", query_rows, key_heads, preferred_element_type=jnp.float32)
            * score_scale
        )
        scores = jnp.where(same_image[None], scores, -1e30)
        probs = jnp.exp(scores - log_rows[:, :, None])
        probs_bf = probs.astype(jnp.bfloat16)
        prob_grad = jnp.einsum(
            "qhd,khd->hqk", grad_rows, value_heads, preferred_element_type=jnp.float32
        )
        row_inner = jnp.sum(probs * prob_grad, axis=2, keepdims=True)
        score_grad = (probs * (prob_grad - row_inner)).astype(jnp.bfloat16)
        query_grad = (
            jnp.einsum("hqk,khd->qhd", score_grad, key_heads, preferred_element_type=jnp.float32)
            * score_scale
        )
        key_sum = (
            key_sum
            + jnp.einsum("hqk,qhd->khd", score_grad, query_rows, preferred_element_type=jnp.float32)
            * score_scale
        )
        value_sum = value_sum + jnp.einsum(
            "hqk,qhd->khd", probs_bf, grad_rows, preferred_element_type=jnp.float32
        )
        return ((key_sum, value_sum), query_grad.reshape(block_rows, model_width))

    empty_sum = jnp.zeros((row_count, head_count, head_size), jnp.float32)
    sums, query_grad = lax.scan(
        backward_block,
        (empty_sum, empty_sum),
        (jnp.arange(block_count, dtype=jnp.int32), log_totals),
    )
    return (
        query_grad.reshape(row_count, model_width),
        sums[0].reshape(row_count, model_width),
        sums[1].reshape(row_count, model_width),
    )


def on_box():
    return lax.axis_size("dp") == 4 and lax.axis_size("fsdp") == 8


def neighbour(index, axis):
    plane, line = index // 8, index % 8
    if axis == "x":
        plane ^= 1
    elif axis == "y":
        plane ^= 2
    elif axis == "core":
        line ^= 1
    else:
        line = (line - 2 * axis) % 8
    return plane * 8 + line


def swap(values, axis):
    return lax.ppermute(values, AXES, [(index, neighbour(index, axis)) for index in range(32)])


HALF_ORDERS = (("x", 1, "y", 2), ("y", 2, "x", 1))


def place():
    plane, line = lax.axis_index("dp"), lax.axis_index("fsdp")
    return plane, line // 2, line % 2


def flipped(plane, flip):
    if flip % 2:
        plane = plane + 1 - 2 * (plane % 2)
    if flip // 2:
        plane = plane + 2 - 4 * (plane // 2)
    return plane


def pick(values, index):
    return lax.dynamic_index_in_dim(values, index, axis=0, keepdims=False)


def gather_blocks(attn_weight, proj_weight, up_weight, down_weight):
    parts = lax.axis_size("dp")
    attn, proj, up, down = [
        lax.all_gather(lax.all_gather(weight, "dp", axis=1, tiled=True), "fsdp", axis=0, tiled=True)
        for weight in (attn_weight, proj_weight, up_weight, down_weight)
    ]
    width = attn.shape[0]

    def by_block(weight):
        return weight.reshape(weight.shape[0], parts, -1).transpose(1, 0, 2)

    joined = jnp.concatenate([by_block(attn), by_block(proj)], axis=2)
    return joined, by_block(up), by_block(down.T.reshape(width, -1))


def scatter_whole(gradient):
    part = lax.psum_scatter(
        gradient.astype(jnp.bfloat16), "dp", scatter_dimension=1, tiled=True
    ).astype(jnp.float32)
    return lax.psum_scatter(part, "fsdp", scatter_dimension=0, tiled=True)


def scatter_rows(pairs):
    return [
        scatter_whole(matmul_tn(left, right.transpose(1, 0, 2).reshape(left.shape[0], -1)))
        for left, right in pairs
    ]


def trade(one_for_all, values, out, send_sems, recv_sems):
    planes, lines = lax.axis_size("dp"), lax.axis_size("fsdp")
    count = planes * lines
    me = lax.axis_index("dp") * lines + lax.axis_index("fsdp")

    def device(index):
        return (index // lines, index % lines)

    def chunk(index):
        return values if one_for_all else values.at[index]

    barrier = pltpu.get_barrier_semaphore()

    @pl.loop(1, count)
    def _(step):
        pl.semaphore_signal(
            barrier,
            inc=1,
            device_id=device((me + step) % count),
            device_id_type=pl.DeviceIdType.MESH,
        )

    pl.semaphore_wait(barrier, count - 1)

    @pl.loop(1, count)
    def _(step):
        peer = (me + step) % count
        pltpu.make_async_remote_copy(
            src_ref=chunk(peer),
            dst_ref=out.at[me],
            send_sem=send_sems.at[step],
            recv_sem=recv_sems.at[step],
            device_id=device(peer),
            device_id_type=pl.DeviceIdType.MESH,
        ).start()

    if one_for_all:
        out[me] = values[...]
    else:
        out[me] = values[me]

    @pl.loop(1, count)
    def _(step):
        peer = (me + step) % count
        copy = pltpu.make_async_remote_copy(
            src_ref=chunk(peer),
            dst_ref=out.at[(me + count - step) % count],
            send_sem=send_sems.at[step],
            recv_sem=recv_sems.at[step],
            device_id=device(peer),
            device_id_type=pl.DeviceIdType.MESH,
        )
        copy.wait()


def exchange(values, collective_id, one_for_all=False):
    count = lax.axis_size("dp") * lax.axis_size("fsdp")
    chunk = values.shape[-2:]
    size = count * chunk[0] * chunk[1] * values.dtype.itemsize
    return pl.pallas_call(
        partial(trade, one_for_all),
        out_shape=jax.ShapeDtypeStruct((count,) + chunk, values.dtype),
        in_specs=[pl.BlockSpec(memory_space=pltpu.VMEM)],
        out_specs=pl.BlockSpec(memory_space=pltpu.VMEM),
        scratch_shapes=[pltpu.SemaphoreType.DMA((count,)), pltpu.SemaphoreType.DMA((count,))],
        compiler_params=pltpu.CompilerParams(
            collective_id=collective_id,
            has_side_effects=True,
            vmem_limit_bytes=3 * size + 4 * 2**20,
        ),
        cost_estimate=pl.CostEstimate(flops=0, bytes_accessed=8 * size, transcendentals=0),
    )(values)


def gather_small(silu_bf, vectors):
    flat = jnp.concatenate([silu_bf.reshape(-1), *vectors])
    width = -(-flat.shape[0] // 2048) * 128
    flat = jnp.pad(flat, (0, 16 * width - flat.shape[0])).reshape(16, width)
    everyone = exchange(flat, 0, one_for_all=True)
    everyone = everyone.reshape(everyone.shape[0], -1)
    begin = silu_bf.size
    silu_all = everyone[:, :begin].reshape(-1, silu_bf.shape[1])
    found = []
    for vector in vectors:
        found.append(everyone[:, begin : begin + vector.shape[0]].reshape(-1))
        begin += vector.shape[0]
    return silu_all, found


def silu_columns(silu_all, ada_weight):
    rows = ada_weight.shape[0]
    return lax.dynamic_slice_in_dim(silu_all, lax.axis_index("fsdp") * rows, rows, axis=1)


def modulate_slots(silu_all, ada_weight, ada_bias):
    planes, lines = lax.axis_size("dp"), lax.axis_size("fsdp")
    columns = ada_weight.shape[1]
    slots = silu_all.shape[0] // (planes * lines)
    silu_part = silu_columns(silu_all, ada_weight)
    term = jnp.dot(silu_part, ada_weight, preferred_element_type=jnp.float32)
    term = exchange(term.reshape(planes * lines, slots, columns), 1)
    term = jnp.sum(term.reshape(planes, lines, slots, columns), axis=1)
    modulation = term.transpose(1, 0, 2).reshape(slots, planes * columns)
    return modulation + ada_bias.astype(jnp.float32), silu_part


def modulation_back(modulation_grad, silu_part, ada_weight, terms):
    planes, lines = lax.axis_size("dp"), lax.axis_size("fsdp")
    devices = planes * lines
    slots = modulation_grad.shape[0]
    rows, columns = ada_weight.shape
    cut = modulation_grad.reshape(slots, planes, columns).transpose(1, 0, 2)
    cut = cut.reshape(planes, 1, 16, slots * columns // 16)
    cut = jnp.broadcast_to(cut, (planes, lines) + cut.shape[2:])
    cut = exchange(cut.reshape((devices,) + cut.shape[2:]), 2)
    return modulation_ends(cut.reshape(devices * slots, columns), silu_part, ada_weight, terms)


def modulation_ends(cut, silu_part, ada_weight, terms):
    planes, lines = lax.axis_size("dp"), lax.axis_size("fsdp")
    devices = planes * lines
    rows, columns = ada_weight.shape
    slots = cut.shape[0] // devices
    ada_grad = matmul_tn(silu_part, cut)
    sums = jnp.sum(cut, axis=0, dtype=jnp.float32)
    bias_width = columns // lines
    ada_bias_grad = lax.dynamic_slice_in_dim(sums, lax.axis_index("fsdp") * bias_width, bias_width)
    silu_grad = matmul_nt(cut, ada_weight).reshape(devices, slots * rows)
    flat = jnp.concatenate([silu_grad] + [term.reshape(devices, -1) for term in terms], axis=1)
    width = -(-flat.shape[1] // 1024) * 128
    flat = jnp.pad(flat, ((0, 0), (0, 8 * width - flat.shape[1])))
    flat = exchange(flat.reshape(devices, 8, width), 3).reshape(devices, -1)
    shared = jnp.sum(flat[:, slots * rows :], axis=0)
    silu_grad = flat[:, : slots * rows].reshape(planes, lines, slots, rows).sum(axis=0)
    silu_grad = silu_grad.transpose(1, 0, 2).reshape(slots, lines * rows)
    found, begin = [], 0
    for term in terms:
        found.append(shared[begin : begin + term.shape[0] // devices])
        begin += term.shape[0] // devices
    return ada_grad, ada_bias_grad, silu_grad, found


def by_columns(values, parts):
    rows, columns = values.shape
    return values.reshape(rows, parts, columns // parts).transpose(1, 0, 2)


SLOPE = math.sqrt(2.0 / math.pi)
WINDOW = 512


def mm(left, right):
    return jnp.dot(left, right, preferred_element_type=jnp.float32)


def shaped(dims, kind=jnp.float32):
    return jax.ShapeDtypeStruct(dims, kind)


def by_rows(count, step, body):
    @pl.loop(0, count // step)
    def _(index):
        body(pl.ds(pl.multiple_of(index * step, step), step))


def by_groups(count, step, body):
    @pl.loop(0, count // step)
    def _(index):
        body(pl.ds(pl.multiple_of(index * step, step), step), index * step // 128)


def lane_index(rows, lanes):
    return lax.broadcasted_iota(jnp.int32, (rows, lanes), 1)


def window_of(block, width, total, span):
    begin = min(block * width // 128 * 128, total - span)
    return begin, block * width - begin


def group_row(table, group, column, width):
    return table[pl.ds(group, 1), column * width : (column + 1) * width]


def add_group(out, group, value):
    out[pl.ds(group, 1), :] += jnp.sum(value, axis=0, keepdims=True)


def centred(value):
    center = value - jnp.mean(value, axis=-1, keepdims=True)
    scale = lax.rsqrt(jnp.mean(center * center, axis=-1, keepdims=True) + 1e-06)
    return center * scale, scale


def norm_back(normed, scale, grad):
    return scale * (
        grad
        - jnp.mean(grad, axis=-1, keepdims=True)
        - normed * jnp.mean(grad * normed, axis=-1, keepdims=True)
    )


def head_window(head, size, total):
    begin = jnp.minimum(head * size // 128 * 128, total - 256)
    begin = pl.multiple_of(begin, 128)
    lane = lane_index(1, 256)
    offset = head * size - begin
    return begin, (lane >= offset) & (lane < offset + size)


def far_device(plane, depth, core):
    return (plane, depth * 2 + core)


class Gather:
    def __init__(self, shards, wholes, send_sems, recv_sems, local_sems):
        self.shards, self.wholes = shards, wholes
        self.send_sems, self.recv_sems, self.local_sems = send_sems, recv_sems, local_sems
        self.plane, self.depth, self.core = place()
        self.started = []
        self.kept = []
        self.counts = [0, 0, 0]

    def partners(self):
        return [
            far_device(flipped(self.plane, 1), self.depth, self.core),
            far_device(flipped(self.plane, 2), self.depth, self.core),
            far_device(self.plane, self.depth, 1 - self.core),
        ]

    def back(self, entry):
        low, high = (3 - self.depth) // 3, self.depth // 3
        return (0, 1 + 2 * low, 3 - low - high, 2 - low + high)[entry]

    def spot(self, weight, flip, back, other=False):
        plane, depth = flipped(self.plane, flip), (self.depth + 4 - back) % 4
        core = 1 - self.core if other else self.core
        if weight < 2:
            return self.wholes[weight].at[plane, depth, core]
        return self.wholes[weight].at[depth, plane, core]

    def send(self, weight, source, target, partner, kind, entry):
        copy = pltpu.make_async_remote_copy(
            src_ref=source,
            dst_ref=target,
            send_sem=self.send_sems.at[weight, self.counts[weight]],
            recv_sem=self.recv_sems.at[weight, kind, entry],
            device_id=partner,
            device_id_type=pl.DeviceIdType.MESH,
        )
        self.counts[weight] += 1
        copy.start()
        self.started.append(copy)

    def arrive(self, weight, region, kind, entry):
        pltpu.make_async_remote_copy(
            src_ref=region,
            dst_ref=region,
            send_sem=self.send_sems.at[weight, 0],
            recv_sem=self.recv_sems.at[weight, kind, entry],
            device_id=self.partners()[2],
            device_id_type=pl.DeviceIdType.MESH,
        ).wait_recv()

    def pass_on(self, weight, source, flip, entry):
        back = self.back(entry)
        target = self.spot(weight, flip, back)
        beside = self.partners()
        if flip == 0 or (flip == 2 and entry % 2 == 1):
            self.send(weight, source, target, beside[0], 1 if flip == 0 else 3, back)
        if flip == 0 or (flip == 1 and entry % 2 == 0):
            self.send(weight, source, target, beside[1], 2 if flip == 0 else 3, back)
        self.send(weight, source, target, beside[2], 4 + flip, back)

    def keep(self, weight):
        keep = pltpu.make_async_copy(
            self.shards[weight], self.spot(weight, 0, 0), self.local_sems.at[weight]
        )
        keep.start()
        self.kept.append(keep)

    def open_plane(self, weight, entry):
        self.pass_on(weight, self.spot(weight, 0, self.back(entry)), 0, entry)

    def along(self, weight, source, back, step, number, start):
        beyond = self.depth + step

        @pl.when((beyond >= 0) & (beyond <= 3))
        def _():
            copy = pltpu.make_async_remote_copy(
                src_ref=source,
                dst_ref=self.spot(weight, 0, back),
                send_sem=self.send_sems.at[weight, number],
                recv_sem=self.recv_sems.at[weight, 0, (back + step + 4) % 4],
                device_id=far_device(self.plane, (beyond + 4) % 4, self.core),
                device_id_type=pl.DeviceIdType.MESH,
            )
            if start:
                copy.start()
            else:
                copy.wait_send()

    def line_sends(self, weight, entry, start):
        back = self.back(entry)
        if entry == 0:
            for number, step in enumerate((1, -1)):
                self.along(weight, self.spot(weight, 0, 0), 0, step, 32 + number, start)
        else:
            step = 2 * ((self.depth - back + 4) // 4) - 1
            self.along(weight, self.spot(weight, 0, back), back, step, 33 + entry, start)

    def open_line(self, weight):
        self.line_sends(weight, 0, True)

    def line_partners(self):
        return [far_device(self.plane, (self.depth + d) % 4, self.core) for d in (1, 2, 3)]

    def on_line(self, weight, entry):
        region = self.spot(weight, 0, self.back(entry))
        self.arrive(weight, region, 0, self.back(entry))
        self.line_sends(weight, entry, True)

    def on_plane(self, weight, flip, entry):
        back = self.back(entry)
        region = self.spot(weight, flip, back)
        self.arrive(weight, region, flip, back)
        self.pass_on(weight, region, flip, entry)

    def plane_steps(self, weight):
        found = []
        for entry in range(4):
            found.append(partial(self.on_plane, weight, 1, entry))
            found.append(partial(self.on_plane, weight, 2, entry))
            if entry:
                found.append(partial(self.on_plane, weight, 3, entry - 1))
        found.append(partial(self.on_plane, weight, 3, 3))
        return found

    def ready(self, weight, entries=(0, 1, 2, 3)):
        for flip in range(4):
            for back in [self.back(entry) for entry in entries]:
                self.arrive(weight, self.spot(weight, flip, back, True), 4 + flip, back)

    def finish(self):
        for copy in self.started:
            copy.wait_send()


def greet(partners):
    barrier = pltpu.get_barrier_semaphore()
    for partner in partners:
        pl.semaphore_signal(
            barrier, inc=1, device_id=partner, device_id_type=pl.DeviceIdType.MESH
        )
    pl.semaphore_wait(barrier, len(partners))


def trade_along(axis, values, land, send_sems, recv_sems, start, same=False):
    count, me = lax.axis_size(axis), lax.axis_index(axis)

    @pl.loop(1, count)
    def _(step):
        peer = (me + step) % count
        target = me if start else (me + count - step) % count
        if axis == "dp":
            device = (peer, lax.axis_index("fsdp"))
        else:
            device = (lax.axis_index("dp"), peer)
        copy = pltpu.make_async_remote_copy(
            src_ref=values if same else values.at[peer],
            dst_ref=land.at[target],
            send_sem=send_sems.at[step],
            recv_sem=recv_sems.at[step],
            device_id=device,
            device_id_type=pl.DeviceIdType.MESH,
        )
        if start:
            copy.start()
        else:
            copy.wait()

    if start:
        land[me] = values[...] if same else values[me]


def greet_all():
    planes, lines = lax.axis_size("dp"), lax.axis_size("fsdp")
    count = planes * lines
    me = lax.axis_index("dp") * lines + lax.axis_index("fsdp")
    barrier = pltpu.get_barrier_semaphore()

    @pl.loop(1, count)
    def _(step):
        peer = (me + step) % count
        pl.semaphore_signal(
            barrier,
            inc=1,
            device_id=(peer // lines, peer % lines),
            device_id_type=pl.DeviceIdType.MESH,
        )

    pl.semaphore_wait(barrier, count - 1)


def spread(axis_peer, values, land, send_sems, recv_sems, start):
    planes, lines = lax.axis_size("dp"), lax.axis_size("fsdp")
    count = planes * lines
    me = lax.axis_index("dp") * lines + lax.axis_index("fsdp")

    @pl.loop(1, count)
    def _(step):
        peer = (me + step) % count
        target = me if start else (me + count - step) % count
        copy = pltpu.make_async_remote_copy(
            src_ref=values.at[peer % lines] if axis_peer else values,
            dst_ref=land.at[target],
            send_sem=send_sems.at[step],
            recv_sem=recv_sems.at[step],
            device_id=(peer // lines, peer % lines),
            device_id_type=pl.DeviceIdType.MESH,
        )
        if start:
            copy.start()
        else:
            copy.wait()

    if start:
        land[me] = values[me % lines] if axis_peer else values[...]


def opening_kernel(
    silu,
    flat,
    ada_weight,
    joined_shard,
    up_shard,
    down_shard,
    joined_whole,
    up_whole,
    down_whole,
    silu_land,
    flat_land,
    plane_land,
    product,
    term,
    term_land,
    plane_term,
    send_sems,
    recv_sems,
    local_sems,
    spread_sems,
    line_sems,
    plane_sems,
):
    gather = Gather(
        (joined_shard, up_shard, down_shard),
        (joined_whole, up_whole, down_whole),
        send_sems,
        recv_sems,
        local_sems,
    )
    for weight in range(3):
        gather.keep(weight)
    greet_all()
    silu_trade = (True, silu, silu_land, spread_sems.at[0], spread_sems.at[1])
    flat_trade = (False, flat, flat_land, spread_sems.at[2], spread_sems.at[3])
    line_trade = (term, term_land, line_sems.at[0], line_sems.at[1])
    plane_trade = (plane_term, plane_land, plane_sems.at[0], plane_sems.at[1])
    spread(*silu_trade, True)
    for copy in gather.kept:
        copy.wait()
    gather.open_line(0)
    gather.open_plane(0, 0)
    spread(*flat_trade, True)
    for entry in (1, 2, 3):
        gather.on_line(0, entry)
        gather.open_plane(0, entry)
    gather.open_line(1)
    gather.open_plane(1, 0)
    spread(*silu_trade, False)
    devices, tall, rows = silu_land.shape
    product[...] = mm(silu_land[...].reshape(devices * tall, rows), ada_weight[...])
    lines, planes, slots = term.shape[:3]
    for line in range(lines):
        for plane in range(planes):
            begin = (plane * lines + line) * tall
            term[line, plane] = product[begin : begin + slots, :]
    trade_along("fsdp", *line_trade, True)
    first, second = gather.plane_steps(0), gather.plane_steps(1)
    for step in first[:2]:
        step()
    gather.on_line(1, 1)
    for step in first[2:5]:
        step()
    gather.on_line(1, 2)
    gather.open_plane(1, 1)
    trade_along("fsdp", *line_trade, False)
    total = term_land[0]
    for line in range(1, lines):
        total = total + term_land[line]
    plane_term[...] = total
    trade_along("dp", *plane_trade, True)
    for step in first[5:8]:
        step()
    gather.on_line(1, 3)
    for step in first[8:] + second[:5]:
        step()
    gather.on_plane(1, 3, 1)
    spread(*flat_trade, False)
    trade_along("dp", *plane_trade, False)
    gather.ready(0)
    gather.ready(1, (0, 1))
    gather.finish()
    for weight in range(2):
        for entry in range(4):
            gather.line_sends(weight, entry, False)


def opening(silu, flat, ada_weight, shards):
    rows, width = shards[1].shape
    lines, tall, short = silu.shape
    slots, part = 4, ada_weight.shape[1]
    whole = shaped((4, 4, 2, rows, width), jnp.bfloat16)
    vmem, away = pl.BlockSpec(memory_space=pltpu.VMEM), pl.BlockSpec(memory_space=pl.ANY)
    return pl.pallas_call(
        opening_kernel,
        out_shape=[
            whole,
            whole,
            whole,
            shaped((4 * lines, tall, short), jnp.bfloat16),
            shaped((4 * lines,) + flat.shape, jnp.bfloat16),
            shaped((4, slots, part)),
        ],
        in_specs=[vmem] * 6,
        out_specs=[away] * 3 + [vmem] * 3,
        scratch_shapes=[
            pltpu.VMEM((4 * lines * tall, part), jnp.float32),
            pltpu.VMEM((lines, 4, slots, part), jnp.float32),
            pltpu.VMEM((lines, 4, slots, part), jnp.float32),
            pltpu.VMEM((4, slots, part), jnp.float32),
            pltpu.SemaphoreType.DMA((3, 40)),
            pltpu.SemaphoreType.DMA((3, 8, 4)),
            pltpu.SemaphoreType.DMA((3,)),
            pltpu.SemaphoreType.DMA((4, 32)),
            pltpu.SemaphoreType.DMA((2, 8)),
            pltpu.SemaphoreType.DMA((2, 4)),
        ],
        compiler_params=pltpu.CompilerParams(
            collective_id=7, has_side_effects=True, vmem_limit_bytes=32 * 2**20
        ),
        cost_estimate=pl.CostEstimate(flops=10**8, bytes_accessed=10**8, transcendentals=0),
    )(silu, flat, ada_weight, *shards)


def forward_kernel(
    tokens,
    places,
    codes,
    slots,
    slot_line,
    group_slots,
    plane_land,
    ada_bias,
    joined_bias,
    out_bias,
    up_bias,
    joined_whole,
    up_start,
    down_start,
    up_whole,
    down_whole,
    joined,
    start,
    table,
    normed_t,
    attended_t,
    normed2_t,
    stats,
    branch,
    middle,
    hidden,
    before,
    room,
    product,
    wide_room,
    bar,
    before_room,
    normed,
    attended,
    normed2,
    strip,
    all_modulation,
    send_sems,
    recv_sems,
    load_sems,
    store_sems,
):
    gather = Gather(
        (None, None, None), (None, up_whole, down_whole), send_sems, recv_sems, None
    )
    loads = [
        pltpu.make_async_copy(joined_whole.at[block], room.at[block], load_sems.at[block])
        for block in range(4)
    ]
    for load in loads:
        load.start()
    greet(gather.partners() + gather.line_partners())
    gather.open_line(2)
    for weight, entry in ((1, 2), (1, 3), (2, 0)):
        gather.open_plane(weight, entry)
    rows, width = tokens.shape
    lane = lane_index(rows, codes.shape[0])
    spot = jnp.where(lane % 64 < 32, places[:, 0:1], places[:, 1:2])
    hot = jnp.where(lane % 32 == spot, 1.0, 0.0).astype(jnp.bfloat16)
    start[...] = mm(hot, codes[...]) + wide(tokens[...])
    strip[...] = jnp.zeros_like(strip)
    slot_count, part = plane_land.shape[1:]
    for plane in range(4):
        strip[:slot_count, :part] = plane_land[plane]
        shift = plane * part % 128
        begin = plane * part - shift
        moved = pltpu.roll(strip[...], shift, 1) if shift else strip[...]
        lane = lane_index(8, strip.shape[1])
        span = pl.ds(begin, strip.shape[1])
        inside = (lane >= shift) & (lane < shift + part)
        all_modulation[:, span] = jnp.where(inside, moved, all_modulation[:, span])
    total = jnp.zeros(table.shape, jnp.float32)
    for slot in range(slot_count):
        row = all_modulation[slot : slot + 1, : table.shape[1]] + ada_bias[...]
        total = total + jnp.where(group_slots[...] == slot, row, 0.0)
    table[...] = total

    def norm_first(at, group):
        hat, _ = centred(start[at, :])
        value = hat * (1.0 + group_row(table, group, 1, width)) + group_row(table, group, 0, width)
        normed[at, :] = low_bits(value)

    by_groups(rows, 64, norm_first)
    line_step, plane_open, plane_step = (
        partial(partial, method) for method in (gather.on_line, gather.open_plane, gather.on_plane)
    )
    later = [line_step(2, 1), plane_open(2, 1), plane_step(1, 1, 2), plane_step(1, 2, 2)]
    later += [line_step(2, 2), plane_open(2, 2), plane_step(1, 1, 3), plane_step(1, 2, 3)]
    later += [line_step(2, 3), plane_open(2, 3), plane_step(1, 3, 2), plane_step(1, 3, 3)]
    later += gather.plane_steps(2)

    def tick(count=1):
        for _ in range(count):
            if later:
                later.pop(0)()

    normed_t[...] = normed[...].T
    columns = joined.shape[1] // 4
    tick(2)
    span = product.shape[1]
    for block in range(4):
        loads[block].wait()
        product[...] = mm(normed[...], room[block].reshape(width, width)[:, :span])
        begin, offset = window_of(block, columns, joined.shape[1], span)

        def put(at):
            moved = product[at, :]
            if offset:
                moved = pltpu.roll(moved, offset, 1)
            lane = lane_index(moved.shape[0], span)
            inside = (lane >= offset) & (lane < offset + columns)
            wide_room[at, begin : begin + span] = jnp.where(
                inside, moved, wide_room[at, begin : begin + span]
            )

        by_rows(rows, 64, put)
        tick(2)

    def settle(at):
        joined[at, :] = (wide_room[at, :] + joined_bias[...]).astype(jnp.bfloat16)

    by_rows(rows, 64, settle)
    bar[...] = jnp.where(slots[...] == slot_line[...], 0.0, -1e30)
    stats[...] = jnp.zeros_like(stats)
    head_size = width // HEADS
    scale = 1.0 / math.sqrt(head_size)
    for group in range(8):

        @pl.loop(2 * group, 2 * group + 2)
        def _(head):
            at, inside = head_window(head, head_size, width)
            query = jnp.where(inside, joined[:, pl.ds(at, 256)], 0.0)
            key = joined[:, pl.ds(pl.multiple_of(at + width, 128), 256)]
            value = joined[:, pl.ds(pl.multiple_of(at + 2 * width, 128), 256)]
            scores = matmul_nt(query, key) * scale + bar[...]
            highest = jnp.max(scores, axis=1, keepdims=True)
            powers = jnp.exp(scores - highest)
            totals = jnp.sum(powers, axis=1, keepdims=True)
            probs = (powers * (1.0 / totals)).astype(jnp.bfloat16)
            found = mm(probs, value)
            wide_room[:, pl.ds(at, 256)] = jnp.where(inside, found, wide_room[:, pl.ds(at, 256)])
            lane = lane_index(rows, 128)
            stats[...] = jnp.where(lane == head, highest + jnp.log(totals), stats[...])

        tick(1)

    attended[...] = wide_room[:, :width].astype(jnp.bfloat16)
    columns = width // 4
    for block in range(4):
        product[:, :WINDOW] = mm(attended[...], room[block].reshape(width, width)[:, width - WINDOW :])
        begin, offset = window_of(block, columns, width, WINDOW)

        def put(at):
            moved = product[at, :WINDOW]
            if offset != WINDOW - columns:
                moved = pltpu.roll(moved, columns + offset, 1)
            lane = lane_index(moved.shape[0], WINDOW)
            inside = (lane >= offset) & (lane < offset + columns)
            branch[at, begin : begin + WINDOW] = jnp.where(
                inside, moved, branch[at, begin : begin + WINDOW]
            )

        by_rows(rows, 64, put)
        tick()

    def combine(at, group):
        value = branch[at, :] + out_bias[...]
        branch[at, :] = value
        value = start[at, :] + group_row(table, group, 2, width) * value
        middle[at, :] = value
        hat, _ = centred(value)
        value = hat * (1.0 + group_row(table, group, 4, width)) + group_row(table, group, 3, width)
        normed2[at, :] = value.astype(jnp.bfloat16)

    by_groups(rows, 64, combine)
    normed2_t[...] = normed2[...].T
    attended_t[...] = attended[...].T
    while len(later) > 12:
        tick()
    gather.ready(1, (2, 3))
    loads = [
        pltpu.make_async_copy(up_whole.at[block], room.at[block], load_sems.at[block])
        for block in range(4)
    ]
    for load in loads:
        load.start()
    stores = [None, None]
    for block in range(4):
        loads[block].wait()
        slot = block % 2
        if stores[slot] is not None:
            stores[slot].wait()
        before_room[slot] = mm(normed2[...], room[block].reshape(width, width)) + up_bias[block]
        stores[slot] = pltpu.make_async_copy(
            before_room.at[slot], before.at[block], store_sems.at[slot]
        )
        stores[slot].start()

        def act(some):
            value = before_room[slot, some, :]
            bend = 1.0 + jnp.tanh(SLOPE * (value + 0.044715 * (value * value * value)))
            hidden[block, some, :] = (value * (0.5 * bend)).astype(jnp.bfloat16)

        by_rows(rows, 64, act)
        tick(3)
    while later:
        tick()
    for store in stores:
        store.wait()
    gather.ready(2)
    gather.finish()
    for entry in range(4):
        gather.line_sends(2, entry, False)


def forward(tokens, places, codes, slots, group_slots, modulation, ada_bias, biases, wholes):
    rows, width = tokens.shape
    deep = width // 8
    whole = shaped((4, 4, 2, deep, width), jnp.bfloat16)
    vmem, away = pl.BlockSpec(memory_space=pltpu.VMEM), pl.BlockSpec(memory_space=pl.ANY)
    part = modulation.shape[2]
    return pl.pallas_call(
        forward_kernel,
        out_shape=[
            whole,
            whole,
            shaped((rows, 3 * width), jnp.bfloat16),
            shaped((rows, width)),
            shaped((8, 4 * part)),
            shaped((width, rows), jnp.bfloat16),
            shaped((width, rows), jnp.bfloat16),
            shaped((width, rows), jnp.bfloat16),
            shaped((rows, 128)),
            shaped((rows, width)),
            shaped((rows, width)),
            shaped((4, rows, width), jnp.bfloat16),
            shaped((4, rows, width)),
        ],
        in_specs=[vmem] * 11 + [away] * 3,
        out_specs=[away] * 2 + [vmem] * 10 + [away],
        input_output_aliases={12: 0, 13: 1},
        scratch_shapes=[
            pltpu.VMEM((4, 4, 2, deep, width), jnp.bfloat16),
            pltpu.VMEM((rows, 1024), jnp.float32),
            pltpu.VMEM((rows, 3 * width), jnp.float32),
            pltpu.VMEM((rows, rows), jnp.float32),
            pltpu.VMEM((2, rows, width), jnp.float32),
            pltpu.VMEM((rows, width), jnp.bfloat16),
            pltpu.VMEM((rows, width), jnp.bfloat16),
            pltpu.VMEM((rows, width), jnp.bfloat16),
            pltpu.VMEM((8, -(-part // 128) * 128), jnp.float32),
            pltpu.VMEM((8, 4 * part + 128), jnp.float32),
            pltpu.SemaphoreType.DMA((3, 40)),
            pltpu.SemaphoreType.DMA((3, 8, 4)),
            pltpu.SemaphoreType.DMA((4,)),
            pltpu.SemaphoreType.DMA((2,)),
        ],
        compiler_params=pltpu.CompilerParams(
            collective_id=4, has_side_effects=True, vmem_limit_bytes=62 * 2**20
        ),
        cost_estimate=pl.CostEstimate(
            flops=2 * 10 * rows * width * width, bytes_accessed=10**8, transcendentals=0
        ),
    )(
        tokens,
        places,
        codes,
        slots.reshape(rows, 1),
        slots.reshape(1, rows),
        group_slots,
        modulation,
        ada_bias,
        *biases,
        *wholes,
    )


def low_bits(value):
    return value.astype(jnp.bfloat16)


def wide(value):
    return value.astype(jnp.float32)


class Scatter:
    def __init__(self, own, lands, stage, outs, send_sems, recv_sems, stage_sems):
        self.own, self.lands, self.stage, self.outs = own, lands, stage, outs
        self.send_sems, self.recv_sems, self.stage_sems = send_sems, recv_sems, stage_sems
        self.plane, self.depth, self.core = place()
        self.started = []
        self.counts = [0] * len(lands)
        self.queue, self.held, self.turn = [], [], 0

    def partners(self):
        found = [
            far_device(flipped(self.plane, 1), self.depth, self.core),
            far_device(flipped(self.plane, 2), self.depth, self.core),
            far_device(self.plane, self.depth, 1 - self.core),
        ]
        return found + [far_device(self.plane, (self.depth + d) % 4, self.core) for d in (1, 2, 3)]

    def sending(self, weight, source, index, partner, number):
        return pltpu.make_async_remote_copy(
            src_ref=source,
            dst_ref=self.lands[weight].at[index],
            send_sem=self.send_sems.at[weight, number],
            recv_sem=self.recv_sems.at[weight, index],
            device_id=self.partners()[partner],
            device_id_type=pl.DeviceIdType.MESH,
        )

    def send(self, weight, source, index, partner):
        copy = self.sending(weight, source, index, partner, self.counts[weight])
        self.counts[weight] += 1
        copy.start()
        return copy

    def term(self, weight, flip, back, rows_of, line_rows):
        plane, depth = flipped(self.plane, flip), (self.depth + 4 - back) % 4
        base = (depth if line_rows else plane) * 2
        self.own[weight % 2, flip, back] = rows_of(base + self.core)[...]
        return self.send(weight, rows_of(base + 1 - self.core), flip * 4 + back, 2)

    def open(self, weight, part, order=(2, 1, 3, 0)):
        for back in order:
            axis, near, far = (0, 1, 2) if back % 2 == 0 else (1, 2, 1)
            jobs = []
            if part == "sent":
                for flip in (3, near):
                    goes = (flip, back, 16 + (4 if flip == 3 else 0) + back, axis)
                    jobs.append((flip * 4 + back, flip, goes))
            elif part == "kept":
                jobs = [(flip * 4 + back, flip, None) for flip in (far, 0)]
            elif part == "first":
                jobs = [(20 + back, far, (far, back, 24 + back, 1 - axis)), (16 + back, 0, None)]
            elif part == "second":
                jobs = [(24 + back, 0, (0, back, 28 + back, 2 + 4 - back) if back else None)]
            elif back:
                self.queue.append((weight, 28 + back, 0, 0, None))
            for index, flip, goes in jobs:
                self.queue.append((weight, index, flip, back, goes))

    def fetch(self, job):
        weight, index = job[0], job[1]
        region = self.lands[weight].at[index]
        pltpu.make_async_remote_copy(
            src_ref=region,
            dst_ref=region,
            send_sem=self.send_sems.at[weight, 0],
            recv_sem=self.recv_sems.at[weight, index],
            device_id=self.partners()[2],
            device_id_type=pl.DeviceIdType.MESH,
        ).wait_recv()
        if self.stage is not None:
            self.staging(weight, index, self.turn).start()
        self.held.append((job, self.turn))
        self.turn = (self.turn + 1) % 2

    def staging(self, weight, index, turn):
        return pltpu.make_async_copy(
            self.lands[weight].at[index], self.stage.at[turn], self.stage_sems.at[turn]
        )

    def merge(self):
        (weight, index, flip, back, goes), turn = self.held.pop(0)
        if self.stage is None:
            arrived = self.lands[weight][index]
        else:
            self.staging(weight, index, turn).wait()
            arrived = self.stage[turn]
        if index >= 28:
            self.outs[weight][...] += wide(arrived)
            return
        if index == 24:
            self.outs[weight][...] = wide(self.own[weight % 2, flip, back]) + wide(arrived)
            return
        self.own[weight % 2, flip, back] = self.own[weight % 2, flip, back] + arrived
        if goes is not None:
            self.started.append((weight, goes, self.counts[weight]))
            self.send(weight, self.own.at[weight % 2, goes[0], goes[1]], goes[2], goes[3])

    def tick(self, count=1):
        for _ in range(count):
            if self.held:
                self.merge()
            if self.queue:
                self.fetch(self.queue.pop(0))
                if self.stage is None:
                    self.merge()

    def clear(self, weight, flip):
        while any(job[0] == weight and flip == 0 for job in self.queue) or any(
            held[0][0] == weight and held[0][2] == flip for held in self.held
        ):
            self.tick()
        for entry in [entry for entry in self.started if entry[0] == weight and entry[1][0] == flip]:
            self.started.remove(entry)
            self.sent(entry)

    def sent(self, entry):
        weight, (flip, back, index, partner), number = entry
        source = self.own.at[weight % 2, flip, back]
        self.sending(weight, source, index, partner, number).wait_send()

    def drain(self):
        while self.queue or self.held:
            self.tick()
        for entry in self.started:
            self.sent(entry)


def multiply_rows(out, left, right, step=384):
    @pl.loop(0, left.shape[0] // step)
    def _(index):
        at = pl.ds(pl.multiple_of(index * step, step), step)
        out[at, :] = mm(left[at, :], right[...]).astype(jnp.bfloat16)


def deep_rows(room, slot, deep):
    def rows_of(row):
        return room.at[slot, pl.ds(pl.multiple_of(row * deep, 16), deep)]

    return rows_of


def backward_kernel(
    hidden_in,
    before_in,
    joined_in,
    joined_whole,
    up_whole,
    down_whole,
    normed_in,
    attended_in,
    start_in,
    middle,
    out_grad,
    branch,
    normed_t,
    stats,
    slots,
    slot_line,
    table,
    bias,
    group_slots,
    down_land,
    up_land,
    joined_land,
    mixed,
    middle_grad,
    slot_sums,
    branch_sums,
    pre_sums,
    joined_sums,
    down_out,
    up_out,
    joined_out,
    line_land,
    windows,
    own,
    stage,
    room,
    acts,
    grads,
    grads_t,
    attended_grad,
    send_sems,
    recv_sems,
    stage_sems,
    load_sems,
    more_sems,
    mod_room,
    strip,
    plane_out,
    plane_land,
    plane_sems,
    line_sems,
):
    rows, width = middle.shape
    deep = width // 8
    scatter = Scatter(
        own,
        (down_land, up_land, joined_land),
        stage,
        (down_out, up_out, joined_out),
        send_sems,
        recv_sems,
        stage_sems,
    )
    others = [far_device(flipped(scatter.plane, flip), scatter.depth, scatter.core) for flip in (1, 2, 3)]
    others.append(scatter.partners()[2])
    for far in (1, 2, 3):
        for core in range(2):
            others.append(far_device(scatter.plane, (scatter.depth + far) % 4, core))
    greet(others)
    slot_sums[...] = jnp.zeros_like(slot_sums)
    branch_sums[...] = jnp.zeros_like(branch_sums)
    pre_sums[...] = jnp.zeros_like(pre_sums)
    joined_sums[...] = jnp.zeros_like(joined_sums)

    def dense(weights, before, total):
        plan = [(down_whole, part) for part in range(4)] * 2 + [(up_whole, part) for part in range(4)]

        def load(step):
            whole, part = plan[step]
            copy = pltpu.make_async_copy(
                whole.at[part], weights.at[step % 2], load_sems.at[step % 2]
            )
            copy.start()
            return copy

        loads = {0: load(0)}
        acting = [
            pltpu.make_async_copy(hidden_in.at[part], acts.at[part], more_sems.at[part])
            for part in range(4)
        ]
        for copy in acting:
            copy.start()

        def next_weight(step):
            if step + 1 < len(plan):
                loads[step + 1] = load(step + 1)
            loads[step].wait()
            return weights.at[step % 2]

        for part in range(4):
            acting[part].wait()
            term = matmul_nt(acts[part], next_weight(part)[...])
            total[...] = term + bias[...] if part == 0 else total[...] + term

        def settle(at, group):
            gate = group_row(table, group, 5, width)
            value = total[at, :]
            grad = wide(out_grad[at, :])
            mixed[at, :] = low_bits(middle[at, :] + gate * value)
            add_group(slot_sums.at[3], group, grad * value)
            value = low_bits(grad * gate)
            grads[at, :] = value
            branch_sums[1:2, :] += jnp.sum(wide(value), axis=0, keepdims=True)

        by_groups(rows, 64, settle)
        grads_t[...] = grads[...].T
        waits = [[], []]
        for number, back in enumerate((2, 1, 3, 0)):
            slot = number % 2
            for copy in waits[slot]:
                copy.wait_send()
            multiply_rows(room.at[slot], grads_t, acts.at[(scatter.depth + 4 - back) % 4])
            rows_of = deep_rows(room, slot, deep)
            waits[slot] = [scatter.term(0, flip, back, rows_of, False) for flip in (3, 1, 2, 0)]
        scatter.open(0, "sent")
        scatter.open(0, "kept")
        befores = [
            pltpu.make_async_copy(before_in.at[part], before.at[part % 2], more_sems.at[part])
            for part in range(4)
        ]
        befores[0].start()
        for part in range(4):
            if part < 3:
                befores[part + 1].start()
            total[...] = mm(grads[...], next_weight(4 + part)[...])
            befores[part].wait()

            def act(at):
                value = before[part % 2, at, :]
                square = value * value
                bend = jnp.tanh(SLOPE * (value + 0.044715 * (square * value)))
                slope = 0.5 * (1.0 + bend) + 0.5 * value * (1.0 - bend * bend) * (
                    SLOPE * (1.0 + 3.0 * 0.044715 * square)
                )
                value = low_bits(total[at, :] * slope)
                acts[part, at, :] = value
                pre_sums[part : part + 1, :] += jnp.sum(wide(value), axis=0, keepdims=True)

            by_rows(rows, 64, act)
            scatter.tick(4 if part else 6)
        for number, flip in enumerate((3, 1, 2, 0)):
            slot = number % 2
            for copy in waits[slot]:
                copy.wait_send()
            multiply_rows(room.at[slot], normed_t, acts.at[flipped(scatter.plane, flip)])
            rows_of = deep_rows(room, slot, deep)
            waits[slot] = [scatter.term(1, flip, back, rows_of, True) for back in (2, 1, 3, 0)]
        scatter.open(1, "sent")
        scatter.open(1, "kept")
        scatter.open(0, "first")
        scatter.open(0, "second")
        scatter.open(1, "first")
        scatter.open(1, "second")
        for part in range(4):
            term = matmul_nt(acts[part], next_weight(8 + part)[...])
            total[...] = term if part == 0 else total[...] + term
            scatter.tick(4)

        def turn(at, group):
            grad = total[at, :]
            hat, scale = centred(middle[at, :])
            add_group(slot_sums.at[1], group, grad)
            add_group(slot_sums.at[2], group, grad * hat)
            grad = grad * (1.0 + group_row(table, group, 4, width))
            grad = wide(out_grad[at, :]) + norm_back(hat, scale, grad)
            middle_grad[at, :] = grad
            add_group(slot_sums.at[0], group, grad * branch[at, :])
            value = wide(low_bits(grad * group_row(table, group, 2, width)))
            total[at, :] = value
            branch_sums[0:1, :] += jnp.sum(value, axis=0, keepdims=True)

        by_groups(rows, 64, turn)
        scatter.tick(8)
        for slot in range(2):
            for copy in waits[slot]:
                copy.wait_send()
        columns = width // 4
        span = pl.ds(width - WINDOW, WINDOW)
        sides = []
        for block in range(4):
            copy = pltpu.make_async_copy(
                joined_whole.at[block, :, span],
                weights.at[block // 2, :, pl.ds(block % 2 * WINDOW, WINDOW)],
                more_sems.at[block],
            )
            copy.start()
            sides.append(copy)
        for block in range(4):
            begin, offset = window_of(block, columns, width, WINDOW)

            def cut(at):
                moved = total[at, begin : begin + WINDOW]
                if offset != WINDOW - columns:
                    moved = pltpu.roll(moved, (2 * WINDOW - columns - offset) % WINDOW, 1)
                lane = lane_index(moved.shape[0], WINDOW)
                moved = jnp.where(lane >= WINDOW - columns, moved, 0.0)
                windows[block, at, :] = low_bits(moved)

            by_rows(rows, 64, cut)
        for block in range(4):
            sides[block].wait()
            side = weights[block // 2, :, block % 2 * WINDOW : (block % 2 + 1) * WINDOW]
            term = matmul_nt(windows[block], side)
            total[...] = term if block == 0 else total[...] + term
        attended_grad[...] = low_bits(total[...])

    pl.run_scoped(
        dense,
        pltpu.VMEM((2, width, width), jnp.bfloat16),
        pltpu.VMEM((2, rows, width), jnp.float32),
        pltpu.VMEM((rows, width), jnp.float32),
    )

    def heads(joined, found_room, bar):
        load = pltpu.make_async_copy(joined_in, joined, load_sems.at[0])
        load.start()
        size = width // HEADS
        scale = 1.0 / math.sqrt(size)
        bar[...] = jnp.where(slots[...] == slot_line[...], 0.0, -1e30)
        load.wait()
        for head_static in range(0, HEADS, 2):

            @pl.loop(head_static, head_static + 2)
            def _(head):
                begin, inside = head_window(head, size, width)
                columns = [pl.ds(pl.multiple_of(begin + part * width, 128), 256) for part in range(3)]
                query = jnp.where(inside, joined[:, columns[0]], 0.0)
                key = joined[:, columns[1]]
                value = joined[:, columns[2]]
                out_part = jnp.where(inside, attended_grad[:, columns[0]], 0.0)
                lane = lane_index(rows, 128)
                stat = jnp.sum(jnp.where(lane == head, stats[...], 0.0), axis=1, keepdims=True)
                probs = jnp.exp(matmul_nt(query, key) * scale + bar[...] - stat)
                prob_grad = matmul_nt(out_part, value)
                inner = jnp.sum(probs * prob_grad, axis=1, keepdims=True)
                score_grad = low_bits(probs * (prob_grad - inner))
                found = (
                    mm(score_grad, key) * scale,
                    matmul_tn(score_grad, query) * scale,
                    matmul_tn(low_bits(probs), out_part),
                )
                for part in range(3):
                    found_room[:, columns[part]] = jnp.where(
                        inside, found[part], found_room[:, columns[part]]
                    )

            scatter.tick((0, 0, 0, 2, 2, 2, 3, 3)[head_static // 2])

        span = 1024
        block_width = 3 * width // 4

        def add_up(at):
            joined_sums[...] += jnp.sum(wide(low_bits(found_room[at, :])), axis=0, keepdims=True)

        by_rows(rows, 64, add_up)
        for block in range(4):
            begin, offset = window_of(block, block_width, 3 * width, span)

            def cut(at):
                moved = found_room[at, begin : begin + span]
                if offset:
                    moved = pltpu.roll(moved, span - offset, 1)
                lane = lane_index(moved.shape[0], span)
                acts[block, at, :span] = low_bits(jnp.where(lane < block_width, moved, 0.0))

            by_rows(rows, 64, cut)

    pl.run_scoped(
        heads,
        pltpu.VMEM((rows, 3 * width), jnp.bfloat16),
        pltpu.VMEM((rows, 3 * width), jnp.float32),
        pltpu.VMEM((rows, rows), jnp.float32),
    )
    span = 1024

    def last(weights, attended_t, start, total):
        left = pltpu.make_async_copy(normed_in, grads_t, more_sems.at[0])
        other = pltpu.make_async_copy(attended_in, attended_t, more_sems.at[1])
        begin_copy = pltpu.make_async_copy(start_in, start, more_sems.at[2])
        for copy in (left, other, begin_copy):
            copy.start()

        def load(part):
            copy = pltpu.make_async_copy(
                joined_whole.at[part, :, pl.ds(0, span)], weights.at[part % 2], load_sems.at[part % 2]
            )
            copy.start()
            return copy

        loads = [load(0), load(1)]
        left.wait()
        other.wait()
        low, high = span, width - WINDOW
        waits = [[], []]
        for number, flip in enumerate((3, 1, 2, 0)):
            slot = number % 2
            for copy in waits[slot]:
                copy.wait_send()
            at = flipped(scatter.plane, flip)

            @pl.loop(0, 3)
            def _(index):
                some = pl.ds(pl.multiple_of(index * (width // 3), width // 3), width // 3)
                head = mm(grads_t[some, :], acts[at, :, :span])
                tail = mm(attended_t[some, :], windows[at])
                room[slot, some, :high] = low_bits(head[:, :high])
                room[slot, some, high:low] = low_bits(head[:, high:low] + tail[:, : low - high])
                room[slot, some, low:] = low_bits(tail[:, low - high :])

            scatter.clear(0, flip)
            rows_of = deep_rows(room, slot, deep)
            waits[slot] = [scatter.term(2, flip, back, rows_of, True) for back in (2, 1, 3, 0)]
            scatter.tick(1)
        early, late = (2, 1), (3, 0)
        scatter.open(2, "sent", early)
        scatter.open(2, "kept", early)
        scatter.open(2, "kept", late)
        scatter.open(0, "line")
        scatter.open(2, "first", early)
        scatter.open(2, "sent", late)
        scatter.open(2, "second", early)
        scatter.open(1, "line")
        scatter.open(2, "first", late)
        scatter.open(2, "second", late)
        scatter.open(2, "line")
        for part in range(4):
            loads[part].wait()
            term = matmul_nt(acts[part, :, :span], weights[part % 2])
            total[...] = term if part == 0 else total[...] + term
            if part < 2:
                loads.append(load(part + 2))
            scatter.tick(4)
        begin_copy.wait()

        def turn(at, group):
            grad = total[at, :]
            hat, scale = centred(start[at, :])
            add_group(slot_sums.at[4], group, grad)
            add_group(slot_sums.at[5], group, grad * hat)
            grad = grad * (1.0 + group_row(table, group, 1, width))
            middle_grad[at, :] = middle_grad[at, :] + norm_back(hat, scale, grad)

        for part in range(4):

            @pl.loop(0, rows // 256)
            def _(index):
                begin = part * (rows // 4) + index * 64
                turn(pl.ds(pl.multiple_of(begin, 64), 64), begin // 128)

            if part == 1:
                scatter.tick(2)
        for slot in range(2):
            for copy in waits[slot]:
                copy.wait_send()

    pl.run_scoped(
        last,
        pltpu.VMEM((2, width, span), jnp.bfloat16),
        pltpu.VMEM((width, rows), jnp.bfloat16),
        pltpu.VMEM((rows, width), jnp.float32),
        pltpu.VMEM((rows, width), jnp.float32),
    )
    mod_room[...] = jnp.zeros_like(mod_room)
    slot_count, part = plane_out.shape[1:]
    for slot in range(slot_count):
        for number, kind in enumerate((4, 5, 0, 1, 2, 3)):
            value = jnp.where(group_slots[...] == slot, slot_sums[kind], 0.0)
            value = wide(low_bits(jnp.sum(value, axis=0, keepdims=True)))
            mod_room[slot : slot + 1, number * width : (number + 1) * width] = value
    reach = strip.shape[1]
    for plane in range(4):
        shift = plane * part % 128
        begin = plane * part - shift
        moved = mod_room[:, begin : begin + reach]
        strip[...] = pltpu.roll(moved, reach - shift, 1) if shift else moved
        plane_out[plane] = strip[:slot_count, :part]
    plane_trade = (plane_out, plane_land, plane_sems.at[0], plane_sems.at[1])
    line_trade = (plane_land, line_land, line_sems.at[0], line_sems.at[1])
    trade_along("dp", *plane_trade, True)
    while len(scatter.queue) > 12:
        scatter.tick()
    trade_along("dp", *plane_trade, False)
    trade_along("fsdp", *line_trade, True, True)
    scatter.drain()
    trade_along("fsdp", *line_trade, False, True)


def backward(away_ins, near_ins, slots, table, bias, group_slots):
    middle = near_ins[0]
    rows, width = middle.shape
    deep = width // 8
    part = 6 * width // 4
    vmem, away = pl.BlockSpec(memory_space=pltpu.VMEM), pl.BlockSpec(memory_space=pl.ANY)
    land = shaped((32, deep, width), jnp.bfloat16)
    return pl.pallas_call(
        backward_kernel,
        out_shape=[
            land,
            land,
            land,
            shaped((rows, width), jnp.bfloat16),
            shaped((rows, width)),
            shaped((6, 8, width)),
            shaped((8, width)),
            shaped((8, width)),
            shaped((1, 3 * width)),
            shaped((deep, width)),
            shaped((deep, width)),
            shaped((deep, width)),
            shaped((8, 4, 4, part)),
        ],
        in_specs=[away] * 9 + [vmem] * 10,
        out_specs=[away] * 3 + [vmem] * 10,
        scratch_shapes=[
            pltpu.VMEM((4, rows, WINDOW), jnp.bfloat16),
            pltpu.VMEM((2, 4, 4, deep, width), jnp.bfloat16),
            pltpu.VMEM((2, deep, width), jnp.bfloat16),
            pltpu.VMEM((2, width, width), jnp.bfloat16),
            pltpu.VMEM((4, rows, width), jnp.bfloat16),
            pltpu.VMEM((rows, width), jnp.bfloat16),
            pltpu.VMEM((width, rows), jnp.bfloat16),
            pltpu.VMEM((rows, width), jnp.bfloat16),
            pltpu.SemaphoreType.DMA((3, 32)),
            pltpu.SemaphoreType.DMA((3, 32)),
            pltpu.SemaphoreType.DMA((2,)),
            pltpu.SemaphoreType.DMA((2,)),
            pltpu.SemaphoreType.DMA((4,)),
            pltpu.VMEM((8, 4 * part), jnp.float32),
            pltpu.VMEM((8, -(-part // 128) * 128), jnp.float32),
            pltpu.VMEM((4, 4, part), jnp.float32),
            pltpu.VMEM((4, 4, part), jnp.float32),
            pltpu.SemaphoreType.DMA((2, 4)),
            pltpu.SemaphoreType.DMA((2, 8)),
        ],
        compiler_params=pltpu.CompilerParams(
            collective_id=5, has_side_effects=True, vmem_limit_bytes=62 * 2**20
        ),
        cost_estimate=pl.CostEstimate(
            flops=2 * 30 * rows * width * width, bytes_accessed=10**8, transcendentals=0
        ),
    )(
        *away_ins,
        *near_ins,
        slots.reshape(rows, 1),
        slots.reshape(1, rows),
        table,
        bias,
        group_slots,
    )


def code_parts(width):
    quarter = width // 4
    exponent = jnp.arange(quarter, dtype=jnp.float32) / quarter
    frequency = 1.0 / 10000.0**exponent
    angle = jnp.arange(32, dtype=jnp.float32)[:, None] * frequency[None, :]
    half = jnp.concatenate([jnp.sin(angle), jnp.cos(angle)], axis=1)
    none = jnp.zeros_like(half)
    left = jnp.concatenate(
        [jnp.concatenate([half, none], axis=1), jnp.concatenate([none, half], axis=1)], axis=0
    )
    parts = []
    for _ in range(3):
        part = lax.reduce_precision(left, 8, 7)
        parts.append(part.astype(jnp.bfloat16))
        left = left - part
    return jnp.concatenate(parts, axis=0)


def box_device(
    tokens,
    condition,
    kept_index,
    segment,
    grid_side,
    ada_weight,
    ada_bias,
    attn_weight,
    attn_bias,
    proj_weight,
    out_bias,
    up_weight,
    up_bias,
    down_weight,
    grad_out,
):
    rows, width = tokens.shape
    slot_count = condition.shape[0]
    core = place()[2]
    columns = attn_weight.shape[1]
    turned = down_weight.T.reshape(2, up_weight.shape[0], down_weight.shape[0])
    mine, theirs = pick(turned, core), pick(turned, 1 - core)
    arrived = swap(theirs, "core")
    down_shard = jnp.where(
        core == 0,
        jnp.concatenate([mine, arrived], axis=1),
        jnp.concatenate([arrived, mine], axis=1),
    )
    silu_cond, silu_back = jax.vjp(jax.nn.silu, condition.astype(jnp.float32))
    silu_bf = silu_cond.astype(jnp.bfloat16)
    vectors = (ada_bias, attn_bias, out_bias, up_bias)
    flat = jnp.concatenate(vectors)
    flat = jnp.pad(flat, (0, 2048 - flat.shape[0])).reshape(16, 128)
    cut = silu_bf.reshape(slot_count, 8, -1).transpose(1, 0, 2)
    cut = jnp.pad(cut, ((0, 0), (0, 16 - slot_count), (0, 0)))
    joined_whole, up_start, down_start, silu_land, flat_land, modulation = opening(
        cut,
        flat,
        ada_weight,
        (jnp.concatenate([attn_weight, proj_weight], axis=1), up_weight, down_shard),
    )
    silu_part = silu_land[:, :slot_count].reshape(32 * slot_count, -1)
    flat_land = flat_land.reshape(32, -1)
    found, begin = [], 0
    for vector in vectors:
        found.append(flat_land[:, begin : begin + vector.shape[0]].reshape(-1))
        begin += vector.shape[0]
    ada_bfull, attn_bfull, out_bfull, up_bfull = found
    group_slots = segment.reshape(rows // 128, 128)[:, 0]
    group_column = jnp.pad(group_slots, (0, 8 - rows // 128), constant_values=-1)[:, None]
    group_sides = jnp.sum(
        jnp.where(group_slots[:, None] == jnp.arange(slot_count)[None, :], grid_side[None, :], 0), axis=1
    )
    side_rows = jnp.repeat(group_sides, 128)
    places = jnp.stack([kept_index % side_rows, kept_index // side_rows], axis=1)
    zeros = jnp.zeros((width,), jnp.bfloat16)
    joined_bias = jnp.concatenate([attn_bfull[:width], zeros, attn_bfull[width:]])
    out_bias_f = out_bfull.astype(jnp.float32)
    (
        up_whole,
        down_whole,
        joined,
        start,
        table,
        normed_t,
        attended_t,
        normed2_t,
        stats,
        branch1,
        middle,
        hidden,
        before,
    ) = forward(
        tokens,
        places,
        code_parts(width),
        segment,
        group_column,
        modulation,
        ada_bfull.astype(jnp.float32)[None],
        (
            joined_bias.astype(jnp.float32)[None],
            out_bias_f[None, :width],
            up_bfull.astype(jnp.float32).reshape(4, 1, -1),
        ),
        (joined_whole, up_start, down_start),
    )
    wholes = [whole.reshape(4, width, width) for whole in (joined_whole, up_whole, down_whole)]
    (
        _,
        _,
        _,
        mixed,
        tokens_grad,
        slot_sums,
        branch_sums,
        pre_sums,
        joined_sums,
        down_total,
        up_weight_grad,
        joined_total,
        line_land,
    ) = backward(
        (hidden, before, joined, *wholes, normed_t, attended_t, start),
        (middle, grad_out, branch1, normed2_t, stats),
        segment,
        table,
        out_bias_f[None, width:],
        group_column,
    )
    half = down_total.shape[1] // 2
    cut = down_total.reshape(-1, 2, half).transpose(1, 0, 2)
    mine, theirs = pick(cut, core), pick(cut, 1 - core)
    arrived = swap(theirs, "core")
    down_weight_grad = jnp.where(
        core == 0, jnp.concatenate([mine, arrived]), jnp.concatenate([arrived, mine])
    ).T
    cut = line_land.transpose(1, 0, 2, 3).reshape(32 * slot_count, -1).astype(jnp.bfloat16)
    joined_sums = joined_sums[0]
    terms = (
        jnp.concatenate([joined_sums[:width], joined_sums[2 * width :]]),
        branch_sums[:2].reshape(-1),
        pre_sums[:4].reshape(-1),
    )
    ada_weight_grad, ada_bias_grad, silu_grad, bias_grads = modulation_ends(cut, silu_part, ada_weight, terms)
    attn_bias_grad, out_bias_grad, up_bias_grad = bias_grads
    return (
        mixed,
        tokens_grad,
        silu_back(silu_grad)[0],
        ada_weight_grad,
        ada_bias_grad,
        joined_total[:, :columns],
        attn_bias_grad,
        joined_total[:, columns:],
        out_bias_grad,
        up_weight_grad,
        up_bias_grad,
        down_weight_grad,
    )


def per_device(
    tokens,
    condition,
    kept_index,
    segment,
    grid_side,
    ada_weight,
    ada_bias,
    attn_weight,
    attn_bias,
    proj_weight,
    out_bias,
    up_weight,
    up_bias,
    down_weight,
    grad_out,
):
    if on_box():
        return box_device(
            tokens,
            condition,
            kept_index,
            segment,
            grid_side,
            ada_weight,
            ada_bias,
            attn_weight,
            attn_bias,
            proj_weight,
            out_bias,
            up_weight,
            up_bias,
            down_weight,
            grad_out,
        )
    model_width = tokens.shape[1]
    slot_count = condition.shape[0]
    planes = lax.axis_size("dp")
    joined_w, up_w, down_w = gather_blocks(attn_weight, proj_weight, up_weight, down_weight)
    attn_columns = attn_weight.shape[1]
    slot_ids = jnp.arange(slot_count, dtype=jnp.int32)
    same_slot = segment[:, None] == slot_ids[None, :]
    slot_table = same_slot.astype(jnp.float32)
    side_rows = jnp.sum(jnp.where(same_slot, grid_side[None, :], 0), axis=1)
    start = tokens.astype(jnp.float32) + position_code(kept_index, side_rows, model_width)
    condition_f = condition.astype(jnp.float32)
    silu_cond, silu_back = jax.vjp(jax.nn.silu, condition_f)
    silu_bf = silu_cond.astype(jnp.bfloat16)
    silu_all, (ada_bfull, attn_bfull, out_bfull, up_bfull) = gather_small(
        silu_bf, (ada_bias, attn_bias, out_bias, up_bias)
    )
    modulation, silu_part = modulate_slots(silu_all, ada_weight, ada_bfull)
    mod_rows = jnp.dot(
        slot_table, modulation, precision=lax.Precision.HIGHEST, preferred_element_type=jnp.float32
    )
    shift_one, scale_one, gate_one, shift_two, scale_two, gate_two = jnp.split(mod_rows, 6, axis=1)
    normed1, norm1_back = jax.vjp(norm_modulate, start, shift_one, scale_one)
    normed1_bf = normed1.astype(jnp.bfloat16)
    projected = jnp.concatenate(
        [
            jnp.dot(normed1_bf, joined_w[part, :, :attn_columns], preferred_element_type=jnp.float32)
            for part in range(planes)
        ],
        axis=1,
    )
    proj_full = joined_w[:, :, attn_columns:].transpose(1, 0, 2).reshape(model_width, model_width)
    attn_bias_f = attn_bfull.astype(jnp.float32)
    query_bf = (projected[:, :model_width] + attn_bias_f[:model_width]).astype(jnp.bfloat16)
    key_bf = projected[:, model_width : 2 * model_width].astype(jnp.bfloat16)
    value_bf = (projected[:, 2 * model_width :] + attn_bias_f[model_width:]).astype(jnp.bfloat16)
    attended, log_totals = attend_forward(query_bf, key_bf, value_bf, segment, HEADS)
    attended_bf = attended.astype(jnp.bfloat16)
    out_bias_f = out_bfull.astype(jnp.float32)
    branch1 = (
        jnp.dot(attended_bf, proj_full, preferred_element_type=jnp.float32)
        + out_bias_f[:model_width]
    )
    middle = start + gate_one * branch1
    normed2, norm2_back = jax.vjp(norm_modulate, middle, shift_two, scale_two)
    normed2_bf = normed2.astype(jnp.bfloat16)
    hidden_parts, gelu_parts = [], []
    up_bias_f = up_bfull.astype(jnp.float32).reshape(planes, -1)
    branch2 = out_bias_f[model_width:]
    for part in range(planes):
        hidden_pre = (
            jnp.dot(normed2_bf, up_w[part], preferred_element_type=jnp.float32) + up_bias_f[part]
        )
        hidden_act, gelu_back = jax.vjp(partial(jax.nn.gelu, approximate=True), hidden_pre)
        hidden_parts.append(hidden_act.astype(jnp.bfloat16))
        gelu_parts.append(gelu_back)
        branch2 = branch2 + matmul_nt(hidden_parts[part], down_w[part])
    mixed = (middle + gate_two * branch2).astype(jnp.bfloat16)
    out_grad = grad_out.astype(jnp.float32)
    grad_gate_two = out_grad * branch2
    grad_branch2 = (out_grad * gate_two).astype(jnp.bfloat16)
    down_weight_grad = scatter_whole(matmul_tn(jnp.concatenate(hidden_parts, axis=1), grad_branch2))
    pre_parts = []
    for part in range(planes):
        hidden_grad = jnp.dot(grad_branch2, down_w[part], preferred_element_type=jnp.float32)
        pre_parts.append(gelu_parts[part](hidden_grad)[0].astype(jnp.bfloat16))
    pre_grad = jnp.stack(pre_parts)
    (up_weight_grad,) = scatter_rows([(normed2_bf, pre_grad)])
    up_bias_term = jnp.sum(pre_grad, axis=1, dtype=jnp.float32).reshape(-1)
    normed2_grad = sum(matmul_nt(pre_parts[part], up_w[part]) for part in range(planes))
    middle_part, grad_shift_two, grad_scale_two = norm2_back(normed2_grad)
    middle_grad = out_grad + middle_part
    grad_gate_one = middle_grad * branch1
    grad_branch1 = (middle_grad * gate_one).astype(jnp.bfloat16)
    attended_grad = matmul_nt(grad_branch1, proj_full).astype(jnp.bfloat16)
    query_grad, key_grad, value_grad = attend_backward(
        query_bf, key_bf, value_bf, attended_grad, segment, log_totals, HEADS
    )
    query_grad_bf = query_grad.astype(jnp.bfloat16)
    value_grad_bf = value_grad.astype(jnp.bfloat16)
    joined_grad = jnp.concatenate(
        [query_grad_bf, key_grad.astype(jnp.bfloat16), value_grad_bf], axis=1
    )
    joined_parts = by_columns(joined_grad, planes)
    attn_weight_grad, proj_weight_grad = scatter_rows(
        [(normed1_bf, joined_parts), (attended_bf, by_columns(grad_branch1, planes))]
    )
    attn_bias_term = jnp.concatenate(
        [
            jnp.sum(query_grad_bf, axis=0, dtype=jnp.float32),
            jnp.sum(value_grad_bf, axis=0, dtype=jnp.float32),
        ]
    )
    normed1_grad = sum(
        matmul_nt(joined_parts[part], joined_w[part, :, :attn_columns]) for part in range(planes)
    )
    start_part, grad_shift_one, grad_scale_one = norm1_back(normed1_grad)
    tokens_grad = middle_grad + start_part
    mod_rows_grad = jnp.concatenate(
        [
            grad_shift_one,
            grad_scale_one,
            grad_gate_one,
            grad_shift_two,
            grad_scale_two,
            grad_gate_two,
        ],
        axis=1,
    )
    modulation_grad = lax.dot_general(
        slot_table,
        mod_rows_grad,
        (((0,), (0,)), ((), ())),
        precision=lax.Precision.HIGHEST,
        preferred_element_type=jnp.float32,
    ).astype(jnp.bfloat16)
    out_bias_term = jnp.concatenate(
        [
            jnp.sum(grad_branch1, axis=0, dtype=jnp.float32),
            jnp.sum(grad_branch2, axis=0, dtype=jnp.float32),
        ]
    )
    ada_weight_grad, ada_bias_grad, silu_grad, bias_grads = modulation_back(
        modulation_grad, silu_part, ada_weight, (attn_bias_term, out_bias_term, up_bias_term)
    )
    attn_bias_grad, out_bias_grad, up_bias_grad = bias_grads
    condition_grad = silu_back(silu_grad)[0]
    return (
        mixed,
        tokens_grad,
        condition_grad,
        ada_weight_grad,
        ada_bias_grad,
        attn_weight_grad,
        attn_bias_grad,
        proj_weight_grad,
        out_bias_grad,
        up_weight_grad,
        up_bias_grad,
        down_weight_grad,
    )


def solution(mesh):
    return jax.shard_map(
        per_device,
        mesh=mesh,
        in_specs=(
            P(("dp", "fsdp"), None),
            P(("dp", "fsdp"), None),
            P(("dp", "fsdp")),
            P(("dp", "fsdp")),
            P(("dp", "fsdp")),
            P("fsdp", "dp"),
            P(("dp", "fsdp")),
            P("fsdp", "dp"),
            P(("dp", "fsdp")),
            P("fsdp", "dp"),
            P(("dp", "fsdp")),
            P("fsdp", "dp"),
            P(("dp", "fsdp")),
            P("fsdp", "dp"),
            P(("dp", "fsdp"), None),
        ),
        out_specs=(
            P(("dp", "fsdp"), None),
            P(("dp", "fsdp"), None),
            P(("dp", "fsdp"), None),
            P("fsdp", "dp"),
            P(("dp", "fsdp")),
            P("fsdp", "dp"),
            P(("dp", "fsdp")),
            P("fsdp", "dp"),
            P(("dp", "fsdp")),
            P("fsdp", "dp"),
            P(("dp", "fsdp")),
            P("fsdp", "dp"),
        ),
        check_vma=False,
    )
```
